32 devices in a mesh: dp: 8 (over y, x, core), mp: 4 (over z).
Axes of the slice: x: 2, y: 2, z: 4, core: 2. Of those that a mesh axis runs over, the one named last changes fastest.
Arguments:
- answers: bfloat16 [32, 32, 1024], P('dp'), may hold values from -6 to 6
- targets: int32 [32, 32], P('dp'), may hold values from 0 to 25599
- doc_scores: float32 [32, 8], P('dp'), may hold values from -6 to 6
- memory: bfloat16 [256, 400, 1024], P('dp', 'mp'), may hold values from -6 to 6
- lengths: int32 [256], P('dp'), may hold values from 1 to 400, as said below
- self_query: bfloat16 [1024, 1024], P('dp', 'mp'), may hold values from -0.1875 to 0.1875
- self_key: bfloat16 [1024, 1024], P('dp', 'mp'), may hold values from -0.1875 to 0.1875
- self_value: bfloat16 [1024, 1024], P('dp', 'mp'), may hold values from -0.1875 to 0.1875
- query_bias: bfloat16 [16, 64], P('mp', 'dp'), may hold values from -2 to 2
- value_bias: bfloat16 [16, 64], P('mp', 'dp'), may hold values from -2 to 2
- self_output: bfloat16 [1024, 1024], P('mp', 'dp'), may hold values from -0.375 to 0.375
- output_bias: bfloat16 [1024], P('dp'), may hold values from -2 to 2
- first_gain: bfloat16 [1024], P('dp'), may hold values from 0.5 to 1.5
- first_shift: bfloat16 [1024], P('dp'), may hold values from -2 to 2
- cross_query: bfloat16 [1024, 1024], P('dp', 'mp'), may hold values from -0.1875 to 0.1875
- crossq_bias: bfloat16 [16, 64], P('mp', 'dp'), may hold values from -2 to 2
- cross_key: bfloat16 [1024, 1024], P(('dp', 'mp')), may hold values from -0.1875 to 0.1875
- cross_value: bfloat16 [1024, 1024], P(('dp', 'mp')), may hold values from -0.1875 to 0.1875
- crossv_bias: bfloat16 [1024], P(('dp', 'mp')), may hold values from -2 to 2
- cross_output: bfloat16 [1024, 1024], P('mp', 'dp'), may hold values from -0.5 to 0.5
- crosso_bias: bfloat16 [1024], P('dp'), may hold values from -2 to 2
- second_gain: bfloat16 [1024], P('dp'), may hold values from 0.5 to 1.5
- second_shift: bfloat16 [1024], P('dp'), may hold values from -2 to 2
- expand_weight: bfloat16 [1024, 4096], P('dp', 'mp'), may hold values from -0.1875 to 0.1875
- expand_bias: bfloat16 [32, 128], P('mp', 'dp'), may hold values from -2 to 2
- shrink_weight: bfloat16 [4096, 1024], P('mp', 'dp'), may hold values from -0.09375 to 0.09375
- shrink_bias: bfloat16 [1024], P('dp'), may hold values from -2 to 2
- third_gain: bfloat16 [1024], P('dp'), may hold values from 0.5 to 1.5
- third_shift: bfloat16 [1024], P('dp'), may hold values from -2 to 2
- word_table: bfloat16 [25600, 1024], P('mp', 'dp'), may hold values from -0.375 to 0.375
Outputs:
- question_loss: float32 [32], P('dp')
- answer_grad: float32 [32, 32, 1024], P('dp')
- memory_grad: float32 [256, 400, 1024], P('dp', 'mp')
- self_query_grad: float32 [1024, 1024], P('dp', 'mp')
- self_key_grad: float32 [1024, 1024], P('dp', 'mp')
- self_value_grad: float32 [1024, 1024], P('dp', 'mp')
- query_bias_grad: float32 [16, 64], P('mp', 'dp')
- value_bias_grad: float32 [16, 64], P('mp', 'dp')
- self_output_grad: float32 [1024, 1024], P('mp', 'dp')
- output_bias_grad: float32 [1024], P('dp')
- first_gain_grad: float32 [1024], P('dp')
- first_shift_grad: float32 [1024], P('dp')
- cross_query_grad: float32 [1024, 1024], P('dp', 'mp')
- crossq_bias_grad: float32 [16, 64], P('mp', 'dp')
- cross_key_grad: float32 [1024, 1024], P(('dp', 'mp'))
- cross_value_grad: float32 [1024, 1024], P(('dp', 'mp'))
- crossv_bias_grad: float32 [1024], P(('dp', 'mp'))
- cross_output_grad: float32 [1024, 1024], P('mp', 'dp')
- crosso_bias_grad: float32 [1024], P('dp')
- second_gain_grad: float32 [1024], P('dp')
- second_shift_grad: float32 [1024], P('dp')
- expand_weight_grad: float32 [1024, 4096], P('dp', 'mp')
- expand_bias_grad: float32 [32, 128], P('mp', 'dp')
- shrink_weight_grad: float32 [4096, 1024], P('mp', 'dp')
- shrink_bias_grad: float32 [1024], P('dp')
- third_gain_grad: float32 [1024], P('dp')
- third_shift_grad: float32 [1024], P('dp')
The draws below stay inside these ranges and needn't reach their ends.
Inputs may be any that keep to these rules, and one draw needn't show every extreme that they name: `lengths`: slot j of a row's memory is used when j < its length; some row has all 400 slots used.
All inputs are finite; a program needn't handle non-finite values.
Results may differ from the reference program's by a relative error of at most 0.02.
Values may be sent and summed in bfloat16 or wider, within the bound.
A program may use at most 320 MiB of HBM per device.

```python
import math
import jax
import jax.numpy as jnp
import numpy as np
from jax import lax

D = 1024
H = 16
HD = 64
FF = 4096
VOCAB = 25600
TOK = 32
MEM = 400
K = 8
Q = 32
ROWS = 256
RDEV = 32
PIECE = 4


def draw_lengths(key, part):
    key_full, key_short = jax.random.split(key, 2)
    short = jax.random.randint(key_short, (ROWS,), MEM // 4 - MEM // 16, MEM // 4 + MEM // 16 + 1)
    filled = jax.random.randint(key_full, (ROWS,), 0, 3) == 0
    drawn = jnp.where(filled, MEM, short)
    return drawn.at[0].set(MEM).astype(jnp.int32)


def set_ends(values, stream_key, smallest, high):
    longest = values.shape.index(max(values.shape))
    spots = []
    for shift in (0, 1):
        where = [jax.random.randint(jax.random.fold_in(stream_key, axis), (), 0, length) for axis, length in enumerate(values.shape)]
        where[longest] = (where[longest] + shift) % values.shape[longest]
        spots.append(tuple(where))
    return values.at[spots[0]].set(smallest).at[spots[1]].set(high)


def block_levels(rng, extent, pieces, smallest, largest):
    factor_of = 1.0
    for position, shards_of in pieces:
        heights = jax.random.uniform(jax.random.fold_in(jax.random.fold_in(rng, 6), position), (shards_of,), jnp.float32, smallest / len(pieces), largest / len(pieces))
        factor_of = factor_of * jnp.repeat(jnp.exp(heights), extent[position] // shards_of).reshape((-1,) + (1,) * (len(extent) - 1 - position))
    return factor_of


def rank_table(count, skew):
    loads = [(1 << 20) // math.isqrt(grade ** skew) + 1 for grade in range(1, count + 1)]
    deviation = 1 + sum(loads) // (1 << 30)
    return np.cumsum(np.array([max(1, weight // deviation) for weight in loads]))


def ranked_ids(own_key, dims, number_of, skew):
    listing = rank_table(number_of, skew)
    pick = jax.random.randint(jax.random.fold_in(own_key, 1), dims, 0, int(listing[number_of - 1]))
    standing = jnp.searchsorted(jnp.asarray(listing, jnp.int32), pick, side="right")
    return jax.random.permutation(jax.random.fold_in(own_key, 2), number_of)[standing].astype(jnp.int32)


def scatter_about(key, shape, scale, most, shards=(), kind=jnp.bfloat16):
    values = scale * jax.random.normal(key, shape, jnp.float32)
    if shards:
        values = values * block_levels(key, shape, shards, -0.22, 0.18)
    return jnp.clip(values, -most, most).astype(kind)


def setup_inputs(seed: int = 0) -> dict:
    seeds = jax.random.split(jax.random.key(seed), 31)
    return {
        "answers": scatter_about(seeds[0], (Q, TOK, D), 1.0, 6.0, ((0, 8),)),
        "targets": set_ends(ranked_ids(seeds[1], (Q, TOK), VOCAB, 2), jax.random.fold_in(seeds[1], 3), 0, VOCAB - 1).astype(jnp.int32),
        "doc_scores": scatter_about(seeds[2], (Q, K), 1.0, 6.0, ((0, 8),), jnp.float32),
        "memory": scatter_about(seeds[3], (ROWS, MEM, D), 1.0, 6.0, ((0, 8), (1, 4))),
        "lengths": draw_lengths(jax.random.fold_in(seeds[30], 71), 0),
        "self_query": scatter_about(seeds[5], (D, D), D ** -0.5, 0.1875, ((0, 8), (1, 4))),
        "self_key": scatter_about(seeds[6], (D, D), D ** -0.5, 0.1875, ((0, 8), (1, 4))),
        "self_value": scatter_about(seeds[7], (D, D), D ** -0.5, 0.1875, ((0, 8), (1, 4))),
        "query_bias": scatter_about(seeds[8], (H, HD), 0.3, 2.0, ((0, 4), (1, 8))),
        "value_bias": scatter_about(seeds[9], (H, HD), 0.3, 2.0, ((0, 4), (1, 8))),
        "self_output": scatter_about(seeds[10], (D, D), (D // 4) ** -0.5, 0.375, ((0, 4), (1, 8))),
        "output_bias": scatter_about(seeds[11], (D,), 0.3, 2.0, ((0, 8),)),
        "first_gain": jnp.clip(1.0 + 0.1 * jax.random.normal(seeds[12], (D,), jnp.float32), 0.5, 1.5).astype(jnp.bfloat16),
        "first_shift": scatter_about(seeds[13], (D,), 0.3, 2.0, ((0, 8),)),
        "cross_query": scatter_about(seeds[14], (D, D), D ** -0.5, 0.1875, ((0, 8), (1, 4))),
        "crossq_bias": scatter_about(seeds[15], (H, HD), 0.3, 2.0, ((0, 4), (1, 8))),
        "cross_key": scatter_about(seeds[16], (D, D), D ** -0.5, 0.1875, ((0, 32),)),
        "cross_value": scatter_about(seeds[17], (D, D), D ** -0.5, 0.1875, ((0, 32),)),
        "crossv_bias": scatter_about(seeds[18], (D,), 0.3, 2.0, ((0, 32),)),
        "cross_output": scatter_about(seeds[19], (D, D), (D // 8) ** -0.5, 0.5, ((0, 4), (1, 8))),
        "crosso_bias": scatter_about(seeds[20], (D,), 0.3, 2.0, ((0, 8),)),
        "second_gain": jnp.clip(1.0 + 0.1 * jax.random.normal(seeds[21], (D,), jnp.float32), 0.5, 1.5).astype(jnp.bfloat16),
        "second_shift": scatter_about(seeds[22], (D,), 0.3, 2.0, ((0, 8),)),
        "expand_weight": scatter_about(seeds[23], (D, FF), D ** -0.5, 0.1875, ((0, 8), (1, 4))),
        "expand_bias": scatter_about(seeds[24], (FF // 128, 128), 0.3, 2.0, ((0, 4), (1, 8))),
        "shrink_weight": scatter_about(seeds[25], (FF, D), FF ** -0.5, 0.09375, ((0, 4), (1, 8))),
        "shrink_bias": scatter_about(seeds[26], (D,), 0.3, 2.0, ((0, 8),)),
        "third_gain": jnp.clip(1.0 + 0.1 * jax.random.normal(seeds[27], (D,), jnp.float32), 0.5, 1.5).astype(jnp.bfloat16),
        "third_shift": scatter_about(seeds[28], (D,), 0.3, 2.0, ((0, 8),)),
        "word_table": scatter_about(seeds[29], (VOCAB, D), (D // 4) ** -0.5, 0.375, ((0, 4), (1, 8))),
    }


@jax.custom_vjp
def low(v):
    return lax.optimization_barrier(v.astype(jnp.bfloat16)).astype(jnp.float32)

@jax.custom_vjp
def low_back(v):
    return v

def low_keep(v):
    return (low(v), None)

def low_pass(kept, grad):
    return (grad,)

def back_keep(v):
    return (v, None)

def back_low(kept, grad):
    return (low(grad),)
low.defvjp(low_keep, low_pass)
low_back.defvjp(back_keep, back_low)
EPS = 1e-05
NEG = -1e+30
SCALE = 0.125
HIGH = lax.Precision.HIGHEST

def product(former, latter):
    return jnp.matmul(former, latter, precision=HIGH)

def layer_norm(entries, norm_gain, norm_shift):
    center = entries - lax.optimization_barrier(jnp.mean(entries, axis=-1, keepdims=True))
    inverse = lax.rsqrt(lax.optimization_barrier(jnp.mean(center * center, axis=-1, keepdims=True)) + EPS)
    return center * inverse * norm_gain + norm_shift

def attend(queries, key_heads, value_heads, allowed):
    scores = jnp.einsum('rqhe,rkhe->rhqk', queries, key_heads, precision=HIGH)
    scores = low_back(jnp.where(allowed, scores, NEG))
    attn_probs = low(jax.nn.softmax(scores, axis=-1))
    context = jnp.einsum('rhqk,rkhe->rqhe', attn_probs, value_heads, precision=HIGH)
    return low_back(low(context))

def rows_forward(params, table_f, answer_rows, memory_rows, row_lengths, row_targets):
    self_query, self_key, self_value, query_bias, value_bias, self_output, output_bias, first_gain, first_shift, cross_query, crossq_bias, cross_key, cross_value, crossv_bias, cross_output, crosso_bias, second_gain, second_shift, expand_weight, expand_bias, shrink_weight, shrink_bias, third_gain, third_shift = params
    row_count = answer_rows.shape[0]
    heads_shape = (row_count, TOK, H, HD)
    inputs = low_back(answer_rows)
    queries = low_back(low((product(inputs, self_query) + query_bias.reshape(-1)) * SCALE)).reshape(heads_shape)
    self_keys = low_back(low(product(inputs, self_key))).reshape(heads_shape)
    self_values = low_back(low(product(inputs, self_value) + value_bias.reshape(-1))).reshape(heads_shape)
    causal = (lax.broadcasted_iota(jnp.int32, (TOK, TOK), 1) <= lax.broadcasted_iota(jnp.int32, (TOK, TOK), 0))[None, None]
    context = attend(queries, self_keys, self_values, causal).reshape(row_count, TOK, D)
    hidden_one = layer_norm(inputs + low_back(product(context, self_output)) + output_bias, first_gain, first_shift)
    cross_in = low(hidden_one)
    cross_queries = low_back(low((product(cross_in, cross_query) + crossq_bias.reshape(-1)) * SCALE)).reshape(heads_shape)
    memory_shape = (row_count, MEM, H, HD)
    memory_keys = low_back(low(product(memory_rows, cross_key))).reshape(memory_shape)
    memory_values = low_back(low(product(memory_rows, cross_value) + crossv_bias)).reshape(memory_shape)
    visible = lax.broadcasted_iota(jnp.int32, (row_count, 1, 1, MEM), 3) < row_lengths[:, None, None, None]
    context_two = attend(cross_queries, memory_keys, memory_values, visible).reshape(row_count, TOK, D)
    hidden_two = layer_norm(hidden_one + low_back(product(context_two, cross_output)) + crosso_bias, second_gain, second_shift)
    expanded = low_back(product(low(hidden_two), expand_weight) + expand_bias.reshape(-1))
    activated = low(jax.nn.gelu(expanded, approximate=False))
    hidden_three = layer_norm(hidden_two + low_back(product(activated, shrink_weight)) + shrink_bias, third_gain, third_shift)
    logits = low_back(jnp.einsum('rtd,vd->rtv', low(hidden_three), table_f, precision=HIGH))
    picked = jnp.take_along_axis(logits, row_targets[..., None], axis=-1)[..., 0]
    return picked - jax.nn.logsumexp(logits, axis=-1)

def slot_order():
    indices = jnp.arange(ROWS, dtype=jnp.int32)
    return indices % RDEV // PIECE * RDEV + indices // RDEV * PIECE + indices % PIECE

def reference(answers, targets, doc_scores, memory, lengths, self_query, self_key, self_value, query_bias, value_bias, self_output, output_bias, first_gain, first_shift, cross_query, crossq_bias, cross_key, cross_value, crossv_bias, cross_output, crosso_bias, second_gain, second_shift, expand_weight, expand_bias, shrink_weight, shrink_bias, third_gain, third_shift, word_table):
    params = jax.tree.map(lambda member: member.astype(jnp.float32), (self_query, self_key, self_value, query_bias, value_bias, self_output, output_bias, first_gain, first_shift, cross_query, crossq_bias, cross_key, cross_value, crossv_bias, cross_output, crosso_bias, second_gain, second_shift, expand_weight, expand_bias, shrink_weight, shrink_bias, third_gain, third_shift))
    table_f = word_table.astype(jnp.float32)
    answer_f = answers.astype(jnp.float32)
    memory_f = memory.astype(jnp.float32)
    order_idx = slot_order()
    owner_q = (order_idx // K).astype(jnp.int32)
    blocks = ROWS // RDEV

    def objective(weights, answer_in, memory_in):

        def block_fn(carry, items):
            memory_block, length_block, owner_block = items
            loglik = rows_forward(weights, table_f, answer_in[owner_block], memory_block, length_block, targets[owner_block])
            return (carry, loglik)
        unused_carry, loglik = lax.scan(jax.checkpoint(block_fn), jnp.zeros((), jnp.float32), (memory_in.reshape(blocks, RDEV, MEM, D), lengths.reshape(blocks, RDEV), owner_q.reshape(blocks, RDEV)))
        loglik = loglik.reshape(ROWS, TOK)[order_idx]
        joined = jax.nn.log_softmax(doc_scores, axis=1)[:, :, None] + loglik.reshape(Q, K, TOK)
        marginal = jax.nn.logsumexp(joined, axis=1)
        return (-jnp.sum(marginal), -lax.optimization_barrier(jnp.mean(marginal, axis=1)))
    unused_total, pullback, question_loss = jax.vjp(objective, params, answer_f, memory_f, has_aux=True)
    param_grads, answer_grad, memory_grad = pullback(jnp.ones((), jnp.float32))
    return (question_loss, answer_grad, memory_grad, param_grads[0], param_grads[1], param_grads[2], param_grads[3], param_grads[4], param_grads[5], param_grads[6], param_grads[7], param_grads[8], param_grads[9], param_grads[10], param_grads[11], param_grads[12], param_grads[13], param_grads[14], param_grads[15], param_grads[16], param_grads[17], param_grads[18], param_grads[19], param_grads[20], param_grads[21], param_grads[22], param_grads[23])
```

```python
import functools

import jax
import jax.numpy as jnp
from jax import lax
from jax.experimental import pallas as pl
from jax.experimental.pallas import tpu as pltpu
from jax.sharding import PartitionSpec as P

D = 1024
H = 16
HD = 64
TOK = 32
K = 8
G = 4
GH = 4
GC = GH * HD
GL = GH * TOK

EPS = 1e-05
NEG = -1e30
SCALE = 0.125
BF = jnp.bfloat16
F32 = jnp.float32
MESH = pl.DeviceIdType.MESH
VMEM_BYTES = 60 * 1024 * 1024


def product(former, latter):
    return jnp.dot(former, latter, preferred_element_type=F32)


def product_back(former, latter):
    return lax.dot_general(former, latter, (((1,), (1,)), ((), ())), preferred_element_type=F32)


def weight_grad(former, latter):
    return lax.dot_general(former, latter, (((0,), (0,)), ((), ())), preferred_element_type=F32)


def gelu_exact(entries):
    return jax.nn.gelu(entries, approximate=False)


def layer_norm(entries, norm_gain, norm_shift):
    center = entries - jnp.mean(entries, axis=-1, keepdims=True)
    inverse = lax.rsqrt(jnp.mean(center * center, axis=-1, keepdims=True) + EPS)
    normed = center * inverse
    return (normed * norm_gain + norm_shift, normed, inverse)


def norm_back(upstream, normed, inverse, norm_gain):
    scaled = upstream * norm_gain
    dentries = inverse * (
        scaled
        - jnp.mean(scaled, axis=-1, keepdims=True)
        - normed * jnp.mean(scaled * normed, axis=-1, keepdims=True)
    )
    return (dentries, jnp.sum(upstream * normed, axis=0), jnp.sum(upstream, axis=0))


class Exchange:
    def __init__(self, entries):
        self.dp_ways, self.mp_ways = lax.axis_size("dp"), lax.axis_size("mp")
        self.chips = self.dp_ways // 2
        self.ways = {"z": self.mp_ways, "chips": self.chips, "pair": 2, "dp": self.dp_ways}
        self.arrays = [entry[0] for entry in entries]
        self.kinds = [entry[1] for entry in entries]
        self.groups = [entry[2] for entry in entries]
        self.count = len(entries)
        shapes = []
        for array, kind, group in entries:
            shape = array.shape
            if kind == "gather":
                shape = (self.ways[group],) + shape
            elif kind == "move":
                shape = (self.ways[group] - 1,) + shape[1:]
            elif kind == "move1":
                shape = (self.ways[group] - 1, shape[0]) + shape[2:]
            elif kind == "near":
                shape = (self.dp_ways,) + shape
            elif kind == "nearswap":
                shape = (self.dp_ways,) + shape[1:]
            else:
                shape = (self.dp_ways, self.mp_ways) + shape
            shapes.append(jax.ShapeDtypeStruct(shape, array.dtype))
        self.shapes = shapes
        self.specs = [pl.BlockSpec(memory_space=pl.ANY)] * self.count
        dma = pltpu.SemaphoreType.DMA
        most = max(self.dp_ways, self.mp_ways)
        self.scratch = [dma((self.count, most)) for _ in range(6)] + [dma((self.count,))]

    def bind(self, ins, outs, sems):
        self.ins, self.outs = ins, outs
        self.zs, self.zr, self.cs, self.cr, self.ps, self.pr, self.own = sems
        dp, mp = lax.axis_index("dp"), lax.axis_index("mp")
        self.dp, self.mp = dp, mp
        self.parity, self.chip = lax.rem(dp, 2), dp // 2
        self.place = {"z": mp, "chips": self.chip, "pair": self.parity, "dp": dp}

    def device(self, group, j):
        if group == "z":
            return (self.dp, j)
        if group == "chips":
            return (2 * j + self.parity, self.mp)
        if group == "pair":
            return (self.dp - self.parity + j, self.mp)
        return (j, self.mp)

    def peer(self, group, off):
        return lax.rem(self.place[group] + off, self.ways[group])

    def remote(self, source, target, send, recv, device):
        return pltpu.make_async_remote_copy(
            src_ref=source,
            dst_ref=target,
            send_sem=send,
            recv_sem=recv,
            device_id=device,
            device_id_type=MESH,
        )

    def meet(self):
        needed = set()
        for kind, group in zip(self.kinds, self.groups):
            if kind in ("near", "nearswap", "wide"):
                needed |= {"chips", "pair"}
                if kind == "wide":
                    needed.add("z")
            else:
                needed.add(group)
        barrier = pltpu.get_barrier_semaphore()
        total = 0
        for group in sorted(needed):
            for off in range(1, self.ways[group]):
                pl.semaphore_signal(
                    barrier,
                    inc=1,
                    device_id=self.device(group, self.peer(group, off)),
                    device_id_type=MESH,
                )
                total += 1
        pl.semaphore_wait(barrier, total)

    def first(self, i):
        kind, group = self.kinds[i], self.groups[i]
        ref, out = self.ins[i], self.outs[i]
        copies = []
        if kind in ("near", "nearswap"):
            return copies
        if kind == "wide":
            group, slot = "z", out.at[self.dp, self.mp]
        for off in range(1, self.ways[group]):
            peer = self.peer(group, off)
            if kind == "wide":
                source, target = ref, slot
            elif kind == "gather":
                source, target = ref, out.at[self.place[group]]
            elif kind == "move":
                source, target = ref.at[peer], out.at[off - 1]
            else:
                source, target = ref.at[:, peer], out.at[off - 1]
            copies.append(
                self.remote(
                    source,
                    target,
                    self.zs.at[i, off - 1],
                    self.zr.at[i, off - 1],
                    self.device(group, peer),
                )
            )
        return copies

    def local(self, i):
        kind, group = self.kinds[i], self.groups[i]
        ref, out = self.ins[i], self.outs[i]
        if kind == "wide":
            source, target = ref, out.at[self.dp, self.mp]
        elif kind == "gather":
            source, target = ref, out.at[self.place[group]]
        elif kind in ("near", "nearswap"):
            source, target = self.mine(i), out.at[self.dp]
        else:
            return None
        return pltpu.make_async_copy(source, target, self.own.at[i])

    def mine(self, i):
        kind = self.kinds[i]
        if kind == "wide":
            return self.outs[i].at[self.dp]
        return self.ins[i].at[self.chip] if kind == "nearswap" else self.ins[i]

    def spread(self, i):
        copies = []
        for off in range(1, self.chips):
            peer = self.peer("chips", off)
            source = self.ins[i].at[peer] if self.kinds[i] == "nearswap" else self.mine(i)
            copies.append(
                self.remote(
                    source,
                    self.outs[i].at[self.dp],
                    self.cs.at[i, off - 1],
                    self.cr.at[i, off - 1],
                    self.device("chips", peer),
                )
            )
        return copies

    def hand(self, i, off):
        owner = 2 * lax.rem(self.chip + self.chips - off, self.chips) + self.parity
        return self.remote(
            self.mine(i) if off == 0 else self.outs[i].at[owner],
            self.outs[i].at[owner],
            self.ps.at[i, off],
            self.pr.at[i, off],
            self.device("pair", 1 - self.parity),
        )

    def begin(self):
        self.meet()
        for i in range(self.count):
            for copy in self.first(i):
                copy.start()
            if self.kinds[i] in ("near", "nearswap"):
                for copy in self.spread(i):
                    copy.start()
                self.hand(i, 0).start()
        for i in range(self.count):
            local = self.local(i)
            if local is not None:
                local.start()

    def finish(self):
        shared = [i for i in range(self.count) if self.kinds[i] in ("near", "nearswap", "wide")]
        for i in shared:
            if self.kinds[i] == "wide":
                for copy in self.first(i):
                    copy.wait()
                self.local(i).wait()
                for copy in self.spread(i):
                    copy.start()
                self.hand(i, 0).start()
        for i in shared:
            for off, copy in enumerate(self.spread(i), 1):
                copy.wait_recv()
                self.hand(i, off).start()
        for i in range(self.count):
            if i in shared:
                for copy in self.spread(i):
                    copy.wait_send()
                for off in range(self.chips):
                    self.hand(i, off).wait()
                if self.kinds[i] != "wide":
                    self.local(i).wait()
            else:
                for copy in self.first(i):
                    copy.wait()
                local = self.local(i)
                if local is not None:
                    local.wait()


def exchange_kernel(plan, *refs):
    count = plan.count
    plan.bind(refs[:count], refs[count : 2 * count], refs[2 * count :])
    plan.begin()
    plan.finish()


def exchange(entries, cid):
    plan = Exchange(entries)
    return pl.pallas_call(
        functools.partial(exchange_kernel, plan),
        out_shape=plan.shapes,
        in_specs=plan.specs,
        out_specs=plan.specs,
        scratch_shapes=plan.scratch,
        compiler_params=pltpu.CompilerParams(collective_id=cid, has_side_effects=True),
        name=f"exchange_{cid}",
    )(*plan.arrays)


def added(array, received, group):
    place = {
        "z": lax.axis_index("mp"),
        "chips": lax.axis_index("dp") // 2,
        "pair": lax.rem(lax.axis_index("dp"), 2),
    }[group]
    axis = 1 if group == "pair" else 0
    own = lax.dynamic_index_in_dim(array, place, axis, keepdims=False)
    return own.astype(F32) + jnp.sum(received.astype(F32), axis=0)


def beside(plan, kernel, inputs, outputs, scratches, *refs):
    n = plan.count
    first, last = pl.program_id(0) == 0, pl.program_id(0) == pl.num_programs(0) - 1
    ins = refs[:inputs]
    sends = refs[inputs : inputs + n]
    outs = refs[inputs + n : inputs + n + outputs]
    lands = refs[inputs + n + outputs : inputs + 2 * n + outputs]
    own = refs[inputs + 2 * n + outputs : inputs + 2 * n + outputs + scratches]
    plan.bind(sends, lands, refs[inputs + 2 * n + outputs + scratches :])
    pl.when(first)(plan.begin)
    kernel(*ins, *outs, *own)
    pl.when(last)(plan.finish)


def memory_call(plan, cid, kernel, name, grid, inputs, in_specs, out_specs, out_shape, scratch, flops):
    return pl.pallas_call(
        functools.partial(beside, plan, kernel, len(inputs), len(out_shape), len(scratch)),
        grid=(grid,),
        in_specs=in_specs + plan.specs,
        out_specs=out_specs + plan.specs,
        out_shape=out_shape + plan.shapes,
        scratch_shapes=scratch + plan.scratch,
        compiler_params=pltpu.CompilerParams(
            vmem_limit_bytes=VMEM_BYTES, collective_id=cid, has_side_effects=True
        ),
        cost_estimate=pl.CostEstimate(flops=flops, bytes_accessed=flops // 200, transcendentals=0),
        name=name,
    )(*inputs, *plan.arrays)


MEM_BLOCK = 16
BACK_BLOCK = 8


def memory_kernel(slots, padded, mem_ref, wk_ref, wv_ref, vb_ref, k_ref, v_ref, rows_ref, wide):
    for c in range(0, D, 128):
        cols = slice(c, c + 128)
        wide[...] = mem_ref[:, :, cols].reshape(slots * MEM_BLOCK, 128).astype(F32)
        for r in range(MEM_BLOCK):
            own = wide[pl.ds(r, slots, stride=MEM_BLOCK), :]
            rows_ref[r * padded : (r + 1) * padded, cols] = jnp.concatenate(
                [own, jnp.zeros((padded - slots, 128), F32)], axis=0
            ).astype(BF)
    rows = rows_ref[...]
    for c in range(0, D, 512):
        cols = slice(c, c + 512)
        k_ref[:, cols] = product(rows, wk_ref[:, cols]).astype(BF)
        v_ref[:, cols] = (product(rows, wv_ref[:, cols]) + vb_ref[:, cols]).astype(BF)


def memory_products(memory, key_weight, value_weight, vbias, padded, plan, cid):
    rows, slots, _ = memory.shape
    whole = lambda a: pl.BlockSpec(a.shape, lambda i: (0,) * a.ndim)
    out = jax.ShapeDtypeStruct((rows * padded, D), BF)
    out_spec = pl.BlockSpec((MEM_BLOCK * padded, D), lambda i: (i, 0))
    return memory_call(
        plan,
        cid,
        functools.partial(memory_kernel, slots, padded),
        "memory_products",
        rows // MEM_BLOCK,
        [jnp.transpose(memory, (1, 0, 2)), key_weight, value_weight, vbias],
        [
            pl.BlockSpec((slots, MEM_BLOCK, D), lambda i: (0, i, 0)),
            whole(key_weight),
            whole(value_weight),
            whole(vbias),
        ],
        [out_spec] * 3,
        [out] * 3,
        [pltpu.VMEM((slots * MEM_BLOCK, 128), F32)],
        4 * rows * padded * D * D,
    )


def memory_weight_kernel(rows_ref, dk_ref, dv_ref, wk_ref, wv_ref, vb_ref, key_sum, value_sum):
    step = pl.program_id(0)

    @pl.when(step == 0)
    def _():
        key_sum[...] = jnp.zeros_like(key_sum)
        value_sum[...] = jnp.zeros_like(value_sum)
        vb_ref[...] = jnp.zeros_like(vb_ref)

    rows = rows_ref[...]
    vb_ref[...] += jnp.sum(dv_ref[...].astype(F32), axis=0, keepdims=True)
    for c in range(0, D, 512):
        cols = slice(c, c + 512)
        key_sum[:, cols] += weight_grad(rows, dk_ref[:, cols])
        value_sum[:, cols] += weight_grad(rows, dv_ref[:, cols])

    @pl.when(step == pl.num_programs(0) - 1)
    def _():
        wk_ref[...] = key_sum[...].astype(BF)
        wv_ref[...] = value_sum[...].astype(BF)


def memory_weights(memory_rows, dkeys, dvalues, rows, padded):
    spec = pl.BlockSpec((BACK_BLOCK * padded, D), lambda i: (i, 0))
    whole = pl.BlockSpec((D, D), lambda i: (0, 0))
    return pl.pallas_call(
        memory_weight_kernel,
        grid=(rows // BACK_BLOCK,),
        in_specs=[spec, spec, spec],
        out_specs=[whole, whole, pl.BlockSpec((1, D), lambda i: (0, 0))],
        out_shape=[
            jax.ShapeDtypeStruct((D, D), BF),
            jax.ShapeDtypeStruct((D, D), BF),
            jax.ShapeDtypeStruct((1, D), F32),
        ],
        scratch_shapes=[pltpu.VMEM((D, D), F32), pltpu.VMEM((D, D), F32)],
        compiler_params=pltpu.CompilerParams(vmem_limit_bytes=VMEM_BYTES),
        cost_estimate=pl.CostEstimate(
            flops=4 * rows * padded * D * D, bytes_accessed=6 * rows * padded * D, transcendentals=0
        ),
        name="memory_weights",
    )(memory_rows, dkeys, dvalues)


def memory_grad_kernel(slots, padded, dk_ref, dv_ref, wk_ref, wv_ref, out_ref, wide):
    for c in range(0, D, 256):
        cols = slice(c, c + 256)
        term = product_back(dk_ref[...], wk_ref[cols, :]) + product_back(dv_ref[...], wv_ref[cols, :])
        for part in range(0, 256, 128):
            for r in range(BACK_BLOCK):
                wide[pl.ds(r, slots, stride=BACK_BLOCK), :] = term[
                    r * padded : r * padded + slots, part : part + 128
                ]
            out_ref[:, :, c + part : c + part + 128] = wide[...].reshape(slots, BACK_BLOCK, 128)


def memory_back(dkeys, dvalues, key_weight, value_weight, rows, slots, padded, plan, cid):
    spec = pl.BlockSpec((BACK_BLOCK * padded, D), lambda i: (i, 0))
    whole = pl.BlockSpec((D, D), lambda i: (0, 0))
    out, *rest = memory_call(
        plan,
        cid,
        functools.partial(memory_grad_kernel, slots, padded),
        "memory_back",
        rows // BACK_BLOCK,
        [dkeys, dvalues, key_weight, value_weight],
        [spec, spec, whole, whole],
        [pl.BlockSpec((slots, BACK_BLOCK, D), lambda i: (0, i, 0))],
        [jax.ShapeDtypeStruct((slots, rows, D), F32)],
        [pltpu.VMEM((slots * BACK_BLOCK, 128), F32)],
        4 * rows * padded * D * D,
    )
    return jnp.transpose(out, (1, 0, 2)), rest


def own_heads(result, keep):
    kept = result * keep
    total = kept[0:TOK]
    for h in range(1, GH):
        total = total + kept[h * TOK : (h + 1) * TOK]
    return total


def cross_kernel(piece, padded, used, k_ref, v_ref, q_ref, keep_ref, ctx_ref, peak_ref, total_ref):
    step = pl.program_id(0)
    keep = keep_ref[...]
    keep_wide = keep.astype(F32)
    slot = lax.broadcasted_iota(jnp.int32, (padded, GL), 0)
    for g in range(G):
        cols = slice(g * GC, (g + 1) * GC)
        query = jnp.concatenate([q_ref[:, cols]] * GH, axis=0) * keep
        scores = product_back(k_ref[:, cols], query)
        for r in range(piece):
            rows = slice(r * padded, (r + 1) * padded)
            seen = slot < used[step * piece + r]
            own = jnp.where(seen, scores[rows], NEG)
            peak = jnp.max(own, axis=0, keepdims=True)
            exponent = jnp.where(seen, jnp.exp(own - peak), 0.0)
            total = jnp.sum(exponent, axis=0, keepdims=True)
            probs = (exponent * (1.0 / jnp.maximum(total, 1e-30))).astype(BF)
            ctx = own_heads(weight_grad(probs, v_ref[rows, cols]), keep_wide)
            ctx_ref[r * TOK : (r + 1) * TOK, cols] = ctx.astype(BF)
            peak_ref[r, g : g + 1, :] = peak
            total_ref[r, g : g + 1, :] = total


def cross_forward(used, keys, values, queries, keep, piece, padded):
    steps = queries.shape[0] // TOK
    rows = steps * piece
    big = pl.BlockSpec((piece * padded, D), lambda i, u: (i, 0))
    stat = pl.BlockSpec((piece, G, GL), lambda i, u: (i, 0, 0))
    return pl.pallas_call(
        functools.partial(cross_kernel, piece, padded),
        grid_spec=pltpu.PrefetchScalarGridSpec(
            num_scalar_prefetch=1,
            grid=(steps,),
            in_specs=[
                big,
                big,
                pl.BlockSpec((TOK, D), lambda i, u: (i, 0)),
                pl.BlockSpec((GL, GC), lambda i, u: (0, 0)),
            ],
            out_specs=[pl.BlockSpec((piece * TOK, D), lambda i, u: (i, 0)), stat, stat],
        ),
        out_shape=[
            jax.ShapeDtypeStruct((rows * TOK, D), BF),
            jax.ShapeDtypeStruct((rows, G, GL), F32),
            jax.ShapeDtypeStruct((rows, G, GL), F32),
        ],
        compiler_params=pltpu.CompilerParams(vmem_limit_bytes=VMEM_BYTES),
        cost_estimate=pl.CostEstimate(
            flops=4 * rows * padded * GL * D,
            bytes_accessed=4 * rows * padded * D,
            transcendentals=rows * padded * G * GL,
        ),
        name="cross_forward",
    )(used, keys, values, queries, keep)


def cross_back_kernel(
    piece, padded, used, k_ref, v_ref, q_ref, dc_ref, norm_ref, mid_ref, keep_ref, dq_ref, dk_ref, dv_ref
):
    step = pl.program_id(0)
    keep = keep_ref[...]
    keep_wide = keep.astype(F32)
    slot = lax.broadcasted_iota(jnp.int32, (padded, GL), 0)
    for g in range(G):
        cols = slice(g * GC, (g + 1) * GC)
        query = jnp.concatenate([q_ref[:, cols]] * GH, axis=0) * keep
        scores = product_back(k_ref[:, cols], query)
        parts = []
        for r in range(piece):
            rows = slice(r * padded, (r + 1) * padded)
            dctx = jnp.concatenate([dc_ref[r * TOK : (r + 1) * TOK, cols]] * GH, axis=0) * keep
            dprobs = product_back(v_ref[rows, cols], dctx)
            seen = slot < used[step * piece + r]
            probs = jnp.where(seen, jnp.exp(scores[rows] - norm_ref[r, g : g + 1, :]), 0.0)
            parts.append((probs * (dprobs - mid_ref[r, g : g + 1, :])).astype(BF))
            dv_ref[rows, cols] = product(probs.astype(BF), dctx).astype(BF)
        dscores = jnp.concatenate(parts, axis=0)
        dk_ref[:, cols] = product(dscores, query).astype(BF)
        dq_ref[:, cols] = own_heads(weight_grad(dscores, k_ref[:, cols]), keep_wide).astype(BF)


def cross_back(used, keys, values, queries, dctx, norm, middle, keep, piece, padded):
    steps = queries.shape[0] // TOK
    rows = steps * piece
    big = pl.BlockSpec((piece * padded, D), lambda i, u: (i, 0))
    stat = pl.BlockSpec((piece, G, GL), lambda i, u: (i, 0, 0))
    small = pl.BlockSpec((TOK, D), lambda i, u: (i, 0))
    return pl.pallas_call(
        functools.partial(cross_back_kernel, piece, padded),
        grid_spec=pltpu.PrefetchScalarGridSpec(
            num_scalar_prefetch=1,
            grid=(steps,),
            in_specs=[
                big,
                big,
                small,
                pl.BlockSpec((piece * TOK, D), lambda i, u: (i, 0)),
                stat,
                stat,
                pl.BlockSpec((GL, GC), lambda i, u: (0, 0)),
            ],
            out_specs=[small, big, big],
        ),
        out_shape=[
            jax.ShapeDtypeStruct((steps * TOK, D), BF),
            jax.ShapeDtypeStruct((rows * padded, D), BF),
            jax.ShapeDtypeStruct((rows * padded, D), BF),
        ],
        compiler_params=pltpu.CompilerParams(vmem_limit_bytes=VMEM_BYTES),
        cost_estimate=pl.CostEstimate(
            flops=10 * rows * padded * GL * D,
            bytes_accessed=8 * rows * padded * D,
            transcendentals=rows * padded * G * GL,
        ),
        name="cross_back",
    )(used, keys, values, queries, dctx, norm, middle, keep)


def words_of(table_ref):
    return jnp.concatenate([table_ref[i] for i in range(table_ref.shape[0])], axis=-1)


def vocab_kernel(tile, h_ref, target_ref, table_ref, peak_ref, total_ref, pick_ref):
    step = pl.program_id(0)

    @pl.when(step == 0)
    def _():
        peak_ref[...] = jnp.full_like(peak_ref, NEG)
        total_ref[...] = jnp.zeros_like(total_ref)
        pick_ref[...] = jnp.zeros_like(pick_ref)

    words = words_of(table_ref)
    block = 256
    word = lax.broadcasted_iota(jnp.int32, (block, tile), 1) + step * tile
    for t in range(0, h_ref.shape[0], block):
        rows = slice(t, t + block)
        logits = product_back(h_ref[rows, :], words)
        former = peak_ref[rows, :]
        peak = jnp.maximum(former, jnp.max(logits, axis=1, keepdims=True))
        total = jnp.sum(jnp.exp(logits - peak), axis=1, keepdims=True)
        total_ref[rows, :] = total_ref[rows, :] * jnp.exp(former - peak) + total
        peak_ref[rows, :] = peak
        hit = jnp.where(word == target_ref[rows, :], logits, 0.0)
        pick_ref[rows, :] += jnp.sum(hit, axis=1, keepdims=True)


def vocab_forward(hidden, target, table, tile):
    tokens = hidden.shape[0]
    parts, words, width = table.shape
    col = pl.BlockSpec((tokens, 1), lambda i: (0, 0))
    return pl.pallas_call(
        functools.partial(vocab_kernel, tile),
        grid=(words // tile,),
        in_specs=[
            pl.BlockSpec((tokens, D), lambda i: (0, 0)),
            col,
            pl.BlockSpec((parts, tile, width), lambda i: (0, i, 0)),
        ],
        out_specs=[col, col, col],
        out_shape=[jax.ShapeDtypeStruct((tokens, 1), F32)] * 3,
        compiler_params=pltpu.CompilerParams(vmem_limit_bytes=VMEM_BYTES),
        cost_estimate=pl.CostEstimate(
            flops=2 * tokens * words * D, bytes_accessed=2 * words * D, transcendentals=tokens * words
        ),
        name="vocab_forward",
    )(hidden, target, table)


def vocab_back_kernel(tile, h_ref, target_ref, norm_ref, rate_ref, table_ref, out_ref):
    step = pl.program_id(0)

    @pl.when(step == 0)
    def _():
        out_ref[...] = jnp.zeros_like(out_ref)

    words = words_of(table_ref)
    block = 256
    word = lax.broadcasted_iota(jnp.int32, (block, tile), 1) + step * tile
    for t in range(0, h_ref.shape[0], block):
        rows = slice(t, t + block)
        logits = product_back(h_ref[rows, :], words)
        probs = jnp.exp(logits - norm_ref[rows, :])
        hit = jnp.where(word == target_ref[rows, :], 1.0, 0.0)
        dlogits = (rate_ref[rows, :] * (hit - probs)).astype(BF)
        out_ref[rows, :] += product(dlogits, words)


def vocab_back(hidden, target, norm, rate, table, tile):
    tokens = hidden.shape[0]
    parts, words, width = table.shape
    col = pl.BlockSpec((tokens, 1), lambda i: (0, 0))
    return pl.pallas_call(
        functools.partial(vocab_back_kernel, tile),
        grid=(words // tile,),
        in_specs=[
            pl.BlockSpec((tokens, D), lambda i: (0, 0)),
            col,
            col,
            col,
            pl.BlockSpec((parts, tile, width), lambda i: (0, i, 0)),
        ],
        out_specs=pl.BlockSpec((tokens, D), lambda i: (0, 0)),
        out_shape=jax.ShapeDtypeStruct((tokens, D), F32),
        compiler_params=pltpu.CompilerParams(vmem_limit_bytes=VMEM_BYTES),
        cost_estimate=pl.CostEstimate(
            flops=4 * tokens * words * D, bytes_accessed=2 * words * D, transcendentals=tokens * words
        ),
        name="vocab_back",
    )(hidden, target, norm, rate, table)


def self_probs(queries, key_heads):
    causal = (
        lax.broadcasted_iota(jnp.int32, (TOK, TOK), 1)
        <= lax.broadcasted_iota(jnp.int32, (TOK, TOK), 0)
    )[None, None]
    scores = jnp.einsum("rqhe,rkhe->rhqk", queries, key_heads, preferred_element_type=F32)
    return jax.nn.softmax(jnp.where(causal, scores, NEG), axis=-1)


def column_parts(gathered):
    return jnp.concatenate([gathered[i] for i in range(gathered.shape[0])], axis=-1)


def block_rows(array, ways):
    rows, columns = array.shape
    width = columns // ways
    return jnp.stack([array[:, i * width : (i + 1) * width] for i in range(ways)])


def local(
    answers,
    targets,
    doc_scores,
    memory,
    lengths,
    self_query,
    self_key,
    self_value,
    query_bias,
    value_bias,
    self_output,
    output_bias,
    first_gain,
    first_shift,
    cross_query,
    crossq_bias,
    cross_key,
    cross_value,
    crossv_bias,
    cross_output,
    crosso_bias,
    second_gain,
    second_shift,
    expand_weight,
    expand_bias,
    shrink_weight,
    shrink_bias,
    third_gain,
    third_shift,
    word_table,
):
    dp_ways, mp_ways = lax.axis_size("dp"), lax.axis_size("mp")
    chips = dp_ways // 2
    dp, mp = lax.axis_index("dp"), lax.axis_index("mp")
    groups = answers.shape[0]
    rows, slots, _ = memory.shape
    piece = rows // dp_ways
    own_q = dp_ways
    uniq = own_q * TOK
    tokens = rows * TOK
    padded = -(-slots // 16) * 16
    shard_rows = rows // mp_ways
    shard_tokens = shard_rows * TOK
    shard_q = own_q // mp_ways
    shard_uniq = shard_q * TOK
    local_heads = H // mp_ways
    head_cols = local_heads * HD
    hidden_cols = expand_weight.shape[1]
    vec = D // dp_ways

    small = jnp.concatenate(
        [
            output_bias,
            first_gain,
            first_shift,
            crosso_bias,
            second_gain,
            second_shift,
            shrink_bias,
            third_gain,
            third_shift,
            query_bias.reshape(-1),
            value_bias.reshape(-1),
            crossq_bias.reshape(-1),
            expand_bias.reshape(-1),
            crossv_bias,
        ]
    )
    sizes = [vec] * 9 + [a.size for a in (query_bias, value_bias, crossq_bias, expand_bias, crossv_bias)]
    small_rows = -(-small.shape[0] // 2048) * 16
    small = jnp.pad(small, (0, small_rows * 128 - small.shape[0])).reshape(small_rows, 128)
    memory_shard = jnp.concatenate([cross_key, cross_value], axis=0)
    wide_rows = cross_key.shape[0]
    self_shard = jnp.concatenate([self_query, self_key, self_value], axis=1)
    target_rows = jnp.pad(targets.reshape(1, -1), ((0, 7), (0, 0)))
    doc_rows = jnp.pad(doc_scores.reshape(1, -1), ((0, 7), (0, 128 - doc_scores.size)))
    wanted = jnp.stack([answers[(2 * c * piece) // K] for c in range(chips)])
    memory_all, small_all, cquery_z, cout_z = exchange(
        [
            (memory_shard, "wide", ""),
            (small, "wide", ""),
            (cross_query, "gather", "z"),
            (cross_output, "gather", "z"),
        ],
        0,
    )
    small_all = small_all.reshape(dp_ways, mp_ways, -1)
    starts = [sum(sizes[:i]) for i in range(len(sizes) + 1)]
    taken = [small_all[:, :, starts[i] : starts[i + 1]] for i in range(len(sizes))]
    (full_obias, gain_one, shift_one, full_cobias, gain_two, shift_two, full_sbias, gain_three, shift_three) = [
        taken[i][:, 0].reshape(D) for i in range(9)
    ]

    def head_bias(part, count, width):
        part = part.reshape(dp_ways, mp_ways, count, width)
        return jnp.transpose(part, (1, 2, 0, 3)).reshape(mp_ways, -1)

    mine = lambda a: lax.dynamic_index_in_dim(a, mp, 0, keepdims=False)
    qbias = mine(head_bias(taken[9], *query_bias.shape))
    vbias = mine(head_bias(taken[10], *value_bias.shape))
    cqbias = head_bias(taken[11], *crossq_bias.shape).reshape(-1)
    ebias = head_bias(taken[12], *expand_bias.shape).reshape(-1)
    cvbias = taken[13].reshape(1, D)
    key_weight = memory_all[:, :, :wide_rows].reshape(D, D)
    value_weight = memory_all[:, :, wide_rows:].reshape(D, D)

    plan = Exchange(
        [
            (expand_weight, "gather", "z"),
            (shrink_weight, "gather", "z"),
            (self_shard, "near", ""),
            (self_output, "near", ""),
            (target_rows, "near", ""),
            (doc_rows, "near", ""),
            (wanted, "nearswap", ""),
            (cquery_z, "near", ""),
            (cout_z, "near", ""),
        ]
    )
    (keys, values, memory_rows, expand_z, shrink_z, self_all, output_all, target_all, doc_all, x_all, cquery_all, cout_all) = (
        memory_products(memory, key_weight, value_weight, cvbias, padded, plan, 1)
    )
    expand_all = lax.all_gather(expand_z, "dp", axis=0, tiled=False)
    shrink_all = lax.all_gather(shrink_z, "dp", axis=0, tiled=False)
    table_all = lax.all_gather(word_table, "dp", axis=0, tiled=False)
    if word_table.shape[1] < 128:
        table_all = column_parts(table_all)[None]
    rows_first = lambda a: jnp.transpose(a, (0, 2, 1, 3)).reshape(dp_ways * a.shape[2], -1)
    columns_first = lambda a: column_parts(a.reshape(dp_ways, -1, a.shape[-1]))
    full_expand = rows_first(expand_all)
    full_shrink = columns_first(shrink_all)
    full_cquery = rows_first(cquery_all)
    full_cout = columns_first(cout_all)
    self_weight = self_all.reshape(D, 3 * head_cols)
    full_output = column_parts(output_all)
    my_group = (dp * piece) // K
    row_targets = lax.dynamic_index_in_dim(
        target_all[:, 0].reshape(dp_ways, groups, TOK), my_group, 1, keepdims=False
    )
    x_rows = x_all.reshape(uniq, D)

    qkv = product(x_rows, self_weight)
    queries = ((qkv[:, :head_cols] + qbias) * SCALE).astype(BF)
    self_keys = qkv[:, head_cols : 2 * head_cols].astype(BF)
    self_values = (qkv[:, 2 * head_cols :] + vbias).astype(BF)
    heads = lambda a: a.reshape(own_q, TOK, local_heads, HD)
    probs = self_probs(heads(queries), heads(self_keys))
    context = jnp.einsum(
        "rhqk,rkhe->rqhe", probs.astype(BF), heads(self_values), preferred_element_type=F32
    )
    context = context.astype(BF).reshape(uniq, head_cols)
    partial = product(context, full_output).astype(BF).reshape(mp_ways, shard_uniq, D)
    (received,) = exchange([(partial, "move", "z")], 2)
    x_own = lax.dynamic_slice_in_dim(x_rows, mp * shard_uniq, shard_uniq, 0)
    first_in = x_own.astype(F32) + added(partial, received, "z") + full_obias
    hidden_one, normed_one, inverse_one = layer_norm(first_in, gain_one, shift_one)
    hidden_low1 = hidden_one.astype(BF)
    cross_queries = ((product(hidden_low1, full_cquery) + cqbias) * SCALE).astype(BF)
    (cross_queries,) = exchange([(cross_queries, "gather", "z")], 3)
    cross_queries = cross_queries.reshape(uniq, D)

    used = jnp.clip(lengths - mp * slots, 0, slots).astype(jnp.int32)
    keep = (
        lax.broadcasted_iota(jnp.int32, (GL, GC), 0) // TOK
        == lax.broadcasted_iota(jnp.int32, (GL, GC), 1) // HD
    ).astype(BF)
    ctx_part, peak_part, total_part = cross_forward(
        used, keys, values, cross_queries, keep, piece, padded
    )
    ctx_part = ctx_part.reshape(mp_ways, shard_tokens, D)
    stat_part = jnp.stack([peak_part, total_part], axis=1).reshape(mp_ways, shard_rows, 2, G, GL)
    ctx_got, stat_got = exchange([(ctx_part, "move", "z"), (stat_part, "move", "z")], 4)
    stat_own = lax.dynamic_index_in_dim(stat_part, mp, 0, keepdims=True)
    stat_got = jnp.concatenate([stat_own, stat_got], axis=0)
    peak_got, total_got = stat_got[:, :, 0], stat_got[:, :, 1]
    peak = jnp.max(peak_got, axis=0)
    weight = total_got * jnp.exp(peak_got - peak)
    total = jnp.sum(weight, axis=0)
    cross_norm = peak + jnp.log(total)
    weight = weight / total

    def to_token_heads(a):
        lead = a.shape[:-3]
        a = a.reshape(lead + (shard_rows, H, TOK))
        return jnp.swapaxes(a, -1, -2).reshape(lead + (shard_tokens, H))

    weight = jnp.repeat(to_token_heads(weight), HD, axis=-1)
    ctx_own = lax.dynamic_index_in_dim(ctx_part, mp, 0, keepdims=False)
    context_two = (
        ctx_own.astype(F32) * weight[0] + jnp.sum(ctx_got.astype(F32) * weight[1:], axis=0)
    ).astype(BF)

    def to_rows(a):
        a = jnp.broadcast_to(a.reshape(shard_q, 1, TOK, D), (shard_q, piece, TOK, D))
        return a.reshape(shard_tokens, D)

    second_in = to_rows(hidden_one) + product(context_two, full_cout) + full_cobias
    hidden_two, normed_two, inverse_two = layer_norm(second_in, gain_two, shift_two)
    hidden_low2 = hidden_two.astype(BF)

    expanded = product(hidden_low2, full_expand) + ebias
    activated = gelu_exact(expanded).astype(BF)
    third_in = hidden_two + product(activated, full_shrink) + full_sbias
    hidden_three, normed_three, inverse_three = layer_norm(third_in, gain_three, shift_three)
    (hidden_low3,) = exchange([(hidden_three.astype(BF), "gather", "z")], 5)
    hidden_low3 = hidden_low3.reshape(tokens, D)

    vocab_local = table_all.shape[1]
    tile = 640 if vocab_local % 640 == 0 else vocab_local
    token_targets = jnp.broadcast_to(
        row_targets.reshape(own_q, 1, TOK), (own_q, piece, TOK)
    ).reshape(tokens, 1)
    local_target = token_targets - mp * vocab_local
    peak, total, picked = vocab_forward(hidden_low3, local_target, table_all, tile)
    stats = jnp.concatenate([peak, total, picked], axis=1).T.reshape(3, tokens // 128, 128)
    (stats,) = exchange([(stats, "gather", "z")], 6)
    stats = stats.reshape(mp_ways, 3, tokens)
    top = jnp.max(stats[:, 0], axis=0)
    norm_log = top + jnp.log(jnp.sum(stats[:, 1] * jnp.exp(stats[:, 0] - top), axis=0))
    loglik = jnp.sum(stats[:, 2], axis=0) - norm_log
    (loglik_all,) = exchange([(loglik.reshape(tokens // 128, 128), "gather", "dp")], 7)
    loglik_all = loglik_all.reshape(dp_ways, own_q, piece, TOK)
    loglik_all = jnp.transpose(loglik_all, (1, 0, 2, 3)).reshape(own_q, groups, K, TOK)
    doc_logp = jax.nn.log_softmax(doc_all[:, 0, : groups * K].reshape(own_q, groups, K), axis=2)
    joined = doc_logp[..., None] + loglik_all
    marginal = jax.nn.logsumexp(joined, axis=2, keepdims=True)
    question_loss = -jnp.mean(
        lax.dynamic_index_in_dim(marginal[:, :, 0], dp, 0, keepdims=False), axis=1
    )
    posterior = jnp.exp(joined - marginal).reshape(own_q, groups * K, TOK)
    rate = -lax.dynamic_slice_in_dim(posterior, dp * piece, piece, 1).reshape(tokens, 1)
    dthree = vocab_back(hidden_low3, local_target, norm_log.reshape(tokens, 1), rate, table_all, tile)
    dthree = dthree.astype(BF).reshape(mp_ways, shard_tokens, D)
    (received,) = exchange([(dthree, "move", "z")], 8)
    dhidden_three = added(dthree, received, "z")

    dthird, dgain_three, dshift_three = norm_back(
        dhidden_three, normed_three, inverse_three, gain_three
    )
    dshrink_bias = jnp.sum(dthird, axis=0)
    dshrink_in = dthird.astype(BF)
    dactivated = product_back(dshrink_in, full_shrink)
    dexpanded = jax.vjp(gelu_exact, expanded)[1](dactivated)[0].astype(BF)
    dexpand_bias = jnp.sum(dexpanded, axis=0, dtype=F32)
    dshrink = weight_grad(activated, dshrink_in)
    dexpand = weight_grad(hidden_low2, dexpanded)
    shrink_dp = lax.psum_scatter(
        block_rows(dshrink.astype(BF), dp_ways), "dp", scatter_dimension=0, tiled=False
    )
    expand_dp = lax.psum_scatter(dexpand.astype(BF), "dp", scatter_dimension=0, tiled=True)
    dhidden_two = dthird + product_back(dexpanded, full_expand)

    dsecond, dgain_two, dshift_two = norm_back(dhidden_two, normed_two, inverse_two, gain_two)
    dcout_bias = jnp.sum(dsecond, axis=0)
    dcout_in = dsecond.astype(BF)
    dcontext_two = product_back(dcout_in, full_cout).astype(BF)
    middle = jnp.sum(
        (dcontext_two.astype(F32) * context_two.astype(F32)).reshape(shard_tokens, H, HD), axis=-1
    )
    middle = jnp.swapaxes(middle.reshape(shard_rows, TOK, H), 1, 2).reshape(shard_rows, G, GL)
    stat_all = jnp.stack([cross_norm, middle])
    dctx_all, stat_all = exchange([(dcontext_two, "gather", "z"), (stat_all, "gather", "z")], 9)
    norm_all = stat_all[:, 0].reshape(rows, G, GL)
    middle_all = stat_all[:, 1].reshape(rows, G, GL)
    dcout = weight_grad(context_two, dcout_in)
    dcross_q, dkeys, dvalues = cross_back(
        used,
        keys,
        values,
        cross_queries,
        dctx_all.reshape(tokens, D),
        norm_all,
        middle_all,
        keep,
        piece,
        padded,
    )
    dcross_q = dcross_q.reshape(mp_ways, shard_uniq, D)
    (received,) = exchange([(dcross_q, "move", "z")], 10)
    dkey_weight, dvalue_weight, dvalue_bias = memory_weights(
        memory_rows, dkeys, dvalues, rows, padded
    )
    dcross_low = (added(dcross_q, received, "z") * SCALE).astype(BF)
    dcquery = weight_grad(hidden_low1, dcross_low)
    dcq_bias = jnp.sum(dcross_low, axis=0, dtype=F32)
    dhidden_one = jnp.sum(dsecond.reshape(shard_q, piece, TOK, D), axis=1).reshape(
        shard_uniq, D
    ) + product_back(dcross_low, full_cquery)

    dfirst, dgain_one, dshift_one = norm_back(dhidden_one, normed_one, inverse_one, gain_one)
    dout_bias = jnp.sum(dfirst, axis=0)
    owners = lambda a: a.reshape(chips, 2, -1, a.shape[-1])
    key_blocks = owners(dkey_weight)
    value_blocks = owners(dvalue_weight)
    cq_blocks = owners(
        jnp.transpose(
            dcquery.astype(BF).reshape(dp_ways, vec, mp_ways, head_cols), (0, 2, 1, 3)
        ).reshape(-1, head_cols)
    )
    co_blocks = owners(block_rows(dcout.astype(BF), dp_ways).reshape(-1, vec))
    first_blocks = [key_blocks, value_blocks, cq_blocks, co_blocks]
    dout_in, *received = exchange(
        [(dfirst.astype(BF), "gather", "z")] + [(a, "move1", "pair") for a in first_blocks], 11
    )
    first_blocks = [added(a, b, "pair").astype(BF) for a, b in zip(first_blocks, received)]
    dout_in = dout_in.reshape(uniq, D)
    doutput = weight_grad(context, dout_in)
    dcontext = heads(product_back(dout_in, full_output).astype(BF))
    dvalue_h = jnp.einsum("rhqk,rqhe->rkhe", probs.astype(BF), dcontext, preferred_element_type=F32)
    dprobs = jnp.einsum("rqhe,rkhe->rhqk", dcontext, heads(self_values), preferred_element_type=F32)
    dscores = (probs * (dprobs - jnp.sum(probs * dprobs, axis=-1, keepdims=True))).astype(BF)
    dquery_h = jnp.einsum("rhqk,rkhe->rqhe", dscores, heads(self_keys), preferred_element_type=F32)
    dkey_h = jnp.einsum("rhqk,rqhe->rkhe", dscores, heads(queries), preferred_element_type=F32)
    flat = lambda a: a.reshape(uniq, head_cols)
    dqkv = jnp.concatenate(
        [flat(dquery_h * SCALE).astype(BF), flat(dkey_h).astype(BF), flat(dvalue_h).astype(BF)], axis=1
    )
    dself = weight_grad(x_rows, dqkv)
    dqkv_bias = jnp.sum(dqkv, axis=0, dtype=F32)
    partial = product_back(dqkv, self_weight).astype(BF).reshape(mp_ways, shard_uniq, D)
    received, key_got = exchange([(partial, "move", "z"), (first_blocks[0], "move", "chips")], 12)
    dinputs = (dfirst + added(partial, received, "z")).astype(BF)

    cast = lambda a: a.astype(BF)
    vectors = jnp.stack(
        [
            dout_bias,
            dgain_one,
            dshift_one,
            dcout_bias,
            dgain_two,
            dshift_two,
            dshrink_bias,
            dgain_three,
            dshift_three,
            dvalue_bias[0],
        ]
    )
    by_dp = lambda a, width: jnp.swapaxes(a.reshape(-1, dp_ways, width), 0, 1).reshape(dp_ways, -1)
    vector_parts = [
        by_dp(vectors, vec),
        by_dp(dcq_bias, crossq_bias.shape[1]),
        by_dp(dexpand_bias, expand_bias.shape[1]),
        by_dp(dqkv_bias[:head_cols], query_bias.shape[1]),
        by_dp(dqkv_bias[2 * head_cols :], value_bias.shape[1]),
    ]
    ends = [sum(a.shape[1] for a in vector_parts[: i + 1]) for i in range(5)]
    vector_blocks = jnp.concatenate(vector_parts, axis=1)
    length = vector_blocks.shape[1]
    vector_rows = -(-length // 1024) * 8
    vector_blocks = owners(
        jnp.pad(vector_blocks, ((0, 0), (0, vector_rows * 128 - length))).reshape(-1, 128)
    )
    dinputs, value_got = exchange(
        [(dinputs, "gather", "z"), (first_blocks[1], "move", "chips")], 13
    )
    answer_blocks = dinputs.reshape(chips, 2, TOK, D)
    self_blocks = owners(cast(dself))
    out_blocks = owners(block_rows(cast(doutput), dp_ways).reshape(-1, vec))
    last_blocks = [self_blocks, out_blocks, answer_blocks, vector_blocks]
    received = exchange([(a, "move1", "pair") for a in last_blocks], 14)
    last_blocks = [added(a, b, "pair").astype(a.dtype) for a, b in zip(last_blocks, received)]
    last_blocks = first_blocks[2:] + last_blocks
    expand_blocks = jnp.transpose(
        expand_dp.reshape(vec, mp_ways, -1), (1, 0, 2)
    )
    shrink_blocks = shrink_dp.reshape(mp_ways, -1, vec)
    plan = Exchange(
        [(a, "move", "chips") for a in last_blocks]
        + [(expand_blocks, "move", "z"), (shrink_blocks, "move", "z")]
    )
    memory_grad, received = memory_back(
        dkeys, dvalues, key_weight, value_weight, rows, slots, padded, plan, 15
    )
    expand_grad = added(expand_blocks, received[6], "z")
    shrink_grad = added(shrink_blocks, received[7], "z")
    cq_sum, co_sum, self_grad, out_grad, answers_own, vector_sum = [
        added(a, b, "chips") if i != 4 else (a, b)
        for i, (a, b) in enumerate(zip(last_blocks, received[:6]))
    ]
    key_sum = added(first_blocks[0], key_got, "chips")
    value_sum = added(first_blocks[1], value_got, "chips")
    zblocks = [
        cast(key_sum).reshape(mp_ways, wide_rows, D),
        cast(value_sum).reshape(mp_ways, wide_rows, D),
        cast(cq_sum).reshape(mp_ways, vec, head_cols),
        cast(co_sum).reshape(mp_ways, head_cols, vec),
    ]
    *got_z, vector_all = exchange(
        [(a, "move", "z") for a in zblocks] + [(vector_sum, "gather", "z")], 16
    )
    key_grad, value_grad, cquery_grad, cout_grad = [
        added(a, b, "z") for a, b in zip(zblocks, got_z)
    ]
    vector_all = vector_all.reshape(mp_ways, -1)
    vector_own = jnp.sum(vector_all, axis=0)
    head_own = lax.dynamic_index_in_dim(vector_all, mp, 0, keepdims=False)

    mine_a, others = answers_own
    mine_a = lax.dynamic_index_in_dim(mine_a, dp // 2, 0, keepdims=False)
    returned = jnp.concatenate([mine_a[None], others], axis=0).astype(F32)
    source = lax.rem(dp // 2 + chips - jnp.arange(chips), chips)
    place = (2 * source * piece) // K
    pick = (place[None, :] == jnp.arange(groups)[:, None]).astype(F32)
    answer_grad = jnp.sum(pick[:, :, None, None] * returned[None], axis=1)

    def vec_of(i):
        return vector_own[i * vec : (i + 1) * vec]

    def mp_rows(start, shape):
        part = vector_own[start : start + mp_ways * shape[0] * shape[1]]
        part = part.reshape(mp_ways, shape[0], shape[1])
        return lax.dynamic_index_in_dim(part, mp, 0, keepdims=False)

    return (
        question_loss,
        answer_grad,
        memory_grad,
        self_grad[:, :head_cols],
        self_grad[:, head_cols : 2 * head_cols],
        self_grad[:, 2 * head_cols :],
        head_own[ends[2] : ends[3]].reshape(query_bias.shape),
        head_own[ends[3] : ends[4]].reshape(value_bias.shape),
        out_grad,
        vec_of(0),
        vec_of(1),
        vec_of(2),
        cquery_grad,
        mp_rows(ends[0], crossq_bias.shape),
        key_grad,
        value_grad,
        lax.dynamic_slice_in_dim(vec_of(9), mp * wide_rows, wide_rows, 0),
        cout_grad,
        vec_of(3),
        vec_of(4),
        vec_of(5),
        expand_grad,
        mp_rows(ends[1], expand_bias.shape),
        shrink_grad,
        vec_of(6),
        vec_of(7),
        vec_of(8),
    )


def solution(mesh):
    placed = (
        P("dp", None, None),
        P("dp", None),
        P("dp", None),
        P("dp", "mp", None),
        P("dp"),
        P("dp", "mp"),
        P("dp", "mp"),
        P("dp", "mp"),
        P("mp", "dp"),
        P("mp", "dp"),
        P("mp", "dp"),
        P("dp"),
        P("dp"),
        P("dp"),
        P("dp", "mp"),
        P("mp", "dp"),
        P(("dp", "mp"), None),
        P(("dp", "mp"), None),
        P(("dp", "mp")),
        P("mp", "dp"),
        P("dp"),
        P("dp"),
        P("dp"),
        P("dp", "mp"),
        P("mp", "dp"),
        P("mp", "dp"),
        P("dp"),
        P("dp"),
        P("dp"),
        P("mp", "dp"),
    )
    return jax.shard_map(
        local,
        mesh=mesh,
        in_specs=placed,
        out_specs=(
            P("dp"),
            P("dp", None, None),
            P("dp", "mp", None),
            P("dp", "mp"),
            P("dp", "mp"),
            P("dp", "mp"),
            P("mp", "dp"),
            P("mp", "dp"),
            P("mp", "dp"),
            P("dp"),
            P("dp"),
            P("dp"),
            P("dp", "mp"),
            P("mp", "dp"),
            P(("dp", "mp"), None),
            P(("dp", "mp"), None),
            P(("dp", "mp")),
            P("mp", "dp"),
            P("dp"),
            P("dp"),
            P("dp"),
            P("dp", "mp"),
            P("mp", "dp"),
            P("mp", "dp"),
            P("dp"),
            P("dp"),
            P("dp"),
        ),
        check_vma=False,
    )
```

```python
import functools

import jax
import jax.numpy as jnp
from jax import lax
from jax.experimental import pallas as pl
from jax.experimental.pallas import tpu as pltpu
from jax.sharding import PartitionSpec as P

D = 1024
H = 16
HD = 64
TOK = 32
K = 8
G = 4
GH = 4
GC = GH * HD
GL = GH * TOK

EPS = 1e-05
NEG = -1e30
SCALE = 0.125
BF = jnp.bfloat16
F32 = jnp.float32
MESH = pl.DeviceIdType.MESH
VMEM_BYTES = 60 * 1024 * 1024


def product(former, latter):
    return jnp.dot(former, latter, preferred_element_type=F32)


def product_back(former, latter):
    return lax.dot_general(former, latter, (((1,), (1,)), ((), ())), preferred_element_type=F32)


def weight_grad(former, latter):
    return lax.dot_general(former, latter, (((0,), (0,)), ((), ())), preferred_element_type=F32)


def layer_norm(entries, norm_gain, norm_shift):
    center = entries - jnp.mean(entries, axis=-1, keepdims=True)
    inverse = lax.rsqrt(jnp.mean(center * center, axis=-1, keepdims=True) + EPS)
    normed = center * inverse
    return (normed * norm_gain + norm_shift, normed, inverse)


def norm_back(upstream, normed, inverse, norm_gain):
    scaled = upstream * norm_gain
    dentries = inverse * (
        scaled
        - jnp.mean(scaled, axis=-1, keepdims=True)
        - normed * jnp.mean(scaled * normed, axis=-1, keepdims=True)
    )
    return (dentries, jnp.sum(upstream * normed, axis=0), jnp.sum(upstream, axis=0))


class Exchange:
    def __init__(self, entries):
        self.dp_ways, self.mp_ways = lax.axis_size("dp"), lax.axis_size("mp")
        self.chips = self.dp_ways // 2
        self.ways = {"z": self.mp_ways, "chips": self.chips, "pair": 2, "dp": self.dp_ways}
        self.arrays = [entry[0] for entry in entries]
        self.kinds = [entry[1] for entry in entries]
        self.groups = [entry[2] for entry in entries]
        self.count = len(entries)
        shapes = []
        for array, kind, group in entries:
            shape = array.shape
            if kind == "gather":
                shape = (self.ways[group],) + shape
            elif kind == "move":
                shape = (self.ways[group] - 1,) + shape[1:]
            elif kind == "move1":
                shape = (self.ways[group] - 1, shape[0]) + shape[2:]
            elif kind == "near":
                shape = (self.dp_ways,) + shape
            elif kind == "nearswap":
                shape = (self.dp_ways,) + shape[1:]
            else:
                shape = (self.dp_ways, self.mp_ways) + shape
            shapes.append(jax.ShapeDtypeStruct(shape, array.dtype))
        self.shapes = shapes
        self.specs = [pl.BlockSpec(memory_space=pl.ANY)] * self.count
        dma = pltpu.SemaphoreType.DMA
        most = max(self.dp_ways, self.mp_ways)
        self.scratch = [dma((self.count, most)) for _ in range(6)] + [dma((self.count,))]

    def bind(self, ins, outs, sems):
        self.ins, self.outs = ins, outs
        self.zs, self.zr, self.cs, self.cr, self.ps, self.pr, self.own = sems
        dp, mp = lax.axis_index("dp"), lax.axis_index("mp")
        self.dp, self.mp = dp, mp
        self.parity, self.chip = lax.rem(dp, 2), dp // 2
        self.place = {"z": mp, "chips": self.chip, "pair": self.parity, "dp": dp}

    def device(self, group, j):
        if group == "z":
            return (self.dp, j)
        if group == "chips":
            return (2 * j + self.parity, self.mp)
        if group == "pair":
            return (self.dp - self.parity + j, self.mp)
        return (j, self.mp)

    def peer(self, group, off):
        return lax.rem(self.place[group] + off, self.ways[group])

    def remote(self, source, target, send, recv, device):
        return pltpu.make_async_remote_copy(
            src_ref=source,
            dst_ref=target,
            send_sem=send,
            recv_sem=recv,
            device_id=device,
            device_id_type=MESH,
        )

    def meet(self):
        needed = set()
        for kind, group in zip(self.kinds, self.groups):
            if kind in ("near", "nearswap", "wide"):
                needed |= {"chips", "pair"}
                if kind == "wide":
                    needed.add("z")
            else:
                needed.add(group)
        barrier = pltpu.get_barrier_semaphore()
        total = 0
        for group in sorted(needed):
            for off in range(1, self.ways[group]):
                pl.semaphore_signal(
                    barrier,
                    inc=1,
                    device_id=self.device(group, self.peer(group, off)),
                    device_id_type=MESH,
                )
                total += 1
        pl.semaphore_wait(barrier, total)

    def first(self, i):
        kind, group = self.kinds[i], self.groups[i]
        ref, out = self.ins[i], self.outs[i]
        copies = []
        if kind in ("near", "nearswap"):
            return copies
        if kind == "wide":
            group, slot = "z", out.at[self.dp, self.mp]
        for off in range(1, self.ways[group]):
            peer = self.peer(group, off)
            if kind == "wide":
                source, target = ref, slot
            elif kind == "gather":
                source, target = ref, out.at[self.place[group]]
            elif kind == "move":
                source, target = ref.at[peer], out.at[off - 1]
            else:
                source, target = ref.at[:, peer], out.at[off - 1]
            copies.append(
                self.remote(
                    source,
                    target,
                    self.zs.at[i, off - 1],
                    self.zr.at[i, off - 1],
                    self.device(group, peer),
                )
            )
        return copies

    def local(self, i):
        kind, group = self.kinds[i], self.groups[i]
        ref, out = self.ins[i], self.outs[i]
        if kind == "wide":
            source, target = ref, out.at[self.dp, self.mp]
        elif kind == "gather":
            source, target = ref, out.at[self.place[group]]
        elif kind in ("near", "nearswap"):
            source, target = self.mine(i), out.at[self.dp]
        else:
            return None
        return pltpu.make_async_copy(source, target, self.own.at[i])

    def mine(self, i):
        kind = self.kinds[i]
        if kind == "wide":
            return self.outs[i].at[self.dp]
        return self.ins[i].at[self.chip] if kind == "nearswap" else self.ins[i]

    def spread(self, i):
        copies = []
        for off in range(1, self.chips):
            peer = self.peer("chips", off)
            source = self.ins[i].at[peer] if self.kinds[i] == "nearswap" else self.mine(i)
            copies.append(
                self.remote(
                    source,
                    self.outs[i].at[self.dp],
                    self.cs.at[i, off - 1],
                    self.cr.at[i, off - 1],
                    self.device("chips", peer),
                )
            )
        return copies

    def hand(self, i, off):
        owner = 2 * lax.rem(self.chip + self.chips - off, self.chips) + self.parity
        return self.remote(
            self.mine(i) if off == 0 else self.outs[i].at[owner],
            self.outs[i].at[owner],
            self.ps.at[i, off],
            self.pr.at[i, off],
            self.device("pair", 1 - self.parity),
        )

    def begin(self):
        self.meet()
        for i in range(self.count):
            for copy in self.first(i):
                copy.start()
            if self.kinds[i] in ("near", "nearswap"):
                for copy in self.spread(i):
                    copy.start()
                self.hand(i, 0).start()
        for i in range(self.count):
            local = self.local(i)
            if local is not None:
                local.start()

    def finish(self):
        shared = [i for i in range(self.count) if self.kinds[i] in ("near", "nearswap", "wide")]
        for i in shared:
            if self.kinds[i] == "wide":
                for copy in self.first(i):
                    copy.wait()
                self.local(i).wait()
                for copy in self.spread(i):
                    copy.start()
                self.hand(i, 0).start()
        for i in shared:
            for off, copy in enumerate(self.spread(i), 1):
                copy.wait_recv()
                self.hand(i, off).start()
        for i in range(self.count):
            if i in shared:
                for copy in self.spread(i):
                    copy.wait_send()
                for off in range(self.chips):
                    self.hand(i, off).wait()
                if self.kinds[i] != "wide":
                    self.local(i).wait()
            else:
                for copy in self.first(i):
                    copy.wait()
                local = self.local(i)
                if local is not None:
                    local.wait()


def exchange_kernel(plan, *refs):
    count = plan.count
    plan.bind(refs[:count], refs[count : 2 * count], refs[2 * count :])
    plan.begin()
    plan.finish()


def exchange(entries, cid):
    plan = Exchange(entries)
    return pl.pallas_call(
        functools.partial(exchange_kernel, plan),
        out_shape=plan.shapes,
        in_specs=plan.specs,
        out_specs=plan.specs,
        scratch_shapes=plan.scratch,
        compiler_params=pltpu.CompilerParams(collective_id=cid, has_side_effects=True),
        name=f"exchange_{cid}",
    )(*plan.arrays)


def added(array, received, group):
    place = {
        "z": lax.axis_index("mp"),
        "chips": lax.axis_index("dp") // 2,
        "pair": lax.rem(lax.axis_index("dp"), 2),
    }[group]
    axis = 1 if group == "pair" else 0
    own = lax.dynamic_index_in_dim(array, place, axis, keepdims=False)
    return own.astype(F32) + jnp.sum(received.astype(F32), axis=0)


def beside(plan, kernel, inputs, outputs, scratches, *refs):
    n = plan.count
    first, last = pl.program_id(0) == 0, pl.program_id(0) == pl.num_programs(0) - 1
    ins = refs[:inputs]
    sends = refs[inputs : inputs + n]
    outs = refs[inputs + n : inputs + n + outputs]
    lands = refs[inputs + n + outputs : inputs + 2 * n + outputs]
    own = refs[inputs + 2 * n + outputs : inputs + 2 * n + outputs + scratches]
    plan.bind(sends, lands, refs[inputs + 2 * n + outputs + scratches :])
    pl.when(first)(plan.begin)
    kernel(*ins, *outs, *own)
    pl.when(last)(plan.finish)


def memory_call(plan, cid, kernel, name, grid, inputs, in_specs, out_specs, out_shape, scratch, flops):
    return pl.pallas_call(
        functools.partial(beside, plan, kernel, len(inputs), len(out_shape), len(scratch)),
        grid=(grid,),
        in_specs=in_specs + plan.specs,
        out_specs=out_specs + plan.specs,
        out_shape=out_shape + plan.shapes,
        scratch_shapes=scratch + plan.scratch,
        compiler_params=pltpu.CompilerParams(
            vmem_limit_bytes=VMEM_BYTES, collective_id=cid, has_side_effects=True
        ),
        cost_estimate=pl.CostEstimate(flops=flops, bytes_accessed=flops // 200, transcendentals=0),
        name=name,
    )(*inputs, *plan.arrays)


MEM_BLOCK = 16
BACK_BLOCK = 8


def memory_kernel(slots, padded, mem_ref, wk_ref, wv_ref, vb_ref, k_ref, v_ref, rows_ref, wide):
    for c in range(0, D, 128):
        cols = slice(c, c + 128)
        wide[...] = mem_ref[:, :, cols].reshape(slots * MEM_BLOCK, 128).astype(F32)
        for r in range(MEM_BLOCK):
            own = wide[pl.ds(r, slots, stride=MEM_BLOCK), :]
            rows_ref[r * padded : (r + 1) * padded, cols] = jnp.concatenate(
                [own, jnp.zeros((padded - slots, 128), F32)], axis=0
            ).astype(BF)
    rows = rows_ref[...]
    for c in range(0, D, 512):
        cols = slice(c, c + 512)
        k_ref[:, cols] = product(rows, wk_ref[:, cols]).astype(BF)
        v_ref[:, cols] = (product(rows, wv_ref[:, cols]) + vb_ref[:, cols]).astype(BF)


def memory_products(memory, key_weight, value_weight, vbias, padded, plan, cid):
    rows, slots, _ = memory.shape
    whole = lambda a: pl.BlockSpec(a.shape, lambda i: (0,) * a.ndim)
    out = jax.ShapeDtypeStruct((rows * padded, D), BF)
    out_spec = pl.BlockSpec((MEM_BLOCK * padded, D), lambda i: (i, 0))
    return memory_call(
        plan,
        cid,
        functools.partial(memory_kernel, slots, padded),
        "memory_products",
        rows // MEM_BLOCK,
        [jnp.transpose(memory, (1, 0, 2)), key_weight, value_weight, vbias],
        [
            pl.BlockSpec((slots, MEM_BLOCK, D), lambda i: (0, i, 0)),
            whole(key_weight),
            whole(value_weight),
            whole(vbias),
        ],
        [out_spec] * 3,
        [out] * 3,
        [pltpu.VMEM((slots * MEM_BLOCK, 128), F32)],
        4 * rows * padded * D * D,
    )


def memory_weight_kernel(rows_ref, dk_ref, dv_ref, wk_ref, wv_ref, vb_ref, key_sum, value_sum):
    step = pl.program_id(0)

    @pl.when(step == 0)
    def _():
        key_sum[...] = jnp.zeros_like(key_sum)
        value_sum[...] = jnp.zeros_like(value_sum)
        vb_ref[...] = jnp.zeros_like(vb_ref)

    rows = rows_ref[...]
    vb_ref[...] += jnp.sum(dv_ref[...].astype(F32), axis=0, keepdims=True)
    for c in range(0, D, 512):
        cols = slice(c, c + 512)
        key_sum[:, cols] += weight_grad(rows, dk_ref[:, cols])
        value_sum[:, cols] += weight_grad(rows, dv_ref[:, cols])

    @pl.when(step == pl.num_programs(0) - 1)
    def _():
        wk_ref[...] = key_sum[...].astype(BF)
        wv_ref[...] = value_sum[...].astype(BF)


def memory_weights(memory_rows, dkeys, dvalues, rows, padded, plan, cid):
    spec = pl.BlockSpec((BACK_BLOCK * padded, D), lambda i: (i, 0))
    whole = pl.BlockSpec((D, D), lambda i: (0, 0))
    return memory_call(
        plan,
        cid,
        memory_weight_kernel,
        "memory_weights",
        rows // BACK_BLOCK,
        [memory_rows, dkeys, dvalues],
        [spec, spec, spec],
        [whole, whole, pl.BlockSpec((1, D), lambda i: (0, 0))],
        [
            jax.ShapeDtypeStruct((D, D), BF),
            jax.ShapeDtypeStruct((D, D), BF),
            jax.ShapeDtypeStruct((1, D), F32),
        ],
        [pltpu.VMEM((D, D), F32), pltpu.VMEM((D, D), F32)],
        4 * rows * padded * D * D,
    )


def memory_grad_kernel(slots, padded, dk_ref, dv_ref, wk_ref, wv_ref, out_ref, wide):
    for c in range(0, D, 256):
        cols = slice(c, c + 256)
        term = product_back(dk_ref[...], wk_ref[cols, :]) + product_back(dv_ref[...], wv_ref[cols, :])
        for part in range(0, 256, 128):
            for r in range(BACK_BLOCK):
                wide[pl.ds(r, slots, stride=BACK_BLOCK), :] = term[
                    r * padded : r * padded + slots, part : part + 128
                ]
            out_ref[:, :, c + part : c + part + 128] = wide[...].reshape(slots, BACK_BLOCK, 128)


def memory_back(dkeys, dvalues, key_weight, value_weight, rows, slots, padded, plan, cid):
    spec = pl.BlockSpec((BACK_BLOCK * padded, D), lambda i: (i, 0))
    whole = pl.BlockSpec((D, D), lambda i: (0, 0))
    out, *rest = memory_call(
        plan,
        cid,
        functools.partial(memory_grad_kernel, slots, padded),
        "memory_back",
        rows // BACK_BLOCK,
        [dkeys, dvalues, key_weight, value_weight],
        [spec, spec, whole, whole],
        [pl.BlockSpec((slots, BACK_BLOCK, D), lambda i: (0, i, 0))],
        [jax.ShapeDtypeStruct((slots, rows, D), F32)],
        [pltpu.VMEM((slots * BACK_BLOCK, 128), F32)],
        4 * rows * padded * D * D,
    )
    return jnp.transpose(out, (1, 0, 2)), rest


def own_heads(result, keep):
    kept = result * keep
    total = kept[0:TOK]
    for h in range(1, GH):
        total = total + kept[h * TOK : (h + 1) * TOK]
    return total


def cross_kernel(piece, padded, used, k_ref, v_ref, q_ref, keep_ref, ctx_ref, peak_ref, total_ref):
    step = pl.program_id(0)
    keep = keep_ref[...]
    keep_wide = keep.astype(F32)
    slot = lax.broadcasted_iota(jnp.int32, (padded, GL), 0)
    for g in range(G):
        cols = slice(g * GC, (g + 1) * GC)
        query = jnp.concatenate([q_ref[:, cols]] * GH, axis=0) * keep
        scores = product_back(k_ref[:, cols], query)
        for r in range(piece):
            rows = slice(r * padded, (r + 1) * padded)
            seen = slot < used[step * piece + r]
            own = jnp.where(seen, scores[rows], NEG)
            peak = jnp.max(own, axis=0, keepdims=True)
            exponent = jnp.where(seen, jnp.exp(own - peak), 0.0)
            total = jnp.sum(exponent, axis=0, keepdims=True)
            probs = (exponent * (1.0 / jnp.maximum(total, 1e-30))).astype(BF)
            ctx = own_heads(weight_grad(probs, v_ref[rows, cols]), keep_wide)
            ctx_ref[r * TOK : (r + 1) * TOK, cols] = ctx.astype(BF)
            peak_ref[r, g : g + 1, :] = peak
            total_ref[r, g : g + 1, :] = total


def cross_forward(used, keys, values, queries, keep, piece, padded):
    steps = queries.shape[0] // TOK
    rows = steps * piece
    big = pl.BlockSpec((piece * padded, D), lambda i, u: (i, 0))
    stat = pl.BlockSpec((piece, G, GL), lambda i, u: (i, 0, 0))
    return pl.pallas_call(
        functools.partial(cross_kernel, piece, padded),
        grid_spec=pltpu.PrefetchScalarGridSpec(
            num_scalar_prefetch=1,
            grid=(steps,),
            in_specs=[
                big,
                big,
                pl.BlockSpec((TOK, D), lambda i, u: (i, 0)),
                pl.BlockSpec((GL, GC), lambda i, u: (0, 0)),
            ],
            out_specs=[pl.BlockSpec((piece * TOK, D), lambda i, u: (i, 0)), stat, stat],
        ),
        out_shape=[
            jax.ShapeDtypeStruct((rows * TOK, D), BF),
            jax.ShapeDtypeStruct((rows, G, GL), F32),
            jax.ShapeDtypeStruct((rows, G, GL), F32),
        ],
        compiler_params=pltpu.CompilerParams(vmem_limit_bytes=VMEM_BYTES),
        cost_estimate=pl.CostEstimate(
            flops=4 * rows * padded * GL * D,
            bytes_accessed=4 * rows * padded * D,
            transcendentals=rows * padded * G * GL,
        ),
        name="cross_forward",
    )(used, keys, values, queries, keep)


def cross_back_kernel(
    piece, padded, used, k_ref, v_ref, q_ref, dc_ref, norm_ref, mid_ref, keep_ref, dq_ref, dk_ref, dv_ref
):
    step = pl.program_id(0)
    keep = keep_ref[...]
    keep_wide = keep.astype(F32)
    slot = lax.broadcasted_iota(jnp.int32, (padded, GL), 0)
    for g in range(G):
        cols = slice(g * GC, (g + 1) * GC)
        query = jnp.concatenate([q_ref[:, cols]] * GH, axis=0) * keep
        scores = product_back(k_ref[:, cols], query)
        parts = []
        for r in range(piece):
            rows = slice(r * padded, (r + 1) * padded)
            dctx = jnp.concatenate([dc_ref[r * TOK : (r + 1) * TOK, cols]] * GH, axis=0) * keep
            dprobs = product_back(v_ref[rows, cols], dctx)
            seen = slot < used[step * piece + r]
            probs = jnp.where(seen, jnp.exp(scores[rows] - norm_ref[r, g : g + 1, :]), 0.0)
            parts.append((probs * (dprobs - mid_ref[r, g : g + 1, :])).astype(BF))
            dv_ref[rows, cols] = product(probs.astype(BF), dctx).astype(BF)
        dscores = jnp.concatenate(parts, axis=0)
        dk_ref[:, cols] = product(dscores, query).astype(BF)
        dq_ref[:, cols] = own_heads(weight_grad(dscores, k_ref[:, cols]), keep_wide).astype(BF)


def cross_back(used, keys, values, queries, dctx, norm, middle, keep, piece, padded):
    steps = queries.shape[0] // TOK
    rows = steps * piece
    big = pl.BlockSpec((piece * padded, D), lambda i, u: (i, 0))
    stat = pl.BlockSpec((piece, G, GL), lambda i, u: (i, 0, 0))
    small = pl.BlockSpec((TOK, D), lambda i, u: (i, 0))
    return pl.pallas_call(
        functools.partial(cross_back_kernel, piece, padded),
        grid_spec=pltpu.PrefetchScalarGridSpec(
            num_scalar_prefetch=1,
            grid=(steps,),
            in_specs=[
                big,
                big,
                small,
                pl.BlockSpec((piece * TOK, D), lambda i, u: (i, 0)),
                stat,
                stat,
                pl.BlockSpec((GL, GC), lambda i, u: (0, 0)),
            ],
            out_specs=[small, big, big],
        ),
        out_shape=[
            jax.ShapeDtypeStruct((steps * TOK, D), BF),
            jax.ShapeDtypeStruct((rows * padded, D), BF),
            jax.ShapeDtypeStruct((rows * padded, D), BF),
        ],
        compiler_params=pltpu.CompilerParams(vmem_limit_bytes=VMEM_BYTES),
        cost_estimate=pl.CostEstimate(
            flops=10 * rows * padded * GL * D,
            bytes_accessed=8 * rows * padded * D,
            transcendentals=rows * padded * G * GL,
        ),
        name="cross_back",
    )(used, keys, values, queries, dctx, norm, middle, keep)


def z_copy(source, target, send, recv, device):
    return pltpu.make_async_remote_copy(
        src_ref=source,
        dst_ref=target,
        send_sem=send,
        recv_sem=recv,
        device_id=(lax.axis_index("dp"), device),
        device_id_type=MESH,
    )


def z_meet(ways):
    dp, mp = lax.axis_index("dp"), lax.axis_index("mp")
    barrier = pltpu.get_barrier_semaphore()
    for off in range(1, ways):
        pl.semaphore_signal(
            barrier, inc=1, device_id=(dp, lax.rem(mp + off, ways)), device_id_type=MESH
        )
    pl.semaphore_wait(barrier, ways - 1)


def nearest(c, ways):
    mp = lax.axis_index("mp")
    left_n, right_n = mp, ways - 1 - mp
    fewer = jnp.minimum(left_n, right_n)
    paired = c <= 2 * fewer
    distance = jnp.where(paired, (c + 1) // 2, c - fewer)
    left = jnp.where(paired, lax.rem(c, 2) == 1, left_n > right_n)
    return jnp.where(left, mp - distance, mp + distance), distance, left, paired


def table_words(table, start, count):
    if table.shape[0] == 1:
        return table[0, pl.ds(start, count), :]
    return jnp.concatenate([table[i, pl.ds(start, count), :] for i in range(table.shape[0])], axis=-1)


def table_load(table_ref, table, sems, tile, c, t):
    tiles = table.shape[1] // tile

    def copy(k):
        rows = pl.ds(k * tile, tile)
        return pltpu.make_async_copy(table_ref.at[:, rows, :], table.at[:, rows, :], sems.at[k])

    @pl.when((c == 0) & (t == 0))
    def _():
        for k in range(tiles):
            copy(k).start()

    for k in range(tiles):

        @pl.when((c == 0) & (t == k))
        def _(k=k):
            copy(k).wait()


def vocab_kernel(
    ways, tile, sub, chunk, h_ref, target_ref, table_ref, exp_ref, tops_ref, stats_ref,
    table, held, run, stats, table_sem, left_send, left_recv, right_send, right_recv,
    stat_send, stat_recv, own,
):
    c, t = pl.program_id(0), pl.program_id(1)
    last = pl.num_programs(1) - 1
    mp = lax.axis_index("mp")
    slot, distance, left, paired = nearest(c, ways)

    def to_right(source, place, hop):
        return z_copy(source, held.at[place], right_send.at[hop], right_recv.at[hop], mp + 1)

    def to_left(source, place, hop):
        return z_copy(source, held.at[place], left_send.at[hop], left_recv.at[hop], mp - 1)

    def stats_copy(off):
        return z_copy(
            stats,
            stats_ref.at[mp],
            stat_send.at[off - 1],
            stat_recv.at[off - 1],
            lax.rem(mp + off, ways),
        )

    @pl.when((c == 0) & (t == 0))
    def _():
        z_meet(ways)

        @pl.when(mp < ways - 1)
        def _():
            to_right(h_ref, mp, 0).start()

        @pl.when(mp > 0)
        def _():
            to_left(h_ref, mp, 0).start()

        local = pltpu.make_async_copy(h_ref, held.at[mp], own.at[0])
        local.start()
        local.wait()

    from_left = left | (paired & (lax.rem(c, 2) == 1))
    from_right = jnp.logical_not(left) | (paired & (lax.rem(c, 2) == 1))
    due = (c > 0) & (t == 0) & jnp.logical_not(paired & (lax.rem(c, 2) == 0))

    @pl.when(due & from_left)
    def _():
        place = mp - distance
        to_right(held.at[place], place, distance - 1).wait_recv()

        @pl.when(mp < ways - 1)
        def _():
            to_right(held.at[place], place, distance).start()

    @pl.when(due & from_right)
    def _():
        place = mp + distance
        to_left(held.at[place], place, distance - 1).wait_recv()

        @pl.when(mp > 0)
        def _():
            to_left(held.at[place], place, distance).start()

    table_load(table_ref, table, table_sem, tile, c, t)

    @pl.when(t == 0)
    def _():
        run[0:1, :] = jnp.full((1, chunk), NEG, F32)
        run[1:3, :] = jnp.zeros((2, chunk), F32)

    tokens = held[slot]
    target = target_ref[slot]
    parts = []
    for i in range(tile // sub):
        start = t * tile + i * sub
        logits = product_back(table_words(table, start, sub), tokens)
        top = jnp.max(logits, axis=0, keepdims=True)
        exponent = jnp.exp(logits - top)
        word = lax.broadcasted_iota(jnp.int32, (sub, chunk), 0) + start
        hit = jnp.where(word == target, logits, 0.0)
        exp_ref[0, i * sub : (i + 1) * sub, :] = exponent.astype(BF)
        tops_ref[0, pl.ds(t * (tile // sub) + i, 1), :] = top
        parts.append(
            (top, jnp.sum(exponent, axis=0, keepdims=True), jnp.sum(hit, axis=0, keepdims=True))
        )
    former = run[0:1, :]
    peak = former
    for top, total, hit in parts:
        peak = jnp.maximum(peak, top)
    sums = run[1:2, :] * jnp.exp(former - peak)
    hits = run[2:3, :]
    for top, total, hit in parts:
        sums += total * jnp.exp(top - peak)
        hits += hit
    run[0:1, :] = peak
    run[1:2, :] = sums
    run[2:3, :] = hits

    @pl.when(t == last)
    def _():
        stats[slot] = run[...]

    @pl.when((c == ways - 1) & (t == last))
    def _():
        for off in range(1, ways):
            stats_copy(off).start()
        local = pltpu.make_async_copy(stats, stats_ref.at[mp], own.at[1])
        local.start()
        for hop in range(ways - 1):

            @pl.when((mp < ways - 1) & (hop <= mp))
            def _(hop=hop):
                to_right(held.at[mp - hop], mp - hop, hop).wait_send()

            @pl.when((mp > 0) & (hop <= ways - 1 - mp))
            def _(hop=hop):
                to_left(held.at[mp + hop], mp + hop, hop).wait_send()

        for off in range(1, ways):
            stats_copy(off).wait()
        local.wait()


def vocab_sizes(words):
    tile = 1280 if words % 1280 == 0 else words
    sub = 256 if tile % 256 == 0 else tile
    return tile, sub


def vocab_forward(hidden, target, table, cid):
    ways = lax.axis_size("mp")
    chunk = hidden.shape[0]
    parts, words, width = table.shape
    tile, sub = vocab_sizes(words)
    tiles = words // tile
    top_rows = -(-(words // sub) // 8) * 8
    dma = pltpu.SemaphoreType.DMA
    return pl.pallas_call(
        functools.partial(vocab_kernel, ways, tile, sub, chunk),
        grid=(ways, tiles),
        in_specs=[
            pl.BlockSpec(memory_space=pl.ANY),
            pl.BlockSpec((ways, 1, chunk), lambda c, t: (0, 0, 0)),
            pl.BlockSpec(memory_space=pl.ANY),
        ],
        out_specs=[
            pl.BlockSpec((1, tile, chunk), lambda c, t: (c, t, 0)),
            pl.BlockSpec((1, top_rows, chunk), lambda c, t: (c, 0, 0)),
            pl.BlockSpec(memory_space=pl.ANY),
        ],
        out_shape=[
            jax.ShapeDtypeStruct((ways, words, chunk), BF),
            jax.ShapeDtypeStruct((ways, top_rows, chunk), F32),
            jax.ShapeDtypeStruct((ways, ways, 8, chunk), F32),
        ],
        scratch_shapes=[
            pltpu.VMEM(table.shape, BF),
            pltpu.VMEM((ways, chunk, D), BF),
            pltpu.VMEM((8, chunk), F32),
            pltpu.VMEM((ways, 8, chunk), F32),
            dma((tiles,)),
            dma((ways,)),
            dma((ways,)),
            dma((ways,)),
            dma((ways,)),
            dma((ways,)),
            dma((ways,)),
            dma((2,)),
        ],
        compiler_params=pltpu.CompilerParams(
            vmem_limit_bytes=VMEM_BYTES, collective_id=cid, has_side_effects=True
        ),
        cost_estimate=pl.CostEstimate(
            flops=2 * ways * chunk * words * D,
            bytes_accessed=2 * ways * words * D,
            transcendentals=ways * chunk * words,
        ),
        name="vocab_forward",
    )(hidden, target, table)


def vocab_back_kernel(
    ways, tile, sub, chunk, exp_ref, tops_ref, target_ref, norm_ref, rate_ref, table_ref, out_ref,
    table, total, leaving, landing, table_sem, send, recv,
):
    c, t = pl.program_id(0), pl.program_id(1)
    last = pl.num_programs(1) - 1
    mp = lax.axis_index("mp")
    slot = nearest(ways - 1 - c, ways)[0]

    def copy(k):
        to = nearest(ways - 1 - k, ways)[0]
        off = lax.rem(to - mp + ways, ways)
        return z_copy(leaving.at[k], landing.at[off - 1], send.at[k], recv.at[off - 1], to)

    @pl.when((c == 0) & (t == 0))
    def _():
        z_meet(ways)

    table_load(table_ref, table, table_sem, tile, c, t)
    target, norm, rate = target_ref[slot], norm_ref[slot], rate_ref[slot]
    term = None
    for i in range(tile // sub):
        start = t * tile + i * sub
        factor = jnp.exp(tops_ref[0, pl.ds(t * (tile // sub) + i, 1), :] - norm) * -rate
        word = lax.broadcasted_iota(jnp.int32, (sub, chunk), 0) + start
        hit = jnp.where(word == target, rate, 0.0)
        dlogits = hit + exp_ref[0, i * sub : (i + 1) * sub, :].astype(F32) * factor
        part = weight_grad(dlogits.astype(BF), table_words(table, start, sub))
        term = part if term is None else term + part

    @pl.when(t == 0)
    def _():
        total[...] = term

    @pl.when(t > 0)
    def _():
        total[...] += term

    for k in range(ways - 1):

        @pl.when((c == k) & (t == last))
        def _(k=k):
            leaving[k] = total[...].astype(BF)
            copy(k).start()

    @pl.when((c == ways - 1) & (t == last))
    def _():
        for k in range(ways - 1):
            copy(k).wait_send()
        for off in range(1, ways):
            z_copy(
                leaving.at[0], landing.at[off - 1], send.at[0], recv.at[off - 1], lax.rem(mp + off, ways)
            ).wait_recv()
        out = total[...]
        for k in range(ways - 1):
            out += landing[k].astype(F32)
        out_ref[...] = out


def vocab_back(exponents, tops, target, norm, rate, table, cid):
    ways, words, chunk = exponents.shape
    tile, sub = vocab_sizes(words)
    tiles = words // tile
    whole = pl.BlockSpec((ways, 1, chunk), lambda c, t: (0, 0, 0))
    dma = pltpu.SemaphoreType.DMA
    return pl.pallas_call(
        functools.partial(vocab_back_kernel, ways, tile, sub, chunk),
        grid=(ways, tiles),
        in_specs=[
            pl.BlockSpec((1, tile, chunk), lambda c, t: (ways - 1 - c, t, 0)),
            pl.BlockSpec((1, tops.shape[1], chunk), lambda c, t: (ways - 1 - c, 0, 0)),
            whole,
            whole,
            whole,
            pl.BlockSpec(memory_space=pl.ANY),
        ],
        out_specs=pl.BlockSpec((chunk, D), lambda c, t: (0, 0)),
        out_shape=jax.ShapeDtypeStruct((chunk, D), F32),
        scratch_shapes=[
            pltpu.VMEM(table.shape, BF),
            pltpu.VMEM((chunk, D), F32),
            pltpu.VMEM((ways - 1, chunk, D), BF),
            pltpu.VMEM((ways - 1, chunk, D), BF),
            dma((tiles,)),
            dma((ways,)),
            dma((ways,)),
        ],
        compiler_params=pltpu.CompilerParams(
            vmem_limit_bytes=VMEM_BYTES, collective_id=cid, has_side_effects=True
        ),
        cost_estimate=pl.CostEstimate(
            flops=2 * ways * chunk * words * D, bytes_accessed=2 * ways * words * D, transcendentals=0
        ),
        name="vocab_back",
    )(exponents, tops, target, norm, rate, table)


HIDDEN_TILE = 512
ROOT_HALF = 0.7071067811865476
ROOT_TAU = 0.3989422804014327


def expand_tile(ref):
    return ref[...].reshape(D, ref.shape[-1])


def shrink_tile(ref):
    if ref.shape[0] == 1:
        return ref[0, 0]
    return jnp.concatenate([ref[i, 0] for i in range(ref.shape[0])], axis=-1)


def feed_kernel(h_ref, expand_ref, bias_ref, shrink_ref, a_ref, out_ref):
    t = pl.program_id(0)
    hidden = product(h_ref[...], expand_tile(expand_ref)) + bias_ref[0]
    a_ref[...] = hidden
    active = (hidden * (0.5 + 0.5 * lax.erf(hidden * ROOT_HALF))).astype(BF)
    term = product(active, shrink_tile(shrink_ref))

    @pl.when(t == 0)
    def _():
        out_ref[...] = term

    @pl.when(t > 0)
    def _():
        out_ref[...] += term


def feed_specs(expand_all, shrink_all):
    per = expand_all.shape[3] // HIDDEN_TILE
    parts, _, rows, _ = expand_all.shape
    return (
        pl.BlockSpec((parts, 1, rows, HIDDEN_TILE), lambda t: (0, t // per, 0, t % per)),
        pl.BlockSpec((1, 1, HIDDEN_TILE), lambda t: (t, 0, 0)),
        pl.BlockSpec(
            (shrink_all.shape[0], 1, HIDDEN_TILE, shrink_all.shape[3]),
            lambda t: (0, t // per, t % per, 0),
        ),
        expand_all.shape[1] * per,
    )


def feed_forward(hidden, expand_all, bias, shrink_all):
    tokens = hidden.shape[0]
    expand_spec, bias_spec, shrink_spec, tiles = feed_specs(expand_all, shrink_all)
    whole = pl.BlockSpec((tokens, D), lambda t: (0, 0))
    units = tiles * HIDDEN_TILE
    return pl.pallas_call(
        feed_kernel,
        grid=(tiles,),
        in_specs=[whole, expand_spec, bias_spec, shrink_spec],
        out_specs=[pl.BlockSpec((tokens, HIDDEN_TILE), lambda t: (0, t)), whole],
        out_shape=[
            jax.ShapeDtypeStruct((tokens, units), F32),
            jax.ShapeDtypeStruct((tokens, D), F32),
        ],
        compiler_params=pltpu.CompilerParams(vmem_limit_bytes=VMEM_BYTES),
        cost_estimate=pl.CostEstimate(
            flops=4 * tokens * units * D, bytes_accessed=4 * units * D, transcendentals=tokens * units
        ),
        name="feed_forward",
    )(hidden, expand_all, bias.reshape(tiles, 1, HIDDEN_TILE), shrink_all)


def feed_back_kernel(
    dout_ref, h_ref, a_ref, expand_ref, shrink_ref, dexpand_ref, dshrink_ref, dbias_ref, dh_ref
):
    t = pl.program_id(0)
    dout = dout_ref[...]
    hidden = a_ref[...]
    below = 0.5 + 0.5 * lax.erf(hidden * ROOT_HALF)
    slope = below + hidden * (ROOT_TAU * jnp.exp(-0.5 * hidden * hidden))
    active = (hidden * below).astype(BF)
    dhidden = (slope * product_back(dout, shrink_tile(shrink_ref))).astype(BF)
    dbias_ref[0] = jnp.sum(dhidden.astype(F32), axis=0, keepdims=True)
    dshrink = weight_grad(active, dout).astype(BF)
    width = dshrink_ref.shape[2]
    for i in range(dshrink_ref.shape[0]):
        dshrink_ref[i] = dshrink[:, i * width : (i + 1) * width]
    dexpand_ref[...] = weight_grad(h_ref[...], dhidden).astype(BF)
    term = product_back(dhidden, expand_tile(expand_ref))

    @pl.when(t == 0)
    def _():
        dh_ref[...] = term

    @pl.when(t > 0)
    def _():
        dh_ref[...] += term


def feed_back(dout, hidden, before, expand_all, shrink_all):
    tokens = hidden.shape[0]
    expand_spec, bias_spec, shrink_spec, tiles = feed_specs(expand_all, shrink_all)
    parts, width = shrink_all.shape[0], shrink_all.shape[3]
    whole = pl.BlockSpec((tokens, D), lambda t: (0, 0))
    units = tiles * HIDDEN_TILE
    return pl.pallas_call(
        feed_back_kernel,
        grid=(tiles,),
        in_specs=[
            whole,
            whole,
            pl.BlockSpec((tokens, HIDDEN_TILE), lambda t: (0, t)),
            expand_spec,
            shrink_spec,
        ],
        out_specs=[
            pl.BlockSpec((D, HIDDEN_TILE), lambda t: (0, t)),
            pl.BlockSpec((parts, HIDDEN_TILE, width), lambda t: (0, t, 0)),
            bias_spec,
            whole,
        ],
        out_shape=[
            jax.ShapeDtypeStruct((D, units), BF),
            jax.ShapeDtypeStruct((parts, units, width), BF),
            jax.ShapeDtypeStruct((tiles, 1, HIDDEN_TILE), F32),
            jax.ShapeDtypeStruct((tokens, D), F32),
        ],
        compiler_params=pltpu.CompilerParams(vmem_limit_bytes=VMEM_BYTES),
        cost_estimate=pl.CostEstimate(
            flops=8 * tokens * units * D, bytes_accessed=8 * units * D, transcendentals=2 * tokens * units
        ),
        name="feed_back",
    )(dout, hidden, before, expand_all, shrink_all)


def self_probs(queries, key_heads):
    causal = (
        lax.broadcasted_iota(jnp.int32, (TOK, TOK), 1)
        <= lax.broadcasted_iota(jnp.int32, (TOK, TOK), 0)
    )[None, None]
    scores = jnp.einsum("rqhe,rkhe->rhqk", queries, key_heads, preferred_element_type=F32)
    return jax.nn.softmax(jnp.where(causal, scores, NEG), axis=-1)


def column_parts(gathered):
    return jnp.concatenate([gathered[i] for i in range(gathered.shape[0])], axis=-1)


def block_rows(array, ways):
    rows, columns = array.shape
    width = columns // ways
    return jnp.stack([array[:, i * width : (i + 1) * width] for i in range(ways)])


def local(
    answers,
    targets,
    doc_scores,
    memory,
    lengths,
    self_query,
    self_key,
    self_value,
    query_bias,
    value_bias,
    self_output,
    output_bias,
    first_gain,
    first_shift,
    cross_query,
    crossq_bias,
    cross_key,
    cross_value,
    crossv_bias,
    cross_output,
    crosso_bias,
    second_gain,
    second_shift,
    expand_weight,
    expand_bias,
    shrink_weight,
    shrink_bias,
    third_gain,
    third_shift,
    word_table,
):
    dp_ways, mp_ways = lax.axis_size("dp"), lax.axis_size("mp")
    chips = dp_ways // 2
    dp, mp = lax.axis_index("dp"), lax.axis_index("mp")
    groups = answers.shape[0]
    rows, slots, _ = memory.shape
    piece = rows // dp_ways
    own_q = dp_ways
    uniq = own_q * TOK
    tokens = rows * TOK
    padded = -(-slots // 16) * 16
    shard_rows = rows // mp_ways
    shard_tokens = shard_rows * TOK
    shard_q = own_q // mp_ways
    shard_uniq = shard_q * TOK
    local_heads = H // mp_ways
    head_cols = local_heads * HD
    hidden_cols = expand_weight.shape[1]
    vec = D // dp_ways

    vectors = (
        output_bias,
        first_gain,
        first_shift,
        crosso_bias,
        second_gain,
        second_shift,
        shrink_bias,
        third_gain,
        third_shift,
        crossv_bias,
    )
    matrices = (query_bias, value_bias, crossq_bias, expand_bias)
    starts, top = [], 16
    for matrix in matrices:
        starts.append(top)
        top += -(-matrix.shape[0] // 8) * 8
    small_rows = -(-top // 16) * 16
    row_of = lax.broadcasted_iota(jnp.int32, (small_rows, 128), 0)
    small = jnp.zeros((small_rows, 128), BF)
    for i, vector in enumerate(vectors):
        vector = jnp.pad(vector, (0, 128 - vector.shape[0]))
        small = jnp.where(row_of == i, vector[None, :], small)
    for start, matrix in zip(starts, matrices):
        count, width = matrix.shape
        small += jnp.pad(matrix, ((start, small_rows - start - count), (0, 128 - width)))
    wide_rows = cross_key.shape[0]
    self_shard = jnp.concatenate([self_query, self_key, self_value], axis=1)
    target_rows = jnp.pad(targets, ((0, 8 - groups), (0, 128 - TOK)))
    doc_rows = jnp.pad(doc_scores, ((0, 8 - groups), (0, 128 - K)))
    if chips == groups:
        wanted = answers
    else:
        wanted = jnp.stack([answers[(2 * c * piece) // K] for c in range(chips)])
    key_all, value_all, small_all, cquery_z, cout_z = exchange(
        [
            (cross_key, "wide", ""),
            (cross_value, "wide", ""),
            (small, "wide", ""),
            (cross_query, "gather", "z"),
            (cross_output, "gather", "z"),
        ],
        0,
    )
    (full_obias, gain_one, shift_one, full_cobias, gain_two, shift_two, full_sbias, gain_three, shift_three) = [
        small_all[:, 0, i, :vec].reshape(D) for i in range(9)
    ]
    cvbias = small_all[:, :, 9, :wide_rows].reshape(1, D)

    def head_bias(i):
        count, width = matrices[i].shape
        part = small_all[:, :, starts[i] : starts[i] + count, :width]
        return jnp.transpose(part, (1, 2, 0, 3)).reshape(mp_ways, -1)

    mine = lambda a: lax.dynamic_index_in_dim(a, mp, 0, keepdims=False)
    qbias = mine(head_bias(0))
    vbias = mine(head_bias(1))
    cqbias = head_bias(2).reshape(-1)
    ebias = head_bias(3).reshape(-1)
    key_weight = key_all.reshape(D, D)
    value_weight = value_all.reshape(D, D)

    plan = Exchange(
        [
            (expand_weight, "gather", "z"),
            (shrink_weight, "gather", "z"),
            (self_shard, "near", ""),
            (self_output, "near", ""),
            (target_rows, "near", ""),
            (doc_rows, "near", ""),
            (wanted, "nearswap", ""),
            (cquery_z, "near", ""),
            (cout_z, "near", ""),
        ]
    )
    (keys, values, memory_rows, expand_z, shrink_z, self_all, output_all, target_all, doc_all, x_all, cquery_all, cout_all) = (
        memory_products(memory, key_weight, value_weight, cvbias, padded, plan, 1)
    )
    table_all = lax.all_gather(word_table, "dp", axis=0, tiled=False)
    expand_z, shrink_z, table_all = lax.optimization_barrier((expand_z, shrink_z, table_all))
    expand_all = lax.all_gather(expand_z, "dp", axis=0, tiled=False)
    shrink_all = lax.all_gather(shrink_z, "dp", axis=0, tiled=False)
    if word_table.shape[1] < 128:
        table_all = column_parts(table_all)[None]
    rows_first = lambda a: jnp.transpose(a, (0, 2, 1, 3)).reshape(dp_ways * a.shape[2], -1)
    columns_first = lambda a: column_parts(a.reshape(dp_ways, -1, a.shape[-1]))
    if shrink_all.shape[-1] < 128:
        shrink_all = columns_first(shrink_all).reshape(1, mp_ways, -1, D)
    full_cquery = rows_first(cquery_all)
    full_cout = columns_first(cout_all)
    self_weight = self_all.reshape(D, 3 * head_cols)
    full_output = column_parts(output_all)
    my_group = (dp * piece) // K
    row_targets = lax.dynamic_index_in_dim(
        target_all[:, :groups, :TOK], my_group, 1, keepdims=False
    )
    x_rows = x_all.reshape(uniq, D)

    qkv = product(x_rows, self_weight)
    queries = ((qkv[:, :head_cols] + qbias) * SCALE).astype(BF)
    self_keys = qkv[:, head_cols : 2 * head_cols].astype(BF)
    self_values = (qkv[:, 2 * head_cols :] + vbias).astype(BF)
    heads = lambda a: a.reshape(own_q, TOK, local_heads, HD)
    probs = self_probs(heads(queries), heads(self_keys))
    context = jnp.einsum(
        "rhqk,rkhe->rqhe", probs.astype(BF), heads(self_values), preferred_element_type=F32
    )
    context = context.astype(BF).reshape(uniq, head_cols)
    partial = product(context, full_output).astype(BF).reshape(mp_ways, shard_uniq, D)
    (received,) = exchange([(partial, "move", "z")], 2)
    x_own = lax.dynamic_slice_in_dim(x_rows, mp * shard_uniq, shard_uniq, 0)
    first_in = x_own.astype(F32) + added(partial, received, "z") + full_obias
    hidden_one, normed_one, inverse_one = layer_norm(first_in, gain_one, shift_one)
    hidden_low1 = hidden_one.astype(BF)
    cross_queries = ((product(hidden_low1, full_cquery) + cqbias) * SCALE).astype(BF)
    (cross_queries,) = exchange([(cross_queries, "gather", "z")], 3)
    cross_queries = cross_queries.reshape(uniq, D)

    used = jnp.clip(lengths - mp * slots, 0, slots).astype(jnp.int32)
    keep = (
        lax.broadcasted_iota(jnp.int32, (GL, GC), 0) // TOK
        == lax.broadcasted_iota(jnp.int32, (GL, GC), 1) // HD
    ).astype(BF)
    ctx_part, peak_part, total_part = cross_forward(
        used, keys, values, cross_queries, keep, piece, padded
    )
    ctx_part = ctx_part.reshape(mp_ways, shard_tokens, D)
    stat_part = jnp.stack([peak_part, total_part], axis=1).reshape(mp_ways, shard_rows, 2, G, GL)
    ctx_got, stat_got = exchange([(ctx_part, "move", "z"), (stat_part, "move", "z")], 4)
    stat_own = lax.dynamic_index_in_dim(stat_part, mp, 0, keepdims=True)
    stat_got = jnp.concatenate([stat_own, stat_got], axis=0)
    peak_got, total_got = stat_got[:, :, 0], stat_got[:, :, 1]
    peak = jnp.max(peak_got, axis=0)
    weight = total_got * jnp.exp(peak_got - peak)
    total = jnp.sum(weight, axis=0)
    cross_norm = peak + jnp.log(total)
    weight = weight / total

    def to_token_heads(a):
        lead = a.shape[:-3]
        a = a.reshape(lead + (shard_rows, H, TOK))
        return jnp.swapaxes(a, -1, -2).reshape(lead + (shard_tokens, H))

    weight = jnp.repeat(to_token_heads(weight), HD, axis=-1)
    ctx_own = lax.dynamic_index_in_dim(ctx_part, mp, 0, keepdims=False)
    context_two = (
        ctx_own.astype(F32) * weight[0] + jnp.sum(ctx_got.astype(F32) * weight[1:], axis=0)
    ).astype(BF)

    def to_rows(a):
        a = jnp.broadcast_to(a.reshape(shard_q, 1, TOK, D), (shard_q, piece, TOK, D))
        return a.reshape(shard_tokens, D)

    second_in = to_rows(hidden_one) + product(context_two, full_cout) + full_cobias
    hidden_two, normed_two, inverse_two = layer_norm(second_in, gain_two, shift_two)
    hidden_low2 = hidden_two.astype(BF)

    expanded, third_in = feed_forward(hidden_low2, expand_all, ebias, shrink_all)
    third_in = hidden_two + third_in + full_sbias
    hidden_three, normed_three, inverse_three = layer_norm(third_in, gain_three, shift_three)

    vocab_local = table_all.shape[1]
    token_targets = jnp.broadcast_to(row_targets.reshape(own_q, 1, TOK), (own_q, piece, TOK))
    local_target = token_targets.reshape(mp_ways, 1, shard_tokens) - mp * vocab_local
    exponents, tops, stats = vocab_forward(hidden_three.astype(BF), local_target, table_all, 5)
    stats = jnp.transpose(stats[:, :, :3], (0, 2, 1, 3)).reshape(mp_ways, 3, tokens)
    top = jnp.max(stats[:, 0], axis=0)
    norm_log = top + jnp.log(jnp.sum(stats[:, 1] * jnp.exp(stats[:, 0] - top), axis=0))
    loglik = jnp.sum(stats[:, 2], axis=0) - norm_log
    (loglik_all,) = exchange([(loglik.reshape(tokens // 128, 128), "gather", "dp")], 7)
    loglik_all = loglik_all.reshape(dp_ways, own_q, piece, TOK)
    loglik_all = jnp.transpose(loglik_all, (1, 0, 2, 3)).reshape(own_q, groups, K, TOK)
    doc_logp = jax.nn.log_softmax(doc_all[:, :groups, :K], axis=2)
    joined = doc_logp[..., None] + loglik_all
    marginal = jax.nn.logsumexp(joined, axis=2, keepdims=True)
    question_loss = -jnp.mean(
        lax.dynamic_index_in_dim(marginal[:, :, 0], dp, 0, keepdims=False), axis=1
    )
    posterior = jnp.exp(joined - marginal).reshape(own_q, groups * K, TOK)
    rate = -lax.dynamic_slice_in_dim(posterior, dp * piece, piece, 1)
    by_slot = lambda a: a.reshape(mp_ways, 1, shard_tokens)
    dhidden_three = vocab_back(
        exponents, tops, local_target, by_slot(norm_log), by_slot(rate), table_all, 8
    )

    dthird, dgain_three, dshift_three = norm_back(
        dhidden_three, normed_three, inverse_three, gain_three
    )
    dshrink_bias = jnp.sum(dthird, axis=0)
    dshrink_in = dthird.astype(BF)
    dexpand, dshrink, dexpand_bias, dhidden_two = feed_back(
        dshrink_in, hidden_low2, expanded, expand_all, shrink_all
    )
    dexpand_bias = dexpand_bias.reshape(-1)
    if dshrink.shape[0] < dp_ways:
        dshrink = block_rows(dshrink[0], dp_ways)
    shrink_dp = lax.psum_scatter(dshrink, "dp", scatter_dimension=0, tiled=False)
    expand_dp = lax.psum_scatter(dexpand, "dp", scatter_dimension=0, tiled=True)
    dhidden_two = dthird + dhidden_two

    dsecond, dgain_two, dshift_two = norm_back(dhidden_two, normed_two, inverse_two, gain_two)
    dcout_bias = jnp.sum(dsecond, axis=0)
    dcout_in = dsecond.astype(BF)
    dcontext_two = product_back(dcout_in, full_cout).astype(BF)
    middle = jnp.sum(
        (dcontext_two.astype(F32) * context_two.astype(F32)).reshape(shard_tokens, H, HD), axis=-1
    )
    middle = jnp.swapaxes(middle.reshape(shard_rows, TOK, H), 1, 2).reshape(shard_rows, G, GL)
    owners = lambda a: a.reshape(chips, 2, -1, a.shape[-1])
    cast = lambda a: a.astype(BF)
    co_blocks = owners(cast(weight_grad(dcout_in, context_two)))
    stat_all = jnp.stack([cross_norm, middle])
    dctx_all, stat_all, received = exchange(
        [(dcontext_two, "gather", "z"), (stat_all, "gather", "z"), (co_blocks, "move1", "pair")], 9
    )
    co_blocks = cast(added(co_blocks, received, "pair"))
    norm_all = stat_all[:, 0].reshape(rows, G, GL)
    middle_all = stat_all[:, 1].reshape(rows, G, GL)
    dcross_q, dkeys, dvalues = cross_back(
        used,
        keys,
        values,
        cross_queries,
        dctx_all.reshape(tokens, D),
        norm_all,
        middle_all,
        keep,
        piece,
        padded,
    )
    dcross_q = dcross_q.reshape(mp_ways, shard_uniq, D)
    expand_blocks = jnp.transpose(expand_dp.reshape(vec, mp_ways, -1), (1, 0, 2))
    plan = Exchange(
        [(dcross_q, "move", "z"), (co_blocks, "move", "chips"), (expand_blocks, "move", "z")]
    )
    dkey_weight, dvalue_weight, dvalue_bias, received, co_got, expand_got = memory_weights(
        memory_rows, dkeys, dvalues, rows, padded, plan, 10
    )
    dcross_low = (added(dcross_q, received, "z") * SCALE).astype(BF)
    dcquery = weight_grad(hidden_low1, dcross_low)
    dcq_bias = jnp.sum(dcross_low, axis=0, dtype=F32)
    dhidden_one = jnp.sum(dsecond.reshape(shard_q, piece, TOK, D), axis=1).reshape(
        shard_uniq, D
    ) + product_back(dcross_low, full_cquery)

    dfirst, dgain_one, dshift_one = norm_back(dhidden_one, normed_one, inverse_one, gain_one)
    dout_bias = jnp.sum(dfirst, axis=0)
    first_blocks = [owners(dkey_weight), owners(dvalue_weight), owners(cast(dcquery))]
    dout_in, *received = exchange(
        [(cast(dfirst), "gather", "z")] + [(a, "move1", "pair") for a in first_blocks], 11
    )
    key_blocks, value_blocks, cq_blocks = [
        cast(added(a, b, "pair")) for a, b in zip(first_blocks, received)
    ]
    dout_in = dout_in.reshape(uniq, D)
    doutput = weight_grad(dout_in, context)
    dcontext = heads(product_back(dout_in, full_output).astype(BF))
    dvalue_h = jnp.einsum("rhqk,rqhe->rkhe", probs.astype(BF), dcontext, preferred_element_type=F32)
    dprobs = jnp.einsum("rqhe,rkhe->rhqk", dcontext, heads(self_values), preferred_element_type=F32)
    dscores = (probs * (dprobs - jnp.sum(probs * dprobs, axis=-1, keepdims=True))).astype(BF)
    dquery_h = jnp.einsum("rhqk,rkhe->rqhe", dscores, heads(self_keys), preferred_element_type=F32)
    dkey_h = jnp.einsum("rhqk,rqhe->rkhe", dscores, heads(queries), preferred_element_type=F32)
    flat = lambda a: a.reshape(uniq, head_cols)
    dqkv = jnp.concatenate(
        [flat(dquery_h * SCALE).astype(BF), flat(dkey_h).astype(BF), flat(dvalue_h).astype(BF)], axis=1
    )
    dself = weight_grad(x_rows, dqkv)
    dqkv_bias = jnp.sum(dqkv, axis=0, dtype=F32)
    partial = product_back(dqkv, self_weight).astype(BF).reshape(mp_ways, shard_uniq, D)
    received, key_got = exchange([(partial, "move", "z"), (key_blocks, "move", "chips")], 12)
    dinputs = cast(dfirst + added(partial, received, "z"))

    vectors = jnp.stack(
        [
            dout_bias,
            dgain_one,
            dshift_one,
            dcout_bias,
            dgain_two,
            dshift_two,
            dshrink_bias,
            dgain_three,
            dshift_three,
            dvalue_bias[0],
        ]
    )
    by_dp = lambda a, width: jnp.swapaxes(a.reshape(-1, dp_ways, width), 0, 1).reshape(dp_ways, -1)
    vector_parts = [
        by_dp(vectors, vec),
        by_dp(dcq_bias, crossq_bias.shape[1]),
        by_dp(dexpand_bias, expand_bias.shape[1]),
        by_dp(dqkv_bias[:head_cols], query_bias.shape[1]),
        by_dp(dqkv_bias[2 * head_cols :], value_bias.shape[1]),
    ]
    ends = [sum(a.shape[1] for a in vector_parts[: i + 1]) for i in range(5)]
    vector_blocks = jnp.concatenate(vector_parts, axis=1)
    length = vector_blocks.shape[1]
    vector_rows = -(-length // 1024) * 8
    vector_blocks = owners(
        jnp.pad(vector_blocks, ((0, 0), (0, vector_rows * 128 - length))).reshape(-1, 128)
    )
    self_blocks = owners(cast(dself))
    out_blocks = owners(cast(doutput))
    last_blocks = [self_blocks, out_blocks, vector_blocks]
    dinputs, value_got, *received = exchange(
        [(dinputs, "gather", "z"), (value_blocks, "move", "chips")]
        + [(a, "move1", "pair") for a in last_blocks],
        13,
    )
    last_blocks = [added(a, b, "pair").astype(a.dtype) for a, b in zip(last_blocks, received)]
    answer_blocks = dinputs.reshape(chips, 2, TOK, D)
    last_blocks = [cq_blocks, *last_blocks, answer_blocks]
    shrink_blocks = shrink_dp.reshape(mp_ways, -1, vec)
    plan = Exchange(
        [(a, "move", "chips") for a in last_blocks] + [(shrink_blocks, "move", "z")]
    )
    memory_grad, received = memory_back(
        dkeys, dvalues, key_weight, value_weight, rows, slots, padded, plan, 15
    )
    expand_grad = added(expand_blocks, expand_got, "z")
    shrink_grad = added(shrink_blocks, received[5], "z")
    cq_sum, self_grad, out_grad, vector_sum = [
        added(a, b, "chips") for a, b in zip(last_blocks[:4], received[:4])
    ]

    own_answers = lax.dynamic_index_in_dim(answer_blocks, dp // 2, 0, keepdims=True)
    returned = jnp.concatenate([own_answers, received[4]], axis=0).astype(F32)
    source = lax.rem(dp // 2 + chips - jnp.arange(chips), chips)
    place = (2 * source * piece) // K
    pick = (place[None, :] == jnp.arange(groups)[:, None]).astype(F32)
    answer_part = cast(jnp.sum(pick[:, :, None, None, None] * returned[None], axis=1))

    key_sum = added(key_blocks, key_got, "chips")
    value_sum = added(value_blocks, value_got, "chips")
    co_sum = added(co_blocks, co_got, "chips")
    by_columns = lambda a: jnp.transpose(a.reshape(vec, mp_ways, -1), (1, 0, 2))
    zblocks = [
        cast(key_sum).reshape(mp_ways, wide_rows, D),
        cast(value_sum).reshape(mp_ways, wide_rows, D),
        by_columns(cast(cq_sum)),
        by_columns(cast(co_sum)),
    ]
    *got_z, vector_all, answer_got = exchange(
        [(a, "move", "z") for a in zblocks]
        + [(vector_sum, "gather", "z"), (answer_part, "move1", "pair")],
        16,
    )
    key_grad, value_grad, cquery_grad, cout_grad = [
        added(a, b, "z") for a, b in zip(zblocks, got_z)
    ]
    cout_grad = cout_grad.T
    out_grad = out_grad.T
    answer_grad = added(answer_part, answer_got, "pair")
    vector_all = vector_all.reshape(mp_ways, -1)
    vector_own = jnp.sum(vector_all, axis=0)
    head_own = lax.dynamic_index_in_dim(vector_all, mp, 0, keepdims=False)

    def vec_of(i):
        return vector_own[i * vec : (i + 1) * vec]

    def mp_rows(start, shape):
        part = vector_own[start : start + mp_ways * shape[0] * shape[1]]
        part = part.reshape(mp_ways, shape[0], shape[1])
        return lax.dynamic_index_in_dim(part, mp, 0, keepdims=False)

    return (
        question_loss,
        answer_grad,
        memory_grad,
        self_grad[:, :head_cols],
        self_grad[:, head_cols : 2 * head_cols],
        self_grad[:, 2 * head_cols :],
        head_own[ends[2] : ends[3]].reshape(query_bias.shape),
        head_own[ends[3] : ends[4]].reshape(value_bias.shape),
        out_grad,
        vec_of(0),
        vec_of(1),
        vec_of(2),
        cquery_grad,
        mp_rows(ends[0], crossq_bias.shape),
        key_grad,
        value_grad,
        lax.dynamic_slice_in_dim(vec_of(9), mp * wide_rows, wide_rows, 0),
        cout_grad,
        vec_of(3),
        vec_of(4),
        vec_of(5),
        expand_grad,
        mp_rows(ends[1], expand_bias.shape),
        shrink_grad,
        vec_of(6),
        vec_of(7),
        vec_of(8),
    )


def solution(mesh):
    placed = (
        P("dp", None, None),
        P("dp", None),
        P("dp", None),
        P("dp", "mp", None),
        P("dp"),
        P("dp", "mp"),
        P("dp", "mp"),
        P("dp", "mp"),
        P("mp", "dp"),
        P("mp", "dp"),
        P("mp", "dp"),
        P("dp"),
        P("dp"),
        P("dp"),
        P("dp", "mp"),
        P("mp", "dp"),
        P(("dp", "mp"), None),
        P(("dp", "mp"), None),
        P(("dp", "mp")),
        P("mp", "dp"),
        P("dp"),
        P("dp"),
        P("dp"),
        P("dp", "mp"),
        P("mp", "dp"),
        P("mp", "dp"),
        P("dp"),
        P("dp"),
        P("dp"),
        P("mp", "dp"),
    )
    return jax.shard_map(
        local,
        mesh=mesh,
        in_specs=placed,
        out_specs=(
            P("dp"),
            P("dp", None, None),
            P("dp", "mp", None),
            P("dp", "mp"),
            P("dp", "mp"),
            P("dp", "mp"),
            P("mp", "dp"),
            P("mp", "dp"),
            P("mp", "dp"),
            P("dp"),
            P("dp"),
            P("dp"),
            P("dp", "mp"),
            P("mp", "dp"),
            P(("dp", "mp"), None),
            P(("dp", "mp"), None),
            P(("dp", "mp")),
            P("mp", "dp"),
            P("dp"),
            P("dp"),
            P("dp"),
            P("dp", "mp"),
            P("mp", "dp"),
            P("mp", "dp"),
            P("dp"),
            P("dp"),
            P("dp"),
        ),
        check_vma=False,
    )
```

```python
import functools

import jax
import jax.numpy as jnp
from jax import lax
from jax.experimental import pallas as pl
from jax.experimental.pallas import tpu as pltpu
from jax.sharding import PartitionSpec as P

D = 1024
H = 16
HD = 64
TOK = 32
K = 8
G = 4
GH = 4
GC = GH * HD
GL = GH * TOK

EPS = 1e-05
NEG = -1e30
SCALE = 0.125
BF = jnp.bfloat16
F32 = jnp.float32
MESH = pl.DeviceIdType.MESH
DP, MP = "dp", "mp"
GATHER, LATE, MOVE, MOVE1, COLS, NEAR, NEARSWAP, WIDE = range(8)
Z, CHIPS, PAIR = range(3)
PLAIN, COLUMNS, TURNED = range(3)
VMEM_BYTES = 60 * 1024 * 1024


def product(former, latter):
    return jnp.dot(former, latter, preferred_element_type=F32)


def product_back(former, latter):
    return lax.dot_general(former, latter, (((1,), (1,)), ((), ())), preferred_element_type=F32)


def weight_grad(former, latter):
    return lax.dot_general(former, latter, (((0,), (0,)), ((), ())), preferred_element_type=F32)


def layer_norm(entries, norm_gain, norm_shift):
    center = entries - jnp.mean(entries, axis=-1, keepdims=True)
    inverse = lax.rsqrt(jnp.mean(center * center, axis=-1, keepdims=True) + EPS)
    normed = center * inverse
    return (normed * norm_gain + norm_shift, normed, inverse)


def norm_back(upstream, normed, inverse, norm_gain):
    scaled = upstream * norm_gain
    dentries = inverse * (
        scaled
        - jnp.mean(scaled, axis=-1, keepdims=True)
        - normed * jnp.mean(scaled * normed, axis=-1, keepdims=True)
    )
    return (dentries, jnp.sum(upstream * normed, axis=0), jnp.sum(upstream, axis=0))


class Exchange:
    def __init__(self, entries):
        self.dp_ways, self.mp_ways = lax.axis_size(DP), lax.axis_size(MP)
        self.chips = self.dp_ways // 2
        self.ways = {Z: self.mp_ways, CHIPS: self.chips, PAIR: 2, DP: self.dp_ways}
        self.arrays = [entry[0] for entry in entries]
        self.kinds = [entry[1] for entry in entries]
        self.groups = [entry[2] for entry in entries]
        self.count = len(entries)
        shapes = []
        for array, kind, group in entries:
            shape = array.shape
            if kind in (GATHER, LATE):
                shape = (self.ways[group],) + shape
            elif kind == MOVE:
                shape = (self.ways[group] - 1,) + shape[1:]
            elif kind == MOVE1:
                shape = (self.ways[group] - 1, shape[0]) + shape[2:]
            elif kind == COLS:
                shape = (self.ways[group] - 1,) + shape[:-1] + (shape[-1] // self.ways[group],)
            elif kind == NEAR:
                shape = (self.dp_ways,) + shape
            elif kind == NEARSWAP:
                shape = (self.dp_ways,) + shape[1:]
            else:
                shape = (self.dp_ways, self.mp_ways) + shape
            shapes.append(jax.ShapeDtypeStruct(shape, array.dtype))
        self.shapes = shapes
        self.specs = [pl.BlockSpec(memory_space=pl.ANY)] * self.count
        dma = pltpu.SemaphoreType.DMA
        most = max(self.dp_ways, self.mp_ways)
        self.scratch = [dma((self.count, most)) for _ in range(6)] + [dma((self.count,))]

    def bind(self, ins, outs, sems):
        self.ins, self.outs = ins, outs
        self.zs, self.zr, self.cs, self.cr, self.ps, self.pr, self.own = sems
        dp, mp = lax.axis_index(DP), lax.axis_index(MP)
        self.dp, self.mp = dp, mp
        self.parity, self.chip = lax.rem(dp, 2), dp // 2
        self.place = {Z: mp, CHIPS: self.chip, PAIR: self.parity, DP: dp}

    def device(self, group, j):
        if group == Z:
            return (self.dp, j)
        if group == CHIPS:
            return (2 * j + self.parity, self.mp)
        if group == PAIR:
            return (self.dp - self.parity + j, self.mp)
        return (j, self.mp)

    def peer(self, group, off):
        return lax.rem(self.place[group] + off, self.ways[group])

    def remote(self, source, target, send, recv, device):
        return pltpu.make_async_remote_copy(
            src_ref=source,
            dst_ref=target,
            send_sem=send,
            recv_sem=recv,
            device_id=device,
            device_id_type=MESH,
        )

    def meet(self, also=()):
        needed = set(also)
        for kind, group in zip(self.kinds, self.groups):
            if kind in (NEAR, NEARSWAP, WIDE):
                needed |= {CHIPS, PAIR}
                if kind == WIDE:
                    needed.add(Z)
            else:
                needed.add(group)
        barrier = pltpu.get_barrier_semaphore()
        total = 0
        for group in sorted(needed, key=str):
            for off in range(1, self.ways[group]):
                pl.semaphore_signal(
                    barrier,
                    inc=1,
                    device_id=self.device(group, self.peer(group, off)),
                    device_id_type=MESH,
                )
                total += 1
        pl.semaphore_wait(barrier, total)

    def first(self, i):
        kind, group = self.kinds[i], self.groups[i]
        ref, out = self.ins[i], self.outs[i]
        copies = []
        if kind in (NEAR, NEARSWAP):
            return copies
        if kind == WIDE:
            group, slot = Z, out.at[self.dp, self.mp]
        for off in range(1, self.ways[group]):
            peer = self.peer(group, off)
            if kind == WIDE:
                source, target = ref, slot
            elif kind in (GATHER, LATE):
                source, target = ref, out.at[self.place[group]]
            elif kind == MOVE:
                source, target = ref.at[peer], out.at[off - 1]
            elif kind == COLS:
                width = out.shape[-1]
                part = pl.ds(pl.multiple_of(peer * width, width), width)
                source, target = ref.at[:, :, part], out.at[off - 1]
            else:
                source, target = ref.at[:, peer], out.at[off - 1]
            copies.append(
                self.remote(
                    source,
                    target,
                    self.zs.at[i, off - 1],
                    self.zr.at[i, off - 1],
                    self.device(group, peer),
                )
            )
        return copies

    def local(self, i):
        kind, group = self.kinds[i], self.groups[i]
        ref, out = self.ins[i], self.outs[i]
        if kind == WIDE:
            source, target = ref, out.at[self.dp, self.mp]
        elif kind in (GATHER, LATE):
            source, target = ref, out.at[self.place[group]]
        elif kind in (NEAR, NEARSWAP):
            source, target = self.mine(i), out.at[self.dp]
        else:
            return None
        return pltpu.make_async_copy(source, target, self.own.at[i])

    def mine(self, i):
        kind = self.kinds[i]
        if kind == WIDE:
            return self.outs[i].at[self.dp]
        return self.ins[i].at[self.chip] if kind == NEARSWAP else self.ins[i]

    def spread(self, i):
        copies = []
        for off in range(1, self.chips):
            peer = self.peer(CHIPS, off)
            source = self.ins[i].at[peer] if self.kinds[i] == NEARSWAP else self.mine(i)
            copies.append(
                self.remote(
                    source,
                    self.outs[i].at[self.dp],
                    self.cs.at[i, off - 1],
                    self.cr.at[i, off - 1],
                    self.device(CHIPS, peer),
                )
            )
        return copies

    def hand(self, i, off):
        owner = 2 * lax.rem(self.chip + self.chips - off, self.chips) + self.parity
        return self.remote(
            self.mine(i) if off == 0 else self.outs[i].at[owner],
            self.outs[i].at[owner],
            self.ps.at[i, off],
            self.pr.at[i, off],
            self.device(PAIR, 1 - self.parity),
        )

    def begin(self, also=()):
        self.meet(also)
        for i in range(self.count):
            if self.kinds[i] == LATE:
                continue
            for copy in self.first(i):
                copy.start()
            if self.kinds[i] in (NEAR, NEARSWAP):
                for copy in self.spread(i):
                    copy.start()
                self.hand(i, 0).start()
        for i in range(self.count):
            local = self.local(i)
            if local is not None:
                local.start()

    def finish(self):
        shared = [i for i in range(self.count) if self.kinds[i] in (NEAR, NEARSWAP, WIDE)]
        for i in shared:
            if self.kinds[i] == WIDE:
                for copy in self.first(i):
                    copy.wait()
                self.local(i).wait()
                for copy in self.spread(i):
                    copy.start()
                self.hand(i, 0).start()
        for i in range(self.count):
            if self.kinds[i] == LATE:
                for copy in self.first(i):
                    copy.start()
        for i in shared:
            for off, copy in enumerate(self.spread(i), 1):
                copy.wait_recv()
                self.hand(i, off).start()
        for i in range(self.count):
            if i in shared:
                for copy in self.spread(i):
                    copy.wait_send()
                for off in range(self.chips):
                    self.hand(i, off).wait()
                if self.kinds[i] != WIDE:
                    self.local(i).wait()
            else:
                for copy in self.first(i):
                    copy.wait()
                local = self.local(i)
                if local is not None:
                    local.wait()


def exchange_kernel(plan, *refs):
    count = plan.count
    plan.bind(refs[:count], refs[count : 2 * count], refs[2 * count :])
    plan.begin()
    plan.finish()


def exchange(entries, cid):
    plan = Exchange(entries)
    return pl.pallas_call(
        functools.partial(exchange_kernel, plan),
        out_shape=plan.shapes,
        in_specs=plan.specs,
        out_specs=plan.specs,
        scratch_shapes=plan.scratch,
        compiler_params=pltpu.CompilerParams(collective_id=cid, has_side_effects=True),
    )(*plan.arrays)


def added(array, received, group):
    place = {
        Z: lax.axis_index(MP),
        CHIPS: lax.axis_index(DP) // 2,
        PAIR: lax.rem(lax.axis_index(DP), 2),
        DP: lax.axis_index(DP),
    }[group]
    axis = 1 if group == PAIR else 0
    own = lax.dynamic_index_in_dim(array, place, axis, keepdims=False)
    return own.astype(F32) + jnp.sum(received.astype(F32), axis=0)


def sums_kernel(kinds, shapes, *refs):
    n = len(kinds)
    arrays, received, outs = refs[:n], refs[n : 2 * n], refs[2 * n :]
    dp, mp = lax.axis_index(DP), lax.axis_index(MP)
    place = {Z: mp, CHIPS: dp // 2, PAIR: lax.rem(dp, 2)}
    for array, got, out, (kind, group, form) in zip(arrays, received, outs, kinds):
        if kind == GATHER:
            total = jnp.sum(array[...].astype(F32), axis=0)
        else:
            if kind == MOVE:
                own = array[place[group]]
            elif kind == MOVE1:
                own = array[:, place[group]]
            else:
                width = got.shape[-1]
                own = array[:, :, pl.ds(pl.multiple_of(place[group] * width, width), width)]
            total = own.astype(F32)
            for i in range(got.shape[0]):
                total += got[i].astype(F32)
        if form == COLUMNS:
            width = out.shape[-1]
            for i in range(out.shape[0]):
                out[i] = total[:, i * width : (i + 1) * width].astype(out.dtype)
        elif form == TURNED:
            out[...] = total.T
        else:
            out[...] = total.astype(out.dtype)


def sums(entries):
    mp_ways = lax.axis_size(MP)
    arrays, received, shapes, kinds = [], [], [], []
    for array, got, kind, group, form, dtype in entries:
        shape = got.shape[1:]
        if form == COLUMNS:
            shape = (mp_ways, shape[0], shape[1] // mp_ways)
        elif form == TURNED:
            shape = shape[::-1]
        arrays.append(array)
        received.append(got if kind != GATHER else got[:1])
        shapes.append(jax.ShapeDtypeStruct(shape, dtype))
        kinds.append((kind, group, form))
    vmem = pl.BlockSpec(memory_space=pltpu.VMEM)
    return pl.pallas_call(
        functools.partial(sums_kernel, kinds, shapes),
        in_specs=[vmem] * (2 * len(entries)),
        out_specs=[vmem] * len(entries),
        out_shape=shapes,
        compiler_params=pltpu.CompilerParams(vmem_limit_bytes=VMEM_BYTES),
    )(*arrays, *received)


def beside(plan, kernel, inputs, outputs, scratches, *refs):
    n = plan.count
    first, last = pl.program_id(0) == 0, pl.program_id(0) == pl.num_programs(0) - 1
    ins = refs[:inputs]
    sends = refs[inputs : inputs + n]
    outs = refs[inputs + n : inputs + n + outputs]
    lands = refs[inputs + n + outputs : inputs + 2 * n + outputs]
    own = refs[inputs + 2 * n + outputs : inputs + 2 * n + outputs + scratches]
    plan.bind(sends, lands, refs[inputs + 2 * n + outputs + scratches :])
    pl.when(first)(plan.begin)
    kernel(*ins, *outs, *own)
    pl.when(last)(plan.finish)


def memory_call(plan, cid, kernel, name, grid, inputs, in_specs, out_specs, out_shape, scratch, flops):
    return pl.pallas_call(
        functools.partial(beside, plan, kernel, len(inputs), len(out_shape), len(scratch)),
        grid=(grid,),
        in_specs=in_specs + plan.specs,
        out_specs=out_specs + plan.specs,
        out_shape=out_shape + plan.shapes,
        scratch_shapes=scratch + plan.scratch,
        compiler_params=pltpu.CompilerParams(
            vmem_limit_bytes=VMEM_BYTES, collective_id=cid, has_side_effects=True
        ),
        cost_estimate=pl.CostEstimate(flops=flops, bytes_accessed=flops // 200, transcendentals=0),
        name=name,
    )(*inputs, *plan.arrays)


MEM_BLOCK = 16
BACK_BLOCK = 8


def memory_kernel(slots, padded, mem_ref, wk_ref, wv_ref, vb_ref, k_ref, v_ref, rows_ref, wide):
    for c in range(0, D, 128):
        cols = slice(c, c + 128)
        wide[...] = mem_ref[:, :, cols].reshape(slots * MEM_BLOCK, 128).astype(F32)
        for r in range(MEM_BLOCK):
            own = wide[pl.ds(r, slots, stride=MEM_BLOCK), :]
            rows_ref[r * padded : (r + 1) * padded, cols] = jnp.concatenate(
                [own, jnp.zeros((padded - slots, 128), F32)], axis=0
            ).astype(BF)
    rows = rows_ref[...]
    for c in range(0, D, 512):
        cols = slice(c, c + 512)
        k_ref[:, cols] = product(rows, wk_ref[:, cols]).astype(BF)
        v_ref[:, cols] = (product(rows, wv_ref[:, cols]) + vb_ref[:, cols]).astype(BF)


def memory_products(memory, key_weight, value_weight, vbias, padded, plan, cid):
    rows, slots, _ = memory.shape
    whole = lambda a: pl.BlockSpec(a.shape, lambda i: (0,) * a.ndim)
    out = jax.ShapeDtypeStruct((rows * padded, D), BF)
    out_spec = pl.BlockSpec((MEM_BLOCK * padded, D), lambda i: (i, 0))
    return memory_call(
        plan,
        cid,
        functools.partial(memory_kernel, slots, padded),
        "memory_products",
        rows // MEM_BLOCK,
        [jnp.transpose(memory, (1, 0, 2)), key_weight, value_weight, vbias],
        [
            pl.BlockSpec((slots, MEM_BLOCK, D), lambda i: (0, i, 0)),
            whole(key_weight),
            whole(value_weight),
            whole(vbias),
        ],
        [out_spec] * 3,
        [out] * 3,
        [pltpu.VMEM((slots * MEM_BLOCK, 128), F32)],
        4 * rows * padded * D * D,
    )


def memory_weight_kernel(rows_ref, dk_ref, dv_ref, wk_ref, wv_ref, vb_ref, key_sum, value_sum):
    step = pl.program_id(0)

    @pl.when(step == 0)
    def _():
        key_sum[...] = jnp.zeros_like(key_sum)
        value_sum[...] = jnp.zeros_like(value_sum)
        vb_ref[...] = jnp.zeros_like(vb_ref)

    rows = rows_ref[...]
    vb_ref[...] += jnp.sum(dv_ref[...].astype(F32), axis=0, keepdims=True)
    for c in range(0, D, 512):
        cols = slice(c, c + 512)
        key_sum[:, cols] += weight_grad(rows, dk_ref[:, cols])
        value_sum[:, cols] += weight_grad(rows, dv_ref[:, cols])

    @pl.when(step == pl.num_programs(0) - 1)
    def _():
        wk_ref[...] = key_sum[...].astype(BF)
        wv_ref[...] = value_sum[...].astype(BF)


def memory_weights(memory_rows, dkeys, dvalues, rows, padded, plan, cid):
    spec = pl.BlockSpec((BACK_BLOCK * padded, D), lambda i: (i, 0))
    whole = pl.BlockSpec((D, D), lambda i: (0, 0))
    return memory_call(
        plan,
        cid,
        memory_weight_kernel,
        "memory_weights",
        rows // BACK_BLOCK,
        [memory_rows, dkeys, dvalues],
        [spec, spec, spec],
        [whole, whole, pl.BlockSpec((1, D), lambda i: (0, 0))],
        [
            jax.ShapeDtypeStruct((D, D), BF),
            jax.ShapeDtypeStruct((D, D), BF),
            jax.ShapeDtypeStruct((1, D), F32),
        ],
        [pltpu.VMEM((D, D), F32), pltpu.VMEM((D, D), F32)],
        4 * rows * padded * D * D,
    )


def memory_grad_kernel(slots, padded, dk_ref, dv_ref, wk_ref, wv_ref, out_ref, wide):
    for c in range(0, D, 256):
        cols = slice(c, c + 256)
        term = product_back(dk_ref[...], wk_ref[cols, :]) + product_back(dv_ref[...], wv_ref[cols, :])
        for part in range(0, 256, 128):
            for r in range(BACK_BLOCK):
                wide[pl.ds(r, slots, stride=BACK_BLOCK), :] = term[
                    r * padded : r * padded + slots, part : part + 128
                ]
            out_ref[:, :, c + part : c + part + 128] = wide[...].reshape(slots, BACK_BLOCK, 128)


def memory_back(dkeys, dvalues, key_weight, value_weight, rows, slots, padded, plan, cid):
    spec = pl.BlockSpec((BACK_BLOCK * padded, D), lambda i: (i, 0))
    whole = pl.BlockSpec((D, D), lambda i: (0, 0))
    out, *rest = memory_call(
        plan,
        cid,
        functools.partial(memory_grad_kernel, slots, padded),
        "memory_back",
        rows // BACK_BLOCK,
        [dkeys, dvalues, key_weight, value_weight],
        [spec, spec, whole, whole],
        [pl.BlockSpec((slots, BACK_BLOCK, D), lambda i: (0, i, 0))],
        [jax.ShapeDtypeStruct((slots, rows, D), F32)],
        [pltpu.VMEM((slots * BACK_BLOCK, 128), F32)],
        4 * rows * padded * D * D,
    )
    return jnp.transpose(out, (1, 0, 2)), rest


def z_copy(source, target, send, recv, device):
    return pltpu.make_async_remote_copy(
        src_ref=source,
        dst_ref=target,
        send_sem=send,
        recv_sem=recv,
        device_id=(lax.axis_index(DP), device),
        device_id_type=MESH,
    )


def z_meet(ways):
    dp, mp = lax.axis_index(DP), lax.axis_index(MP)
    barrier = pltpu.get_barrier_semaphore()
    for off in range(1, ways):
        pl.semaphore_signal(
            barrier, inc=1, device_id=(dp, lax.rem(mp + off, ways)), device_id_type=MESH
        )
    pl.semaphore_wait(barrier, ways - 1)


def nearest(c, ways):
    mp = lax.axis_index(MP)
    left_n, right_n = mp, ways - 1 - mp
    fewer = jnp.minimum(left_n, right_n)
    paired = c <= 2 * fewer
    distance = jnp.where(paired, (c + 1) // 2, c - fewer)
    left = jnp.where(paired, lax.rem(c, 2) == 1, left_n > right_n)
    return jnp.where(left, mp - distance, mp + distance), distance, left, paired


class LineGather:
    def __init__(self, entries, sems, ways):
        self.entries, self.ways = entries, ways
        self.left_send, self.left_recv, self.right_send, self.right_recv, self.own = sems
        self.mp = lax.axis_index(MP)

    def to_right(self, i, source, place, hop):
        held = self.entries[i][1]
        return z_copy(
            source, held.at[place], self.right_send.at[i, hop], self.right_recv.at[i, hop], self.mp + 1
        )

    def to_left(self, i, source, place, hop):
        held = self.entries[i][1]
        return z_copy(
            source, held.at[place], self.left_send.at[i, hop], self.left_recv.at[i, hop], self.mp - 1
        )

    def begin(self):
        mp, every = self.mp, range(len(self.entries))

        @pl.when(mp < self.ways - 1)
        def _():
            for i in every:
                self.to_right(i, self.entries[i][0], mp, 0).start()

        @pl.when(mp > 0)
        def _():
            for i in every:
                self.to_left(i, self.entries[i][0], mp, 0).start()

        for i in every:
            local = pltpu.make_async_copy(self.entries[i][0], self.entries[i][1].at[mp], self.own.at[i])
            local.start()
            local.wait()

    def arrive(self, c, first):
        mp, every = self.mp, range(len(self.entries))
        _, distance, left, paired = nearest(c, self.ways)
        odd = lax.rem(c, 2) == 1
        due = (c > 0) & first & jnp.logical_not(paired & jnp.logical_not(odd))

        @pl.when(due & (left | (paired & odd)))
        def _():
            place = mp - distance
            for i in every:
                held = self.entries[i][1].at[place]
                self.to_right(i, held, place, distance - 1).wait_recv()

                @pl.when(mp < self.ways - 1)
                def _(i=i, held=held):
                    self.to_right(i, held, place, distance).start()

        @pl.when(due & (jnp.logical_not(left) | (paired & odd)))
        def _():
            place = mp + distance
            for i in every:
                held = self.entries[i][1].at[place]
                self.to_left(i, held, place, distance - 1).wait_recv()

                @pl.when(mp > 0)
                def _(i=i, held=held):
                    self.to_left(i, held, place, distance).start()

    def finish(self):
        mp = self.mp
        for hop in range(self.ways - 1):

            @pl.when((mp < self.ways - 1) & (hop <= mp))
            def _(hop=hop):
                for i, (_, held) in enumerate(self.entries):
                    self.to_right(i, held.at[mp - hop], mp - hop, hop).wait_send()

            @pl.when((mp > 0) & (hop <= self.ways - 1 - mp))
            def _(hop=hop):
                for i, (_, held) in enumerate(self.entries):
                    self.to_left(i, held.at[mp + hop], mp + hop, hop).wait_send()


def line_sems(count, ways):
    dma = pltpu.SemaphoreType.DMA
    return [dma((count, ways)) for _ in range(4)] + [dma((count,))]


def own_heads(result, keep):
    kept = result * keep
    total = kept[0:TOK]
    for h in range(1, GH):
        total = total + kept[h * TOK : (h + 1) * TOK]
    return total


def cross_kernel(
    ways, per, piece, padded, used_ref, k_ref, v_ref, q_ref, keep_ref, ctx_ref, stat_ref, ctx_got, stat_got,
    ctx_out, stat_out, send, recv,
):
    c, j = pl.program_id(0), pl.program_id(1)
    mp = lax.axis_index(MP)
    span = piece * TOK

    @pl.when((c == 0) & (j == 0))
    def _():
        z_meet(ways)

    keep = keep_ref[...]
    keep_wide = keep.astype(F32)
    slot = lax.broadcasted_iota(jnp.int32, (padded, GL), 0)
    for g in range(G):
        cols = slice(g * GC, (g + 1) * GC)
        query = jnp.concatenate([q_ref[:, cols]] * GH, axis=0) * keep
        scores = product_back(k_ref[:, cols], query)
        for r in range(piece):
            rows = slice(r * padded, (r + 1) * padded)
            seen = slot < used_ref[r]
            own = jnp.where(seen, scores[rows], NEG)
            peak = jnp.max(own, axis=0, keepdims=True)
            exponent = jnp.where(seen, jnp.exp(own - peak), 0.0)
            total = jnp.sum(exponent, axis=0, keepdims=True)
            probs = (exponent * (1.0 / jnp.maximum(total, 1e-30))).astype(BF)
            ctx = own_heads(weight_grad(probs, v_ref[rows, cols]), keep_wide)
            ctx_out[c, pl.ds(j * span + r * TOK, TOK), cols] = ctx.astype(BF)
            stat_out[c, 0, j * piece + r, g : g + 1, :] = peak
            stat_out[c, 1, j * piece + r, g : g + 1, :] = total

    def copies(k):
        to = nearest(ways - 1 - k, ways)[0]
        off = lax.rem(to - mp + ways, ways)
        return [
            z_copy(a.at[k], b.at[off - 1], send.at[i, k], recv.at[i, off - 1], to)
            for i, (a, b) in enumerate([(ctx_out, ctx_got), (stat_out, stat_got)])
        ]

    for k in range(ways - 1):

        @pl.when((c == k) & (j == per - 1))
        def _(k=k):
            for copy in copies(k):
                copy.start()

    @pl.when((c == ways - 1) & (j == per - 1))
    def _():
        ctx_ref[...] = ctx_out[ways - 1]
        stat_ref[...] = stat_out[ways - 1]
        for k in range(ways - 1):
            for copy in copies(k):
                copy.wait_send()
        for off in range(1, ways):
            to = lax.rem(mp + off, ways)
            for i, (a, b) in enumerate([(ctx_out, ctx_got), (stat_out, stat_got)]):
                z_copy(a.at[0], b.at[off - 1], send.at[i, 0], recv.at[i, off - 1], to).wait_recv()


def cross_forward(used, keys, values, queries, keep, piece, padded, cid):
    ways = lax.axis_size(MP)
    per = queries.shape[0] // TOK // ways
    rows = per * ways * piece
    shard = per * piece
    at = lambda c, j: nearest(ways - 1 - c, ways)[0] * per + j
    big = pl.BlockSpec((piece * padded, D), lambda c, j: (at(c, j), 0))
    anywhere = pl.BlockSpec(memory_space=pl.ANY)
    dma = pltpu.SemaphoreType.DMA
    return pl.pallas_call(
        functools.partial(cross_kernel, ways, per, piece, padded),
        grid=(ways, per),
        in_specs=[
            pl.BlockSpec((piece, 1, GL), lambda c, j: (at(c, j), 0, 0)),
            big,
            big,
            pl.BlockSpec((TOK, D), lambda c, j: (at(c, j), 0)),
            pl.BlockSpec((GL, GC), lambda c, j: (0, 0)),
        ],
        out_specs=[
            pl.BlockSpec((shard * TOK, D), lambda c, j: (0, 0)),
            pl.BlockSpec((2, shard, G, GL), lambda c, j: (0, 0, 0, 0)),
            anywhere,
            anywhere,
        ],
        out_shape=[
            jax.ShapeDtypeStruct((shard * TOK, D), BF),
            jax.ShapeDtypeStruct((2, shard, G, GL), F32),
            jax.ShapeDtypeStruct((ways - 1, shard * TOK, D), BF),
            jax.ShapeDtypeStruct((ways - 1, 2, shard, G, GL), F32),
        ],
        scratch_shapes=[
            pltpu.VMEM((ways, shard * TOK, D), BF),
            pltpu.VMEM((ways, 2, shard, G, GL), F32),
            dma((2, ways)),
            dma((2, ways)),
        ],
        compiler_params=pltpu.CompilerParams(
            vmem_limit_bytes=VMEM_BYTES, collective_id=cid, has_side_effects=True
        ),
        cost_estimate=pl.CostEstimate(
            flops=4 * rows * padded * GL * D,
            bytes_accessed=4 * rows * padded * D,
            transcendentals=rows * padded * G * GL,
        ),
    )(used, keys, values, queries, keep)


def cross_back_kernel(
    ways, per, piece, padded, used_ref, k_ref, v_ref, q_ref, keep_ref, dctx_ref, stat_ref,
    dk_ref, dv_ref, dq_ref,
    dctx_all, stat_all, dq_out, dq_got, left_send, left_recv, right_send, right_recv, own, send, recv,
):
    c, j = pl.program_id(0), pl.program_id(1)
    mp = lax.axis_index(MP)
    place = nearest(c, ways)[0]
    span = piece * TOK
    line = LineGather(
        [(dctx_ref, dctx_all), (stat_ref, stat_all)],
        (left_send, left_recv, right_send, right_recv, own),
        ways,
    )

    @pl.when((c == 0) & (j == 0))
    def _():
        z_meet(ways)
        line.begin()

    line.arrive(c, j == 0)
    keep = keep_ref[...]
    keep_wide = keep.astype(F32)
    slot = lax.broadcasted_iota(jnp.int32, (padded, GL), 0)
    for g in range(G):
        cols = slice(g * GC, (g + 1) * GC)
        query = jnp.concatenate([q_ref[:, cols]] * GH, axis=0) * keep
        scores = product_back(k_ref[:, cols], query)
        parts = []
        for r in range(piece):
            rows = slice(r * padded, (r + 1) * padded)
            dctx = dctx_all[place, pl.ds(j * span + r * TOK, TOK), cols]
            dctx = jnp.concatenate([dctx] * GH, axis=0) * keep
            dprobs = product_back(v_ref[rows, cols], dctx)
            seen = slot < used_ref[r]
            norm = stat_all[place, 0, j * piece + r, g : g + 1, :]
            middle = stat_all[place, 1, j * piece + r, g : g + 1, :]
            probs = jnp.where(seen, jnp.exp(scores[rows] - norm), 0.0)
            parts.append((probs * (dprobs - middle)).astype(BF))
            dv_ref[rows, cols] = product(probs.astype(BF), dctx).astype(BF)
        dscores = jnp.concatenate(parts, axis=0)
        dk_ref[:, cols] = product(dscores, query).astype(BF)
        dquery = own_heads(weight_grad(dscores, k_ref[:, cols]), keep_wide)
        dq_out[c, pl.ds(j * TOK, TOK), cols] = dquery.astype(BF)

    def copy(k):
        to = nearest(k, ways)[0]
        off = lax.rem(to - mp + ways, ways)
        return z_copy(dq_out.at[k], dq_got.at[off - 1], send.at[k], recv.at[off - 1], to)

    for k in range(1, ways):

        @pl.when((c == k) & (j == per - 1))
        def _(k=k):
            copy(k).start()

    @pl.when((c == ways - 1) & (j == per - 1))
    def _():
        line.finish()
        for k in range(1, ways):
            copy(k).wait_send()
        total = dq_out[0].astype(F32)
        for off in range(1, ways):
            z_copy(
                dq_out.at[0], dq_got.at[off - 1], send.at[0], recv.at[off - 1], lax.rem(mp + off, ways)
            ).wait_recv()
            total += dq_got[off - 1].astype(F32)
        dq_ref[...] = total


def cross_back(used, keys, values, queries, dctx, stats, keep, piece, padded, cid):
    ways = lax.axis_size(MP)
    per = queries.shape[0] // TOK // ways
    rows = per * ways * piece
    shard = per * piece
    at = lambda c, j: nearest(c, ways)[0] * per + j
    big = pl.BlockSpec((piece * padded, D), lambda c, j: (at(c, j), 0))
    anywhere = pl.BlockSpec(memory_space=pl.ANY)
    dma = pltpu.SemaphoreType.DMA
    return pl.pallas_call(
        functools.partial(cross_back_kernel, ways, per, piece, padded),
        grid=(ways, per),
        in_specs=[
            pl.BlockSpec((piece, 1, GL), lambda c, j: (at(c, j), 0, 0)),
            big,
            big,
            pl.BlockSpec((TOK, D), lambda c, j: (at(c, j), 0)),
            pl.BlockSpec((GL, GC), lambda c, j: (0, 0)),
            anywhere,
            anywhere,
        ],
        out_specs=[big, big, pl.BlockSpec((per * TOK, D), lambda c, j: (0, 0))],
        out_shape=[
            jax.ShapeDtypeStruct((rows * padded, D), BF),
            jax.ShapeDtypeStruct((rows * padded, D), BF),
            jax.ShapeDtypeStruct((per * TOK, D), F32),
        ],
        scratch_shapes=[
            pltpu.VMEM((ways, shard * TOK, D), BF),
            pltpu.VMEM((ways, 2, shard, G, GL), F32),
            pltpu.VMEM((ways, per * TOK, D), BF),
            pltpu.VMEM((ways - 1, per * TOK, D), BF),
            *line_sems(2, ways),
            dma((ways,)),
            dma((ways,)),
        ],
        compiler_params=pltpu.CompilerParams(
            vmem_limit_bytes=VMEM_BYTES, collective_id=cid, has_side_effects=True
        ),
        cost_estimate=pl.CostEstimate(
            flops=10 * rows * padded * GL * D,
            bytes_accessed=8 * rows * padded * D,
            transcendentals=rows * padded * G * GL,
        ),
    )(used, keys, values, queries, keep, dctx, stats)


def table_words(table, start, count):
    if table.shape[0] == 1:
        return table[0, pl.ds(start, count), :]
    return jnp.concatenate([table[i, pl.ds(start, count), :] for i in range(table.shape[0])], axis=-1)


def table_load(table_refs, table, sems, tile, c, t):
    tiles = table.shape[1] // tile
    places = [(ref, j * tile) for ref in table_refs for j in range(ref.shape[1] // tile)]

    def copy(k):
        ref, start = places[k]
        source = ref.at[:, pl.ds(start, tile), :]
        return pltpu.make_async_copy(source, table.at[:, pl.ds(k * tile, tile), :], sems.at[k])

    @pl.when((c == 0) & (t == 0))
    def _():
        for k in range(tiles):
            copy(k).start()

    for k in range(tiles):

        @pl.when((c == 0) & (t == k))
        def _(k=k):
            copy(k).wait()


def vocab_kernel(
    ways, tile, sub, chunk, count, h_ref, target_ref, *refs
):
    table_refs, refs = refs[:count], refs[count:]
    vocab_steps(ways, tile, sub, chunk, table_refs, h_ref, target_ref, *refs)


def vocab_steps(
    ways, tile, sub, chunk, table_refs, h_ref, target_ref, exp_ref, tops_ref, stats_ref,
    table, held, run, stats, table_sem, left_send, left_recv, right_send, right_recv, own,
    stat_send, stat_recv, stat_own,
):
    c, t = pl.program_id(0), pl.program_id(1)
    last = pl.num_programs(1) - 1
    mp = lax.axis_index(MP)
    slot = nearest(c, ways)[0]
    line = LineGather(
        [(h_ref, held)], (left_send, left_recv, right_send, right_recv, own), ways
    )

    def stats_copy(off):
        return z_copy(
            stats,
            stats_ref.at[mp],
            stat_send.at[off - 1],
            stat_recv.at[off - 1],
            lax.rem(mp + off, ways),
        )

    @pl.when((c == 0) & (t == 0))
    def _():
        z_meet(ways)
        line.begin()

    line.arrive(c, t == 0)
    table_load(table_refs, table, table_sem, tile, c, t)

    @pl.when(t == 0)
    def _():
        run[0:1, :] = jnp.full((1, chunk), NEG, F32)
        run[1:3, :] = jnp.zeros((2, chunk), F32)

    tokens = held[slot]
    target = target_ref[slot]
    parts = []
    for i in range(tile // sub):
        start = t * tile + i * sub
        logits = product_back(table_words(table, start, sub), tokens)
        top = jnp.max(logits, axis=0, keepdims=True)
        exponent = jnp.exp(logits - top)
        word = lax.broadcasted_iota(jnp.int32, (sub, chunk), 0) + start
        hit = jnp.where(word == target, logits, 0.0)
        exp_ref[0, i * sub : (i + 1) * sub, :] = exponent.astype(BF)
        tops_ref[0, pl.ds(t * (tile // sub) + i, 1), :] = top
        parts.append(
            (top, jnp.sum(exponent, axis=0, keepdims=True), jnp.sum(hit, axis=0, keepdims=True))
        )
    former = run[0:1, :]
    peak = former
    for top, total, hit in parts:
        peak = jnp.maximum(peak, top)
    sums = run[1:2, :] * jnp.exp(former - peak)
    hits = run[2:3, :]
    for top, total, hit in parts:
        sums += total * jnp.exp(top - peak)
        hits += hit
    run[0:1, :] = peak
    run[1:2, :] = sums
    run[2:3, :] = hits

    @pl.when(t == last)
    def _():
        stats[slot] = run[...]

    @pl.when((c == ways - 1) & (t == last))
    def _():
        for off in range(1, ways):
            stats_copy(off).start()
        local = pltpu.make_async_copy(stats, stats_ref.at[mp], stat_own.at[0])
        local.start()
        line.finish()
        for off in range(1, ways):
            stats_copy(off).wait()
        local.wait()


def vocab_sizes(words):
    tile = 1280 if words % 1280 == 0 else words
    sub = 256 if tile % 256 == 0 else tile
    return tile, sub


def vocab_forward(hidden, target, tables, cid):
    ways = lax.axis_size(MP)
    chunk = hidden.shape[0]
    parts, _, width = tables[0].shape
    words = sum(a.shape[1] for a in tables)
    tile, sub = vocab_sizes(words)
    tiles = words // tile
    top_rows = -(-(words // sub) // 8) * 8
    dma = pltpu.SemaphoreType.DMA
    return pl.pallas_call(
        functools.partial(vocab_kernel, ways, tile, sub, chunk, len(tables)),
        grid=(ways, tiles),
        in_specs=[
            pl.BlockSpec(memory_space=pl.ANY),
            pl.BlockSpec((ways, 1, chunk), lambda c, t: (0, 0, 0)),
            *[pl.BlockSpec(memory_space=pl.ANY)] * len(tables),
        ],
        out_specs=[
            pl.BlockSpec((1, tile, chunk), lambda c, t: (c, t, 0)),
            pl.BlockSpec((1, top_rows, chunk), lambda c, t: (c, 0, 0)),
            pl.BlockSpec(memory_space=pl.ANY),
        ],
        out_shape=[
            jax.ShapeDtypeStruct((ways, words, chunk), BF),
            jax.ShapeDtypeStruct((ways, top_rows, chunk), F32),
            jax.ShapeDtypeStruct((ways, ways, 8, chunk), F32),
        ],
        scratch_shapes=[
            pltpu.VMEM((parts, words, width), BF),
            pltpu.VMEM((ways, chunk, D), BF),
            pltpu.VMEM((8, chunk), F32),
            pltpu.VMEM((ways, 8, chunk), F32),
            dma((tiles,)),
            *line_sems(1, ways),
            dma((ways,)),
            dma((ways,)),
            dma((1,)),
        ],
        compiler_params=pltpu.CompilerParams(
            vmem_limit_bytes=VMEM_BYTES, collective_id=cid, has_side_effects=True
        ),
        cost_estimate=pl.CostEstimate(
            flops=2 * ways * chunk * words * D,
            bytes_accessed=2 * ways * words * D,
            transcendentals=ways * chunk * words,
        ),
    )(hidden, target, *tables)


def vocab_back_kernel(
    ways, tile, sub, chunk, count, exp_ref, tops_ref, target_ref, norm_ref, rate_ref, *refs
):
    table_refs, refs = refs[:count], refs[count:]
    vocab_back_steps(
        ways, tile, sub, chunk, table_refs, exp_ref, tops_ref, target_ref, norm_ref, rate_ref, *refs
    )


def vocab_back_steps(
    ways, tile, sub, chunk, table_refs, exp_ref, tops_ref, target_ref, norm_ref, rate_ref, out_ref,
    table, total, terms, leaving, landing, table_sem, send, recv,
):
    c, t = pl.program_id(0), pl.program_id(1)
    last = pl.num_programs(1) - 1
    mp = lax.axis_index(MP)
    slot = nearest(ways - 1 - c, ways)[0]

    def copy(to):
        right = to > mp
        spot = jnp.where(right | (to < mp - 1), to, ways)
        return z_copy(
            leaving.at[to],
            landing.at[spot],
            send.at[to],
            recv.at[spot],
            jnp.where(right, mp + 1, mp - 1),
        )

    def arrived(spot):
        z_copy(
            leaving.at[0], landing.at[spot], send.at[0], recv.at[spot], lax.rem(mp + 1, ways)
        ).wait_recv()

    @pl.when((c == 0) & (t == 0))
    def _():
        z_meet(ways)

    table_load(table_refs, table, table_sem, tile, c, t)
    target, norm, rate = target_ref[slot], norm_ref[slot], rate_ref[slot]
    term = None
    for i in range(tile // sub):
        start = t * tile + i * sub
        factor = jnp.exp(tops_ref[0, pl.ds(t * (tile // sub) + i, 1), :] - norm) * -rate
        word = lax.broadcasted_iota(jnp.int32, (sub, chunk), 0) + start
        hit = jnp.where(word == target, rate, 0.0)
        dlogits = hit + exp_ref[0, i * sub : (i + 1) * sub, :].astype(F32) * factor
        part = weight_grad(dlogits.astype(BF), table_words(table, start, sub))
        term = part if term is None else term + part

    @pl.when(t == 0)
    def _():
        total[...] = term

    @pl.when(t > 0)
    def _():
        total[...] += term

    for k in range(ways - 1):
        to = nearest(ways - 1 - k, ways)[0]
        beyond = jnp.where(to > mp, mp > 0, mp < ways - 1)

        @pl.when((c == k) & (t == last) & jnp.logical_not(beyond))
        def _(to=to):
            leaving[to] = total[...].astype(BF)
            copy(to).start()

        @pl.when((c == k) & (t == last) & beyond)
        def _(k=k):
            terms[k] = total[...]

    for k in range(ways - 1):
        to = nearest(ways - 1 - k, ways)[0]
        beyond = jnp.where(to > mp, mp > 0, mp < ways - 1)

        @pl.when((c == min(k + 2, ways - 1)) & (t == last) & beyond)
        def _(k=k, to=to):
            arrived(to)
            leaving[to] = (terms[k] + landing[to].astype(F32)).astype(BF)
            copy(to).start()

    @pl.when((c == ways - 1) & (t == last))
    def _():
        out_ref[...] = total[...]

        @pl.when(mp > 0)
        def _():
            arrived(mp)
            out_ref[...] += landing[mp].astype(F32)

        @pl.when(mp < ways - 1)
        def _():
            arrived(ways)
            out_ref[...] += landing[ways].astype(F32)

        for k in range(ways - 1):
            copy(nearest(ways - 1 - k, ways)[0]).wait_send()


def vocab_back(exponents, tops, target, norm, rate, tables, cid):
    ways, words, chunk = exponents.shape
    tile, sub = vocab_sizes(words)
    tiles = words // tile
    whole = pl.BlockSpec((ways, 1, chunk), lambda c, t: (0, 0, 0))
    dma = pltpu.SemaphoreType.DMA
    return pl.pallas_call(
        functools.partial(vocab_back_kernel, ways, tile, sub, chunk, len(tables)),
        grid=(ways, tiles),
        in_specs=[
            pl.BlockSpec((1, tile, chunk), lambda c, t: (ways - 1 - c, t, 0)),
            pl.BlockSpec((1, tops.shape[1], chunk), lambda c, t: (ways - 1 - c, 0, 0)),
            whole,
            whole,
            whole,
            *[pl.BlockSpec(memory_space=pl.ANY)] * len(tables),
        ],
        out_specs=pl.BlockSpec((chunk, D), lambda c, t: (0, 0)),
        out_shape=jax.ShapeDtypeStruct((chunk, D), F32),
        scratch_shapes=[
            pltpu.VMEM((tables[0].shape[0], words, tables[0].shape[2]), BF),
            pltpu.VMEM((chunk, D), F32),
            pltpu.VMEM((ways - 1, chunk, D), F32),
            pltpu.VMEM((ways, chunk, D), BF),
            pltpu.VMEM((ways + 1, chunk, D), BF),
            dma((tiles,)),
            dma((ways,)),
            dma((ways + 1,)),
        ],
        compiler_params=pltpu.CompilerParams(
            vmem_limit_bytes=VMEM_BYTES, collective_id=cid, has_side_effects=True
        ),
        cost_estimate=pl.CostEstimate(
            flops=2 * ways * chunk * words * D, bytes_accessed=2 * ways * words * D, transcendentals=0
        ),
    )(exponents, tops, target, norm, rate, *tables)


HIDDEN_TILE = 512
ROOT_HALF = 0.7071067811865476
ROOT_TAU = 0.3989422804014327


def weight_tile(ref):
    return ref[...].reshape(D, ref.shape[-1])


def feed_kernel(h_ref, expand_ref, bias_ref, shrink_ref, a_ref, out_ref):
    t = pl.program_id(0)
    hidden = product(h_ref[...], weight_tile(expand_ref)) + bias_ref[0]
    a_ref[...] = hidden
    active = (hidden * (0.5 + 0.5 * lax.erf(hidden * ROOT_HALF))).astype(BF)
    term = product_back(active, weight_tile(shrink_ref))

    @pl.when(t == 0)
    def _():
        out_ref[...] = term

    @pl.when(t > 0)
    def _():
        out_ref[...] += term


def feed_specs(weights):
    parts, ways, _, rows, units = weights.shape
    per = units // HIDDEN_TILE
    tile = lambda which: pl.BlockSpec(
        (parts, 1, 1, rows, HIDDEN_TILE), lambda t: (0, t // per, which, 0, t % per)
    )
    bias = pl.BlockSpec((1, 1, HIDDEN_TILE), lambda t: (t, 0, 0))
    return tile(0), bias, tile(1), ways * per


def feed_forward(hidden, weights, bias):
    tokens = hidden.shape[0]
    expand_spec, bias_spec, shrink_spec, tiles = feed_specs(weights)
    whole = pl.BlockSpec((tokens, D), lambda t: (0, 0))
    units = tiles * HIDDEN_TILE
    return pl.pallas_call(
        feed_kernel,
        grid=(tiles,),
        in_specs=[whole, expand_spec, bias_spec, shrink_spec],
        out_specs=[pl.BlockSpec((tokens, HIDDEN_TILE), lambda t: (0, t)), whole],
        out_shape=[
            jax.ShapeDtypeStruct((tokens, units), F32),
            jax.ShapeDtypeStruct((tokens, D), F32),
        ],
        compiler_params=pltpu.CompilerParams(vmem_limit_bytes=VMEM_BYTES),
        cost_estimate=pl.CostEstimate(
            flops=4 * tokens * units * D, bytes_accessed=4 * units * D, transcendentals=tokens * units
        ),
    )(hidden, weights, bias.reshape(tiles, 1, HIDDEN_TILE), weights)


def feed_back_kernel(
    dout_ref, h_ref, a_ref, expand_ref, shrink_ref, dweights_ref, dbias_ref, dh_ref
):
    t = pl.program_id(0)
    dout = dout_ref[...]
    hidden = a_ref[...]
    below = 0.5 + 0.5 * lax.erf(hidden * ROOT_HALF)
    slope = below + hidden * (ROOT_TAU * jnp.exp(-0.5 * hidden * hidden))
    active = (hidden * below).astype(BF)
    dhidden = (slope * product(dout, weight_tile(shrink_ref))).astype(BF)
    dbias_ref[0] = jnp.sum(dhidden.astype(F32), axis=0, keepdims=True)
    parts, _, rows, width = dweights_ref.shape
    dweights_ref[:, 0] = weight_grad(h_ref[...], dhidden).astype(BF).reshape(parts, rows, width)
    dweights_ref[:, 1] = weight_grad(dout, active).astype(BF).reshape(parts, rows, width)
    term = product_back(dhidden, weight_tile(expand_ref))

    @pl.when(t == 0)
    def _():
        dh_ref[...] = term

    @pl.when(t > 0)
    def _():
        dh_ref[...] += term


def feed_back(dout, hidden, before, weights):
    tokens = hidden.shape[0]
    expand_spec, bias_spec, shrink_spec, tiles = feed_specs(weights)
    parts, rows = weights.shape[0], weights.shape[3]
    whole = pl.BlockSpec((tokens, D), lambda t: (0, 0))
    units = tiles * HIDDEN_TILE
    return pl.pallas_call(
        feed_back_kernel,
        grid=(tiles,),
        in_specs=[
            whole,
            whole,
            pl.BlockSpec((tokens, HIDDEN_TILE), lambda t: (0, t)),
            expand_spec,
            shrink_spec,
        ],
        out_specs=[
            pl.BlockSpec((parts, 2, rows, HIDDEN_TILE), lambda t: (0, 0, 0, t)),
            bias_spec,
            whole,
        ],
        out_shape=[
            jax.ShapeDtypeStruct((parts, 2, rows, units), BF),
            jax.ShapeDtypeStruct((tiles, 1, HIDDEN_TILE), F32),
            jax.ShapeDtypeStruct((tokens, D), F32),
        ],
        compiler_params=pltpu.CompilerParams(vmem_limit_bytes=VMEM_BYTES),
        cost_estimate=pl.CostEstimate(
            flops=8 * tokens * units * D, bytes_accessed=8 * units * D, transcendentals=2 * tokens * units
        ),
    )(dout, hidden, before, weights, weights)


def self_back_kernel(
    plan, x_ref, dout_ref, ctx_ref, q_ref, k_ref, v_ref, wo_ref, wqkv_ref, keep_ref, dfirst_ref, *refs
):
    n = plan.count
    sends, rest = refs[:n], refs[n:]
    bias_ref, dself_ref, dwo_ref, din_ref = rest[:4]
    lands, rest = rest[4 : 4 + n], rest[4 + n :]
    dctx, dqkv, part, part_got, din, dself, dself_got, dwo, dwo_got = rest[:9]
    send, recv, own = rest[9:12]
    plan.bind(sends, lands, rest[12:])
    ways = plan.mp_ways
    mp, parity = plan.mp, plan.parity

    def part_copy(off):
        to = plan.peer(Z, off)
        return z_copy(part.at[to], part_got.at[off - 1], send.at[0, off], recv.at[0, off], to)

    def din_copy(off):
        return z_copy(din, din_ref.at[mp], send.at[1, off], recv.at[1, off], plan.peer(Z, off))

    def core_copies():
        return [
            plan.remote(a.at[:, 1 - parity], b, send.at[2, i], recv.at[2, i], plan.device(PAIR, 1 - parity))
            for i, (a, b) in enumerate([(dself, dself_got), (dwo, dwo_got)])
        ]

    plan.begin((Z, PAIR))
    keep = keep_ref[...]
    keep_wide = keep.astype(F32)
    dctx[...] = product_back(dout_ref[...], wo_ref[...]).astype(BF)
    key_place = lax.broadcasted_iota(jnp.int32, (TOK, GL), 0)
    query_place = lax.rem(lax.broadcasted_iota(jnp.int32, (TOK, GL), 1), TOK)
    seen = key_place <= query_place

    @pl.loop(0, x_ref.shape[0] // TOK)
    def _(question):
        rows = pl.ds(pl.multiple_of(question * TOK, TOK), TOK)
        keys, values = k_ref[rows, :], v_ref[rows, :]
        query = jnp.concatenate([q_ref[rows, :]] * GH, axis=0) * keep
        upstream = jnp.concatenate([dctx[rows, :]] * GH, axis=0) * keep
        scores = jnp.where(seen, product_back(keys, query), NEG)
        exponent = jnp.exp(scores - jnp.max(scores, axis=0, keepdims=True))
        probs = exponent / jnp.sum(exponent, axis=0, keepdims=True)
        dprobs = product_back(values, upstream)
        middle = jnp.sum(probs * dprobs, axis=0, keepdims=True)
        dscores = (probs * (dprobs - middle)).astype(BF)
        dquery = own_heads(weight_grad(dscores, keys), keep_wide)
        dqkv[rows, 0:GC] = (dquery * SCALE).astype(BF)
        dqkv[rows, GC : 2 * GC] = product(dscores, query).astype(BF)
        dqkv[rows, 2 * GC : 3 * GC] = product(probs.astype(BF), upstream).astype(BF)

    grads = dqkv[...]
    part[...] = product_back(grads, wqkv_ref[...]).astype(BF).reshape(part.shape)
    for off in range(1, ways):
        part_copy(off).start()
    dself[...] = weight_grad(x_ref[...], grads).astype(BF).reshape(dself.shape)
    dwo[...] = weight_grad(dout_ref[...], ctx_ref[...]).astype(BF).reshape(dwo.shape)
    for copy in core_copies():
        copy.start()
    bias_ref[...] = jnp.sum(grads.astype(F32), axis=0, keepdims=True)
    total = dfirst_ref[...] + part[mp].astype(F32)
    for off in range(1, ways):
        part_copy(off).wait_recv()
        total += part_got[off - 1].astype(F32)
    din[...] = total.astype(BF)
    for off in range(1, ways):
        din_copy(off).start()
    local = pltpu.make_async_copy(din, din_ref.at[mp], own.at[0])
    local.start()
    for copy in core_copies():
        copy.wait()
    dself_ref[...] = (dself[:, parity].astype(F32) + dself_got[...].astype(F32)).astype(BF)
    dwo_ref[...] = (dwo[:, parity].astype(F32) + dwo_got[...].astype(F32)).astype(BF)
    plan.finish()
    for off in range(1, ways):
        part_copy(off).wait_send()
        din_copy(off).wait()
    local.wait()


def self_back(x, dout, ctx, queries, keys, values, wo, wqkv, keep, dfirst, plan, cid):
    uniq, shard = x.shape[0], dfirst.shape[0]
    ways, chips = plan.mp_ways, plan.chips
    vec = D // plan.dp_ways
    inputs = [x, dout, ctx, queries, keys, values, wo, wqkv, keep, dfirst]
    vmem = pl.BlockSpec(memory_space=pltpu.VMEM)
    dma = pltpu.SemaphoreType.DMA
    cols = wqkv.shape[1]
    return pl.pallas_call(
        functools.partial(self_back_kernel, plan),
        in_specs=[vmem] * len(inputs) + plan.specs,
        out_specs=[vmem, vmem, vmem, pl.BlockSpec(memory_space=pl.ANY)] + plan.specs,
        out_shape=[
            jax.ShapeDtypeStruct((1, cols), F32),
            jax.ShapeDtypeStruct((chips, vec, cols), BF),
            jax.ShapeDtypeStruct((chips, vec, GC), BF),
            jax.ShapeDtypeStruct((ways, shard, D), BF),
        ]
        + plan.shapes,
        scratch_shapes=[
            pltpu.VMEM((uniq, GC), BF),
            pltpu.VMEM((uniq, cols), BF),
            pltpu.VMEM((ways, shard, D), BF),
            pltpu.VMEM((ways - 1, shard, D), BF),
            pltpu.VMEM((shard, D), BF),
            pltpu.VMEM((chips, 2, vec, cols), BF),
            pltpu.VMEM((chips, vec, cols), BF),
            pltpu.VMEM((chips, 2, vec, GC), BF),
            pltpu.VMEM((chips, vec, GC), BF),
            dma((3, ways)),
            dma((3, ways)),
            dma((1,)),
            *plan.scratch,
        ],
        compiler_params=pltpu.CompilerParams(
            vmem_limit_bytes=VMEM_BYTES, collective_id=cid, has_side_effects=True
        ),
        cost_estimate=pl.CostEstimate(
            flops=4 * uniq * D * cols, bytes_accessed=8 * uniq * D, transcendentals=uniq * GL
        ),
    )(*inputs, *plan.arrays)


def self_probs(queries, key_heads):
    causal = (
        lax.broadcasted_iota(jnp.int32, (TOK, TOK), 1)
        <= lax.broadcasted_iota(jnp.int32, (TOK, TOK), 0)
    )[None, None]
    scores = jnp.einsum("rqhe,rkhe->rhqk", queries, key_heads, preferred_element_type=F32)
    return jax.nn.softmax(jnp.where(causal, scores, NEG), axis=-1)


def column_parts(gathered):
    return jnp.concatenate([gathered[i] for i in range(gathered.shape[0])], axis=-1)


def block_rows(array, ways):
    rows, columns = array.shape
    width = columns // ways
    return jnp.stack([array[:, i * width : (i + 1) * width] for i in range(ways)])


def local(
    answers,
    targets,
    doc_scores,
    memory,
    lengths,
    self_query,
    self_key,
    self_value,
    query_bias,
    value_bias,
    self_output,
    output_bias,
    first_gain,
    first_shift,
    cross_query,
    crossq_bias,
    cross_key,
    cross_value,
    crossv_bias,
    cross_output,
    crosso_bias,
    second_gain,
    second_shift,
    expand_weight,
    expand_bias,
    shrink_weight,
    shrink_bias,
    third_gain,
    third_shift,
    word_table,
):
    dp_ways, mp_ways = lax.axis_size(DP), lax.axis_size(MP)
    chips = dp_ways // 2
    dp, mp = lax.axis_index(DP), lax.axis_index(MP)
    groups = answers.shape[0]
    rows, slots, _ = memory.shape
    piece = rows // dp_ways
    own_q = dp_ways
    uniq = own_q * TOK
    tokens = rows * TOK
    padded = -(-slots // 16) * 16
    shard_rows = rows // mp_ways
    shard_tokens = shard_rows * TOK
    shard_q = own_q // mp_ways
    shard_uniq = shard_q * TOK
    local_heads = H // mp_ways
    head_cols = local_heads * HD
    hidden_cols = expand_weight.shape[1]
    vec = D // dp_ways

    vectors = (
        output_bias,
        first_gain,
        first_shift,
        crosso_bias,
        second_gain,
        second_shift,
        shrink_bias,
        third_gain,
        third_shift,
        crossv_bias,
    )
    matrices = (query_bias, value_bias, crossq_bias, expand_bias)
    starts, top = [], 16
    for matrix in matrices:
        starts.append(top)
        top += -(-matrix.shape[0] // 8) * 8
    small_rows = -(-top // 16) * 16
    row_of = lax.broadcasted_iota(jnp.int32, (small_rows, 128), 0)
    small = jnp.zeros((small_rows, 128), BF)
    for i, vector in enumerate(vectors):
        vector = jnp.pad(vector, (0, 128 - vector.shape[0]))
        small = jnp.where(row_of == i, vector[None, :], small)
    for start, matrix in zip(starts, matrices):
        count, width = matrix.shape
        small += jnp.pad(matrix, ((start, small_rows - start - count), (0, 128 - width)))
    wide_rows = cross_key.shape[0]
    self_shard = jnp.concatenate([self_query, self_key, self_value], axis=1)
    target_rows = jnp.pad(targets, ((0, 8 - groups), (0, 128 - TOK)))
    doc_rows = jnp.pad(doc_scores, ((0, 8 - groups), (0, 128 - K)))
    if chips == groups:
        wanted = answers
    else:
        wanted = jnp.stack([answers[(2 * c * piece) // K] for c in range(chips)])
    feed_shard = jnp.stack([expand_weight, shrink_weight.T]).reshape(4, vec // 2, -1)
    key_all, value_all, small_all, cquery_z, cout_z, feed_first = exchange(
        [
            (cross_key, WIDE, Z),
            (cross_value, WIDE, Z),
            (small, WIDE, Z),
            (cross_query, LATE, Z),
            (cross_output, LATE, Z),
            (feed_shard[0], LATE, Z),
        ],
        0,
    )
    (full_obias, gain_one, shift_one, full_cobias, gain_two, shift_two, full_sbias, gain_three, shift_three) = [
        small_all[:, 0, i, :vec].reshape(D) for i in range(9)
    ]
    cvbias = small_all[:, :, 9, :wide_rows].reshape(1, D)

    def head_bias(i):
        count, width = matrices[i].shape
        part = small_all[:, :, starts[i] : starts[i] + count, :width]
        return jnp.transpose(part, (1, 2, 0, 3)).reshape(mp_ways, -1)

    mine = lambda a: lax.dynamic_index_in_dim(a, mp, 0, keepdims=False)
    qbias = mine(head_bias(0))
    vbias = mine(head_bias(1))
    cqbias = head_bias(2).reshape(-1)
    ebias = head_bias(3).reshape(-1)
    key_weight = key_all.reshape(D, D)
    value_weight = value_all.reshape(D, D)

    plan = Exchange(
        [
            (feed_shard[1:], GATHER, Z),
            (self_shard, NEAR, Z),
            (self_output, NEAR, Z),
            (target_rows, NEAR, Z),
            (doc_rows, NEAR, Z),
            (wanted, NEARSWAP, Z),
            (cquery_z, NEAR, Z),
            (cout_z, NEAR, Z),
        ]
    )
    (keys, values, memory_rows, feed_rest, self_all, output_all, target_all, doc_all, x_all, cquery_all, cout_all) = (
        memory_products(memory, key_weight, value_weight, cvbias, padded, plan, 1)
    )
    words = word_table.shape[0]
    early = words // 1280 * 3 // 5 * 1280 if words % 1280 == 0 else 0
    feed_z = jnp.concatenate([feed_first[:, None], feed_rest], axis=1)
    tables = []
    if early:
        part, _ = lax.optimization_barrier((word_table[:early], small_all))
        part = lax.all_gather(part, DP, axis=0, tiled=False)
        feed_z, part = lax.optimization_barrier((feed_z, part))
        tables.append(part)
    feed_all = lax.all_gather(feed_z, DP, axis=0, tiled=False)
    feed_all = feed_all.reshape(dp_ways, mp_ways, 2, vec, -1)
    tables.append(lax.all_gather(word_table[early:], DP, axis=0, tiled=False))
    if word_table.shape[1] < 128:
        tables = [column_parts(a)[None] for a in tables]
    rows_first = lambda a: jnp.transpose(a, (0, 2, 1, 3)).reshape(dp_ways * a.shape[2], -1)
    columns_first = lambda a: column_parts(a.reshape(dp_ways, -1, a.shape[-1]))
    self_weight = self_all.reshape(D, 3 * head_cols)
    full_output = column_parts(output_all)
    my_group = (dp * piece) // K
    row_targets = lax.dynamic_index_in_dim(
        target_all[:, :groups, :TOK], my_group, 1, keepdims=False
    )
    x_rows = x_all.reshape(uniq, D)

    qkv = product(x_rows, self_weight)
    queries = ((qkv[:, :head_cols] + qbias) * SCALE).astype(BF)
    self_keys = qkv[:, head_cols : 2 * head_cols].astype(BF)
    self_values = (qkv[:, 2 * head_cols :] + vbias).astype(BF)
    heads = lambda a: a.reshape(own_q, TOK, local_heads, HD)
    probs = self_probs(heads(queries), heads(self_keys))
    context = jnp.einsum(
        "rhqk,rkhe->rqhe", probs.astype(BF), heads(self_values), preferred_element_type=F32
    )
    context = context.astype(BF).reshape(uniq, head_cols)
    partial = product(context, full_output).astype(BF).reshape(mp_ways, shard_uniq, D)
    (received,) = exchange([(partial, MOVE, Z)], 2)
    full_cquery = rows_first(cquery_all)
    x_own = lax.dynamic_slice_in_dim(x_rows, mp * shard_uniq, shard_uniq, 0)
    first_in = x_own.astype(F32) + added(partial, received, Z) + full_obias
    hidden_one, normed_one, inverse_one = layer_norm(first_in, gain_one, shift_one)
    hidden_low1 = hidden_one.astype(BF)
    cross_queries = ((product(hidden_low1, full_cquery) + cqbias) * SCALE).astype(BF)
    (cross_queries,) = exchange([(cross_queries, GATHER, Z)], 3)
    full_cout = columns_first(cout_all)
    cross_queries = cross_queries.reshape(uniq, D)

    used = jnp.clip(lengths - mp * slots, 0, slots).astype(jnp.int32)
    used = jnp.broadcast_to(used[:, None, None], (rows, 1, GL))
    keep = (
        lax.broadcasted_iota(jnp.int32, (GL, GC), 0) // TOK
        == lax.broadcasted_iota(jnp.int32, (GL, GC), 1) // HD
    ).astype(BF)
    ctx_own, stat_own, ctx_got, stat_got = cross_forward(
        used, keys, values, cross_queries, keep, piece, padded, 4
    )
    stat_got = jnp.concatenate([stat_own[None], stat_got], axis=0)
    peak_got, total_got = stat_got[:, 0], stat_got[:, 1]
    peak = jnp.max(peak_got, axis=0)
    weight = total_got * jnp.exp(peak_got - peak)
    total = jnp.sum(weight, axis=0)
    cross_norm = peak + jnp.log(total)
    weight = weight / total

    def to_token_heads(a):
        lead = a.shape[:-3]
        a = a.reshape(lead + (shard_rows, H, TOK))
        return jnp.swapaxes(a, -1, -2).reshape(lead + (shard_tokens, H))

    weight = jnp.repeat(to_token_heads(weight), HD, axis=-1)
    context_two = (
        ctx_own.astype(F32) * weight[0] + jnp.sum(ctx_got.astype(F32) * weight[1:], axis=0)
    ).astype(BF)

    def to_rows(a):
        a = jnp.broadcast_to(a.reshape(shard_q, 1, TOK, D), (shard_q, piece, TOK, D))
        return a.reshape(shard_tokens, D)

    second_in = to_rows(hidden_one) + product(context_two, full_cout) + full_cobias
    hidden_two, normed_two, inverse_two = layer_norm(second_in, gain_two, shift_two)
    hidden_low2 = hidden_two.astype(BF)

    expanded, third_in = feed_forward(hidden_low2, feed_all, ebias)
    third_in = hidden_two + third_in + full_sbias
    hidden_three, normed_three, inverse_three = layer_norm(third_in, gain_three, shift_three)

    vocab_local = words
    token_targets = jnp.broadcast_to(row_targets.reshape(own_q, 1, TOK), (own_q, piece, TOK))
    local_target = token_targets.reshape(mp_ways, 1, shard_tokens) - mp * vocab_local
    exponents, tops, stats = vocab_forward(hidden_three.astype(BF), local_target, tables, 5)
    stats = jnp.transpose(stats[:, :, :3], (0, 2, 1, 3)).reshape(mp_ways, 3, tokens)
    top = jnp.max(stats[:, 0], axis=0)
    norm_log = top + jnp.log(jnp.sum(stats[:, 1] * jnp.exp(stats[:, 0] - top), axis=0))
    loglik = jnp.sum(stats[:, 2], axis=0) - norm_log
    (loglik_all,) = exchange([(loglik.reshape(tokens // 128, 128), GATHER, DP)], 7)
    loglik_all = loglik_all.reshape(dp_ways, own_q, piece, TOK)
    loglik_all = jnp.transpose(loglik_all, (1, 0, 2, 3)).reshape(own_q, groups, K, TOK)
    doc_logp = jax.nn.log_softmax(doc_all[:, :groups, :K], axis=2)
    joined = doc_logp[..., None] + loglik_all
    marginal = jax.nn.logsumexp(joined, axis=2, keepdims=True)
    question_loss = -jnp.mean(
        lax.dynamic_index_in_dim(marginal[:, :, 0], dp, 0, keepdims=False), axis=1
    )
    posterior = jnp.exp(joined - marginal).reshape(own_q, groups * K, TOK)
    rate = -lax.dynamic_slice_in_dim(posterior, dp * piece, piece, 1)
    by_slot = lambda a: a.reshape(mp_ways, 1, shard_tokens)
    dhidden_three = vocab_back(
        exponents, tops, local_target, by_slot(norm_log), by_slot(rate), tables, 8
    )

    dthird, dgain_three, dshift_three = norm_back(
        dhidden_three, normed_three, inverse_three, gain_three
    )
    dshrink_bias = jnp.sum(dthird, axis=0)
    dshrink_in = dthird.astype(BF)
    dfeed, dexpand_bias, dhidden_two = feed_back(dshrink_in, hidden_low2, expanded, feed_all)
    dexpand_bias = dexpand_bias.reshape(-1)
    feed_dp = lax.psum_scatter(dfeed, DP, scatter_dimension=0, tiled=False)
    dhidden_two = dthird + dhidden_two

    dsecond, dgain_two, dshift_two = norm_back(dhidden_two, normed_two, inverse_two, gain_two)
    dcout_bias = jnp.sum(dsecond, axis=0)
    dcout_in = dsecond.astype(BF)
    dcontext_two = product_back(dcout_in, full_cout).astype(BF)
    middle = jnp.sum(
        (dcontext_two.astype(F32) * context_two.astype(F32)).reshape(shard_tokens, H, HD), axis=-1
    )
    middle = jnp.swapaxes(middle.reshape(shard_rows, TOK, H), 1, 2).reshape(shard_rows, G, GL)
    owners = lambda a: a.reshape(chips, 2, -1, a.shape[-1])
    cast = lambda a: a.astype(BF)
    co_blocks = owners(cast(weight_grad(dcout_in, context_two)))
    stat_all = jnp.stack([cross_norm, middle])
    dkeys, dvalues, dcross_q = cross_back(
        used, keys, values, cross_queries, dcontext_two, stat_all, keep, piece, padded, 9
    )
    dcross_low = (dcross_q * SCALE).astype(BF)
    dcquery = weight_grad(hidden_low1, dcross_low)
    dcq_bias = jnp.sum(dcross_low, axis=0, dtype=F32)
    dhidden_one = jnp.sum(dsecond.reshape(shard_q, piece, TOK, D), axis=1).reshape(
        shard_uniq, D
    ) + product_back(dcross_low, full_cquery)

    dfirst, dgain_one, dshift_one = norm_back(dhidden_one, normed_one, inverse_one, gain_one)
    dout_bias = jnp.sum(dfirst, axis=0)
    cq_blocks = owners(cast(dcquery))
    plan = Exchange(
        [
            (cast(dfirst), GATHER, Z),
            (co_blocks, MOVE1, PAIR),
            (cq_blocks, MOVE1, PAIR),
        ]
    )
    dkey_weight, dvalue_weight, dvalue_bias, dout_in, co_got, cq_got = memory_weights(
        memory_rows, dkeys, dvalues, rows, padded, plan, 11
    )
    co_blocks, cq_blocks = sums(
        [
            (co_blocks, co_got, MOVE1, PAIR, PLAIN, BF),
            (cq_blocks, cq_got, MOVE1, PAIR, PLAIN, BF),
        ]
    )
    dout_in = dout_in.reshape(uniq, D)
    memory_blocks = [owners(dkey_weight), owners(dvalue_weight)]
    plan = Exchange(
        [(co_blocks, MOVE, CHIPS), (cq_blocks, MOVE, CHIPS)]
        + [(a, MOVE1, PAIR) for a in memory_blocks]
    )
    dqkv_bias, self_blocks, out_blocks, dinputs, co_got, cq_got, *memory_got = self_back(
        x_rows, dout_in, context, queries, self_keys, self_values, full_output, self_weight, keep,
        dfirst, plan, 12,
    )
    dqkv_bias = dqkv_bias[0]
    key_blocks, value_blocks = sums(
        [(a, b, MOVE1, PAIR, PLAIN, BF) for a, b in zip(memory_blocks, memory_got)]
    )

    vectors = jnp.stack(
        [
            dout_bias,
            dgain_one,
            dshift_one,
            dcout_bias,
            dgain_two,
            dshift_two,
            dshrink_bias,
            dgain_three,
            dshift_three,
            dvalue_bias[0],
            dcq_bias,
            jnp.pad(dqkv_bias, (0, D - 3 * head_cols)),
        ]
    )
    vectors = jnp.concatenate([vectors, dexpand_bias.reshape(-1, D)], axis=0)
    answer_blocks = dinputs.reshape(chips, 2, TOK, D)
    plan = Exchange(
        [(feed_dp, COLS, Z)]
        + [
            (a, MOVE, CHIPS)
            for a in (value_blocks, self_blocks, out_blocks, key_blocks, answer_blocks)
        ]
        + [(vectors, GATHER, DP)]
    )
    memory_grad, received = memory_back(
        dkeys, dvalues, key_weight, value_weight, rows, slots, padded, plan, 15
    )
    feed_got, value_got, self_got, out_got, key_got, answer_got, vector_all = received
    key_sum, value_sum, cq_sum, co_sum, self_grad, out_grad, feed_grad, vector_sum = sums(
        [
            (key_blocks, key_got, MOVE, CHIPS, PLAIN, BF),
            (value_blocks, value_got, MOVE, CHIPS, PLAIN, BF),
            (cq_blocks, cq_got, MOVE, CHIPS, COLUMNS, BF),
            (co_blocks, co_got, MOVE, CHIPS, COLUMNS, BF),
            (self_blocks, self_got, MOVE, CHIPS, PLAIN, F32),
            (out_blocks, out_got, MOVE, CHIPS, TURNED, F32),
            (feed_dp, feed_got, COLS, Z, PLAIN, F32),
            (vector_all, vector_all, GATHER, DP, PLAIN, F32),
        ]
    )

    expand_grad, shrink_grad = feed_grad[0], feed_grad[1].T

    own_answers = lax.dynamic_index_in_dim(answer_blocks, dp // 2, 0, keepdims=True)
    returned = jnp.concatenate([own_answers, answer_got], axis=0).astype(F32)
    source = lax.rem(dp // 2 + chips - jnp.arange(chips), chips)
    place = (2 * source * piece) // K
    pick = (place[None, :] == jnp.arange(groups)[:, None]).astype(F32)
    answer_part = cast(jnp.sum(pick[:, :, None, None, None] * returned[None], axis=1))

    zblocks = [
        key_sum.reshape(mp_ways, wide_rows, D),
        value_sum.reshape(mp_ways, wide_rows, D),
        cq_sum,
        co_sum,
    ]
    feature_part = lax.dynamic_slice_in_dim(vector_sum[:10], dp * vec, vec, 1)
    *got_z, feature_all, head_all, answer_got = exchange(
        [(a, MOVE, Z) for a in zblocks]
        + [(feature_part, GATHER, Z), (vector_sum[10:], GATHER, Z)]
        + [(answer_part, MOVE1, PAIR)],
        16,
    )
    forms = [PLAIN, PLAIN, PLAIN, TURNED]
    key_grad, value_grad, cquery_grad, cout_grad, answer_grad = sums(
        [(a, b, MOVE, Z, form, F32) for a, b, form in zip(zblocks, got_z, forms)]
        + [(answer_part, answer_got, MOVE1, PAIR, PLAIN, F32)]
    )
    feature_own = jnp.sum(feature_all, axis=0)
    head_sums = jnp.sum(head_all, axis=0)
    head_own = lax.dynamic_index_in_dim(head_all, mp, 0, keepdims=False)[1]

    def vec_of(i):
        return feature_own[i]

    def of_dp(a, shape):
        a = a.reshape(-1, dp_ways, shape[1])
        return lax.dynamic_index_in_dim(a, dp, 1, keepdims=False)

    def of_mp(a, shape):
        return lax.dynamic_slice_in_dim(of_dp(a.reshape(-1), shape), mp * shape[0], shape[0], 0)

    return (
        question_loss,
        answer_grad,
        memory_grad,
        self_grad[:, :head_cols],
        self_grad[:, head_cols : 2 * head_cols],
        self_grad[:, 2 * head_cols :],
        of_dp(head_own[:head_cols], query_bias.shape),
        of_dp(head_own[2 * head_cols : 3 * head_cols], value_bias.shape),
        out_grad,
        vec_of(0),
        vec_of(1),
        vec_of(2),
        cquery_grad,
        of_mp(head_sums[0], crossq_bias.shape),
        key_grad,
        value_grad,
        lax.dynamic_slice_in_dim(vec_of(9), mp * wide_rows, wide_rows, 0),
        cout_grad,
        vec_of(3),
        vec_of(4),
        vec_of(5),
        expand_grad,
        of_mp(head_sums[2:], expand_bias.shape),
        shrink_grad,
        vec_of(6),
        vec_of(7),
        vec_of(8),
    )


def solution(mesh):
    placed = (
        P(DP, None, None),
        P(DP, None),
        P(DP, None),
        P(DP, MP, None),
        P(DP),
        P(DP, MP),
        P(DP, MP),
        P(DP, MP),
        P(MP, DP),
        P(MP, DP),
        P(MP, DP),
        P(DP),
        P(DP),
        P(DP),
        P(DP, MP),
        P(MP, DP),
        P((DP, MP), None),
        P((DP, MP), None),
        P((DP, MP)),
        P(MP, DP),
        P(DP),
        P(DP),
        P(DP),
        P(DP, MP),
        P(MP, DP),
        P(MP, DP),
        P(DP),
        P(DP),
        P(DP),
        P(MP, DP),
    )
    return jax.shard_map(
        local,
        mesh=mesh,
        in_specs=placed,
        out_specs=(
            P(DP),
            P(DP, None, None),
            P(DP, MP, None),
            P(DP, MP),
            P(DP, MP),
            P(DP, MP),
            P(MP, DP),
            P(MP, DP),
            P(MP, DP),
            P(DP),
            P(DP),
            P(DP),
            P(DP, MP),
            P(MP, DP),
            P((DP, MP), None),
            P((DP, MP), None),
            P((DP, MP)),
            P(MP, DP),
            P(DP),
            P(DP),
            P(DP),
            P(DP, MP),
            P(MP, DP),
            P(MP, DP),
            P(DP),
            P(DP),
            P(DP),
        ),
        check_vma=False,
    )
```

```python
import functools

import jax
import jax.numpy as jnp
from jax import lax
from jax.experimental import pallas as pl
from jax.experimental.pallas import tpu as pltpu
from jax.sharding import PartitionSpec as P

D = 1024
H = 16
HD = 64
TOK = 32
K = 8
G = 4
GH = 4
GC = GH * HD
GL = GH * TOK

EPS = 1e-05
NEG = -1e30
SCALE = 0.125
BF = jnp.bfloat16
F32 = jnp.float32
MESH = pl.DeviceIdType.MESH
DP, MP = "dp", "mp"
GATHER, LATE, MOVE, MOVE1, COLS, NEAR, NEARSWAP, WIDE = range(8)
Z, CHIPS, PAIR = range(3)
PLAIN, COLUMNS, TURNED = range(3)
VMEM_BYTES = 60 * 1024 * 1024


def product(former, latter):
    return jnp.dot(former, latter, preferred_element_type=F32)


def product_back(former, latter):
    return lax.dot_general(former, latter, (((1,), (1,)), ((), ())), preferred_element_type=F32)


def weight_grad(former, latter):
    return lax.dot_general(former, latter, (((0,), (0,)), ((), ())), preferred_element_type=F32)


def layer_norm(entries, norm_gain, norm_shift):
    center = entries - jnp.mean(entries, axis=-1, keepdims=True)
    inverse = lax.rsqrt(jnp.mean(center * center, axis=-1, keepdims=True) + EPS)
    normed = center * inverse
    return (normed * norm_gain + norm_shift, normed, inverse)


def norm_back(upstream, normed, inverse, norm_gain):
    scaled = upstream * norm_gain
    dentries = inverse * (
        scaled
        - jnp.mean(scaled, axis=-1, keepdims=True)
        - normed * jnp.mean(scaled * normed, axis=-1, keepdims=True)
    )
    return (dentries, jnp.sum(upstream * normed, axis=0), jnp.sum(upstream, axis=0))


class Exchange:
    def __init__(self, entries):
        self.dp_ways, self.mp_ways = lax.axis_size(DP), lax.axis_size(MP)
        self.chips = self.dp_ways // 2
        self.ways = {Z: self.mp_ways, CHIPS: self.chips, PAIR: 2, DP: self.dp_ways}
        self.arrays = [entry[0] for entry in entries]
        self.kinds = [entry[1] for entry in entries]
        self.groups = [entry[2] for entry in entries]
        self.count = len(entries)
        shapes = []
        for array, kind, group in entries:
            shape = array.shape
            if kind in (GATHER, LATE):
                shape = (self.ways[group],) + shape
            elif kind == MOVE:
                shape = (self.ways[group] - 1,) + shape[1:]
            elif kind == MOVE1:
                shape = (self.ways[group] - 1, shape[0]) + shape[2:]
            elif kind == COLS:
                shape = (self.ways[group] - 1,) + shape[:-1] + (shape[-1] // self.ways[group],)
            elif kind == NEAR:
                shape = (self.dp_ways,) + shape
            elif kind == NEARSWAP:
                shape = (self.dp_ways,) + shape[1:]
            else:
                shape = (self.dp_ways, self.mp_ways) + shape
            shapes.append(jax.ShapeDtypeStruct(shape, array.dtype))
        self.shapes = shapes
        self.specs = [pl.BlockSpec(memory_space=pl.ANY)] * self.count
        dma = pltpu.SemaphoreType.DMA
        most = max(self.dp_ways, self.mp_ways)
        self.scratch = [dma((self.count, most)) for _ in range(6)] + [dma((self.count,))]

    def bind(self, ins, outs, sems):
        self.ins, self.outs = ins, outs
        self.zs, self.zr, self.cs, self.cr, self.ps, self.pr, self.own = sems
        dp, mp = lax.axis_index(DP), lax.axis_index(MP)
        self.dp, self.mp = dp, mp
        self.parity, self.chip = lax.rem(dp, 2), dp // 2
        self.place = {Z: mp, CHIPS: self.chip, PAIR: self.parity, DP: dp}

    def device(self, group, j):
        if group == Z:
            return (self.dp, j)
        if group == CHIPS:
            return (2 * j + self.parity, self.mp)
        if group == PAIR:
            return (self.dp - self.parity + j, self.mp)
        return (j, self.mp)

    def peer(self, group, off):
        return lax.rem(self.place[group] + off, self.ways[group])

    def remote(self, source, target, send, recv, device):
        return pltpu.make_async_remote_copy(
            src_ref=source,
            dst_ref=target,
            send_sem=send,
            recv_sem=recv,
            device_id=device,
            device_id_type=MESH,
        )

    def meet(self, also=()):
        needed = set(also)
        for kind, group in zip(self.kinds, self.groups):
            if kind in (NEAR, NEARSWAP, WIDE):
                needed |= {CHIPS, PAIR}
                if kind == WIDE:
                    needed.add(Z)
            else:
                needed.add(group)
        barrier = pltpu.get_barrier_semaphore()
        total = 0
        for group in sorted(needed, key=str):
            for off in range(1, self.ways[group]):
                pl.semaphore_signal(
                    barrier,
                    inc=1,
                    device_id=self.device(group, self.peer(group, off)),
                    device_id_type=MESH,
                )
                total += 1
        pl.semaphore_wait(barrier, total)

    def first(self, i):
        kind, group = self.kinds[i], self.groups[i]
        ref, out = self.ins[i], self.outs[i]
        copies = []
        if kind in (NEAR, NEARSWAP):
            return copies
        if kind == WIDE:
            group, slot = Z, out.at[self.dp, self.mp]
        for off in range(1, self.ways[group]):
            peer = self.peer(group, off)
            if kind == WIDE:
                source, target = ref, slot
            elif kind in (GATHER, LATE):
                source, target = ref, out.at[self.place[group]]
            elif kind == MOVE:
                source, target = ref.at[peer], out.at[off - 1]
            elif kind == COLS:
                width = out.shape[-1]
                part = pl.ds(pl.multiple_of(peer * width, width), width)
                source, target = ref.at[:, :, part], out.at[off - 1]
            else:
                source, target = ref.at[:, peer], out.at[off - 1]
            copies.append(
                self.remote(
                    source,
                    target,
                    self.zs.at[i, off - 1],
                    self.zr.at[i, off - 1],
                    self.device(group, peer),
                )
            )
        return copies

    def local(self, i):
        kind, group = self.kinds[i], self.groups[i]
        ref, out = self.ins[i], self.outs[i]
        if kind == WIDE:
            source, target = ref, out.at[self.dp, self.mp]
        elif kind in (GATHER, LATE):
            source, target = ref, out.at[self.place[group]]
        elif kind in (NEAR, NEARSWAP):
            source, target = self.mine(i), out.at[self.dp]
        else:
            return None
        return pltpu.make_async_copy(source, target, self.own.at[i])

    def mine(self, i):
        kind = self.kinds[i]
        if kind == WIDE:
            return self.outs[i].at[self.dp]
        return self.ins[i].at[self.chip] if kind == NEARSWAP else self.ins[i]

    def spread(self, i):
        copies = []
        for off in range(1, self.chips):
            peer = self.peer(CHIPS, off)
            source = self.ins[i].at[peer] if self.kinds[i] == NEARSWAP else self.mine(i)
            copies.append(
                self.remote(
                    source,
                    self.outs[i].at[self.dp],
                    self.cs.at[i, off - 1],
                    self.cr.at[i, off - 1],
                    self.device(CHIPS, peer),
                )
            )
        return copies

    def hand(self, i, off):
        owner = 2 * lax.rem(self.chip + self.chips - off, self.chips) + self.parity
        return self.remote(
            self.mine(i) if off == 0 else self.outs[i].at[owner],
            self.outs[i].at[owner],
            self.ps.at[i, off],
            self.pr.at[i, off],
            self.device(PAIR, 1 - self.parity),
        )

    def begin(self, also=()):
        self.meet(also)
        self.start()

    def start(self):
        for i in range(self.count):
            if self.kinds[i] == LATE:
                continue
            for copy in self.first(i):
                copy.start()
            if self.kinds[i] in (NEAR, NEARSWAP):
                for copy in self.spread(i):
                    copy.start()
                self.hand(i, 0).start()
        for i in range(self.count):
            local = self.local(i)
            if local is not None:
                local.start()

    def finish(self):
        shared = [i for i in range(self.count) if self.kinds[i] in (NEAR, NEARSWAP, WIDE)]
        for i in shared:
            if self.kinds[i] == WIDE:
                for copy in self.first(i):
                    copy.wait()
                self.local(i).wait()
                for copy in self.spread(i):
                    copy.start()
                self.hand(i, 0).start()
        for i in range(self.count):
            if self.kinds[i] == LATE:
                for copy in self.first(i):
                    copy.start()
        for i in shared:
            for off, copy in enumerate(self.spread(i), 1):
                copy.wait_recv()
                self.hand(i, off).start()
        for i in range(self.count):
            if i in shared:
                for copy in self.spread(i):
                    copy.wait_send()
                for off in range(self.chips):
                    self.hand(i, off).wait()
                if self.kinds[i] != WIDE:
                    self.local(i).wait()
            else:
                for copy in self.first(i):
                    copy.wait()
                local = self.local(i)
                if local is not None:
                    local.wait()


def exchange_kernel(plan, *refs):
    count = plan.count
    plan.bind(refs[:count], refs[count : 2 * count], refs[2 * count :])
    plan.begin()
    plan.finish()


def exchange(entries, cid):
    plan = Exchange(entries)
    return pl.pallas_call(
        functools.partial(exchange_kernel, plan),
        out_shape=plan.shapes,
        in_specs=plan.specs,
        out_specs=plan.specs,
        scratch_shapes=plan.scratch,
        compiler_params=pltpu.CompilerParams(collective_id=cid, has_side_effects=True),
    )(*plan.arrays)


def added(array, received, group):
    place = {
        Z: lax.axis_index(MP),
        CHIPS: lax.axis_index(DP) // 2,
        PAIR: lax.rem(lax.axis_index(DP), 2),
        DP: lax.axis_index(DP),
    }[group]
    axis = 1 if group == PAIR else 0
    own = lax.dynamic_index_in_dim(array, place, axis, keepdims=False)
    return own.astype(F32) + jnp.sum(received.astype(F32), axis=0)


def sums_kernel(kinds, shapes, *refs):
    n = len(kinds)
    arrays, received, outs = refs[:n], refs[n : 2 * n], refs[2 * n :]
    dp, mp = lax.axis_index(DP), lax.axis_index(MP)
    place = {Z: mp, CHIPS: dp // 2, PAIR: lax.rem(dp, 2)}
    for array, got, out, (kind, group, form) in zip(arrays, received, outs, kinds):
        if kind == GATHER:
            total = jnp.sum(array[...].astype(F32), axis=0)
        else:
            if kind == MOVE:
                own = array[place[group]]
            elif kind == MOVE1:
                own = array[:, place[group]]
            else:
                width = got.shape[-1]
                own = array[:, :, pl.ds(pl.multiple_of(place[group] * width, width), width)]
            total = own.astype(F32)
            for i in range(got.shape[0]):
                total += got[i].astype(F32)
        if form == COLUMNS:
            width = out.shape[-1]
            for i in range(out.shape[0]):
                out[i] = total[:, i * width : (i + 1) * width].astype(out.dtype)
        elif form == TURNED:
            out[...] = total.T
        else:
            out[...] = total.astype(out.dtype)


def sums(entries):
    mp_ways = lax.axis_size(MP)
    arrays, received, shapes, kinds = [], [], [], []
    for array, got, kind, group, form, dtype in entries:
        shape = got.shape[1:]
        if form == COLUMNS:
            shape = (mp_ways, shape[0], shape[1] // mp_ways)
        elif form == TURNED:
            shape = shape[::-1]
        arrays.append(array)
        received.append(got)
        shapes.append(jax.ShapeDtypeStruct(shape, dtype))
        kinds.append((kind, group, form))
    vmem = pl.BlockSpec(memory_space=pltpu.VMEM)
    return pl.pallas_call(
        functools.partial(sums_kernel, kinds, shapes),
        in_specs=[vmem] * (2 * len(entries)),
        out_specs=[vmem] * len(entries),
        out_shape=shapes,
        compiler_params=pltpu.CompilerParams(vmem_limit_bytes=VMEM_BYTES),
    )(*arrays, *received)


def beside(plan, kernel, inputs, outputs, scratches, *refs):
    n = plan.count
    first, last = pl.program_id(0) == 0, pl.program_id(0) == pl.num_programs(0) - 1
    ins = refs[:inputs]
    sends = refs[inputs : inputs + n]
    outs = refs[inputs + n : inputs + n + outputs]
    lands = refs[inputs + n + outputs : inputs + 2 * n + outputs]
    own = refs[inputs + 2 * n + outputs : inputs + 2 * n + outputs + scratches]
    plan.bind(sends, lands, refs[inputs + 2 * n + outputs + scratches :])
    pl.when(first)(plan.begin)
    kernel(*ins, *outs, *own)
    pl.when(last)(plan.finish)


def memory_call(plan, cid, kernel, name, grid, inputs, in_specs, out_specs, out_shape, scratch, flops):
    return pl.pallas_call(
        functools.partial(beside, plan, kernel, len(inputs), len(out_shape), len(scratch)),
        grid=(grid,),
        in_specs=in_specs + plan.specs,
        out_specs=out_specs + plan.specs,
        out_shape=out_shape + plan.shapes,
        scratch_shapes=scratch + plan.scratch,
        compiler_params=pltpu.CompilerParams(
            vmem_limit_bytes=VMEM_BYTES, collective_id=cid, has_side_effects=True
        ),
        cost_estimate=pl.CostEstimate(flops=flops, bytes_accessed=flops // 200, transcendentals=0),
        name=name,
    )(*inputs, *plan.arrays)


MEM_BLOCK = 16
BACK_BLOCK = 16


def memory_kernel(slots, padded, mem_ref, wk_ref, wv_ref, vb_ref, k_ref, v_ref, rows_ref, wide):
    for c in range(0, D, 128):
        cols = slice(c, c + 128)
        wide[...] = mem_ref[:, :, cols].reshape(slots * MEM_BLOCK, 128).astype(F32)
        for r in range(MEM_BLOCK):
            own = wide[pl.ds(r, slots, stride=MEM_BLOCK), :]
            rows_ref[r * padded : (r + 1) * padded, cols] = jnp.concatenate(
                [own, jnp.zeros((padded - slots, 128), F32)], axis=0
            ).astype(BF)
    rows = rows_ref[...]
    for c in range(0, D, 512):
        cols = slice(c, c + 512)
        k_ref[:, cols] = product(rows, wk_ref[:, cols]).astype(BF)
        v_ref[:, cols] = (product(rows, wv_ref[:, cols]) + vb_ref[:, cols]).astype(BF)


def memory_products(memory, key_weight, value_weight, vbias, padded, plan, cid):
    rows, slots, _ = memory.shape
    whole = lambda a: pl.BlockSpec(a.shape, lambda i: (0,) * a.ndim)
    out = jax.ShapeDtypeStruct((rows * padded, D), BF)
    out_spec = pl.BlockSpec((MEM_BLOCK * padded, D), lambda i: (i, 0))
    return memory_call(
        plan,
        cid,
        functools.partial(memory_kernel, slots, padded),
        "memory_products",
        rows // MEM_BLOCK,
        [jnp.transpose(memory, (1, 0, 2)), key_weight, value_weight, vbias],
        [
            pl.BlockSpec((slots, MEM_BLOCK, D), lambda i: (0, i, 0)),
            whole(key_weight),
            whole(value_weight),
            whole(vbias),
        ],
        [out_spec] * 3,
        [out] * 3,
        [pltpu.VMEM((slots * MEM_BLOCK, 128), F32)],
        4 * rows * padded * D * D,
    )


def memory_grad_kernel(slots, padded, dk_ref, dv_ref, wk_ref, wv_ref, out_ref, wide):
    for c in range(0, D, 256):
        cols = slice(c, c + 256)
        term = product_back(dk_ref[...], wk_ref[cols, :]) + product_back(dv_ref[...], wv_ref[cols, :])
        for part in range(0, 256, 128):
            for r in range(BACK_BLOCK):
                wide[pl.ds(r, slots, stride=BACK_BLOCK), :] = term[
                    r * padded : r * padded + slots, part : part + 128
                ]
            out_ref[:, :, c + part : c + part + 128] = (
                wide[...].reshape(slots, BACK_BLOCK, 128).astype(BF)
            )


def memory_back(dkeys, dvalues, key_weight, value_weight, rows, slots, padded, plan, cid):
    spec = pl.BlockSpec((BACK_BLOCK * padded, D), lambda i: (i, 0))
    whole = pl.BlockSpec((D, D), lambda i: (0, 0))
    out, *rest = memory_call(
        plan,
        cid,
        functools.partial(memory_grad_kernel, slots, padded),
        "memory_back",
        rows // BACK_BLOCK,
        [dkeys, dvalues, key_weight, value_weight],
        [spec, spec, whole, whole],
        [pl.BlockSpec((slots, BACK_BLOCK, D), lambda i: (0, i, 0))],
        [jax.ShapeDtypeStruct((slots, rows, D), BF)],
        [pltpu.VMEM((slots * BACK_BLOCK, 128), F32)],
        4 * rows * padded * D * D,
    )
    return jnp.transpose(out, (1, 0, 2)).astype(F32), rest


def z_copy(source, target, send, recv, device):
    return pltpu.make_async_remote_copy(
        src_ref=source,
        dst_ref=target,
        send_sem=send,
        recv_sem=recv,
        device_id=(lax.axis_index(DP), device),
        device_id_type=MESH,
    )


def z_meet(ways):
    dp, mp = lax.axis_index(DP), lax.axis_index(MP)
    barrier = pltpu.get_barrier_semaphore()
    for off in range(1, ways):
        pl.semaphore_signal(
            barrier, inc=1, device_id=(dp, lax.rem(mp + off, ways)), device_id_type=MESH
        )
    pl.semaphore_wait(barrier, ways - 1)


def nearest(c, ways):
    mp = lax.axis_index(MP)
    left_n, right_n = mp, ways - 1 - mp
    fewer = jnp.minimum(left_n, right_n)
    paired = c <= 2 * fewer
    distance = jnp.where(paired, (c + 1) // 2, c - fewer)
    left = jnp.where(paired, lax.rem(c, 2) == 1, left_n > right_n)
    return jnp.where(left, mp - distance, mp + distance), distance, left, paired


class LineGather:
    def __init__(self, entries, sems, ways):
        self.entries, self.ways = entries, ways
        self.left_send, self.left_recv, self.right_send, self.right_recv, self.own = sems
        self.mp = lax.axis_index(MP)

    def to_right(self, i, source, place, hop):
        held = self.entries[i][1]
        return z_copy(
            source, held.at[place], self.right_send.at[i, hop], self.right_recv.at[i, hop], self.mp + 1
        )

    def to_left(self, i, source, place, hop):
        held = self.entries[i][1]
        return z_copy(
            source, held.at[place], self.left_send.at[i, hop], self.left_recv.at[i, hop], self.mp - 1
        )

    def begin(self):
        mp, every = self.mp, range(len(self.entries))

        @pl.when(mp < self.ways - 1)
        def _():
            for i in every:
                self.to_right(i, self.entries[i][0], mp, 0).start()

        @pl.when(mp > 0)
        def _():
            for i in every:
                self.to_left(i, self.entries[i][0], mp, 0).start()

        for i in every:
            local = pltpu.make_async_copy(self.entries[i][0], self.entries[i][1].at[mp], self.own.at[i])
            local.start()
            local.wait()

    def arrive(self, c, first):
        mp, every = self.mp, range(len(self.entries))
        _, distance, left, paired = nearest(c, self.ways)
        odd = lax.rem(c, 2) == 1
        due = (c > 0) & first & jnp.logical_not(paired & jnp.logical_not(odd))

        @pl.when(due & (left | (paired & odd)))
        def _():
            place = mp - distance
            for i in every:
                held = self.entries[i][1].at[place]
                self.to_right(i, held, place, distance - 1).wait_recv()

                @pl.when(mp < self.ways - 1)
                def _(i=i, held=held):
                    self.to_right(i, held, place, distance).start()

        @pl.when(due & (jnp.logical_not(left) | (paired & odd)))
        def _():
            place = mp + distance
            for i in every:
                held = self.entries[i][1].at[place]
                self.to_left(i, held, place, distance - 1).wait_recv()

                @pl.when(mp > 0)
                def _(i=i, held=held):
                    self.to_left(i, held, place, distance).start()

    def finish(self):
        mp = self.mp
        for hop in range(self.ways - 1):

            @pl.when((mp < self.ways - 1) & (hop <= mp))
            def _(hop=hop):
                for i, (_, held) in enumerate(self.entries):
                    self.to_right(i, held.at[mp - hop], mp - hop, hop).wait_send()

            @pl.when((mp > 0) & (hop <= self.ways - 1 - mp))
            def _(hop=hop):
                for i, (_, held) in enumerate(self.entries):
                    self.to_left(i, held.at[mp + hop], mp + hop, hop).wait_send()


def line_sems(count, ways):
    dma = pltpu.SemaphoreType.DMA
    return [dma((count, ways)) for _ in range(4)] + [dma((count,))]


def own_heads(result, keep):
    kept = result * keep
    total = kept[0:TOK]
    for h in range(1, GH):
        total = total + kept[h * TOK : (h + 1) * TOK]
    return total


def cross_kernel(
    ways, per, piece, padded, used_ref, k_ref, v_ref, q_ref, keep_ref, ctx_ref, stat_ref, ctx_got, stat_got,
    ctx_out, stat_out, send, recv,
):
    c, j = pl.program_id(0), pl.program_id(1)
    mp = lax.axis_index(MP)
    span = piece * TOK

    @pl.when((c == 0) & (j == 0))
    def _():
        z_meet(ways)

    keep = keep_ref[...]
    keep_wide = keep.astype(F32)
    slot = lax.broadcasted_iota(jnp.int32, (padded, GL), 0)
    for g in range(G):
        cols = slice(g * GC, (g + 1) * GC)
        query = jnp.concatenate([q_ref[:, cols]] * GH, axis=0) * keep
        scores = product_back(k_ref[:, cols], query)
        for r in range(piece):
            rows = slice(r * padded, (r + 1) * padded)
            seen = slot < used_ref[r]
            own = jnp.where(seen, scores[rows], NEG)
            peak = jnp.max(own, axis=0, keepdims=True)
            exponent = jnp.where(seen, jnp.exp(own - peak), 0.0)
            total = jnp.sum(exponent, axis=0, keepdims=True)
            probs = (exponent * (1.0 / jnp.maximum(total, 1e-30))).astype(BF)
            ctx = own_heads(weight_grad(probs, v_ref[rows, cols]), keep_wide)
            ctx_out[c, pl.ds(j * span + r * TOK, TOK), cols] = ctx.astype(BF)
            stat_out[c, 0, j * piece + r, g : g + 1, :] = peak
            stat_out[c, 1, j * piece + r, g : g + 1, :] = total

    def copies(k):
        to = nearest(ways - 1 - k, ways)[0]
        off = lax.rem(to - mp + ways, ways)
        return [
            z_copy(a.at[k], b.at[off - 1], send.at[i, k], recv.at[i, off - 1], to)
            for i, (a, b) in enumerate([(ctx_out, ctx_got), (stat_out, stat_got)])
        ]

    for k in range(ways - 1):

        @pl.when((c == k) & (j == per - 1))
        def _(k=k):
            for copy in copies(k):
                copy.start()

    @pl.when((c == ways - 1) & (j == per - 1))
    def _():
        ctx_ref[...] = ctx_out[ways - 1]
        stat_ref[...] = stat_out[ways - 1]
        for k in range(ways - 1):
            for copy in copies(k):
                copy.wait_send()
        for off in range(1, ways):
            to = lax.rem(mp + off, ways)
            for i, (a, b) in enumerate([(ctx_out, ctx_got), (stat_out, stat_got)]):
                z_copy(a.at[0], b.at[off - 1], send.at[i, 0], recv.at[i, off - 1], to).wait_recv()


def cross_forward(used, keys, values, queries, keep, piece, padded, cid):
    ways = lax.axis_size(MP)
    per = queries.shape[0] // TOK // ways
    rows = per * ways * piece
    shard = per * piece
    at = lambda c, j: nearest(ways - 1 - c, ways)[0] * per + j
    big = pl.BlockSpec((piece * padded, D), lambda c, j: (at(c, j), 0))
    anywhere = pl.BlockSpec(memory_space=pl.ANY)
    dma = pltpu.SemaphoreType.DMA
    return pl.pallas_call(
        functools.partial(cross_kernel, ways, per, piece, padded),
        grid=(ways, per),
        in_specs=[
            pl.BlockSpec((piece, 1, GL), lambda c, j: (at(c, j), 0, 0)),
            big,
            big,
            pl.BlockSpec((TOK, D), lambda c, j: (at(c, j), 0)),
            pl.BlockSpec((GL, GC), lambda c, j: (0, 0)),
        ],
        out_specs=[
            pl.BlockSpec((shard * TOK, D), lambda c, j: (0, 0)),
            pl.BlockSpec((2, shard, G, GL), lambda c, j: (0, 0, 0, 0)),
            anywhere,
            anywhere,
        ],
        out_shape=[
            jax.ShapeDtypeStruct((shard * TOK, D), BF),
            jax.ShapeDtypeStruct((2, shard, G, GL), F32),
            jax.ShapeDtypeStruct((ways - 1, shard * TOK, D), BF),
            jax.ShapeDtypeStruct((ways - 1, 2, shard, G, GL), F32),
        ],
        scratch_shapes=[
            pltpu.VMEM((ways, shard * TOK, D), BF),
            pltpu.VMEM((ways, 2, shard, G, GL), F32),
            dma((2, ways)),
            dma((2, ways)),
        ],
        compiler_params=pltpu.CompilerParams(
            vmem_limit_bytes=VMEM_BYTES, collective_id=cid, has_side_effects=True
        ),
        cost_estimate=pl.CostEstimate(
            flops=4 * rows * padded * GL * D,
            bytes_accessed=4 * rows * padded * D,
            transcendentals=rows * padded * G * GL,
        ),
    )(used, keys, values, queries, keep)


def cross_back_kernel(
    ways, per, piece, padded, used_ref, k_ref, v_ref, q_ref, keep_ref, rows_ref, dctx_ref, stat_ref, co_ref,
    dk_ref, dv_ref, dq_ref, key_ref, value_ref, vb_ref, co_sum_ref,
    dctx_all, stat_all, dq_out, dq_got, key_sum, value_sum, low, low_got, co_own, co_got,
    left_send, left_recv, right_send, right_recv, own, send, recv, core_send, core_recv,
):
    c, j = pl.program_id(0), pl.program_id(1)
    dp, mp = lax.axis_index(DP), lax.axis_index(MP)
    parity = lax.rem(dp, 2)
    sibling = (dp + 1 - 2 * parity, mp)
    place = nearest(c, ways)[0]
    span = piece * TOK
    line = LineGather(
        [(dctx_ref, dctx_all), (stat_ref, stat_all)],
        (left_send, left_recv, right_send, right_recv, own),
        ways,
    )

    def core_copy(i):
        source, target = [
            (co_ref, co_got),
            (low.at[0], low_got.at[0]),
            (low.at[1], low_got.at[1]),
        ][i]
        return pltpu.make_async_remote_copy(
            src_ref=source.at[:, 1 - parity],
            dst_ref=target,
            send_sem=core_send.at[i],
            recv_sem=core_recv.at[i],
            device_id=sibling,
            device_id_type=MESH,
        )

    def co_local():
        return pltpu.make_async_copy(co_ref.at[:, parity], co_own, own.at[2])

    @pl.when((c == 0) & (j == 0))
    def _():
        barrier = pltpu.get_barrier_semaphore()
        pl.semaphore_signal(barrier, inc=1, device_id=sibling, device_id_type=MESH)
        for off in range(1, ways):
            pl.semaphore_signal(
                barrier, inc=1, device_id=(dp, lax.rem(mp + off, ways)), device_id_type=MESH
            )
        pl.semaphore_wait(barrier, ways)
        line.begin()
        core_copy(0).start()
        co_local().start()
        key_sum[...] = jnp.zeros_like(key_sum)
        value_sum[...] = jnp.zeros_like(value_sum)
        vb_ref[...] = jnp.zeros_like(vb_ref)

    middle_place = (mp > 0) & (mp < ways - 1)
    line.arrive(c, (j == 0) & jnp.logical_not(middle_place & (c == ways - 1)))
    line.arrive(c + 1, (j == 0) & middle_place & (c == ways - 2))
    keep = keep_ref[...]
    keep_wide = keep.astype(F32)
    slot = lax.broadcasted_iota(jnp.int32, (padded, GL), 0)
    for g in range(G):
        cols = slice(g * GC, (g + 1) * GC)
        query = jnp.concatenate([q_ref[:, cols]] * GH, axis=0) * keep
        scores = product_back(k_ref[:, cols], query)
        parts = []
        for r in range(piece):
            rows = slice(r * padded, (r + 1) * padded)
            dctx = dctx_all[place, pl.ds(j * span + r * TOK, TOK), cols]
            dctx = jnp.concatenate([dctx] * GH, axis=0) * keep
            dprobs = product_back(v_ref[rows, cols], dctx)
            seen = slot < used_ref[r]
            norm = stat_all[place, 0, j * piece + r, g : g + 1, :]
            middle = stat_all[place, 1, j * piece + r, g : g + 1, :]
            probs = jnp.where(seen, jnp.exp(scores[rows] - norm), 0.0)
            parts.append((probs * (dprobs - middle)).astype(BF))
            dv_ref[rows, cols] = product(probs.astype(BF), dctx).astype(BF)
        dscores = jnp.concatenate(parts, axis=0)
        dk_ref[:, cols] = product(dscores, query).astype(BF)
        dquery = own_heads(weight_grad(dscores, k_ref[:, cols]), keep_wide)
        dq_out[c, pl.ds(j * TOK, TOK), cols] = dquery.astype(BF)

    def copy(k):
        to = nearest(k, ways)[0]
        off = lax.rem(to - mp + ways, ways)
        return z_copy(dq_out.at[k], dq_got.at[off - 1], send.at[k], recv.at[off - 1], to)

    for k in range(1, ways):

        @pl.when((c == k) & (j == per - 1))
        def _(k=k):
            copy(k).start()

    memory_rows = rows_ref[...]
    vb_ref[...] += jnp.sum(dv_ref[...].astype(F32), axis=0, keepdims=True)
    for start in range(0, D, 512):
        cols = slice(start, start + 512)
        key_sum[:, cols] += weight_grad(memory_rows, dk_ref[:, cols])
        value_sum[:, cols] += weight_grad(memory_rows, dv_ref[:, cols])

    @pl.when((c == ways - 1) & (j == per - 1))
    def _():
        for i, total in enumerate((key_sum, value_sum)):
            low[i] = total[...].astype(BF).reshape(low.shape[1:])
            core_copy(1 + i).start()
        line.finish()
        for k in range(1, ways):
            copy(k).wait_send()
        total = dq_out[0].astype(F32)
        for off in range(1, ways):
            z_copy(
                dq_out.at[0], dq_got.at[off - 1], send.at[0], recv.at[off - 1], lax.rem(mp + off, ways)
            ).wait_recv()
            total += dq_got[off - 1].astype(F32)
        dq_ref[...] = total
        co_local().wait()
        core_copy(0).wait()
        co_sum_ref[...] = (co_own[...].astype(F32) + co_got[...].astype(F32)).astype(BF)
        for i, out in enumerate((key_ref, value_ref)):
            core_copy(1 + i).wait()
            out[...] = (low[i, :, parity].astype(F32) + low_got[i].astype(F32)).astype(BF)


def cross_back(used, keys, values, queries, memory_rows, dctx, stats, co_blocks, keep, piece, padded, cid):
    ways = lax.axis_size(MP)
    per = queries.shape[0] // TOK // ways
    rows = per * ways * piece
    shard = per * piece
    at = lambda c, j: nearest(c, ways)[0] * per + j
    big = pl.BlockSpec((piece * padded, D), lambda c, j: (at(c, j), 0))
    anywhere = pl.BlockSpec(memory_space=pl.ANY)
    chips, _, vec, _ = co_blocks.shape
    half = (chips, vec, D)
    half_spec = pl.BlockSpec(half, lambda c, j: (0, 0, 0))
    half_shape = jax.ShapeDtypeStruct(half, BF)
    line = line_sems(2, ways)
    dma = pltpu.SemaphoreType.DMA
    return pl.pallas_call(
        functools.partial(cross_back_kernel, ways, per, piece, padded),
        grid=(ways, per),
        in_specs=[
            pl.BlockSpec((piece, 1, GL), lambda c, j: (at(c, j), 0, 0)),
            big,
            big,
            pl.BlockSpec((TOK, D), lambda c, j: (at(c, j), 0)),
            pl.BlockSpec((GL, GC), lambda c, j: (0, 0)),
            big,
            anywhere,
            anywhere,
            anywhere,
        ],
        out_specs=[
            big,
            big,
            pl.BlockSpec((per * TOK, D), lambda c, j: (0, 0)),
            half_spec,
            half_spec,
            pl.BlockSpec((1, D), lambda c, j: (0, 0)),
            half_spec,
        ],
        out_shape=[
            jax.ShapeDtypeStruct((rows * padded, D), BF),
            jax.ShapeDtypeStruct((rows * padded, D), BF),
            jax.ShapeDtypeStruct((per * TOK, D), F32),
            half_shape,
            half_shape,
            jax.ShapeDtypeStruct((1, D), F32),
            half_shape,
        ],
        scratch_shapes=[
            pltpu.VMEM((ways, shard * TOK, D), BF),
            pltpu.VMEM((ways, 2, shard, G, GL), F32),
            pltpu.VMEM((ways, per * TOK, D), BF),
            pltpu.VMEM((ways - 1, per * TOK, D), BF),
            pltpu.VMEM((D, D), F32),
            pltpu.VMEM((D, D), F32),
            pltpu.VMEM((2, chips, 2, vec, D), BF),
            pltpu.VMEM((2,) + half, BF),
            pltpu.VMEM(half, BF),
            pltpu.VMEM(half, BF),
            *line[:4],
            dma((3,)),
            dma((ways,)),
            dma((ways,)),
            dma((3,)),
            dma((3,)),
        ],
        compiler_params=pltpu.CompilerParams(
            vmem_limit_bytes=VMEM_BYTES, collective_id=cid, has_side_effects=True
        ),
        cost_estimate=pl.CostEstimate(
            flops=4 * rows * padded * D * D + 10 * rows * padded * GL * D,
            bytes_accessed=10 * rows * padded * D,
            transcendentals=rows * padded * G * GL,
        ),
    )(used, keys, values, queries, keep, memory_rows, dctx, stats, co_blocks)


def table_words(table, start, count):
    if table.shape[0] == 1:
        return table[0, pl.ds(start, count), :]
    return jnp.concatenate([table[i, pl.ds(start, count), :] for i in range(table.shape[0])], axis=-1)


def table_load(table_refs, table, sems, tile, c, t):
    tiles = table.shape[1] // tile
    places = [(ref, j * tile) for ref in table_refs for j in range(ref.shape[1] // tile)]

    def copy(k):
        ref, start = places[k]
        source = ref.at[:, pl.ds(start, tile), :]
        return pltpu.make_async_copy(source, table.at[:, pl.ds(k * tile, tile), :], sems.at[k])

    @pl.when((c == 0) & (t == 0))
    def _():
        for k in range(tiles):
            copy(k).start()

    for k in range(tiles):

        @pl.when((c == 0) & (t == k))
        def _(k=k):
            copy(k).wait()


def vocab_kernel(
    ways, tile, sub, chunk, count, h_ref, target_ref, *refs
):
    table_refs, refs = refs[:count], refs[count:]
    vocab_steps(ways, tile, sub, chunk, table_refs, h_ref, target_ref, *refs)


def vocab_steps(
    ways, tile, sub, chunk, table_refs, h_ref, target_ref, exp_ref, tops_ref, stats_ref,
    table, held, run, stats, table_sem, left_send, left_recv, right_send, right_recv, own,
    stat_send, stat_recv, stat_own,
):
    c, t = pl.program_id(0), pl.program_id(1)
    last = pl.num_programs(1) - 1
    mp = lax.axis_index(MP)
    slot = nearest(c, ways)[0]
    line = LineGather(
        [(h_ref, held)], (left_send, left_recv, right_send, right_recv, own), ways
    )

    def stats_copy(off):
        return z_copy(
            stats,
            stats_ref.at[mp],
            stat_send.at[off - 1],
            stat_recv.at[off - 1],
            lax.rem(mp + off, ways),
        )

    @pl.when((c == 0) & (t == 0))
    def _():
        z_meet(ways)
        line.begin()

    line.arrive(c, t == 0)
    table_load(table_refs, table, table_sem, tile, c, t)

    @pl.when(t == 0)
    def _():
        run[0:1, :] = jnp.full((1, chunk), NEG, F32)
        run[1:3, :] = jnp.zeros((2, chunk), F32)

    tokens = held[slot]
    target = target_ref[slot]
    parts = []
    for i in range(tile // sub):
        start = t * tile + i * sub
        logits = product_back(table_words(table, start, sub), tokens)
        top = jnp.max(logits, axis=0, keepdims=True)
        exponent = jnp.exp(logits - top)
        word = lax.broadcasted_iota(jnp.int32, (sub, chunk), 0) + start
        hit = jnp.where(word == target, logits, 0.0)
        exp_ref[0, i * sub : (i + 1) * sub, :] = exponent.astype(BF)
        tops_ref[0, pl.ds(t * (tile // sub) + i, 1), :] = top
        parts.append(
            (top, jnp.sum(exponent, axis=0, keepdims=True), jnp.sum(hit, axis=0, keepdims=True))
        )
    former = run[0:1, :]
    peak = former
    for top, total, hit in parts:
        peak = jnp.maximum(peak, top)
    sums = run[1:2, :] * jnp.exp(former - peak)
    hits = run[2:3, :]
    for top, total, hit in parts:
        sums += total * jnp.exp(top - peak)
        hits += hit
    run[0:1, :] = peak
    run[1:2, :] = sums
    run[2:3, :] = hits

    @pl.when(t == last)
    def _():
        stats[slot] = run[...]

    @pl.when((c == ways - 1) & (t == last))
    def _():
        for off in range(1, ways):
            stats_copy(off).start()
        local = pltpu.make_async_copy(stats, stats_ref.at[mp], stat_own.at[0])
        local.start()
        line.finish()
        for off in range(1, ways):
            stats_copy(off).wait()
        local.wait()


def vocab_sizes(words):
    tile = 1280 if words % 1280 == 0 else words
    sub = 256 if tile % 256 == 0 else tile
    return tile, sub


def vocab_forward(hidden, target, tables, cid):
    ways = lax.axis_size(MP)
    chunk = hidden.shape[0]
    parts, _, width = tables[0].shape
    words = sum(a.shape[1] for a in tables)
    tile, sub = vocab_sizes(words)
    tiles = words // tile
    top_rows = -(-(words // sub) // 8) * 8
    dma = pltpu.SemaphoreType.DMA
    return pl.pallas_call(
        functools.partial(vocab_kernel, ways, tile, sub, chunk, len(tables)),
        grid=(ways, tiles),
        in_specs=[
            pl.BlockSpec(memory_space=pl.ANY),
            pl.BlockSpec((ways, 1, chunk), lambda c, t: (0, 0, 0)),
            *[pl.BlockSpec(memory_space=pl.ANY)] * len(tables),
        ],
        out_specs=[
            pl.BlockSpec((1, tile, chunk), lambda c, t: (c, t, 0)),
            pl.BlockSpec((1, top_rows, chunk), lambda c, t: (c, 0, 0)),
            pl.BlockSpec(memory_space=pl.ANY),
        ],
        out_shape=[
            jax.ShapeDtypeStruct((ways, words, chunk), BF),
            jax.ShapeDtypeStruct((ways, top_rows, chunk), F32),
            jax.ShapeDtypeStruct((ways, ways, 8, chunk), F32),
        ],
        scratch_shapes=[
            pltpu.VMEM((parts, words, width), BF),
            pltpu.VMEM((ways, chunk, D), BF),
            pltpu.VMEM((8, chunk), F32),
            pltpu.VMEM((ways, 8, chunk), F32),
            dma((tiles,)),
            *line_sems(1, ways),
            dma((ways,)),
            dma((ways,)),
            dma((1,)),
        ],
        compiler_params=pltpu.CompilerParams(
            vmem_limit_bytes=VMEM_BYTES, collective_id=cid, has_side_effects=True
        ),
        cost_estimate=pl.CostEstimate(
            flops=2 * ways * chunk * words * D,
            bytes_accessed=2 * ways * words * D,
            transcendentals=ways * chunk * words,
        ),
    )(hidden, target, *tables)


def vocab_back_kernel(
    ways, tile, sub, chunk, count, exp_ref, tops_ref, target_ref, norm_ref, rate_ref, *refs
):
    table_refs, refs = refs[:count], refs[count:]
    vocab_back_steps(
        ways, tile, sub, chunk, table_refs, exp_ref, tops_ref, target_ref, norm_ref, rate_ref, *refs
    )


def vocab_back_steps(
    ways, tile, sub, chunk, table_refs, exp_ref, tops_ref, target_ref, norm_ref, rate_ref, out_ref,
    table, total, terms, leaving, landing, table_sem, send, recv,
):
    c, t = pl.program_id(0), pl.program_id(1)
    last = pl.num_programs(1) - 1
    mp = lax.axis_index(MP)
    slot = nearest(ways - 1 - c, ways)[0]

    def copy(to):
        right = to > mp
        spot = jnp.where(right | (to < mp - 1), to, ways)
        return z_copy(
            leaving.at[to],
            landing.at[spot],
            send.at[to],
            recv.at[spot],
            jnp.where(right, mp + 1, mp - 1),
        )

    def arrived(spot):
        z_copy(
            leaving.at[0], landing.at[spot], send.at[0], recv.at[spot], lax.rem(mp + 1, ways)
        ).wait_recv()

    @pl.when((c == 0) & (t == 0))
    def _():
        z_meet(ways)

    table_load(table_refs, table, table_sem, tile, c, t)
    target, norm, rate = target_ref[slot], norm_ref[slot], rate_ref[slot]
    term = None
    for i in range(tile // sub):
        start = t * tile + i * sub
        factor = jnp.exp(tops_ref[0, pl.ds(t * (tile // sub) + i, 1), :] - norm) * -rate
        word = lax.broadcasted_iota(jnp.int32, (sub, chunk), 0) + start
        hit = jnp.where(word == target, rate, 0.0)
        dlogits = hit + exp_ref[0, i * sub : (i + 1) * sub, :].astype(F32) * factor
        part = weight_grad(dlogits.astype(BF), table_words(table, start, sub))
        term = part if term is None else term + part

    @pl.when(t == 0)
    def _():
        total[...] = term

    @pl.when(t > 0)
    def _():
        total[...] += term

    for k in range(ways - 1):
        to = nearest(ways - 1 - k, ways)[0]
        beyond = jnp.where(to > mp, mp > 0, mp < ways - 1)

        @pl.when((c == k) & (t == last) & jnp.logical_not(beyond))
        def _(to=to):
            leaving[to] = total[...].astype(BF)
            copy(to).start()

        @pl.when((c == k) & (t == last) & beyond)
        def _(k=k):
            terms[k] = total[...]

    for k in range(ways - 1):
        to = nearest(ways - 1 - k, ways)[0]
        beyond = jnp.where(to > mp, mp > 0, mp < ways - 1)

        @pl.when((c == min(k + 2, ways - 1)) & (t == last) & beyond)
        def _(k=k, to=to):
            arrived(to)
            leaving[to] = (terms[k] + landing[to].astype(F32)).astype(BF)
            copy(to).start()

    @pl.when((c == ways - 1) & (t == last))
    def _():
        out_ref[...] = total[...]

        @pl.when(mp > 0)
        def _():
            arrived(mp)
            out_ref[...] += landing[mp].astype(F32)

        @pl.when(mp < ways - 1)
        def _():
            arrived(ways)
            out_ref[...] += landing[ways].astype(F32)

        for k in range(ways - 1):
            copy(nearest(ways - 1 - k, ways)[0]).wait_send()


def vocab_back(exponents, tops, target, norm, rate, tables, cid):
    ways, words, chunk = exponents.shape
    tile, sub = vocab_sizes(words)
    tiles = words // tile
    whole = pl.BlockSpec((ways, 1, chunk), lambda c, t: (0, 0, 0))
    dma = pltpu.SemaphoreType.DMA
    return pl.pallas_call(
        functools.partial(vocab_back_kernel, ways, tile, sub, chunk, len(tables)),
        grid=(ways, tiles),
        in_specs=[
            pl.BlockSpec((1, tile, chunk), lambda c, t: (ways - 1 - c, t, 0)),
            pl.BlockSpec((1, tops.shape[1], chunk), lambda c, t: (ways - 1 - c, 0, 0)),
            whole,
            whole,
            whole,
            *[pl.BlockSpec(memory_space=pl.ANY)] * len(tables),
        ],
        out_specs=pl.BlockSpec((chunk, D), lambda c, t: (0, 0)),
        out_shape=jax.ShapeDtypeStruct((chunk, D), F32),
        scratch_shapes=[
            pltpu.VMEM((tables[0].shape[0], words, tables[0].shape[2]), BF),
            pltpu.VMEM((chunk, D), F32),
            pltpu.VMEM((ways - 1, chunk, D), F32),
            pltpu.VMEM((ways, chunk, D), BF),
            pltpu.VMEM((ways + 1, chunk, D), BF),
            dma((tiles,)),
            dma((ways,)),
            dma((ways + 1,)),
        ],
        compiler_params=pltpu.CompilerParams(
            vmem_limit_bytes=VMEM_BYTES, collective_id=cid, has_side_effects=True
        ),
        cost_estimate=pl.CostEstimate(
            flops=2 * ways * chunk * words * D, bytes_accessed=2 * ways * words * D, transcendentals=0
        ),
    )(exponents, tops, target, norm, rate, *tables)


HIDDEN_TILE = 512
ROOT_HALF = 0.7071067811865476
ROOT_TAU = 0.3989422804014327


def weight_tile(ref):
    return ref[...].reshape(D, ref.shape[-1])


def feed_kernel(h_ref, expand_ref, bias_ref, shrink_ref, a_ref, out_ref):
    t = pl.program_id(0)
    hidden = product(h_ref[...], weight_tile(expand_ref)) + bias_ref[0]
    a_ref[...] = hidden
    active = (hidden * (0.5 + 0.5 * lax.erf(hidden * ROOT_HALF))).astype(BF)
    term = product_back(active, weight_tile(shrink_ref))

    @pl.when(t == 0)
    def _():
        out_ref[...] = term

    @pl.when(t > 0)
    def _():
        out_ref[...] += term


def feed_specs(weights):
    parts, ways, _, rows, units = weights.shape
    per = units // HIDDEN_TILE
    tile = lambda which: pl.BlockSpec(
        (parts, 1, 1, rows, HIDDEN_TILE), lambda t: (0, t // per, which, 0, t % per)
    )
    bias = pl.BlockSpec((1, 1, HIDDEN_TILE), lambda t: (t, 0, 0))
    return tile(0), bias, tile(1), ways * per


def feed_forward(hidden, weights, bias):
    tokens = hidden.shape[0]
    expand_spec, bias_spec, shrink_spec, tiles = feed_specs(weights)
    whole = pl.BlockSpec((tokens, D), lambda t: (0, 0))
    units = tiles * HIDDEN_TILE
    return pl.pallas_call(
        feed_kernel,
        grid=(tiles,),
        in_specs=[whole, expand_spec, bias_spec, shrink_spec],
        out_specs=[pl.BlockSpec((tokens, HIDDEN_TILE), lambda t: (0, t)), whole],
        out_shape=[
            jax.ShapeDtypeStruct((tokens, units), F32),
            jax.ShapeDtypeStruct((tokens, D), F32),
        ],
        compiler_params=pltpu.CompilerParams(vmem_limit_bytes=VMEM_BYTES),
        cost_estimate=pl.CostEstimate(
            flops=4 * tokens * units * D, bytes_accessed=4 * units * D, transcendentals=tokens * units
        ),
    )(hidden, weights, bias.reshape(tiles, 1, HIDDEN_TILE), weights)


def feed_back_kernel(
    dout_ref, h_ref, a_ref, expand_ref, shrink_ref, dweights_ref, dbias_ref, dh_ref
):
    t = pl.program_id(0)
    dout = dout_ref[...]
    hidden = a_ref[...]
    below = 0.5 + 0.5 * lax.erf(hidden * ROOT_HALF)
    slope = below + hidden * (ROOT_TAU * jnp.exp(-0.5 * hidden * hidden))
    active = (hidden * below).astype(BF)
    dhidden = (slope * product(dout, weight_tile(shrink_ref))).astype(BF)
    dbias_ref[0] = jnp.sum(dhidden.astype(F32), axis=0, keepdims=True)
    parts, _, rows, width = dweights_ref.shape
    dweights_ref[:, 0] = weight_grad(h_ref[...], dhidden).astype(BF).reshape(parts, rows, width)
    dweights_ref[:, 1] = weight_grad(dout, active).astype(BF).reshape(parts, rows, width)
    term = product_back(dhidden, weight_tile(expand_ref))

    @pl.when(t == 0)
    def _():
        dh_ref[...] = term

    @pl.when(t > 0)
    def _():
        dh_ref[...] += term


def feed_back(dout, hidden, before, weights):
    tokens = hidden.shape[0]
    expand_spec, bias_spec, shrink_spec, tiles = feed_specs(weights)
    parts, rows = weights.shape[0], weights.shape[3]
    whole = pl.BlockSpec((tokens, D), lambda t: (0, 0))
    units = tiles * HIDDEN_TILE
    return pl.pallas_call(
        feed_back_kernel,
        grid=(tiles,),
        in_specs=[
            whole,
            whole,
            pl.BlockSpec((tokens, HIDDEN_TILE), lambda t: (0, t)),
            expand_spec,
            shrink_spec,
        ],
        out_specs=[
            pl.BlockSpec((parts, 2, rows, HIDDEN_TILE), lambda t: (0, 0, 0, t)),
            bias_spec,
            whole,
        ],
        out_shape=[
            jax.ShapeDtypeStruct((parts, 2, rows, units), BF),
            jax.ShapeDtypeStruct((tiles, 1, HIDDEN_TILE), F32),
            jax.ShapeDtypeStruct((tokens, D), F32),
        ],
        compiler_params=pltpu.CompilerParams(vmem_limit_bytes=VMEM_BYTES),
        cost_estimate=pl.CostEstimate(
            flops=8 * tokens * units * D, bytes_accessed=8 * units * D, transcendentals=2 * tokens * units
        ),
    )(dout, hidden, before, weights, weights)


def self_back_kernel(
    plan, x_ref, ctx_ref, q_ref, k_ref, v_ref, wo_ref, wqkv_ref, keep_ref, dfirst_ref, *refs
):
    n = plan.count
    sends, rest = refs[:n], refs[n:]
    bias_ref, dself_ref, dwo_ref, din_ref = rest[:4]
    lands, rest = rest[4 : 4 + n], rest[4 + n :]
    dctx, dqkv, part, part_got, din, dself, dself_got, dwo, dwo_got, dout, dout_all = rest[:11]
    send, recv, own = rest[11:14]
    plan.bind(sends, lands, rest[14:])
    ways = plan.mp_ways
    mp, parity = plan.mp, plan.parity

    def part_copy(off):
        to = plan.peer(Z, off)
        return z_copy(part.at[to], part_got.at[off - 1], send.at[0, off], recv.at[0, off], to)

    def din_copy(off):
        return z_copy(din, din_ref.at[mp], send.at[1, off], recv.at[1, off], plan.peer(Z, off))

    def core_copies():
        return [
            plan.remote(a.at[:, 1 - parity], b, send.at[2, i], recv.at[2, i], plan.device(PAIR, 1 - parity))
            for i, (a, b) in enumerate([(dself, dself_got), (dwo, dwo_got)])
        ]

    def dout_copy(off):
        return z_copy(dout, dout_all.at[mp], send.at[3, off], recv.at[3, off], plan.peer(Z, off))

    plan.meet((Z, PAIR))
    dout[...] = dfirst_ref[...].astype(BF)
    for off in range(1, ways):
        dout_copy(off).start()
    plan.start()
    dout_all[mp] = dout[...]
    keep = keep_ref[...]
    keep_wide = keep.astype(F32)
    for off in range(1, ways):
        dout_copy(off).wait()
    upstreams = dout_all[...].reshape(x_ref.shape)
    dctx[...] = product_back(upstreams, wo_ref[...]).astype(BF)
    key_place = lax.broadcasted_iota(jnp.int32, (TOK, GL), 0)
    query_place = lax.rem(lax.broadcasted_iota(jnp.int32, (TOK, GL), 1), TOK)
    seen = key_place <= query_place

    @pl.loop(0, x_ref.shape[0] // TOK)
    def _(question):
        rows = pl.ds(pl.multiple_of(question * TOK, TOK), TOK)
        keys, values = k_ref[rows, :], v_ref[rows, :]
        query = jnp.concatenate([q_ref[rows, :]] * GH, axis=0) * keep
        upstream = jnp.concatenate([dctx[rows, :]] * GH, axis=0) * keep
        scores = jnp.where(seen, product_back(keys, query), NEG)
        exponent = jnp.exp(scores - jnp.max(scores, axis=0, keepdims=True))
        probs = exponent / jnp.sum(exponent, axis=0, keepdims=True)
        dprobs = product_back(values, upstream)
        middle = jnp.sum(probs * dprobs, axis=0, keepdims=True)
        dscores = (probs * (dprobs - middle)).astype(BF)
        dquery = own_heads(weight_grad(dscores, keys), keep_wide)
        dqkv[rows, 0:GC] = (dquery * SCALE).astype(BF)
        dqkv[rows, GC : 2 * GC] = product(dscores, query).astype(BF)
        dqkv[rows, 2 * GC : 3 * GC] = product(probs.astype(BF), upstream).astype(BF)

    grads = dqkv[...]
    part[...] = product_back(grads, wqkv_ref[...]).astype(BF).reshape(part.shape)
    for off in range(1, ways):
        part_copy(off).start()
    dself[...] = weight_grad(x_ref[...], grads).astype(BF).reshape(dself.shape)
    dwo[...] = weight_grad(upstreams, ctx_ref[...]).astype(BF).reshape(dwo.shape)
    for copy in core_copies():
        copy.start()
    bias_ref[...] = jnp.sum(grads.astype(F32), axis=0, keepdims=True)
    total = dfirst_ref[...] + part[mp].astype(F32)
    for off in range(1, ways):
        part_copy(off).wait_recv()
        total += part_got[off - 1].astype(F32)
    din[...] = total.astype(BF)
    for off in range(1, ways):
        din_copy(off).start()
    local = pltpu.make_async_copy(din, din_ref.at[mp], own.at[0])
    local.start()
    for copy in core_copies():
        copy.wait()
    dself_ref[...] = (dself[:, parity].astype(F32) + dself_got[...].astype(F32)).astype(BF)
    dwo_ref[...] = (dwo[:, parity].astype(F32) + dwo_got[...].astype(F32)).astype(BF)
    plan.finish()
    for off in range(1, ways):
        part_copy(off).wait_send()
        din_copy(off).wait()
    local.wait()


def self_back(x, ctx, queries, keys, values, wo, wqkv, keep, dfirst, plan, cid):
    uniq, shard = x.shape[0], dfirst.shape[0]
    ways, chips = plan.mp_ways, plan.chips
    vec = D // plan.dp_ways
    inputs = [x, ctx, queries, keys, values, wo, wqkv, keep, dfirst]
    vmem = pl.BlockSpec(memory_space=pltpu.VMEM)
    dma = pltpu.SemaphoreType.DMA
    cols = wqkv.shape[1]
    return pl.pallas_call(
        functools.partial(self_back_kernel, plan),
        in_specs=[vmem] * len(inputs) + plan.specs,
        out_specs=[vmem, vmem, vmem, pl.BlockSpec(memory_space=pl.ANY)] + plan.specs,
        out_shape=[
            jax.ShapeDtypeStruct((1, cols), F32),
            jax.ShapeDtypeStruct((chips, vec, cols), BF),
            jax.ShapeDtypeStruct((chips, vec, GC), BF),
            jax.ShapeDtypeStruct((ways, shard, D), BF),
        ]
        + plan.shapes,
        scratch_shapes=[
            pltpu.VMEM((uniq, GC), BF),
            pltpu.VMEM((uniq, cols), BF),
            pltpu.VMEM((ways, shard, D), BF),
            pltpu.VMEM((ways - 1, shard, D), BF),
            pltpu.VMEM((shard, D), BF),
            pltpu.VMEM((chips, 2, vec, cols), BF),
            pltpu.VMEM((chips, vec, cols), BF),
            pltpu.VMEM((chips, 2, vec, GC), BF),
            pltpu.VMEM((chips, vec, GC), BF),
            pltpu.VMEM((shard, D), BF),
            pltpu.VMEM((ways, shard, D), BF),
            dma((4, ways)),
            dma((4, ways)),
            dma((1,)),
            *plan.scratch,
        ],
        compiler_params=pltpu.CompilerParams(
            vmem_limit_bytes=VMEM_BYTES, collective_id=cid, has_side_effects=True
        ),
        cost_estimate=pl.CostEstimate(
            flops=4 * uniq * D * cols, bytes_accessed=8 * uniq * D, transcendentals=uniq * GL
        ),
    )(*inputs, *plan.arrays)


def self_probs(queries, key_heads):
    causal = (
        lax.broadcasted_iota(jnp.int32, (TOK, TOK), 1)
        <= lax.broadcasted_iota(jnp.int32, (TOK, TOK), 0)
    )[None, None]
    scores = jnp.einsum("rqhe,rkhe->rhqk", queries, key_heads, preferred_element_type=F32)
    return jax.nn.softmax(jnp.where(causal, scores, NEG), axis=-1)


def column_parts(gathered):
    return jnp.concatenate([gathered[i] for i in range(gathered.shape[0])], axis=-1)


def block_rows(array, ways):
    rows, columns = array.shape
    width = columns // ways
    return jnp.stack([array[:, i * width : (i + 1) * width] for i in range(ways)])


def local(
    answers,
    targets,
    doc_scores,
    memory,
    lengths,
    self_query,
    self_key,
    self_value,
    query_bias,
    value_bias,
    self_output,
    output_bias,
    first_gain,
    first_shift,
    cross_query,
    crossq_bias,
    cross_key,
    cross_value,
    crossv_bias,
    cross_output,
    crosso_bias,
    second_gain,
    second_shift,
    expand_weight,
    expand_bias,
    shrink_weight,
    shrink_bias,
    third_gain,
    third_shift,
    word_table,
):
    dp_ways, mp_ways = lax.axis_size(DP), lax.axis_size(MP)
    chips = dp_ways // 2
    dp, mp = lax.axis_index(DP), lax.axis_index(MP)
    groups = answers.shape[0]
    rows, slots, _ = memory.shape
    piece = rows // dp_ways
    own_q = dp_ways
    uniq = own_q * TOK
    tokens = rows * TOK
    padded = -(-slots // 16) * 16
    shard_rows = rows // mp_ways
    shard_tokens = shard_rows * TOK
    shard_q = own_q // mp_ways
    shard_uniq = shard_q * TOK
    local_heads = H // mp_ways
    head_cols = local_heads * HD
    hidden_cols = expand_weight.shape[1]
    vec = D // dp_ways

    vectors = (
        output_bias,
        first_gain,
        first_shift,
        crosso_bias,
        second_gain,
        second_shift,
        shrink_bias,
        third_gain,
        third_shift,
        crossv_bias,
    )
    matrices = (query_bias, value_bias, crossq_bias, expand_bias)
    starts, top = [], 16
    for matrix in matrices:
        starts.append(top)
        top += -(-matrix.shape[0] // 8) * 8
    small_rows = -(-top // 16) * 16
    row_of = lax.broadcasted_iota(jnp.int32, (small_rows, 128), 0)
    small = jnp.zeros((small_rows, 128), BF)
    for i, vector in enumerate(vectors):
        vector = jnp.pad(vector, (0, 128 - vector.shape[0]))
        small = jnp.where(row_of == i, vector[None, :], small)
    for start, matrix in zip(starts, matrices):
        count, width = matrix.shape
        small += jnp.pad(matrix, ((start, small_rows - start - count), (0, 128 - width)))
    wide_rows = cross_key.shape[0]
    self_shard = jnp.concatenate([self_query, self_key, self_value], axis=1)
    target_rows = jnp.pad(targets, ((0, 8 - groups), (0, 128 - TOK)))
    doc_rows = jnp.pad(doc_scores, ((0, 8 - groups), (0, 128 - K)))
    if chips == groups:
        wanted = answers
    else:
        wanted = jnp.stack([answers[(2 * c * piece) // K] for c in range(chips)])
    feed_shard = jnp.stack([expand_weight, shrink_weight.T])
    key_all, value_all, small_all, cquery_z, cout_z = exchange(
        [
            (cross_key, WIDE, Z),
            (cross_value, WIDE, Z),
            (small, WIDE, Z),
            (cross_query, LATE, Z),
            (cross_output, LATE, Z),
        ],
        0,
    )
    (full_obias, gain_one, shift_one, full_cobias, gain_two, shift_two, full_sbias, gain_three, shift_three) = [
        small_all[:, 0, i, :vec].reshape(D) for i in range(9)
    ]
    cvbias = small_all[:, :, 9, :wide_rows].reshape(1, D)

    def head_bias(i):
        count, width = matrices[i].shape
        part = small_all[:, :, starts[i] : starts[i] + count, :width]
        return jnp.transpose(part, (1, 2, 0, 3)).reshape(mp_ways, -1)

    mine = lambda a: lax.dynamic_index_in_dim(a, mp, 0, keepdims=False)
    qbias = mine(head_bias(0))
    vbias = mine(head_bias(1))
    cqbias = head_bias(2).reshape(-1)
    ebias = head_bias(3).reshape(-1)
    key_weight = key_all.reshape(D, D)
    value_weight = value_all.reshape(D, D)

    plan = Exchange(
        [
            (feed_shard, GATHER, Z),
            (self_shard, NEAR, Z),
            (self_output, NEAR, Z),
            (target_rows, NEAR, Z),
            (doc_rows, NEAR, Z),
            (wanted, NEARSWAP, Z),
            (cquery_z, NEAR, Z),
            (cout_z, NEAR, Z),
        ]
    )
    (keys, values, memory_rows, feed_z, self_all, output_all, target_all, doc_all, x_all, cquery_all, cout_all) = (
        memory_products(memory, key_weight, value_weight, cvbias, padded, plan, 1)
    )
    words = word_table.shape[0]
    early = words // 1280 * 3 // 5 * 1280 if words % 1280 == 0 else 0
    tables = []
    if early:
        part = lax.all_gather(word_table[:early], DP, axis=0, tiled=False)
        feed_z, part = lax.optimization_barrier((feed_z, part))
        tables.append(part)
    feed_all = lax.all_gather(feed_z, DP, axis=0, tiled=False)
    tables.append(lax.all_gather(word_table[early:], DP, axis=0, tiled=False))
    if word_table.shape[1] < 128:
        tables = [column_parts(a)[None] for a in tables]
    rows_first = lambda a: jnp.transpose(a, (0, 2, 1, 3)).reshape(dp_ways * a.shape[2], -1)
    columns_first = lambda a: column_parts(a.reshape(dp_ways, -1, a.shape[-1]))
    self_weight = self_all.reshape(D, 3 * head_cols)
    full_output = column_parts(output_all)
    my_group = (dp * piece) // K
    row_targets = lax.dynamic_index_in_dim(
        target_all[:, :groups, :TOK], my_group, 1, keepdims=False
    )
    x_rows = x_all.reshape(uniq, D)

    qkv = product(x_rows, self_weight)
    queries = ((qkv[:, :head_cols] + qbias) * SCALE).astype(BF)
    self_keys = qkv[:, head_cols : 2 * head_cols].astype(BF)
    self_values = (qkv[:, 2 * head_cols :] + vbias).astype(BF)
    heads = lambda a: a.reshape(own_q, TOK, local_heads, HD)
    probs = self_probs(heads(queries), heads(self_keys))
    context = jnp.einsum(
        "rhqk,rkhe->rqhe", probs.astype(BF), heads(self_values), preferred_element_type=F32
    )
    context = context.astype(BF).reshape(uniq, head_cols)
    partial = product(context, full_output).astype(BF).reshape(mp_ways, shard_uniq, D)
    (received,) = exchange([(partial, MOVE, Z)], 2)
    full_cquery = rows_first(cquery_all)
    x_own = lax.dynamic_slice_in_dim(x_rows, mp * shard_uniq, shard_uniq, 0)
    first_in = x_own.astype(F32) + added(partial, received, Z) + full_obias
    hidden_one, normed_one, inverse_one = layer_norm(first_in, gain_one, shift_one)
    hidden_low1 = hidden_one.astype(BF)
    cross_queries = ((product(hidden_low1, full_cquery) + cqbias) * SCALE).astype(BF)
    (cross_queries,) = exchange([(cross_queries, GATHER, Z)], 3)
    full_cout = columns_first(cout_all)
    cross_queries = cross_queries.reshape(uniq, D)

    used = jnp.clip(lengths - mp * slots, 0, slots).astype(jnp.int32)
    used = jnp.broadcast_to(used[:, None, None], (rows, 1, GL))
    keep = (
        lax.broadcasted_iota(jnp.int32, (GL, GC), 0) // TOK
        == lax.broadcasted_iota(jnp.int32, (GL, GC), 1) // HD
    ).astype(BF)
    ctx_own, stat_own, ctx_got, stat_got = cross_forward(
        used, keys, values, cross_queries, keep, piece, padded, 4
    )
    stat_got = jnp.concatenate([stat_own[None], stat_got], axis=0)
    peak_got, total_got = stat_got[:, 0], stat_got[:, 1]
    peak = jnp.max(peak_got, axis=0)
    weight = total_got * jnp.exp(peak_got - peak)
    total = jnp.sum(weight, axis=0)
    cross_norm = peak + jnp.log(total)
    weight = weight / total

    def to_token_heads(a):
        lead = a.shape[:-3]
        a = a.reshape(lead + (shard_rows, H, TOK))
        return jnp.swapaxes(a, -1, -2).reshape(lead + (shard_tokens, H))

    weight = jnp.repeat(to_token_heads(weight), HD, axis=-1)
    context_two = (
        ctx_own.astype(F32) * weight[0] + jnp.sum(ctx_got.astype(F32) * weight[1:], axis=0)
    ).astype(BF)

    def to_rows(a):
        a = jnp.broadcast_to(a.reshape(shard_q, 1, TOK, D), (shard_q, piece, TOK, D))
        return a.reshape(shard_tokens, D)

    second_in = to_rows(hidden_one) + product(context_two, full_cout) + full_cobias
    hidden_two, normed_two, inverse_two = layer_norm(second_in, gain_two, shift_two)
    hidden_low2 = hidden_two.astype(BF)

    expanded, third_in = feed_forward(hidden_low2, feed_all, ebias)
    third_in = hidden_two + third_in + full_sbias
    hidden_three, normed_three, inverse_three = layer_norm(third_in, gain_three, shift_three)

    vocab_local = words
    token_targets = jnp.broadcast_to(row_targets.reshape(own_q, 1, TOK), (own_q, piece, TOK))
    local_target = token_targets.reshape(mp_ways, 1, shard_tokens) - mp * vocab_local
    exponents, tops, stats = vocab_forward(hidden_three.astype(BF), local_target, tables, 5)
    stats = jnp.transpose(stats[:, :, :3], (0, 2, 1, 3)).reshape(mp_ways, 3, tokens)
    top = jnp.max(stats[:, 0], axis=0)
    norm_log = top + jnp.log(jnp.sum(stats[:, 1] * jnp.exp(stats[:, 0] - top), axis=0))
    loglik = jnp.sum(stats[:, 2], axis=0) - norm_log
    (loglik_all,) = exchange([(loglik.reshape(tokens // 128, 128), GATHER, DP)], 7)
    loglik_all = loglik_all.reshape(dp_ways, own_q, piece, TOK)
    loglik_all = jnp.transpose(loglik_all, (1, 0, 2, 3)).reshape(own_q, groups, K, TOK)
    doc_logp = jax.nn.log_softmax(doc_all[:, :groups, :K], axis=2)
    joined = doc_logp[..., None] + loglik_all
    marginal = jax.nn.logsumexp(joined, axis=2, keepdims=True)
    question_loss = -jnp.mean(
        lax.dynamic_index_in_dim(marginal[:, :, 0], dp, 0, keepdims=False), axis=1
    )
    posterior = jnp.exp(joined - marginal).reshape(own_q, groups * K, TOK)
    rate = -lax.dynamic_slice_in_dim(posterior, dp * piece, piece, 1)
    by_slot = lambda a: a.reshape(mp_ways, 1, shard_tokens)
    dhidden_three = vocab_back(
        exponents, tops, local_target, by_slot(norm_log), by_slot(rate), tables, 8
    )

    dthird, dgain_three, dshift_three = norm_back(
        dhidden_three, normed_three, inverse_three, gain_three
    )
    dshrink_bias = jnp.sum(dthird, axis=0)
    dshrink_in = dthird.astype(BF)
    dfeed, dexpand_bias, dhidden_two = feed_back(dshrink_in, hidden_low2, expanded, feed_all)
    dexpand_bias = dexpand_bias.reshape(-1)
    feed_dp = lax.psum_scatter(dfeed, DP, scatter_dimension=0, tiled=False)
    dhidden_two = dthird + dhidden_two

    dsecond, dgain_two, dshift_two = norm_back(dhidden_two, normed_two, inverse_two, gain_two)
    dcout_bias = jnp.sum(dsecond, axis=0)
    dcout_in = dsecond.astype(BF)
    dcontext_two = product_back(dcout_in, full_cout).astype(BF)
    middle = jnp.sum(
        (dcontext_two.astype(F32) * context_two.astype(F32)).reshape(shard_tokens, H, HD), axis=-1
    )
    middle = jnp.swapaxes(middle.reshape(shard_rows, TOK, H), 1, 2).reshape(shard_rows, G, GL)
    owners = lambda a: a.reshape(chips, 2, -1, a.shape[-1])
    cast = lambda a: a.astype(BF)
    co_blocks = owners(cast(weight_grad(dcout_in, context_two)))
    stat_all = jnp.stack([cross_norm, middle])
    dkeys, dvalues, dcross_q, key_blocks, value_blocks, dvalue_bias, co_blocks = cross_back(
        used, keys, values, cross_queries, memory_rows, dcontext_two, stat_all, co_blocks, keep, piece,
        padded, 9,
    )
    dcross_low = (dcross_q * SCALE).astype(BF)
    dcquery = weight_grad(hidden_low1, dcross_low)
    dcq_bias = jnp.sum(dcross_low, axis=0, dtype=F32)
    dhidden_one = jnp.sum(dsecond.reshape(shard_q, piece, TOK, D), axis=1).reshape(
        shard_uniq, D
    ) + product_back(dcross_low, full_cquery)

    dfirst, dgain_one, dshift_one = norm_back(dhidden_one, normed_one, inverse_one, gain_one)
    dout_bias = jnp.sum(dfirst, axis=0)
    cq_blocks = owners(cast(dcquery))
    plan = Exchange(
        [(cq_blocks, MOVE1, PAIR), (co_blocks, MOVE, CHIPS)]
    )
    dqkv_bias, self_blocks, out_blocks, dinputs, cq_got, co_got = self_back(
        x_rows, context, queries, self_keys, self_values, full_output, self_weight, keep, dfirst, plan, 12
    )
    dqkv_bias = dqkv_bias[0]
    (cq_blocks,) = sums([(cq_blocks, cq_got, MOVE1, PAIR, PLAIN, BF)])

    vectors = jnp.stack(
        [
            dout_bias,
            dgain_one,
            dshift_one,
            dcout_bias,
            dgain_two,
            dshift_two,
            dshrink_bias,
            dgain_three,
            dshift_three,
            dvalue_bias[0],
            dcq_bias,
            jnp.pad(dqkv_bias, (0, D - 3 * head_cols)),
        ]
    )
    vectors = jnp.concatenate([vectors, dexpand_bias.reshape(-1, D)], axis=0)
    answer_blocks = dinputs.reshape(chips, 2, TOK, D)
    plan = Exchange(
        [(feed_dp, COLS, Z)]
        + [
            (a, MOVE, CHIPS)
            for a in (key_blocks, value_blocks, cq_blocks, answer_blocks)
        ]
        + [(vectors, GATHER, DP)]
    )
    memory_grad, received = memory_back(
        dkeys, dvalues, key_weight, value_weight, rows, slots, padded, plan, 15
    )
    feed_got, key_got, value_got, cq_got, answer_got, vector_all = received
    key_sum, value_sum, cq_sum, co_sum, feed_grad, vector_sum = sums(
        [
            (key_blocks, key_got, MOVE, CHIPS, PLAIN, BF),
            (value_blocks, value_got, MOVE, CHIPS, PLAIN, BF),
            (cq_blocks, cq_got, MOVE, CHIPS, COLUMNS, BF),
            (co_blocks, co_got, MOVE, CHIPS, COLUMNS, BF),
            (feed_dp, feed_got, COLS, Z, PLAIN, F32),
            (vector_all, vector_all, GATHER, DP, PLAIN, F32),
        ]
    )

    expand_grad, shrink_grad = feed_grad[0], feed_grad[1].T

    own_answers = lax.dynamic_index_in_dim(answer_blocks, dp // 2, 0, keepdims=True)
    returned = jnp.concatenate([own_answers, answer_got], axis=0).astype(F32)
    source = lax.rem(dp // 2 + chips - jnp.arange(chips), chips)
    place = (2 * source * piece) // K
    pick = (place[None, :] == jnp.arange(groups)[:, None]).astype(F32)
    answer_part = cast(jnp.sum(pick[:, :, None, None, None] * returned[None], axis=1))

    zblocks = [
        key_sum.reshape(mp_ways, wide_rows, D),
        value_sum.reshape(mp_ways, wide_rows, D),
        cq_sum,
        co_sum,
    ]
    feature_part = lax.dynamic_slice_in_dim(vector_sum[:10], dp * vec, vec, 1)
    *got_z, feature_all, head_all, answer_got, self_got, out_got = exchange(
        [(a, MOVE, Z) for a in zblocks]
        + [(feature_part, GATHER, Z), (vector_sum[10:], GATHER, Z)]
        + [(answer_part, MOVE1, PAIR), (self_blocks, MOVE, CHIPS), (out_blocks, MOVE, CHIPS)],
        16,
    )
    forms = [PLAIN, PLAIN, PLAIN, TURNED]
    key_grad, value_grad, cquery_grad, cout_grad, answer_grad, self_grad, out_grad = sums(
        [(a, b, MOVE, Z, form, F32) for a, b, form in zip(zblocks, got_z, forms)]
        + [
            (answer_part, answer_got, MOVE1, PAIR, PLAIN, F32),
            (self_blocks, self_got, MOVE, CHIPS, PLAIN, F32),
            (out_blocks, out_got, MOVE, CHIPS, TURNED, F32),
        ]
    )
    feature_own = jnp.sum(feature_all, axis=0)
    head_sums = jnp.sum(head_all, axis=0)
    head_own = lax.dynamic_index_in_dim(head_all, mp, 0, keepdims=False)[1]

    def vec_of(i):
        return feature_own[i]

    def of_dp(a, shape):
        a = a.reshape(-1, dp_ways, shape[1])
        return lax.dynamic_index_in_dim(a, dp, 1, keepdims=False)

    def of_mp(a, shape):
        return lax.dynamic_slice_in_dim(of_dp(a.reshape(-1), shape), mp * shape[0], shape[0], 0)

    return (
        question_loss,
        answer_grad,
        memory_grad,
        self_grad[:, :head_cols],
        self_grad[:, head_cols : 2 * head_cols],
        self_grad[:, 2 * head_cols :],
        of_dp(head_own[:head_cols], query_bias.shape),
        of_dp(head_own[2 * head_cols : 3 * head_cols], value_bias.shape),
        out_grad,
        vec_of(0),
        vec_of(1),
        vec_of(2),
        cquery_grad,
        of_mp(head_sums[0], crossq_bias.shape),
        key_grad,
        value_grad,
        lax.dynamic_slice_in_dim(vec_of(9), mp * wide_rows, wide_rows, 0),
        cout_grad,
        vec_of(3),
        vec_of(4),
        vec_of(5),
        expand_grad,
        of_mp(head_sums[2:], expand_bias.shape),
        shrink_grad,
        vec_of(6),
        vec_of(7),
        vec_of(8),
    )


def solution(mesh):
    placed = (
        P(DP, None, None),
        P(DP, None),
        P(DP, None),
        P(DP, MP, None),
        P(DP),
        P(DP, MP),
        P(DP, MP),
        P(DP, MP),
        P(MP, DP),
        P(MP, DP),
        P(MP, DP),
        P(DP),
        P(DP),
        P(DP),
        P(DP, MP),
        P(MP, DP),
        P((DP, MP), None),
        P((DP, MP), None),
        P((DP, MP)),
        P(MP, DP),
        P(DP),
        P(DP),
        P(DP),
        P(DP, MP),
        P(MP, DP),
        P(MP, DP),
        P(DP),
        P(DP),
        P(DP),
        P(MP, DP),
    )
    return jax.shard_map(
        local,
        mesh=mesh,
        in_specs=placed,
        out_specs=(
            P(DP),
            P(DP, None, None),
            P(DP, MP, None),
            P(DP, MP),
            P(DP, MP),
            P(DP, MP),
            P(MP, DP),
            P(MP, DP),
            P(MP, DP),
            P(DP),
            P(DP),
            P(DP),
            P(DP, MP),
            P(MP, DP),
            P((DP, MP), None),
            P((DP, MP), None),
            P((DP, MP)),
            P(MP, DP),
            P(DP),
            P(DP),
            P(DP),
            P(DP, MP),
            P(MP, DP),
            P(MP, DP),
            P(DP),
            P(DP),
            P(DP),
        ),
        check_vma=False,
    )
```

```python
import functools

import jax
import jax.numpy as jnp
from jax import lax
from jax.experimental import pallas as pl
from jax.experimental.pallas import tpu as pltpu
from jax.sharding import PartitionSpec as P

D = 1024
H = 16
HD = 64
TOK = 32
K = 8
G = 4
GH = 4
GC = GH * HD
GL = GH * TOK

EPS = 1e-05
NEG = -1e30
SCALE = 0.125
BF = jnp.bfloat16
F32 = jnp.float32
MESH = pl.DeviceIdType.MESH
DP, MP = "dp", "mp"
GATHER, LATE, MOVE, MOVE1, COLS, NEAR, NEARSWAP, WIDE = range(8)
Z, CHIPS, PAIR = range(3)
PLAIN, COLUMNS, TURNED = range(3)
VMEM_BYTES = 60 * 1024 * 1024


def product(former, latter):
    return jnp.dot(former, latter, preferred_element_type=F32)


def product_back(former, latter):
    return lax.dot_general(former, latter, (((1,), (1,)), ((), ())), preferred_element_type=F32)


def weight_grad(former, latter):
    return lax.dot_general(former, latter, (((0,), (0,)), ((), ())), preferred_element_type=F32)


def layer_norm(entries, norm_gain, norm_shift):
    center = entries - jnp.mean(entries, axis=-1, keepdims=True)
    inverse = lax.rsqrt(jnp.mean(center * center, axis=-1, keepdims=True) + EPS)
    normed = center * inverse
    return (normed * norm_gain + norm_shift, normed, inverse)


def norm_back(upstream, normed, inverse, norm_gain):
    scaled = upstream * norm_gain
    dentries = inverse * (
        scaled
        - jnp.mean(scaled, axis=-1, keepdims=True)
        - normed * jnp.mean(scaled * normed, axis=-1, keepdims=True)
    )
    return (dentries, jnp.sum(upstream * normed, axis=0), jnp.sum(upstream, axis=0))


class Exchange:
    def __init__(self, entries):
        self.dp_ways, self.mp_ways = lax.axis_size(DP), lax.axis_size(MP)
        self.chips = self.dp_ways // 2
        self.ways = {Z: self.mp_ways, CHIPS: self.chips, PAIR: 2, DP: self.dp_ways}
        self.arrays = [entry[0] for entry in entries]
        self.kinds = [entry[1] for entry in entries]
        self.groups = [entry[2] for entry in entries]
        self.count = len(entries)
        shapes = []
        for array, kind, group in entries:
            shape = array.shape
            if kind in (GATHER, LATE):
                shape = (self.ways[group],) + shape
            elif kind == MOVE:
                shape = (self.ways[group] - 1,) + shape[1:]
            elif kind == MOVE1:
                shape = (self.ways[group] - 1, shape[0]) + shape[2:]
            elif kind == COLS:
                shape = (self.ways[group] - 1,) + shape[:-1] + (shape[-1] // self.ways[group],)
            elif kind == NEAR:
                shape = (self.dp_ways,) + shape
            elif kind == NEARSWAP:
                shape = (self.dp_ways,) + shape[1:]
            else:
                shape = (self.dp_ways, self.mp_ways) + shape
            shapes.append(jax.ShapeDtypeStruct(shape, array.dtype))
        self.shapes = shapes
        self.specs = [pl.BlockSpec(memory_space=pl.ANY)] * self.count
        dma = pltpu.SemaphoreType.DMA
        most = max(self.dp_ways, self.mp_ways)
        self.scratch = [dma((self.count, most)) for _ in range(6)] + [dma((self.count,))]

    def bind(self, ins, outs, sems):
        self.ins, self.outs = ins, outs
        self.zs, self.zr, self.cs, self.cr, self.ps, self.pr, self.own = sems
        dp, mp = lax.axis_index(DP), lax.axis_index(MP)
        self.dp, self.mp = dp, mp
        self.parity, self.chip = lax.rem(dp, 2), dp // 2
        self.place = {Z: mp, CHIPS: self.chip, PAIR: self.parity, DP: dp}

    def device(self, group, j):
        if group == Z:
            return (self.dp, j)
        if group == CHIPS:
            return (2 * j + self.parity, self.mp)
        if group == PAIR:
            return (self.dp - self.parity + j, self.mp)
        return (j, self.mp)

    def peer(self, group, off):
        return lax.rem(self.place[group] + off, self.ways[group])

    def remote(self, source, target, send, recv, device):
        return pltpu.make_async_remote_copy(
            src_ref=source,
            dst_ref=target,
            send_sem=send,
            recv_sem=recv,
            device_id=device,
            device_id_type=MESH,
        )

    def meet(self, also=()):
        needed = set(also)
        for kind, group in zip(self.kinds, self.groups):
            if kind in (NEAR, NEARSWAP, WIDE):
                needed |= {CHIPS, PAIR}
                if kind == WIDE:
                    needed.add(Z)
            else:
                needed.add(group)
        barrier = pltpu.get_barrier_semaphore()
        total = 0
        for group in sorted(needed, key=str):
            for off in range(1, self.ways[group]):
                pl.semaphore_signal(
                    barrier,
                    inc=1,
                    device_id=self.device(group, self.peer(group, off)),
                    device_id_type=MESH,
                )
                total += 1
        pl.semaphore_wait(barrier, total)

    def first(self, i):
        kind, group = self.kinds[i], self.groups[i]
        ref, out = self.ins[i], self.outs[i]
        copies = []
        if kind in (NEAR, NEARSWAP):
            return copies
        if kind == WIDE:
            group, slot = Z, out.at[self.dp, self.mp]
        for off in range(1, self.ways[group]):
            peer = self.peer(group, off)
            if kind == WIDE:
                source, target = ref, slot
            elif kind in (GATHER, LATE):
                source, target = ref, out.at[self.place[group]]
            elif kind == MOVE:
                source, target = ref.at[peer], out.at[off - 1]
            elif kind == COLS:
                width = out.shape[-1]
                part = pl.ds(pl.multiple_of(peer * width, width), width)
                source, target = ref.at[:, :, part], out.at[off - 1]
            else:
                source, target = ref.at[:, peer], out.at[off - 1]
            copies.append(
                self.remote(
                    source,
                    target,
                    self.zs.at[i, off - 1],
                    self.zr.at[i, off - 1],
                    self.device(group, peer),
                )
            )
        return copies

    def local(self, i):
        kind, group = self.kinds[i], self.groups[i]
        ref, out = self.ins[i], self.outs[i]
        if kind == WIDE:
            source, target = ref, out.at[self.dp, self.mp]
        elif kind in (GATHER, LATE):
            source, target = ref, out.at[self.place[group]]
        elif kind in (NEAR, NEARSWAP):
            source, target = self.mine(i), out.at[self.dp]
        else:
            return None
        return pltpu.make_async_copy(source, target, self.own.at[i])

    def mine(self, i):
        kind = self.kinds[i]
        if kind == WIDE:
            return self.outs[i].at[self.dp]
        return self.ins[i].at[self.chip] if kind == NEARSWAP else self.ins[i]

    def square(self, i):
        shape = self.shapes[i].shape
        halves = len(shape) > 3 or shape[1] % 32 == 0
        return self.chips == 4 and self.kinds[i] in (NEAR, WIDE) and halves

    def beside(self, chip, k):
        return chip + 1 - 2 * lax.rem(chip, 2) if k == 0 else chip + 2 - 4 * (chip // 2)

    def owner(self, i, k):
        if not self.square(i):
            chip = lax.rem(self.chip + self.chips - k, self.chips)
        elif k == 0:
            chip = self.chip
        elif k < 3:
            chip = self.beside(self.chip, k - 1)
        else:
            chip = self.beside(self.beside(self.chip, 0), 1)
        return 2 * chip + self.parity

    def spread(self, i):
        copies = []
        for k in range(1, 3 if self.square(i) else self.chips):
            peer = self.beside(self.chip, k - 1) if self.square(i) else self.peer(CHIPS, k)
            source = self.ins[i].at[peer] if self.kinds[i] == NEARSWAP else self.mine(i)
            copies.append(
                self.remote(
                    source,
                    self.outs[i].at[self.dp],
                    self.cs.at[i, k - 1],
                    self.cr.at[i, k - 1],
                    self.device(CHIPS, peer),
                )
            )
        return copies

    def forward(self, i, k):
        half = self.outs[i].shape[1] // 2
        part = self.outs[i].at[self.owner(i, k + 1), pl.ds(k * half, half)]
        return self.remote(
            part,
            part,
            self.cs.at[i, 2 + k],
            self.cr.at[i, 2 + k],
            self.device(CHIPS, self.beside(self.chip, 1 - k)),
        )

    def hand(self, i, k):
        owner = self.owner(i, k)
        return self.remote(
            self.mine(i) if k == 0 else self.outs[i].at[owner],
            self.outs[i].at[owner],
            self.ps.at[i, k],
            self.pr.at[i, k],
            self.device(PAIR, 1 - self.parity),
        )

    def begin(self, also=()):
        self.meet(also)
        self.start()

    def start(self):
        for i in range(self.count):
            if self.kinds[i] == LATE:
                continue
            for copy in self.first(i):
                copy.start()
            if self.kinds[i] in (NEAR, NEARSWAP):
                for copy in self.spread(i):
                    copy.start()
                self.hand(i, 0).start()
        for i in range(self.count):
            local = self.local(i)
            if local is not None:
                local.start()

    def finish(self):
        shared = [i for i in range(self.count) if self.kinds[i] in (NEAR, NEARSWAP, WIDE)]
        for i in shared:
            if self.kinds[i] == WIDE:
                for copy in self.first(i):
                    copy.wait()
                self.local(i).wait()
                for copy in self.spread(i):
                    copy.start()
                self.hand(i, 0).start()
        for i in range(self.count):
            if self.kinds[i] == LATE:
                for copy in self.first(i):
                    copy.start()
        for i in shared:
            for k, copy in enumerate(self.spread(i), 1):
                copy.wait_recv()
                if self.square(i):
                    self.forward(i, k - 1).start()
                self.hand(i, k).start()
        for i in shared:
            if self.square(i):
                for k in range(2):
                    self.forward(i, k).wait_recv()
                self.hand(i, 3).start()
        for i in range(self.count):
            if i in shared:
                for copy in self.spread(i):
                    copy.wait_send()
                if self.square(i):
                    for k in range(2):
                        self.forward(i, k).wait_send()
                for off in range(self.chips):
                    self.hand(i, off).wait()
                if self.kinds[i] != WIDE:
                    self.local(i).wait()
            else:
                for copy in self.first(i):
                    copy.wait()
                local = self.local(i)
                if local is not None:
                    local.wait()


def exchange_kernel(plan, *refs):
    count = plan.count
    plan.bind(refs[:count], refs[count : 2 * count], refs[2 * count :])
    plan.begin()
    plan.finish()


def exchange(entries, cid):
    plan = Exchange(entries)
    return pl.pallas_call(
        functools.partial(exchange_kernel, plan),
        out_shape=plan.shapes,
        in_specs=plan.specs,
        out_specs=plan.specs,
        scratch_shapes=plan.scratch,
        compiler_params=pltpu.CompilerParams(collective_id=cid, has_side_effects=True),
    )(*plan.arrays)


def added(array, received, group):
    place = {
        Z: lax.axis_index(MP),
        CHIPS: lax.axis_index(DP) // 2,
        PAIR: lax.rem(lax.axis_index(DP), 2),
        DP: lax.axis_index(DP),
    }[group]
    axis = 1 if group == PAIR else 0
    own = lax.dynamic_index_in_dim(array, place, axis, keepdims=False)
    return own.astype(F32) + jnp.sum(received.astype(F32), axis=0)


def sums_kernel(kinds, shapes, *refs):
    n = len(kinds)
    arrays, received, outs = refs[:n], refs[n : 2 * n], refs[2 * n :]
    dp, mp = lax.axis_index(DP), lax.axis_index(MP)
    place = {Z: mp, CHIPS: dp // 2, PAIR: lax.rem(dp, 2)}
    for array, got, out, (kind, group, form) in zip(arrays, received, outs, kinds):
        if kind == GATHER:
            total = jnp.sum(array[...].astype(F32), axis=0)
        else:
            if kind == MOVE:
                own = array[place[group]]
            elif kind == MOVE1:
                own = array[:, place[group]]
            else:
                width = got.shape[-1]
                own = array[:, :, pl.ds(pl.multiple_of(place[group] * width, width), width)]
            total = own.astype(F32)
            for i in range(got.shape[0]):
                total += got[i].astype(F32)
        if form == COLUMNS:
            width = out.shape[-1]
            for i in range(out.shape[0]):
                out[i] = total[:, i * width : (i + 1) * width].astype(out.dtype)
        elif form == TURNED:
            out[...] = total.T
        else:
            out[...] = total.astype(out.dtype)


def sums(entries):
    mp_ways = lax.axis_size(MP)
    arrays, received, shapes, kinds = [], [], [], []
    for array, got, kind, group, form, dtype in entries:
        shape = got.shape[1:]
        if form == COLUMNS:
            shape = (mp_ways, shape[0], shape[1] // mp_ways)
        elif form == TURNED:
            shape = shape[::-1]
        arrays.append(array)
        received.append(got)
        shapes.append(jax.ShapeDtypeStruct(shape, dtype))
        kinds.append((kind, group, form))
    vmem = pl.BlockSpec(memory_space=pltpu.VMEM)
    return pl.pallas_call(
        functools.partial(sums_kernel, kinds, shapes),
        in_specs=[vmem] * (2 * len(entries)),
        out_specs=[vmem] * len(entries),
        out_shape=shapes,
        compiler_params=pltpu.CompilerParams(vmem_limit_bytes=VMEM_BYTES),
    )(*arrays, *received)


def beside(plan, kernel, inputs, outputs, scratches, *refs):
    n = plan.count
    first, last = pl.program_id(0) == 0, pl.program_id(0) == pl.num_programs(0) - 1
    ins = refs[:inputs]
    sends = refs[inputs : inputs + n]
    outs = refs[inputs + n : inputs + n + outputs]
    lands = refs[inputs + n + outputs : inputs + 2 * n + outputs]
    own = refs[inputs + 2 * n + outputs : inputs + 2 * n + outputs + scratches]
    plan.bind(sends, lands, refs[inputs + 2 * n + outputs + scratches :])
    pl.when(first)(plan.begin)
    kernel(*ins, *outs, *own)
    pl.when(last)(plan.finish)


def memory_call(plan, cid, kernel, name, grid, inputs, in_specs, out_specs, out_shape, scratch, flops):
    return pl.pallas_call(
        functools.partial(beside, plan, kernel, len(inputs), len(out_shape), len(scratch)),
        grid=(grid,),
        in_specs=in_specs + plan.specs,
        out_specs=out_specs + plan.specs,
        out_shape=out_shape + plan.shapes,
        scratch_shapes=scratch + plan.scratch,
        compiler_params=pltpu.CompilerParams(
            vmem_limit_bytes=VMEM_BYTES, collective_id=cid, has_side_effects=True
        ),
        cost_estimate=pl.CostEstimate(flops=flops, bytes_accessed=flops // 200, transcendentals=0),
        name=name,
    )(*inputs, *plan.arrays)


MEM_BLOCK = 16
BACK_BLOCK = 16


def memory_kernel(slots, padded, mem_ref, wk_ref, wv_ref, vb_ref, k_ref, v_ref, rows_ref, wide):
    for c in range(0, D, 128):
        cols = slice(c, c + 128)
        wide[0 : slots * MEM_BLOCK, :] = (
            mem_ref[:, :, cols].reshape(slots * MEM_BLOCK, 128).astype(F32)
        )
        for r in range(MEM_BLOCK):
            own = wide[pl.ds(r, slots, stride=MEM_BLOCK), :]
            rows_ref[r * padded : (r + 1) * padded, cols] = jnp.concatenate(
                [own, jnp.zeros((padded - slots, 128), F32)], axis=0
            ).astype(BF)
    rows = rows_ref[...]
    for c in range(0, D, 512):
        cols = slice(c, c + 512)
        k_ref[:, cols] = product(rows, wk_ref[:, cols]).astype(BF)
        v_ref[:, cols] = (product(rows, wv_ref[:, cols]) + vb_ref[:, cols]).astype(BF)


def memory_products(memory, key_weight, value_weight, vbias, padded, plan, cid):
    rows, slots, _ = memory.shape
    whole = lambda a: pl.BlockSpec(a.shape, lambda i: (0,) * a.ndim)
    out = jax.ShapeDtypeStruct((rows * padded, D), BF)
    out_spec = pl.BlockSpec((MEM_BLOCK * padded, D), lambda i: (i, 0))
    return memory_call(
        plan,
        cid,
        functools.partial(memory_kernel, slots, padded),
        "memory_products",
        rows // MEM_BLOCK,
        [jnp.transpose(memory, (1, 0, 2)), key_weight, value_weight, vbias],
        [
            pl.BlockSpec((slots, MEM_BLOCK, D), lambda i: (0, i, 0)),
            whole(key_weight),
            whole(value_weight),
            whole(vbias),
        ],
        [out_spec] * 3,
        [out] * 3,
        [pltpu.VMEM((-(-slots // 8) * 8 * MEM_BLOCK, 128), F32)],
        4 * rows * padded * D * D,
    )


def memory_grad_kernel(slots, padded, dk_ref, dv_ref, wk_ref, wv_ref, out_ref, wide):
    for c in range(0, D, 256):
        cols = slice(c, c + 256)
        term = product_back(dk_ref[...], wk_ref[cols, :]) + product_back(dv_ref[...], wv_ref[cols, :])
        for part in range(0, 256, 128):
            for r in range(BACK_BLOCK):
                wide[pl.ds(r, slots, stride=BACK_BLOCK), :] = term[
                    r * padded : r * padded + slots, part : part + 128
                ]
            out_ref[:, :, c + part : c + part + 128] = (
                wide[0 : slots * BACK_BLOCK, :].reshape(slots, BACK_BLOCK, 128).astype(BF)
            )


def memory_back(dkeys, dvalues, key_weight, value_weight, rows, slots, padded, plan, cid):
    spec = pl.BlockSpec((BACK_BLOCK * padded, D), lambda i: (i, 0))
    whole = pl.BlockSpec((D, D), lambda i: (0, 0))
    out, *rest = memory_call(
        plan,
        cid,
        functools.partial(memory_grad_kernel, slots, padded),
        "memory_back",
        rows // BACK_BLOCK,
        [dkeys, dvalues, key_weight, value_weight],
        [spec, spec, whole, whole],
        [pl.BlockSpec((slots, BACK_BLOCK, D), lambda i: (0, i, 0))],
        [jax.ShapeDtypeStruct((slots, rows, D), BF)],
        [pltpu.VMEM((-(-slots // 8) * 8 * BACK_BLOCK, 128), F32)],
        4 * rows * padded * D * D,
    )
    return jnp.transpose(out, (1, 0, 2)).astype(F32), rest


def z_copy(source, target, send, recv, device):
    return pltpu.make_async_remote_copy(
        src_ref=source,
        dst_ref=target,
        send_sem=send,
        recv_sem=recv,
        device_id=(lax.axis_index(DP), device),
        device_id_type=MESH,
    )


def z_meet(ways):
    dp, mp = lax.axis_index(DP), lax.axis_index(MP)
    barrier = pltpu.get_barrier_semaphore()
    for off in range(1, ways):
        pl.semaphore_signal(
            barrier, inc=1, device_id=(dp, lax.rem(mp + off, ways)), device_id_type=MESH
        )
    pl.semaphore_wait(barrier, ways - 1)


def nearest(c, ways):
    mp = lax.axis_index(MP)
    left_n, right_n = mp, ways - 1 - mp
    fewer = jnp.minimum(left_n, right_n)
    paired = c <= 2 * fewer
    distance = jnp.where(paired, (c + 1) // 2, c - fewer)
    left = jnp.where(paired, lax.rem(c, 2) == 1, left_n > right_n)
    return jnp.where(left, mp - distance, mp + distance), distance, left, paired


class LineGather:
    def __init__(self, entries, sems, ways):
        self.entries, self.ways = entries, ways
        self.left_send, self.left_recv, self.right_send, self.right_recv, self.own = sems
        self.mp = lax.axis_index(MP)

    def to_right(self, i, source, place, hop):
        held = self.entries[i][1]
        return z_copy(
            source, held.at[place], self.right_send.at[i, hop], self.right_recv.at[i, hop], self.mp + 1
        )

    def to_left(self, i, source, place, hop):
        held = self.entries[i][1]
        return z_copy(
            source, held.at[place], self.left_send.at[i, hop], self.left_recv.at[i, hop], self.mp - 1
        )

    def begin(self):
        mp, every = self.mp, range(len(self.entries))

        @pl.when(mp < self.ways - 1)
        def _():
            for i in every:
                self.to_right(i, self.entries[i][0], mp, 0).start()

        @pl.when(mp > 0)
        def _():
            for i in every:
                self.to_left(i, self.entries[i][0], mp, 0).start()

        for i in every:
            local = pltpu.make_async_copy(self.entries[i][0], self.entries[i][1].at[mp], self.own.at[i])
            local.start()
            local.wait()

    def arrive(self, c, first):
        mp, every = self.mp, range(len(self.entries))
        _, distance, left, paired = nearest(c, self.ways)
        odd = lax.rem(c, 2) == 1
        due = (c > 0) & first & jnp.logical_not(paired & jnp.logical_not(odd))

        @pl.when(due & (left | (paired & odd)))
        def _():
            place = mp - distance
            for i in every:
                held = self.entries[i][1].at[place]
                self.to_right(i, held, place, distance - 1).wait_recv()

                @pl.when(mp < self.ways - 1)
                def _(i=i, held=held):
                    self.to_right(i, held, place, distance).start()

        @pl.when(due & (jnp.logical_not(left) | (paired & odd)))
        def _():
            place = mp + distance
            for i in every:
                held = self.entries[i][1].at[place]
                self.to_left(i, held, place, distance - 1).wait_recv()

                @pl.when(mp > 0)
                def _(i=i, held=held):
                    self.to_left(i, held, place, distance).start()

    def finish(self):
        mp = self.mp
        for hop in range(self.ways - 1):

            @pl.when((mp < self.ways - 1) & (hop <= mp))
            def _(hop=hop):
                for i, (_, held) in enumerate(self.entries):
                    self.to_right(i, held.at[mp - hop], mp - hop, hop).wait_send()

            @pl.when((mp > 0) & (hop <= self.ways - 1 - mp))
            def _(hop=hop):
                for i, (_, held) in enumerate(self.entries):
                    self.to_left(i, held.at[mp + hop], mp + hop, hop).wait_send()


def line_sems(count, ways):
    dma = pltpu.SemaphoreType.DMA
    return [dma((count, ways)) for _ in range(4)] + [dma((count,))]


def own_heads(result, keep):
    kept = result * keep
    total = kept[0:TOK]
    for h in range(1, GH):
        total = total + kept[h * TOK : (h + 1) * TOK]
    return total


def cross_kernel(
    ways, per, piece, padded, used_ref, k_ref, v_ref, q_ref, keep_ref, ctx_ref, stat_ref, ctx_got, stat_got,
    ctx_out, stat_out, send, recv,
):
    c, j = pl.program_id(0), pl.program_id(1)
    mp = lax.axis_index(MP)
    span = piece * TOK

    @pl.when((c == 0) & (j == 0))
    def _():
        z_meet(ways)

    keep = keep_ref[...]
    keep_wide = keep.astype(F32)
    slot = lax.broadcasted_iota(jnp.int32, (padded, GL), 0)
    for g in range(G):
        cols = slice(g * GC, (g + 1) * GC)
        query = jnp.concatenate([q_ref[:, cols]] * GH, axis=0) * keep
        scores = product_back(k_ref[:, cols], query)
        for r in range(piece):
            rows = slice(r * padded, (r + 1) * padded)
            seen = slot < used_ref[r]
            own = jnp.where(seen, scores[rows], NEG)
            peak = jnp.max(own, axis=0, keepdims=True)
            exponent = jnp.where(seen, jnp.exp(own - peak), 0.0)
            total = jnp.sum(exponent, axis=0, keepdims=True)
            probs = (exponent * (1.0 / jnp.maximum(total, 1e-30))).astype(BF)
            ctx = own_heads(weight_grad(probs, v_ref[rows, cols]), keep_wide)
            ctx_out[c, pl.ds(j * span + r * TOK, TOK), cols] = ctx.astype(BF)
            stat_out[c, 0, j * piece + r, g : g + 1, :] = peak
            stat_out[c, 1, j * piece + r, g : g + 1, :] = total

    def copies(k):
        to = nearest(ways - 1 - k, ways)[0]
        off = lax.rem(to - mp + ways, ways)
        return [
            z_copy(a.at[k], b.at[off - 1], send.at[i, k], recv.at[i, off - 1], to)
            for i, (a, b) in enumerate([(ctx_out, ctx_got), (stat_out, stat_got)])
        ]

    for k in range(ways - 1):

        @pl.when((c == k) & (j == per - 1))
        def _(k=k):
            for copy in copies(k):
                copy.start()

    @pl.when((c == ways - 1) & (j == per - 1))
    def _():
        ctx_ref[...] = ctx_out[ways - 1]
        stat_ref[...] = stat_out[ways - 1]
        for k in range(ways - 1):
            for copy in copies(k):
                copy.wait_send()
        for off in range(1, ways):
            to = lax.rem(mp + off, ways)
            for i, (a, b) in enumerate([(ctx_out, ctx_got), (stat_out, stat_got)]):
                z_copy(a.at[0], b.at[off - 1], send.at[i, 0], recv.at[i, off - 1], to).wait_recv()


def cross_forward(used, keys, values, queries, keep, piece, padded, cid):
    ways = lax.axis_size(MP)
    per = queries.shape[0] // TOK // ways
    rows = per * ways * piece
    shard = per * piece
    at = lambda c, j: nearest(ways - 1 - c, ways)[0] * per + j
    big = pl.BlockSpec((piece * padded, D), lambda c, j: (at(c, j), 0))
    anywhere = pl.BlockSpec(memory_space=pl.ANY)
    dma = pltpu.SemaphoreType.DMA
    return pl.pallas_call(
        functools.partial(cross_kernel, ways, per, piece, padded),
        grid=(ways, per),
        in_specs=[
            pl.BlockSpec((piece, 1, GL), lambda c, j: (at(c, j), 0, 0)),
            big,
            big,
            pl.BlockSpec((TOK, D), lambda c, j: (at(c, j), 0)),
            pl.BlockSpec((GL, GC), lambda c, j: (0, 0)),
        ],
        out_specs=[
            pl.BlockSpec((shard * TOK, D), lambda c, j: (0, 0)),
            pl.BlockSpec((2, shard, G, GL), lambda c, j: (0, 0, 0, 0)),
            anywhere,
            anywhere,
        ],
        out_shape=[
            jax.ShapeDtypeStruct((shard * TOK, D), BF),
            jax.ShapeDtypeStruct((2, shard, G, GL), F32),
            jax.ShapeDtypeStruct((ways - 1, shard * TOK, D), BF),
            jax.ShapeDtypeStruct((ways - 1, 2, shard, G, GL), F32),
        ],
        scratch_shapes=[
            pltpu.VMEM((ways, shard * TOK, D), BF),
            pltpu.VMEM((ways, 2, shard, G, GL), F32),
            dma((2, ways)),
            dma((2, ways)),
        ],
        compiler_params=pltpu.CompilerParams(
            vmem_limit_bytes=VMEM_BYTES, collective_id=cid, has_side_effects=True
        ),
        cost_estimate=pl.CostEstimate(
            flops=4 * rows * padded * GL * D,
            bytes_accessed=4 * rows * padded * D,
            transcendentals=rows * padded * G * GL,
        ),
    )(used, keys, values, queries, keep)


def cross_back_kernel(
    ways, per, piece, padded, used_ref, k_ref, v_ref, q_ref, keep_ref, rows_ref, dctx_ref, stat_ref, co_ref,
    dk_ref, dv_ref, dq_ref, key_ref, value_ref, vb_ref, co_sum_ref,
    dctx_all, stat_all, dq_out, dq_got, key_sum, value_sum, low, low_got, co_own, co_got,
    left_send, left_recv, right_send, right_recv, own, send, recv, core_send, core_recv,
):
    c, j = pl.program_id(0), pl.program_id(1)
    dp, mp = lax.axis_index(DP), lax.axis_index(MP)
    parity = lax.rem(dp, 2)
    sibling = (dp + 1 - 2 * parity, mp)
    place = nearest(c, ways)[0]
    span = piece * TOK
    line = LineGather(
        [(dctx_ref, dctx_all), (stat_ref, stat_all)],
        (left_send, left_recv, right_send, right_recv, own),
        ways,
    )

    def core_copy(i):
        source, target = [
            (co_ref, co_got),
            (low.at[0], low_got.at[0]),
            (low.at[1], low_got.at[1]),
        ][i]
        return pltpu.make_async_remote_copy(
            src_ref=source.at[:, 1 - parity],
            dst_ref=target,
            send_sem=core_send.at[i],
            recv_sem=core_recv.at[i],
            device_id=sibling,
            device_id_type=MESH,
        )

    def co_local():
        return pltpu.make_async_copy(co_ref.at[:, parity], co_own, own.at[2])

    @pl.when((c == 0) & (j == 0))
    def _():
        barrier = pltpu.get_barrier_semaphore()
        pl.semaphore_signal(barrier, inc=1, device_id=sibling, device_id_type=MESH)
        for off in range(1, ways):
            pl.semaphore_signal(
                barrier, inc=1, device_id=(dp, lax.rem(mp + off, ways)), device_id_type=MESH
            )
        pl.semaphore_wait(barrier, ways)
        line.begin()
        core_copy(0).start()
        co_local().start()
        key_sum[...] = jnp.zeros_like(key_sum)
        value_sum[...] = jnp.zeros_like(value_sum)
        vb_ref[...] = jnp.zeros_like(vb_ref)

    middle_place = (mp > 0) & (mp < ways - 1)
    line.arrive(c, (j == 0) & jnp.logical_not(middle_place & (c == ways - 1)))
    line.arrive(c + 1, (j == 0) & middle_place & (c == ways - 2))
    keep = keep_ref[...]
    keep_wide = keep.astype(F32)
    slot = lax.broadcasted_iota(jnp.int32, (padded, GL), 0)
    for g in range(G):
        cols = slice(g * GC, (g + 1) * GC)
        query = jnp.concatenate([q_ref[:, cols]] * GH, axis=0) * keep
        scores = product_back(k_ref[:, cols], query)
        parts = []
        for r in range(piece):
            rows = slice(r * padded, (r + 1) * padded)
            dctx = dctx_all[place, pl.ds(j * span + r * TOK, TOK), cols]
            dctx = jnp.concatenate([dctx] * GH, axis=0) * keep
            dprobs = product_back(v_ref[rows, cols], dctx)
            seen = slot < used_ref[r]
            norm = stat_all[place, 0, j * piece + r, g : g + 1, :]
            middle = stat_all[place, 1, j * piece + r, g : g + 1, :]
            probs = jnp.where(seen, jnp.exp(scores[rows] - norm), 0.0)
            parts.append((probs * (dprobs - middle)).astype(BF))
            dv_ref[rows, cols] = product(probs.astype(BF), dctx).astype(BF)
        dscores = jnp.concatenate(parts, axis=0)
        dk_ref[:, cols] = product(dscores, query).astype(BF)
        dquery = own_heads(weight_grad(dscores, k_ref[:, cols]), keep_wide)
        dq_out[c, pl.ds(j * TOK, TOK), cols] = dquery.astype(BF)

    def copy(k):
        to = nearest(k, ways)[0]
        off = lax.rem(to - mp + ways, ways)
        return z_copy(dq_out.at[k], dq_got.at[off - 1], send.at[k], recv.at[off - 1], to)

    for k in range(1, ways):

        @pl.when((c == k) & (j == per - 1))
        def _(k=k):
            copy(k).start()

    memory_rows = rows_ref[...]
    vb_ref[...] += jnp.sum(dv_ref[...].astype(F32), axis=0, keepdims=True)
    for start in range(0, D, 512):
        cols = slice(start, start + 512)
        key_sum[:, cols] += weight_grad(memory_rows, dk_ref[:, cols])
        value_sum[:, cols] += weight_grad(memory_rows, dv_ref[:, cols])

    @pl.when((c == ways - 1) & (j == per - 1))
    def _():
        for i, total in enumerate((key_sum, value_sum)):
            low[i] = total[...].astype(BF).reshape(low.shape[1:])
            core_copy(1 + i).start()
        line.finish()
        for k in range(1, ways):
            copy(k).wait_send()
        total = dq_out[0].astype(F32)
        for off in range(1, ways):
            z_copy(
                dq_out.at[0], dq_got.at[off - 1], send.at[0], recv.at[off - 1], lax.rem(mp + off, ways)
            ).wait_recv()
            total += dq_got[off - 1].astype(F32)
        dq_ref[...] = total
        co_local().wait()
        core_copy(0).wait()
        co_sum_ref[...] = (co_own[...].astype(F32) + co_got[...].astype(F32)).astype(BF)
        for i, out in enumerate((key_ref, value_ref)):
            core_copy(1 + i).wait()
            out[...] = (low[i, :, parity].astype(F32) + low_got[i].astype(F32)).astype(BF)


def cross_back(used, keys, values, queries, memory_rows, dctx, stats, co_blocks, keep, piece, padded, cid):
    ways = lax.axis_size(MP)
    per = queries.shape[0] // TOK // ways
    rows = per * ways * piece
    shard = per * piece
    at = lambda c, j: nearest(c, ways)[0] * per + j
    big = pl.BlockSpec((piece * padded, D), lambda c, j: (at(c, j), 0))
    anywhere = pl.BlockSpec(memory_space=pl.ANY)
    chips, _, vec, _ = co_blocks.shape
    half = (chips, vec, D)
    half_spec = pl.BlockSpec(half, lambda c, j: (0, 0, 0))
    half_shape = jax.ShapeDtypeStruct(half, BF)
    line = line_sems(2, ways)
    dma = pltpu.SemaphoreType.DMA
    return pl.pallas_call(
        functools.partial(cross_back_kernel, ways, per, piece, padded),
        grid=(ways, per),
        in_specs=[
            pl.BlockSpec((piece, 1, GL), lambda c, j: (at(c, j), 0, 0)),
            big,
            big,
            pl.BlockSpec((TOK, D), lambda c, j: (at(c, j), 0)),
            pl.BlockSpec((GL, GC), lambda c, j: (0, 0)),
            big,
            anywhere,
            anywhere,
            anywhere,
        ],
        out_specs=[
            big,
            big,
            pl.BlockSpec((per * TOK, D), lambda c, j: (0, 0)),
            half_spec,
            half_spec,
            pl.BlockSpec((1, D), lambda c, j: (0, 0)),
            half_spec,
        ],
        out_shape=[
            jax.ShapeDtypeStruct((rows * padded, D), BF),
            jax.ShapeDtypeStruct((rows * padded, D), BF),
            jax.ShapeDtypeStruct((per * TOK, D), F32),
            half_shape,
            half_shape,
            jax.ShapeDtypeStruct((1, D), F32),
            half_shape,
        ],
        scratch_shapes=[
            pltpu.VMEM((ways, shard * TOK, D), BF),
            pltpu.VMEM((ways, 2, shard, G, GL), F32),
            pltpu.VMEM((ways, per * TOK, D), BF),
            pltpu.VMEM((ways - 1, per * TOK, D), BF),
            pltpu.VMEM((D, D), F32),
            pltpu.VMEM((D, D), F32),
            pltpu.VMEM((2, chips, 2, vec, D), BF),
            pltpu.VMEM((2,) + half, BF),
            pltpu.VMEM(half, BF),
            pltpu.VMEM(half, BF),
            *line[:4],
            dma((3,)),
            dma((ways,)),
            dma((ways,)),
            dma((3,)),
            dma((3,)),
        ],
        compiler_params=pltpu.CompilerParams(
            vmem_limit_bytes=VMEM_BYTES, collective_id=cid, has_side_effects=True
        ),
        cost_estimate=pl.CostEstimate(
            flops=4 * rows * padded * D * D + 10 * rows * padded * GL * D,
            bytes_accessed=10 * rows * padded * D,
            transcendentals=rows * padded * G * GL,
        ),
    )(used, keys, values, queries, keep, memory_rows, dctx, stats, co_blocks)


def table_words(table, start, count):
    if table.shape[0] == 1:
        return table[0, pl.ds(start, count), :]
    return jnp.concatenate([table[i, pl.ds(start, count), :] for i in range(table.shape[0])], axis=-1)


def table_load(table_refs, table, sems, tile, c, t):
    tiles = table.shape[1] // tile
    places = [(ref, j * tile) for ref in table_refs for j in range(ref.shape[1] // tile)]

    def copy(k):
        ref, start = places[k]
        source = ref.at[:, pl.ds(start, tile), :]
        return pltpu.make_async_copy(source, table.at[:, pl.ds(k * tile, tile), :], sems.at[k])

    @pl.when((c == 0) & (t == 0))
    def _():
        for k in range(tiles):
            copy(k).start()

    for k in range(tiles):

        @pl.when((c == 0) & (t == k))
        def _(k=k):
            copy(k).wait()


def vocab_kernel(
    ways, tile, sub, chunk, count, h_ref, target_ref, *refs
):
    table_refs, refs = refs[:count], refs[count:]
    vocab_steps(ways, tile, sub, chunk, table_refs, h_ref, target_ref, *refs)


def vocab_steps(
    ways, tile, sub, chunk, table_refs, h_ref, target_ref, exp_ref, tops_ref, stats_ref,
    table, held, run, stats, table_sem, left_send, left_recv, right_send, right_recv, own,
    stat_send, stat_recv, stat_own,
):
    c, t = pl.program_id(0), pl.program_id(1)
    last = pl.num_programs(1) - 1
    mp = lax.axis_index(MP)
    slot = nearest(c, ways)[0]
    line = LineGather(
        [(h_ref, held)], (left_send, left_recv, right_send, right_recv, own), ways
    )

    def stats_copy(off):
        return z_copy(
            stats,
            stats_ref.at[mp],
            stat_send.at[off - 1],
            stat_recv.at[off - 1],
            lax.rem(mp + off, ways),
        )

    @pl.when((c == 0) & (t == 0))
    def _():
        z_meet(ways)
        line.begin()

    line.arrive(c, t == 0)
    table_load(table_refs, table, table_sem, tile, c, t)

    @pl.when(t == 0)
    def _():
        run[0:1, :] = jnp.full((1, chunk), NEG, F32)
        run[1:3, :] = jnp.zeros((2, chunk), F32)

    tokens = held[slot]
    target = target_ref[slot]
    parts = []
    for i in range(tile // sub):
        start = t * tile + i * sub
        logits = product_back(table_words(table, start, sub), tokens)
        top = jnp.max(logits, axis=0, keepdims=True)
        exponent = jnp.exp(logits - top)
        word = lax.broadcasted_iota(jnp.int32, (sub, chunk), 0) + start
        hit = jnp.where(word == target, logits, 0.0)
        exp_ref[0, i * sub : (i + 1) * sub, :] = exponent.astype(BF)
        tops_ref[0, pl.ds(t * (tile // sub) + i, 1), :] = top
        parts.append(
            (top, jnp.sum(exponent, axis=0, keepdims=True), jnp.sum(hit, axis=0, keepdims=True))
        )
    former = run[0:1, :]
    peak = former
    for top, total, hit in parts:
        peak = jnp.maximum(peak, top)
    sums = run[1:2, :] * jnp.exp(former - peak)
    hits = run[2:3, :]
    for top, total, hit in parts:
        sums += total * jnp.exp(top - peak)
        hits += hit
    run[0:1, :] = peak
    run[1:2, :] = sums
    run[2:3, :] = hits

    @pl.when(t == last)
    def _():
        stats[slot] = run[...]

    @pl.when((c == ways - 1) & (t == last))
    def _():
        for off in range(1, ways):
            stats_copy(off).start()
        local = pltpu.make_async_copy(stats, stats_ref.at[mp], stat_own.at[0])
        local.start()
        line.finish()
        for off in range(1, ways):
            stats_copy(off).wait()
        local.wait()


def vocab_sizes(words):
    tile = 1280 if words % 1280 == 0 else words
    sub = 256 if tile % 256 == 0 else tile
    return tile, sub


def vocab_forward(hidden, target, tables, cid):
    ways = lax.axis_size(MP)
    chunk = hidden.shape[0]
    parts, _, width = tables[0].shape
    words = sum(a.shape[1] for a in tables)
    tile, sub = vocab_sizes(words)
    tiles = words // tile
    top_rows = -(-(words // sub) // 8) * 8
    dma = pltpu.SemaphoreType.DMA
    return pl.pallas_call(
        functools.partial(vocab_kernel, ways, tile, sub, chunk, len(tables)),
        grid=(ways, tiles),
        in_specs=[
            pl.BlockSpec(memory_space=pl.ANY),
            pl.BlockSpec((ways, 1, chunk), lambda c, t: (0, 0, 0)),
            *[pl.BlockSpec(memory_space=pl.ANY)] * len(tables),
        ],
        out_specs=[
            pl.BlockSpec((1, tile, chunk), lambda c, t: (c, t, 0)),
            pl.BlockSpec((1, top_rows, chunk), lambda c, t: (c, 0, 0)),
            pl.BlockSpec(memory_space=pl.ANY),
        ],
        out_shape=[
            jax.ShapeDtypeStruct((ways, words, chunk), BF),
            jax.ShapeDtypeStruct((ways, top_rows, chunk), F32),
            jax.ShapeDtypeStruct((ways, ways, 8, chunk), F32),
        ],
        scratch_shapes=[
            pltpu.VMEM((parts, words, width), BF),
            pltpu.VMEM((ways, chunk, D), BF),
            pltpu.VMEM((8, chunk), F32),
            pltpu.VMEM((ways, 8, chunk), F32),
            dma((tiles,)),
            *line_sems(1, ways),
            dma((ways,)),
            dma((ways,)),
            dma((1,)),
        ],
        compiler_params=pltpu.CompilerParams(
            vmem_limit_bytes=VMEM_BYTES, collective_id=cid, has_side_effects=True
        ),
        cost_estimate=pl.CostEstimate(
            flops=2 * ways * chunk * words * D,
            bytes_accessed=2 * ways * words * D,
            transcendentals=ways * chunk * words,
        ),
    )(hidden, target, *tables)


def vocab_back_kernel(
    ways, tile, sub, chunk, count, exp_ref, tops_ref, target_ref, norm_ref, rate_ref, *refs
):
    table_refs, refs = refs[:count], refs[count:]
    vocab_back_steps(
        ways, tile, sub, chunk, table_refs, exp_ref, tops_ref, target_ref, norm_ref, rate_ref, *refs
    )


def vocab_back_steps(
    ways, tile, sub, chunk, table_refs, exp_ref, tops_ref, target_ref, norm_ref, rate_ref, out_ref,
    table, total, terms, leaving, landing, table_sem, send, recv,
):
    c, t = pl.program_id(0), pl.program_id(1)
    last = pl.num_programs(1) - 1
    mp = lax.axis_index(MP)
    slot = nearest(ways - 1 - c, ways)[0]

    def copy(to):
        right = to > mp
        spot = jnp.where(right | (to < mp - 1), to, ways)
        return z_copy(
            leaving.at[to],
            landing.at[spot],
            send.at[to],
            recv.at[spot],
            jnp.where(right, mp + 1, mp - 1),
        )

    def arrived(spot):
        z_copy(
            leaving.at[0], landing.at[spot], send.at[0], recv.at[spot], lax.rem(mp + 1, ways)
        ).wait_recv()

    @pl.when((c == 0) & (t == 0))
    def _():
        z_meet(ways)

    table_load(table_refs, table, table_sem, tile, c, t)
    target, norm, rate = target_ref[slot], norm_ref[slot], rate_ref[slot]
    term = None
    for i in range(tile // sub):
        start = t * tile + i * sub
        factor = jnp.exp(tops_ref[0, pl.ds(t * (tile // sub) + i, 1), :] - norm) * -rate
        word = lax.broadcasted_iota(jnp.int32, (sub, chunk), 0) + start
        hit = jnp.where(word == target, rate, 0.0)
        dlogits = hit + exp_ref[0, i * sub : (i + 1) * sub, :].astype(F32) * factor
        part = weight_grad(dlogits.astype(BF), table_words(table, start, sub))
        term = part if term is None else term + part

    @pl.when(t == 0)
    def _():
        total[...] = term

    @pl.when(t > 0)
    def _():
        total[...] += term

    for k in range(ways - 1):
        to = nearest(ways - 1 - k, ways)[0]
        beyond = jnp.where(to > mp, mp > 0, mp < ways - 1)

        @pl.when((c == k) & (t == last) & jnp.logical_not(beyond))
        def _(to=to):
            leaving[to] = total[...].astype(BF)
            copy(to).start()

        @pl.when((c == k) & (t == last) & beyond)
        def _(k=k):
            terms[k] = total[...]

    for k in range(ways - 1):
        to = nearest(ways - 1 - k, ways)[0]
        beyond = jnp.where(to > mp, mp > 0, mp < ways - 1)

        @pl.when((c == min(k + 2, ways - 1)) & (t == last) & beyond)
        def _(k=k, to=to):
            arrived(to)
            leaving[to] = (terms[k] + landing[to].astype(F32)).astype(BF)
            copy(to).start()

    @pl.when((c == ways - 1) & (t == last))
    def _():
        out_ref[...] = total[...]

        @pl.when(mp > 0)
        def _():
            arrived(mp)
            out_ref[...] += landing[mp].astype(F32)

        @pl.when(mp < ways - 1)
        def _():
            arrived(ways)
            out_ref[...] += landing[ways].astype(F32)

        for k in range(ways - 1):
            copy(nearest(ways - 1 - k, ways)[0]).wait_send()


def vocab_back(exponents, tops, target, norm, rate, tables, cid):
    ways, words, chunk = exponents.shape
    tile, sub = vocab_sizes(words)
    tiles = words // tile
    whole = pl.BlockSpec((ways, 1, chunk), lambda c, t: (0, 0, 0))
    dma = pltpu.SemaphoreType.DMA
    return pl.pallas_call(
        functools.partial(vocab_back_kernel, ways, tile, sub, chunk, len(tables)),
        grid=(ways, tiles),
        in_specs=[
            pl.BlockSpec((1, tile, chunk), lambda c, t: (ways - 1 - c, t, 0)),
            pl.BlockSpec((1, tops.shape[1], chunk), lambda c, t: (ways - 1 - c, 0, 0)),
            whole,
            whole,
            whole,
            *[pl.BlockSpec(memory_space=pl.ANY)] * len(tables),
        ],
        out_specs=pl.BlockSpec((chunk, D), lambda c, t: (0, 0)),
        out_shape=jax.ShapeDtypeStruct((chunk, D), F32),
        scratch_shapes=[
            pltpu.VMEM((tables[0].shape[0], words, tables[0].shape[2]), BF),
            pltpu.VMEM((chunk, D), F32),
            pltpu.VMEM((ways - 1, chunk, D), F32),
            pltpu.VMEM((ways, chunk, D), BF),
            pltpu.VMEM((ways + 1, chunk, D), BF),
            dma((tiles,)),
            dma((ways,)),
            dma((ways + 1,)),
        ],
        compiler_params=pltpu.CompilerParams(
            vmem_limit_bytes=VMEM_BYTES, collective_id=cid, has_side_effects=True
        ),
        cost_estimate=pl.CostEstimate(
            flops=2 * ways * chunk * words * D, bytes_accessed=2 * ways * words * D, transcendentals=0
        ),
    )(exponents, tops, target, norm, rate, *tables)


HIDDEN_TILE = 512
ROOT_HALF = 0.7071067811865476
ROOT_TAU = 0.3989422804014327


def weight_tile(ref):
    return ref[...].reshape(D, ref.shape[-1])


def feed_kernel(h_ref, expand_ref, bias_ref, shrink_ref, a_ref, out_ref):
    t = pl.program_id(0)
    hidden = product(h_ref[...], weight_tile(expand_ref)) + bias_ref[0]
    a_ref[...] = hidden
    active = (hidden * (0.5 + 0.5 * lax.erf(hidden * ROOT_HALF))).astype(BF)
    term = product_back(active, weight_tile(shrink_ref))

    @pl.when(t == 0)
    def _():
        out_ref[...] = term

    @pl.when(t > 0)
    def _():
        out_ref[...] += term


def feed_specs(weights):
    parts, ways, _, rows, units = weights.shape
    per = units // HIDDEN_TILE
    tile = lambda which: pl.BlockSpec(
        (parts, 1, 1, rows, HIDDEN_TILE), lambda t: (0, t // per, which, 0, t % per)
    )
    bias = pl.BlockSpec((1, 1, HIDDEN_TILE), lambda t: (t, 0, 0))
    return tile(0), bias, tile(1), ways * per


def feed_forward(hidden, weights, bias):
    tokens = hidden.shape[0]
    expand_spec, bias_spec, shrink_spec, tiles = feed_specs(weights)
    whole = pl.BlockSpec((tokens, D), lambda t: (0, 0))
    units = tiles * HIDDEN_TILE
    return pl.pallas_call(
        feed_kernel,
        grid=(tiles,),
        in_specs=[whole, expand_spec, bias_spec, shrink_spec],
        out_specs=[pl.BlockSpec((tokens, HIDDEN_TILE), lambda t: (0, t)), whole],
        out_shape=[
            jax.ShapeDtypeStruct((tokens, units), F32),
            jax.ShapeDtypeStruct((tokens, D), F32),
        ],
        compiler_params=pltpu.CompilerParams(vmem_limit_bytes=VMEM_BYTES),
        cost_estimate=pl.CostEstimate(
            flops=4 * tokens * units * D, bytes_accessed=4 * units * D, transcendentals=tokens * units
        ),
    )(hidden, weights, bias.reshape(tiles, 1, HIDDEN_TILE), weights)


def feed_back_kernel(
    dout_ref, h_ref, a_ref, expand_ref, shrink_ref, dweights_ref, dbias_ref, dh_ref
):
    t = pl.program_id(0)
    dout = dout_ref[...]
    hidden = a_ref[...]
    below = 0.5 + 0.5 * lax.erf(hidden * ROOT_HALF)
    slope = below + hidden * (ROOT_TAU * jnp.exp(-0.5 * hidden * hidden))
    active = (hidden * below).astype(BF)
    dhidden = (slope * product(dout, weight_tile(shrink_ref))).astype(BF)
    dbias_ref[0] = jnp.sum(dhidden.astype(F32), axis=0, keepdims=True)
    parts, _, rows, width = dweights_ref.shape
    dweights_ref[:, 0] = weight_grad(h_ref[...], dhidden).astype(BF).reshape(parts, rows, width)
    dweights_ref[:, 1] = weight_grad(dout, active).astype(BF).reshape(parts, rows, width)
    term = product_back(dhidden, weight_tile(expand_ref))

    @pl.when(t == 0)
    def _():
        dh_ref[...] = term

    @pl.when(t > 0)
    def _():
        dh_ref[...] += term


def feed_back(dout, hidden, before, weights):
    tokens = hidden.shape[0]
    expand_spec, bias_spec, shrink_spec, tiles = feed_specs(weights)
    parts, rows = weights.shape[0], weights.shape[3]
    whole = pl.BlockSpec((tokens, D), lambda t: (0, 0))
    units = tiles * HIDDEN_TILE
    return pl.pallas_call(
        feed_back_kernel,
        grid=(tiles,),
        in_specs=[
            whole,
            whole,
            pl.BlockSpec((tokens, HIDDEN_TILE), lambda t: (0, t)),
            expand_spec,
            shrink_spec,
        ],
        out_specs=[
            pl.BlockSpec((parts, 2, rows, HIDDEN_TILE), lambda t: (0, 0, 0, t)),
            bias_spec,
            whole,
        ],
        out_shape=[
            jax.ShapeDtypeStruct((parts, 2, rows, units), BF),
            jax.ShapeDtypeStruct((tiles, 1, HIDDEN_TILE), F32),
            jax.ShapeDtypeStruct((tokens, D), F32),
        ],
        compiler_params=pltpu.CompilerParams(vmem_limit_bytes=VMEM_BYTES),
        cost_estimate=pl.CostEstimate(
            flops=8 * tokens * units * D, bytes_accessed=8 * units * D, transcendentals=2 * tokens * units
        ),
    )(dout, hidden, before, weights, weights)


def query_kernel(
    ways, part_ref, x_ref, bias_ref, gain_ref, shift_ref, cq_ref, cqb_ref,
    hidden_ref, normed_ref, inverse_ref, low_ref, full_ref, all_ref, got, queries, send, recv, own,
):
    mp = lax.axis_index(MP)
    count = hidden_ref.shape[0]

    def part_copy(off):
        to = lax.rem(mp + off, ways)
        return z_copy(part_ref.at[to], got.at[off - 1], send.at[0, off], recv.at[0, off], to)

    def query_copy(off):
        to = lax.rem(mp + off, ways)
        return z_copy(queries, all_ref.at[mp], send.at[1, off], recv.at[1, off], to)

    z_meet(ways)
    for off in range(1, ways):
        part_copy(off).start()
    width = full_ref.shape[1] // ways
    for m in range(ways):
        full_ref[:, m * width : (m + 1) * width] = cq_ref[:, m].reshape(D, width)
    rows = pl.ds(pl.multiple_of(mp * count, count), count)
    total = x_ref[rows, :].astype(F32) + part_ref[mp].astype(F32) + bias_ref[...]
    for off in range(1, ways):
        part_copy(off).wait()
        total += got[off - 1].astype(F32)
    hidden, normed, inverse = layer_norm(total, gain_ref[...], shift_ref[...])
    hidden_ref[...] = hidden
    normed_ref[...] = normed
    inverse_ref[...] = inverse
    low_ref[...] = hidden.astype(BF)
    queries[...] = ((product(hidden.astype(BF), full_ref[...]) + cqb_ref[...]) * SCALE).astype(BF)
    for off in range(1, ways):
        query_copy(off).start()
    local = pltpu.make_async_copy(queries, all_ref.at[mp], own.at[0])
    local.start()
    for off in range(1, ways):
        query_copy(off).wait()
    local.wait()


def cross_inputs(partial, x, bias, gain, shift, cquery, cqbias, cid):
    ways, count, _ = partial.shape
    row = lambda a: a.astype(F32).reshape(1, D)
    vmem = pl.BlockSpec(memory_space=pltpu.VMEM)
    dma = pltpu.SemaphoreType.DMA
    return pl.pallas_call(
        functools.partial(query_kernel, ways),
        in_specs=[vmem] * 7,
        out_specs=[vmem] * 5 + [pl.BlockSpec(memory_space=pl.ANY)],
        out_shape=[
            jax.ShapeDtypeStruct((count, D), F32),
            jax.ShapeDtypeStruct((count, D), F32),
            jax.ShapeDtypeStruct((count, 1), F32),
            jax.ShapeDtypeStruct((count, D), BF),
            jax.ShapeDtypeStruct((D, D), BF),
            jax.ShapeDtypeStruct((ways, count, D), BF),
        ],
        scratch_shapes=[
            pltpu.VMEM((ways - 1, count, D), BF),
            pltpu.VMEM((count, D), BF),
            dma((2, ways)),
            dma((2, ways)),
            dma((1,)),
        ],
        compiler_params=pltpu.CompilerParams(
            vmem_limit_bytes=VMEM_BYTES, collective_id=cid, has_side_effects=True
        ),
    )(partial, x, row(bias), row(gain), row(shift), cquery, row(cqbias))


def self_back_kernel(
    plan, x_ref, ctx_ref, q_ref, k_ref, v_ref, wo_ref, wqkv_ref, keep_ref, dfirst_ref, *refs
):
    n = plan.count
    sends, rest = refs[:n], refs[n:]
    bias_ref, dself_ref, dwo_ref, din_ref = rest[:4]
    lands, rest = rest[4 : 4 + n], rest[4 + n :]
    dctx, dqkv, part, part_got, din, dself, dself_got, dwo, dwo_got, dout, dout_all = rest[:11]
    send, recv, own = rest[11:14]
    plan.bind(sends, lands, rest[14:])
    ways = plan.mp_ways
    mp, parity = plan.mp, plan.parity

    def part_copy(off):
        to = plan.peer(Z, off)
        return z_copy(part.at[to], part_got.at[off - 1], send.at[0, off], recv.at[0, off], to)

    def din_copy(off):
        return z_copy(din, din_ref.at[mp], send.at[1, off], recv.at[1, off], plan.peer(Z, off))

    def core_copies():
        return [
            plan.remote(a.at[:, 1 - parity], b, send.at[2, i], recv.at[2, i], plan.device(PAIR, 1 - parity))
            for i, (a, b) in enumerate([(dself, dself_got), (dwo, dwo_got)])
        ]

    def dout_copy(off):
        return z_copy(dout, dout_all.at[mp], send.at[3, off], recv.at[3, off], plan.peer(Z, off))

    plan.meet((Z, PAIR))
    dout[...] = dfirst_ref[...].astype(BF)
    for off in range(1, ways):
        dout_copy(off).start()
    plan.start()
    dout_all[mp] = dout[...]
    keep = keep_ref[...]
    keep_wide = keep.astype(F32)
    for off in range(1, ways):
        dout_copy(off).wait()
    upstreams = dout_all[...].reshape(x_ref.shape)
    dctx[...] = product_back(upstreams, wo_ref[...]).astype(BF)
    key_place = lax.broadcasted_iota(jnp.int32, (TOK, GL), 0)
    query_place = lax.rem(lax.broadcasted_iota(jnp.int32, (TOK, GL), 1), TOK)
    seen = key_place <= query_place

    @pl.loop(0, x_ref.shape[0] // TOK)
    def _(question):
        rows = pl.ds(pl.multiple_of(question * TOK, TOK), TOK)
        keys, values = k_ref[rows, :], v_ref[rows, :]
        query = jnp.concatenate([q_ref[rows, :]] * GH, axis=0) * keep
        upstream = jnp.concatenate([dctx[rows, :]] * GH, axis=0) * keep
        scores = jnp.where(seen, product_back(keys, query), NEG)
        exponent = jnp.exp(scores - jnp.max(scores, axis=0, keepdims=True))
        probs = exponent / jnp.sum(exponent, axis=0, keepdims=True)
        dprobs = product_back(values, upstream)
        middle = jnp.sum(probs * dprobs, axis=0, keepdims=True)
        dscores = (probs * (dprobs - middle)).astype(BF)
        dquery = own_heads(weight_grad(dscores, keys), keep_wide)
        dqkv[rows, 0:GC] = (dquery * SCALE).astype(BF)
        dqkv[rows, GC : 2 * GC] = product(dscores, query).astype(BF)
        dqkv[rows, 2 * GC : 3 * GC] = product(probs.astype(BF), upstream).astype(BF)

    grads = dqkv[...]
    part[...] = product_back(grads, wqkv_ref[...]).astype(BF).reshape(part.shape)
    for off in range(1, ways):
        part_copy(off).start()
    dself[...] = weight_grad(x_ref[...], grads).astype(BF).reshape(dself.shape)
    dwo[...] = weight_grad(upstreams, ctx_ref[...]).astype(BF).reshape(dwo.shape)
    for copy in core_copies():
        copy.start()
    bias_ref[...] = jnp.sum(grads.astype(F32), axis=0, keepdims=True)
    total = dfirst_ref[...] + part[mp].astype(F32)
    for off in range(1, ways):
        part_copy(off).wait_recv()
        total += part_got[off - 1].astype(F32)
    din[...] = total.astype(BF)
    for off in range(1, ways):
        din_copy(off).start()
    local = pltpu.make_async_copy(din, din_ref.at[mp], own.at[0])
    local.start()
    for copy in core_copies():
        copy.wait()
    dself_ref[...] = (dself[:, parity].astype(F32) + dself_got[...].astype(F32)).astype(BF)
    dwo_ref[...] = (dwo[:, parity].astype(F32) + dwo_got[...].astype(F32)).astype(BF)
    plan.finish()
    for off in range(1, ways):
        part_copy(off).wait_send()
        din_copy(off).wait()
    local.wait()


def self_back(x, ctx, queries, keys, values, wo, wqkv, keep, dfirst, plan, cid):
    uniq, shard = x.shape[0], dfirst.shape[0]
    ways, chips = plan.mp_ways, plan.chips
    vec = D // plan.dp_ways
    inputs = [x, ctx, queries, keys, values, wo, wqkv, keep, dfirst]
    vmem = pl.BlockSpec(memory_space=pltpu.VMEM)
    dma = pltpu.SemaphoreType.DMA
    cols = wqkv.shape[1]
    return pl.pallas_call(
        functools.partial(self_back_kernel, plan),
        in_specs=[vmem] * len(inputs) + plan.specs,
        out_specs=[vmem, vmem, vmem, pl.BlockSpec(memory_space=pl.ANY)] + plan.specs,
        out_shape=[
            jax.ShapeDtypeStruct((1, cols), F32),
            jax.ShapeDtypeStruct((chips, vec, cols), BF),
            jax.ShapeDtypeStruct((chips, vec, GC), BF),
            jax.ShapeDtypeStruct((ways, shard, D), BF),
        ]
        + plan.shapes,
        scratch_shapes=[
            pltpu.VMEM((uniq, GC), BF),
            pltpu.VMEM((uniq, cols), BF),
            pltpu.VMEM((ways, shard, D), BF),
            pltpu.VMEM((ways - 1, shard, D), BF),
            pltpu.VMEM((shard, D), BF),
            pltpu.VMEM((chips, 2, vec, cols), BF),
            pltpu.VMEM((chips, vec, cols), BF),
            pltpu.VMEM((chips, 2, vec, GC), BF),
            pltpu.VMEM((chips, vec, GC), BF),
            pltpu.VMEM((shard, D), BF),
            pltpu.VMEM((ways, shard, D), BF),
            dma((4, ways)),
            dma((4, ways)),
            dma((1,)),
            *plan.scratch,
        ],
        compiler_params=pltpu.CompilerParams(
            vmem_limit_bytes=VMEM_BYTES, collective_id=cid, has_side_effects=True
        ),
        cost_estimate=pl.CostEstimate(
            flops=4 * uniq * D * cols, bytes_accessed=8 * uniq * D, transcendentals=uniq * GL
        ),
    )(*inputs, *plan.arrays)


def self_probs(queries, key_heads):
    causal = (
        lax.broadcasted_iota(jnp.int32, (TOK, TOK), 1)
        <= lax.broadcasted_iota(jnp.int32, (TOK, TOK), 0)
    )[None, None]
    scores = jnp.einsum("rqhe,rkhe->rhqk", queries, key_heads, preferred_element_type=F32)
    return jax.nn.softmax(jnp.where(causal, scores, NEG), axis=-1)


def column_parts(gathered):
    return jnp.concatenate([gathered[i] for i in range(gathered.shape[0])], axis=-1)


def block_rows(array, ways):
    rows, columns = array.shape
    width = columns // ways
    return jnp.stack([array[:, i * width : (i + 1) * width] for i in range(ways)])


def local(
    answers,
    targets,
    doc_scores,
    memory,
    lengths,
    self_query,
    self_key,
    self_value,
    query_bias,
    value_bias,
    self_output,
    output_bias,
    first_gain,
    first_shift,
    cross_query,
    crossq_bias,
    cross_key,
    cross_value,
    crossv_bias,
    cross_output,
    crosso_bias,
    second_gain,
    second_shift,
    expand_weight,
    expand_bias,
    shrink_weight,
    shrink_bias,
    third_gain,
    third_shift,
    word_table,
):
    dp_ways, mp_ways = lax.axis_size(DP), lax.axis_size(MP)
    chips = dp_ways // 2
    dp, mp = lax.axis_index(DP), lax.axis_index(MP)
    groups = answers.shape[0]
    rows, slots, _ = memory.shape
    piece = rows // dp_ways
    own_q = dp_ways
    uniq = own_q * TOK
    tokens = rows * TOK
    padded = -(-slots // 16) * 16
    shard_rows = rows // mp_ways
    shard_tokens = shard_rows * TOK
    shard_q = own_q // mp_ways
    shard_uniq = shard_q * TOK
    local_heads = H // mp_ways
    head_cols = local_heads * HD
    hidden_cols = expand_weight.shape[1]
    vec = D // dp_ways

    vectors = (
        output_bias,
        first_gain,
        first_shift,
        crosso_bias,
        second_gain,
        second_shift,
        shrink_bias,
        third_gain,
        third_shift,
        crossv_bias,
    )
    matrices = (query_bias, value_bias, crossq_bias, expand_bias)
    starts, top = [], 16
    for matrix in matrices:
        starts.append(top)
        top += -(-matrix.shape[0] // 8) * 8
    small_rows = -(-top // 16) * 16
    row_of = lax.broadcasted_iota(jnp.int32, (small_rows, 128), 0)
    small = jnp.zeros((small_rows, 128), BF)
    for i, vector in enumerate(vectors):
        vector = jnp.pad(vector, (0, 128 - vector.shape[0]))
        small = jnp.where(row_of == i, vector[None, :], small)
    for start, matrix in zip(starts, matrices):
        count, width = matrix.shape
        small += jnp.pad(matrix, ((start, small_rows - start - count), (0, 128 - width)))
    wide_rows = cross_key.shape[0]
    self_shard = jnp.concatenate([self_query, self_key, self_value], axis=1)
    target_rows = jnp.pad(targets, ((0, 8 - groups), (0, 128 - TOK)))
    doc_rows = jnp.pad(doc_scores, ((0, 8 - groups), (0, 128 - K)))
    if chips == groups:
        wanted = answers
    else:
        wanted = jnp.stack([answers[(2 * c * piece) // K] for c in range(chips)])
    feed_shard = jnp.stack([expand_weight, shrink_weight.T])
    key_all, value_all, small_all, cquery_z, cout_z = exchange(
        [
            (cross_key, WIDE, Z),
            (cross_value, WIDE, Z),
            (small, WIDE, Z),
            (cross_query, LATE, Z),
            (cross_output, LATE, Z),
        ],
        0,
    )
    (full_obias, gain_one, shift_one, full_cobias, gain_two, shift_two, full_sbias, gain_three, shift_three) = [
        small_all[:, 0, i, :vec].reshape(D) for i in range(9)
    ]
    cvbias = small_all[:, :, 9, :wide_rows].reshape(1, D)

    def head_bias(i):
        count, width = matrices[i].shape
        part = small_all[:, :, starts[i] : starts[i] + count, :width]
        return jnp.transpose(part, (1, 2, 0, 3)).reshape(mp_ways, -1)

    mine = lambda a: lax.dynamic_index_in_dim(a, mp, 0, keepdims=False)
    qbias = mine(head_bias(0))
    vbias = mine(head_bias(1))
    cqbias = head_bias(2).reshape(-1)
    ebias = head_bias(3).reshape(-1)
    key_weight = key_all.reshape(D, D)
    value_weight = value_all.reshape(D, D)

    plan = Exchange(
        [
            (feed_shard, GATHER, Z),
            (self_shard, NEAR, Z),
            (self_output, NEAR, Z),
            (target_rows, NEAR, Z),
            (doc_rows, NEAR, Z),
            (wanted, NEARSWAP, Z),
            (cquery_z, NEAR, Z),
            (cout_z, NEAR, Z),
        ]
    )
    (keys, values, memory_rows, feed_z, self_all, output_all, target_all, doc_all, x_all, cquery_all, cout_all) = (
        memory_products(memory, key_weight, value_weight, cvbias, padded, plan, 1)
    )
    words = word_table.shape[0]
    early = words // 1280 * 4 // 5 * 1280 if words % 1280 == 0 else 0
    tables = []
    if early:
        part = lax.all_gather(word_table[:early], DP, axis=0, tiled=False)
        feed_z, part = lax.optimization_barrier((feed_z, part))
        tables.append(part)
    feed_all = lax.all_gather(feed_z, DP, axis=0, tiled=False)
    tables.append(lax.all_gather(word_table[early:], DP, axis=0, tiled=False))
    if word_table.shape[1] < 128:
        tables = [column_parts(a)[None] for a in tables]
    rows_first = lambda a: jnp.transpose(a, (0, 2, 1, 3)).reshape(dp_ways * a.shape[2], -1)
    columns_first = lambda a: column_parts(a.reshape(dp_ways, -1, a.shape[-1]))
    self_weight = self_all.reshape(D, 3 * head_cols)
    full_output = column_parts(output_all)
    my_group = (dp * piece) // K
    row_targets = lax.dynamic_index_in_dim(
        target_all[:, :groups, :TOK], my_group, 1, keepdims=False
    )
    x_rows = x_all.reshape(uniq, D)

    qkv = product(x_rows, self_weight)
    queries = ((qkv[:, :head_cols] + qbias) * SCALE).astype(BF)
    self_keys = qkv[:, head_cols : 2 * head_cols].astype(BF)
    self_values = (qkv[:, 2 * head_cols :] + vbias).astype(BF)
    heads = lambda a: a.reshape(own_q, TOK, local_heads, HD)
    probs = self_probs(heads(queries), heads(self_keys))
    context = jnp.einsum(
        "rhqk,rkhe->rqhe", probs.astype(BF), heads(self_values), preferred_element_type=F32
    )
    context = context.astype(BF).reshape(uniq, head_cols)
    partial = product(context, full_output).astype(BF).reshape(mp_ways, shard_uniq, D)
    hidden_one, normed_one, inverse_one, hidden_low1, full_cquery, cross_queries = cross_inputs(
        partial, x_rows, full_obias, gain_one, shift_one, cquery_all, cqbias, 2
    )
    full_cout = columns_first(cout_all)
    cross_queries = cross_queries.reshape(uniq, D)

    used = jnp.clip(lengths - mp * slots, 0, slots).astype(jnp.int32)
    used = jnp.broadcast_to(used[:, None, None], (rows, 1, GL))
    keep = (
        lax.broadcasted_iota(jnp.int32, (GL, GC), 0) // TOK
        == lax.broadcasted_iota(jnp.int32, (GL, GC), 1) // HD
    ).astype(BF)
    ctx_own, stat_own, ctx_got, stat_got = cross_forward(
        used, keys, values, cross_queries, keep, piece, padded, 4
    )
    stat_got = jnp.concatenate([stat_own[None], stat_got], axis=0)
    peak_got, total_got = stat_got[:, 0], stat_got[:, 1]
    peak = jnp.max(peak_got, axis=0)
    weight = total_got * jnp.exp(peak_got - peak)
    total = jnp.sum(weight, axis=0)
    cross_norm = peak + jnp.log(total)
    weight = weight / total

    def to_token_heads(a):
        lead = a.shape[:-3]
        a = a.reshape(lead + (shard_rows, H, TOK))
        return jnp.swapaxes(a, -1, -2).reshape(lead + (shard_tokens, H))

    weight = jnp.repeat(to_token_heads(weight), HD, axis=-1)
    context_two = (
        ctx_own.astype(F32) * weight[0] + jnp.sum(ctx_got.astype(F32) * weight[1:], axis=0)
    ).astype(BF)

    def to_rows(a):
        a = jnp.broadcast_to(a.reshape(shard_q, 1, TOK, D), (shard_q, piece, TOK, D))
        return a.reshape(shard_tokens, D)

    second_in = to_rows(hidden_one) + product(context_two, full_cout) + full_cobias
    hidden_two, normed_two, inverse_two = layer_norm(second_in, gain_two, shift_two)
    hidden_low2 = hidden_two.astype(BF)

    expanded, third_in = feed_forward(hidden_low2, feed_all, ebias)
    third_in = hidden_two + third_in + full_sbias
    hidden_three, normed_three, inverse_three = layer_norm(third_in, gain_three, shift_three)

    vocab_local = words
    token_targets = jnp.broadcast_to(row_targets.reshape(own_q, 1, TOK), (own_q, piece, TOK))
    local_target = token_targets.reshape(mp_ways, 1, shard_tokens) - mp * vocab_local
    exponents, tops, stats = vocab_forward(hidden_three.astype(BF), local_target, tables, 5)
    stats = jnp.transpose(stats[:, :, :3], (0, 2, 1, 3)).reshape(mp_ways, 3, tokens)
    top = jnp.max(stats[:, 0], axis=0)
    norm_log = top + jnp.log(jnp.sum(stats[:, 1] * jnp.exp(stats[:, 0] - top), axis=0))
    loglik = jnp.sum(stats[:, 2], axis=0) - norm_log
    (loglik_all,) = exchange([(loglik.reshape(tokens // 128, 128), GATHER, DP)], 7)
    loglik_all = loglik_all.reshape(dp_ways, own_q, piece, TOK)
    loglik_all = jnp.transpose(loglik_all, (1, 0, 2, 3)).reshape(own_q, groups, K, TOK)
    doc_logp = jax.nn.log_softmax(doc_all[:, :groups, :K], axis=2)
    joined = doc_logp[..., None] + loglik_all
    marginal = jax.nn.logsumexp(joined, axis=2, keepdims=True)
    question_loss = -jnp.mean(
        lax.dynamic_index_in_dim(marginal[:, :, 0], dp, 0, keepdims=False), axis=1
    )
    posterior = jnp.exp(joined - marginal).reshape(own_q, groups * K, TOK)
    rate = -lax.dynamic_slice_in_dim(posterior, dp * piece, piece, 1)
    by_slot = lambda a: a.reshape(mp_ways, 1, shard_tokens)
    dhidden_three = vocab_back(
        exponents, tops, local_target, by_slot(norm_log), by_slot(rate), tables, 8
    )

    dthird, dgain_three, dshift_three = norm_back(
        dhidden_three, normed_three, inverse_three, gain_three
    )
    dshrink_bias = jnp.sum(dthird, axis=0)
    dshrink_in = dthird.astype(BF)
    dfeed, dexpand_bias, dhidden_two = feed_back(dshrink_in, hidden_low2, expanded, feed_all)
    dexpand_bias = dexpand_bias.reshape(-1)
    feed_dp = lax.psum_scatter(dfeed, DP, scatter_dimension=0, tiled=False)
    dhidden_two = dthird + dhidden_two

    dsecond, dgain_two, dshift_two = norm_back(dhidden_two, normed_two, inverse_two, gain_two)
    dcout_bias = jnp.sum(dsecond, axis=0)
    dcout_in = dsecond.astype(BF)
    dcontext_two = product_back(dcout_in, full_cout).astype(BF)
    middle = jnp.sum(
        (dcontext_two.astype(F32) * context_two.astype(F32)).reshape(shard_tokens, H, HD), axis=-1
    )
    middle = jnp.swapaxes(middle.reshape(shard_rows, TOK, H), 1, 2).reshape(shard_rows, G, GL)
    owners = lambda a: a.reshape(chips, 2, -1, a.shape[-1])
    cast = lambda a: a.astype(BF)
    co_blocks = owners(cast(weight_grad(dcout_in, context_two)))
    stat_all = jnp.stack([cross_norm, middle])
    dkeys, dvalues, dcross_q, key_blocks, value_blocks, dvalue_bias, co_blocks = cross_back(
        used, keys, values, cross_queries, memory_rows, dcontext_two, stat_all, co_blocks, keep, piece,
        padded, 9,
    )
    dcross_low = (dcross_q * SCALE).astype(BF)
    dcquery = weight_grad(hidden_low1, dcross_low)
    dcq_bias = jnp.sum(dcross_low, axis=0, dtype=F32)
    dhidden_one = jnp.sum(dsecond.reshape(shard_q, piece, TOK, D), axis=1).reshape(
        shard_uniq, D
    ) + product_back(dcross_low, full_cquery)

    dfirst, dgain_one, dshift_one = norm_back(dhidden_one, normed_one, inverse_one, gain_one)
    dout_bias = jnp.sum(dfirst, axis=0)
    cq_blocks = owners(cast(dcquery))
    plan = Exchange(
        [(cq_blocks, MOVE1, PAIR), (co_blocks, MOVE, CHIPS)]
    )
    dqkv_bias, self_blocks, out_blocks, dinputs, cq_got, co_got = self_back(
        x_rows, context, queries, self_keys, self_values, full_output, self_weight, keep, dfirst, plan, 12
    )
    dqkv_bias = dqkv_bias[0]
    (cq_blocks,) = sums([(cq_blocks, cq_got, MOVE1, PAIR, PLAIN, BF)])

    vectors = jnp.stack(
        [
            dout_bias,
            dgain_one,
            dshift_one,
            dcout_bias,
            dgain_two,
            dshift_two,
            dshrink_bias,
            dgain_three,
            dshift_three,
            dvalue_bias[0],
            dcq_bias,
            jnp.pad(dqkv_bias, (0, D - 3 * head_cols)),
        ]
    )
    vectors = jnp.concatenate([vectors, dexpand_bias.reshape(-1, D)], axis=0)
    answer_blocks = dinputs.reshape(chips, 2, TOK, D)
    plan = Exchange(
        [(feed_dp, COLS, Z)]
        + [
            (a, MOVE, CHIPS)
            for a in (key_blocks, value_blocks, cq_blocks, answer_blocks)
        ]
        + [(vectors, GATHER, DP)]
    )
    memory_grad, received = memory_back(
        dkeys, dvalues, key_weight, value_weight, rows, slots, padded, plan, 15
    )
    feed_got, key_got, value_got, cq_got, answer_got, vector_all = received
    key_sum, value_sum, cq_sum, co_sum, feed_grad, vector_sum = sums(
        [
            (key_blocks, key_got, MOVE, CHIPS, PLAIN, BF),
            (value_blocks, value_got, MOVE, CHIPS, PLAIN, BF),
            (cq_blocks, cq_got, MOVE, CHIPS, COLUMNS, BF),
            (co_blocks, co_got, MOVE, CHIPS, COLUMNS, BF),
            (feed_dp, feed_got, COLS, Z, PLAIN, F32),
            (vector_all, vector_all, GATHER, DP, PLAIN, F32),
        ]
    )

    expand_grad, shrink_grad = feed_grad[0], feed_grad[1].T

    own_answers = lax.dynamic_index_in_dim(answer_blocks, dp // 2, 0, keepdims=True)
    returned = jnp.concatenate([own_answers, answer_got], axis=0).astype(F32)
    source = lax.rem(dp // 2 + chips - jnp.arange(chips), chips)
    place = (2 * source * piece) // K
    pick = (place[None, :] == jnp.arange(groups)[:, None]).astype(F32)
    answer_part = cast(jnp.sum(pick[:, :, None, None, None] * returned[None], axis=1))

    zblocks = [
        key_sum.reshape(mp_ways, wide_rows, D),
        value_sum.reshape(mp_ways, wide_rows, D),
        cq_sum,
        co_sum,
    ]
    feature_part = lax.dynamic_slice_in_dim(vector_sum[:10], dp * vec, vec, 1)
    *got_z, feature_all, head_all, answer_got, self_got, out_got = exchange(
        [(a, MOVE, Z) for a in zblocks]
        + [(feature_part, GATHER, Z), (vector_sum[10:], GATHER, Z)]
        + [(answer_part, MOVE1, PAIR), (self_blocks, MOVE, CHIPS), (out_blocks, MOVE, CHIPS)],
        16,
    )
    forms = [PLAIN, PLAIN, PLAIN, TURNED]
    key_grad, value_grad, cquery_grad, cout_grad, answer_grad, self_grad, out_grad = sums(
        [(a, b, MOVE, Z, form, F32) for a, b, form in zip(zblocks, got_z, forms)]
        + [
            (answer_part, answer_got, MOVE1, PAIR, PLAIN, F32),
            (self_blocks, self_got, MOVE, CHIPS, PLAIN, F32),
            (out_blocks, out_got, MOVE, CHIPS, TURNED, F32),
        ]
    )
    feature_own = jnp.sum(feature_all, axis=0)
    head_sums = jnp.sum(head_all, axis=0)
    head_own = lax.dynamic_index_in_dim(head_all, mp, 0, keepdims=False)[1]

    def vec_of(i):
        return feature_own[i]

    def of_dp(a, shape):
        a = a.reshape(-1, dp_ways, shape[1])
        return lax.dynamic_index_in_dim(a, dp, 1, keepdims=False)

    def of_mp(a, shape):
        return lax.dynamic_slice_in_dim(of_dp(a.reshape(-1), shape), mp * shape[0], shape[0], 0)

    return (
        question_loss,
        answer_grad,
        memory_grad,
        self_grad[:, :head_cols],
        self_grad[:, head_cols : 2 * head_cols],
        self_grad[:, 2 * head_cols :],
        of_dp(head_own[:head_cols], query_bias.shape),
        of_dp(head_own[2 * head_cols : 3 * head_cols], value_bias.shape),
        out_grad,
        vec_of(0),
        vec_of(1),
        vec_of(2),
        cquery_grad,
        of_mp(head_sums[0], crossq_bias.shape),
        key_grad,
        value_grad,
        lax.dynamic_slice_in_dim(vec_of(9), mp * wide_rows, wide_rows, 0),
        cout_grad,
        vec_of(3),
        vec_of(4),
        vec_of(5),
        expand_grad,
        of_mp(head_sums[2:], expand_bias.shape),
        shrink_grad,
        vec_of(6),
        vec_of(7),
        vec_of(8),
    )


def solution(mesh):
    placed = (
        P(DP, None, None),
        P(DP, None),
        P(DP, None),
        P(DP, MP, None),
        P(DP),
        P(DP, MP),
        P(DP, MP),
        P(DP, MP),
        P(MP, DP),
        P(MP, DP),
        P(MP, DP),
        P(DP),
        P(DP),
        P(DP),
        P(DP, MP),
        P(MP, DP),
        P((DP, MP), None),
        P((DP, MP), None),
        P((DP, MP)),
        P(MP, DP),
        P(DP),
        P(DP),
        P(DP),
        P(DP, MP),
        P(MP, DP),
        P(MP, DP),
        P(DP),
        P(DP),
        P(DP),
        P(MP, DP),
    )
    return jax.shard_map(
        local,
        mesh=mesh,
        in_specs=placed,
        out_specs=(
            P(DP),
            P(DP, None, None),
            P(DP, MP, None),
            P(DP, MP),
            P(DP, MP),
            P(DP, MP),
            P(MP, DP),
            P(MP, DP),
            P(MP, DP),
            P(DP),
            P(DP),
            P(DP),
            P(DP, MP),
            P(MP, DP),
            P((DP, MP), None),
            P((DP, MP), None),
            P((DP, MP)),
            P(MP, DP),
            P(DP),
            P(DP),
            P(DP),
            P(DP, MP),
            P(MP, DP),
            P(MP, DP),
            P(DP),
            P(DP),
            P(DP),
        ),
        check_vma=False,
    )
```

```python
import functools

import jax
import jax.numpy as jnp
from jax import lax
from jax.experimental import pallas as pl
from jax.experimental.pallas import tpu as pltpu
from jax.sharding import PartitionSpec as P

D = 1024
H = 16
HD = 64
TOK = 32
K = 8
G = 4
GH = 4
GC = GH * HD
GL = GH * TOK

EPS = 1e-05
NEG = -1e30
SCALE = 0.125
BF = jnp.bfloat16
F32 = jnp.float32
MESH = pl.DeviceIdType.MESH
DP, MP = "dp", "mp"
GATHER, LATE, MOVE, MOVE1, COLS, NEAR, NEARSWAP, WIDE = range(8)
Z, CHIPS, PAIR = range(3)
PLAIN, COLUMNS, TURNED = range(3)
VMEM_BYTES = 60 * 1024 * 1024


def product(former, latter):
    return jnp.dot(former, latter, preferred_element_type=F32)


def product_back(former, latter):
    return lax.dot_general(former, latter, (((1,), (1,)), ((), ())), preferred_element_type=F32)


def weight_grad(former, latter):
    return lax.dot_general(former, latter, (((0,), (0,)), ((), ())), preferred_element_type=F32)


def layer_norm(entries, norm_gain, norm_shift):
    center = entries - jnp.mean(entries, axis=-1, keepdims=True)
    inverse = lax.rsqrt(jnp.mean(center * center, axis=-1, keepdims=True) + EPS)
    normed = center * inverse
    return (normed * norm_gain + norm_shift, normed, inverse)


def norm_back(upstream, normed, inverse, norm_gain):
    scaled = upstream * norm_gain
    dentries = inverse * (
        scaled
        - jnp.mean(scaled, axis=-1, keepdims=True)
        - normed * jnp.mean(scaled * normed, axis=-1, keepdims=True)
    )
    return (dentries, jnp.sum(upstream * normed, axis=0), jnp.sum(upstream, axis=0))


class Exchange:
    def __init__(self, entries):
        self.dp_ways, self.mp_ways = lax.axis_size(DP), lax.axis_size(MP)
        self.chips = self.dp_ways // 2
        self.ways = {Z: self.mp_ways, CHIPS: self.chips, PAIR: 2, DP: self.dp_ways}
        self.arrays = [entry[0] for entry in entries]
        self.kinds = [entry[1] for entry in entries]
        self.groups = [entry[2] for entry in entries]
        self.count = len(entries)
        shapes = []
        for array, kind, group in entries:
            shape = array.shape
            if kind in (GATHER, LATE):
                shape = (self.ways[group],) + shape
            elif kind == MOVE:
                shape = (self.ways[group] - 1,) + shape[1:]
            elif kind == MOVE1:
                shape = (self.ways[group] - 1, shape[0]) + shape[2:]
            elif kind == COLS:
                shape = (self.ways[group] - 1,) + shape[:-1] + (shape[-1] // self.ways[group],)
            elif kind == NEAR:
                shape = (self.dp_ways,) + shape
            elif kind == NEARSWAP:
                shape = (self.dp_ways,) + shape[1:]
            else:
                shape = (self.dp_ways, self.mp_ways) + shape
            shapes.append(jax.ShapeDtypeStruct(shape, array.dtype))
        self.shapes = shapes
        self.specs = [pl.BlockSpec(memory_space=pl.ANY)] * self.count
        dma = pltpu.SemaphoreType.DMA
        most = max(self.dp_ways, self.mp_ways)
        self.scratch = [dma((self.count, most)) for _ in range(6)] + [dma((self.count,))]

    def bind(self, ins, outs, sems):
        self.ins, self.outs = ins, outs
        self.zs, self.zr, self.cs, self.cr, self.ps, self.pr, self.own = sems
        dp, mp = lax.axis_index(DP), lax.axis_index(MP)
        self.dp, self.mp = dp, mp
        self.parity, self.chip = lax.rem(dp, 2), dp // 2
        self.place = {Z: mp, CHIPS: self.chip, PAIR: self.parity, DP: dp}

    def device(self, group, j):
        if group == Z:
            return (self.dp, j)
        if group == CHIPS:
            return (2 * j + self.parity, self.mp)
        if group == PAIR:
            return (self.dp - self.parity + j, self.mp)
        return (j, self.mp)

    def peer(self, group, off):
        return lax.rem(self.place[group] + off, self.ways[group])

    def remote(self, source, target, send, recv, device):
        return pltpu.make_async_remote_copy(
            src_ref=source,
            dst_ref=target,
            send_sem=send,
            recv_sem=recv,
            device_id=device,
            device_id_type=MESH,
        )

    def meet(self, also=()):
        needed = set(also)
        for kind, group in zip(self.kinds, self.groups):
            if kind in (NEAR, NEARSWAP, WIDE):
                needed |= {CHIPS, PAIR}
                if kind == WIDE:
                    needed.add(Z)
            else:
                needed.add(group)
        barrier = pltpu.get_barrier_semaphore()
        total = 0
        for group in sorted(needed, key=str):
            for off in range(1, self.ways[group]):
                pl.semaphore_signal(
                    barrier,
                    inc=1,
                    device_id=self.device(group, self.peer(group, off)),
                    device_id_type=MESH,
                )
                total += 1
        pl.semaphore_wait(barrier, total)

    def first(self, i):
        kind, group = self.kinds[i], self.groups[i]
        ref, out = self.ins[i], self.outs[i]
        copies = []
        if kind in (NEAR, NEARSWAP):
            return copies
        if kind == WIDE:
            group, slot = Z, out.at[self.dp, self.mp]
        for off in range(1, self.ways[group]):
            peer = self.peer(group, off)
            if kind == WIDE:
                source, target = ref, slot
            elif kind in (GATHER, LATE):
                source, target = ref, out.at[self.place[group]]
            elif kind == MOVE:
                source, target = ref.at[peer], out.at[off - 1]
            elif kind == COLS:
                width = out.shape[-1]
                part = pl.ds(pl.multiple_of(peer * width, width), width)
                source, target = ref.at[:, :, part], out.at[off - 1]
            else:
                source, target = ref.at[:, peer], out.at[off - 1]
            copies.append(
                self.remote(
                    source,
                    target,
                    self.zs.at[i, off - 1],
                    self.zr.at[i, off - 1],
                    self.device(group, peer),
                )
            )
        return copies

    def local(self, i):
        kind, group = self.kinds[i], self.groups[i]
        ref, out = self.ins[i], self.outs[i]
        if kind == WIDE:
            source, target = ref, out.at[self.dp, self.mp]
        elif kind in (GATHER, LATE):
            source, target = ref, out.at[self.place[group]]
        elif kind in (NEAR, NEARSWAP):
            source, target = self.mine(i), out.at[self.dp]
        else:
            return None
        return pltpu.make_async_copy(source, target, self.own.at[i])

    def mine(self, i):
        kind = self.kinds[i]
        if kind == WIDE:
            return self.outs[i].at[self.dp]
        return self.ins[i].at[self.chip] if kind == NEARSWAP else self.ins[i]

    def square(self, i):
        shape = self.shapes[i].shape
        halves = len(shape) > 3 or shape[1] % 32 == 0
        return self.chips == 4 and self.kinds[i] in (NEAR, WIDE) and halves

    def beside(self, chip, k):
        return chip + 1 - 2 * lax.rem(chip, 2) if k == 0 else chip + 2 - 4 * (chip // 2)

    def owner(self, i, k):
        if not self.square(i):
            chip = lax.rem(self.chip + self.chips - k, self.chips)
        elif k == 0:
            chip = self.chip
        elif k < 3:
            chip = self.beside(self.chip, k - 1)
        else:
            chip = self.beside(self.beside(self.chip, 0), 1)
        return 2 * chip + self.parity

    def spread(self, i):
        copies = []
        for k in range(1, 3 if self.square(i) else self.chips):
            peer = self.beside(self.chip, k - 1) if self.square(i) else self.peer(CHIPS, k)
            source = self.ins[i].at[peer] if self.kinds[i] == NEARSWAP else self.mine(i)
            copies.append(
                self.remote(
                    source,
                    self.outs[i].at[self.dp],
                    self.cs.at[i, k - 1],
                    self.cr.at[i, k - 1],
                    self.device(CHIPS, peer),
                )
            )
        return copies

    def forward(self, i, k):
        half = self.outs[i].shape[1] // 2
        part = self.outs[i].at[self.owner(i, k + 1), pl.ds(k * half, half)]
        return self.remote(
            part,
            part,
            self.cs.at[i, 2 + k],
            self.cr.at[i, 2 + k],
            self.device(CHIPS, self.beside(self.chip, 1 - k)),
        )

    def hand(self, i, k):
        owner = self.owner(i, k)
        return self.remote(
            self.mine(i) if k == 0 else self.outs[i].at[owner],
            self.outs[i].at[owner],
            self.ps.at[i, k],
            self.pr.at[i, k],
            self.device(PAIR, 1 - self.parity),
        )

    def begin(self, also=()):
        self.meet(also)
        self.start()

    def start(self):
        for i in range(self.count):
            if self.kinds[i] == LATE:
                continue
            for copy in self.first(i):
                copy.start()
            if self.kinds[i] in (NEAR, NEARSWAP):
                for copy in self.spread(i):
                    copy.start()
                self.hand(i, 0).start()
        for i in range(self.count):
            local = self.local(i)
            if local is not None:
                local.start()

    def finish(self):
        shared = [i for i in range(self.count) if self.kinds[i] in (NEAR, NEARSWAP, WIDE)]
        for i in shared:
            if self.kinds[i] == WIDE:
                for copy in self.first(i):
                    copy.wait()
                self.local(i).wait()
                for copy in self.spread(i):
                    copy.start()
                self.hand(i, 0).start()
        for i in range(self.count):
            if self.kinds[i] == LATE:
                for copy in self.first(i):
                    copy.start()
        for i in shared:
            for k, copy in enumerate(self.spread(i), 1):
                copy.wait_recv()
                if self.square(i):
                    self.forward(i, k - 1).start()
                self.hand(i, k).start()
        for i in shared:
            if self.square(i):
                for k in range(2):
                    self.forward(i, k).wait_recv()
                self.hand(i, 3).start()
        for i in range(self.count):
            if i in shared:
                for copy in self.spread(i):
                    copy.wait_send()
                if self.square(i):
                    for k in range(2):
                        self.forward(i, k).wait_send()
                for off in range(self.chips):
                    self.hand(i, off).wait()
                if self.kinds[i] != WIDE:
                    self.local(i).wait()
            else:
                for copy in self.first(i):
                    copy.wait()
                local = self.local(i)
                if local is not None:
                    local.wait()


def exchange_kernel(plan, *refs):
    count = plan.count
    plan.bind(refs[:count], refs[count : 2 * count], refs[2 * count :])
    plan.begin()
    plan.finish()


def exchange(entries, cid):
    plan = Exchange(entries)
    return pl.pallas_call(
        functools.partial(exchange_kernel, plan),
        out_shape=plan.shapes,
        in_specs=plan.specs,
        out_specs=plan.specs,
        scratch_shapes=plan.scratch,
        compiler_params=pltpu.CompilerParams(collective_id=cid, has_side_effects=True),
    )(*plan.arrays)


def added(array, received, group):
    place = {
        Z: lax.axis_index(MP),
        CHIPS: lax.axis_index(DP) // 2,
        PAIR: lax.rem(lax.axis_index(DP), 2),
        DP: lax.axis_index(DP),
    }[group]
    axis = 1 if group == PAIR else 0
    own = lax.dynamic_index_in_dim(array, place, axis, keepdims=False)
    return own.astype(F32) + jnp.sum(received.astype(F32), axis=0)


def sums_kernel(kinds, shapes, *refs):
    n = len(kinds)
    arrays, received, outs = refs[:n], refs[n : 2 * n], refs[2 * n :]
    dp, mp = lax.axis_index(DP), lax.axis_index(MP)
    place = {Z: mp, CHIPS: dp // 2, PAIR: lax.rem(dp, 2)}
    for array, got, out, (kind, group, form) in zip(arrays, received, outs, kinds):
        if kind == GATHER:
            total = jnp.sum(array[...].astype(F32), axis=0)
        else:
            if kind == MOVE:
                own = array[place[group]]
            elif kind == MOVE1:
                own = array[:, place[group]]
            else:
                width = got.shape[-1]
                own = array[:, :, pl.ds(pl.multiple_of(place[group] * width, width), width)]
            total = own.astype(F32)
            for i in range(got.shape[0]):
                total += got[i].astype(F32)
        if form == COLUMNS:
            width = out.shape[-1]
            for i in range(out.shape[0]):
                out[i] = total[:, i * width : (i + 1) * width].astype(out.dtype)
        elif form == TURNED:
            out[...] = total.T
        else:
            out[...] = total.astype(out.dtype)


def sums(entries):
    mp_ways = lax.axis_size(MP)
    arrays, received, shapes, kinds = [], [], [], []
    for array, got, kind, group, form, dtype in entries:
        shape = got.shape[1:]
        if form == COLUMNS:
            shape = (mp_ways, shape[0], shape[1] // mp_ways)
        elif form == TURNED:
            shape = shape[::-1]
        arrays.append(array)
        received.append(got)
        shapes.append(jax.ShapeDtypeStruct(shape, dtype))
        kinds.append((kind, group, form))
    vmem = pl.BlockSpec(memory_space=pltpu.VMEM)
    return pl.pallas_call(
        functools.partial(sums_kernel, kinds, shapes),
        in_specs=[vmem] * (2 * len(entries)),
        out_specs=[vmem] * len(entries),
        out_shape=shapes,
        compiler_params=pltpu.CompilerParams(vmem_limit_bytes=VMEM_BYTES),
    )(*arrays, *received)


def beside(plan, kernel, inputs, outputs, scratches, *refs):
    n = plan.count
    first, last = pl.program_id(0) == 0, pl.program_id(0) == pl.num_programs(0) - 1
    ins = refs[:inputs]
    sends = refs[inputs : inputs + n]
    outs = refs[inputs + n : inputs + n + outputs]
    lands = refs[inputs + n + outputs : inputs + 2 * n + outputs]
    own = refs[inputs + 2 * n + outputs : inputs + 2 * n + outputs + scratches]
    plan.bind(sends, lands, refs[inputs + 2 * n + outputs + scratches :])
    pl.when(first)(plan.begin)
    kernel(*ins, *outs, *own)
    pl.when(last)(plan.finish)


def memory_call(plan, cid, kernel, name, grid, inputs, in_specs, out_specs, out_shape, scratch, flops):
    return pl.pallas_call(
        functools.partial(beside, plan, kernel, len(inputs), len(out_shape), len(scratch)),
        grid=(grid,),
        in_specs=in_specs + plan.specs,
        out_specs=out_specs + plan.specs,
        out_shape=out_shape + plan.shapes,
        scratch_shapes=scratch + plan.scratch,
        compiler_params=pltpu.CompilerParams(
            vmem_limit_bytes=VMEM_BYTES, collective_id=cid, has_side_effects=True
        ),
        cost_estimate=pl.CostEstimate(flops=flops, bytes_accessed=flops // 200, transcendentals=0),
        name=name,
    )(*inputs, *plan.arrays)


MEM_BLOCK = 16
BACK_BLOCK = 16


def memory_kernel(slots, padded, mem_ref, wk_ref, wv_ref, vb_ref, k_ref, v_ref, rows_ref, wide):
    for c in range(0, D, 128):
        cols = slice(c, c + 128)
        wide[0 : slots * MEM_BLOCK, :] = (
            mem_ref[:, :, cols].reshape(slots * MEM_BLOCK, 128).astype(F32)
        )
        for r in range(MEM_BLOCK):
            own = wide[pl.ds(r, slots, stride=MEM_BLOCK), :]
            rows_ref[r * padded : (r + 1) * padded, cols] = jnp.concatenate(
                [own, jnp.zeros((padded - slots, 128), F32)], axis=0
            ).astype(BF)
    rows = rows_ref[...]
    for c in range(0, D, 512):
        cols = slice(c, c + 512)
        k_ref[:, cols] = product(rows, wk_ref[:, cols]).astype(BF)
        v_ref[:, cols] = (product(rows, wv_ref[:, cols]) + vb_ref[:, cols]).astype(BF)


def memory_products(memory, key_weight, value_weight, vbias, padded, plan, cid):
    rows, slots, _ = memory.shape
    whole = lambda a: pl.BlockSpec(a.shape, lambda i: (0,) * a.ndim)
    out = jax.ShapeDtypeStruct((rows * padded, D), BF)
    out_spec = pl.BlockSpec((MEM_BLOCK * padded, D), lambda i: (i, 0))
    return memory_call(
        plan,
        cid,
        functools.partial(memory_kernel, slots, padded),
        "memory_products",
        rows // MEM_BLOCK,
        [jnp.transpose(memory, (1, 0, 2)), key_weight, value_weight, vbias],
        [
            pl.BlockSpec((slots, MEM_BLOCK, D), lambda i: (0, i, 0)),
            whole(key_weight),
            whole(value_weight),
            whole(vbias),
        ],
        [out_spec] * 3,
        [out] * 3,
        [pltpu.VMEM((-(-slots // 8) * 8 * MEM_BLOCK, 128), F32)],
        4 * rows * padded * D * D,
    )


def memory_grad_kernel(slots, padded, dk_ref, dv_ref, wk_ref, wv_ref, out_ref, wide):
    for c in range(0, D, 256):
        cols = slice(c, c + 256)
        term = product_back(dk_ref[...], wk_ref[cols, :]) + product_back(dv_ref[...], wv_ref[cols, :])
        for part in range(0, 256, 128):
            for r in range(BACK_BLOCK):
                wide[pl.ds(r, slots, stride=BACK_BLOCK), :] = term[
                    r * padded : r * padded + slots, part : part + 128
                ]
            out_ref[:, :, c + part : c + part + 128] = (
                wide[0 : slots * BACK_BLOCK, :].reshape(slots, BACK_BLOCK, 128).astype(BF)
            )


def memory_back(dkeys, dvalues, key_weight, value_weight, rows, slots, padded, plan, cid):
    spec = pl.BlockSpec((BACK_BLOCK * padded, D), lambda i: (i, 0))
    whole = pl.BlockSpec((D, D), lambda i: (0, 0))
    out, *rest = memory_call(
        plan,
        cid,
        functools.partial(memory_grad_kernel, slots, padded),
        "memory_back",
        rows // BACK_BLOCK,
        [dkeys, dvalues, key_weight, value_weight],
        [spec, spec, whole, whole],
        [pl.BlockSpec((slots, BACK_BLOCK, D), lambda i: (0, i, 0))],
        [jax.ShapeDtypeStruct((slots, rows, D), BF)],
        [pltpu.VMEM((-(-slots // 8) * 8 * BACK_BLOCK, 128), F32)],
        4 * rows * padded * D * D,
    )
    return jnp.transpose(out, (1, 0, 2)).astype(F32), rest


def z_copy(source, target, send, recv, device):
    return pltpu.make_async_remote_copy(
        src_ref=source,
        dst_ref=target,
        send_sem=send,
        recv_sem=recv,
        device_id=(lax.axis_index(DP), device),
        device_id_type=MESH,
    )


def z_meet(ways):
    dp, mp = lax.axis_index(DP), lax.axis_index(MP)
    barrier = pltpu.get_barrier_semaphore()
    for off in range(1, ways):
        pl.semaphore_signal(
            barrier, inc=1, device_id=(dp, lax.rem(mp + off, ways)), device_id_type=MESH
        )
    pl.semaphore_wait(barrier, ways - 1)


def nearest(c, ways):
    mp = lax.axis_index(MP)
    left_n, right_n = mp, ways - 1 - mp
    fewer = jnp.minimum(left_n, right_n)
    paired = c <= 2 * fewer
    distance = jnp.where(paired, (c + 1) // 2, c - fewer)
    left = jnp.where(paired, lax.rem(c, 2) == 1, left_n > right_n)
    return jnp.where(left, mp - distance, mp + distance), distance, left, paired


class LineGather:
    def __init__(self, entries, sems, ways):
        self.entries, self.ways = entries, ways
        self.left_send, self.left_recv, self.right_send, self.right_recv, self.own = sems
        self.mp = lax.axis_index(MP)

    def to_right(self, i, source, place, hop):
        held = self.entries[i][1]
        return z_copy(
            source, held.at[place], self.right_send.at[i, hop], self.right_recv.at[i, hop], self.mp + 1
        )

    def to_left(self, i, source, place, hop):
        held = self.entries[i][1]
        return z_copy(
            source, held.at[place], self.left_send.at[i, hop], self.left_recv.at[i, hop], self.mp - 1
        )

    def begin(self):
        mp, every = self.mp, range(len(self.entries))

        @pl.when(mp < self.ways - 1)
        def _():
            for i in every:
                self.to_right(i, self.entries[i][0], mp, 0).start()

        @pl.when(mp > 0)
        def _():
            for i in every:
                self.to_left(i, self.entries[i][0], mp, 0).start()

        for i in every:
            local = pltpu.make_async_copy(self.entries[i][0], self.entries[i][1].at[mp], self.own.at[i])
            local.start()
            local.wait()

    def arrive(self, c, first):
        mp, every = self.mp, range(len(self.entries))
        _, distance, left, paired = nearest(c, self.ways)
        odd = lax.rem(c, 2) == 1
        due = (c > 0) & first & jnp.logical_not(paired & jnp.logical_not(odd))

        @pl.when(due & (left | (paired & odd)))
        def _():
            place = mp - distance
            for i in every:
                held = self.entries[i][1].at[place]
                self.to_right(i, held, place, distance - 1).wait_recv()

                @pl.when(mp < self.ways - 1)
                def _(i=i, held=held):
                    self.to_right(i, held, place, distance).start()

        @pl.when(due & (jnp.logical_not(left) | (paired & odd)))
        def _():
            place = mp + distance
            for i in every:
                held = self.entries[i][1].at[place]
                self.to_left(i, held, place, distance - 1).wait_recv()

                @pl.when(mp > 0)
                def _(i=i, held=held):
                    self.to_left(i, held, place, distance).start()

    def finish(self):
        mp = self.mp
        for hop in range(self.ways - 1):

            @pl.when((mp < self.ways - 1) & (hop <= mp))
            def _(hop=hop):
                for i, (_, held) in enumerate(self.entries):
                    self.to_right(i, held.at[mp - hop], mp - hop, hop).wait_send()

            @pl.when((mp > 0) & (hop <= self.ways - 1 - mp))
            def _(hop=hop):
                for i, (_, held) in enumerate(self.entries):
                    self.to_left(i, held.at[mp + hop], mp + hop, hop).wait_send()


def line_sems(count, ways):
    dma = pltpu.SemaphoreType.DMA
    return [dma((count, ways)) for _ in range(4)] + [dma((count,))]


def feed_sum_kernel(array, got, out):
    width = got.shape[-1]
    start = pl.multiple_of(lax.axis_index(MP) * width, width)
    total = array[:, :, pl.ds(start, width)].astype(F32)
    for i in range(got.shape[0]):
        total += got[i].astype(F32)
    out[...] = total


def feed_sum(array, got, plan, cid):
    whole = lambda shape: pl.BlockSpec(shape, lambda i: (0,) * len(shape))
    shape = got.shape[1:]
    return memory_call(
        plan,
        cid,
        feed_sum_kernel,
        "feed_sum",
        1,
        [array, got],
        [whole(array.shape), whole(got.shape)],
        [whole(shape)],
        [jax.ShapeDtypeStruct(shape, F32)],
        [],
        4 * array.size,
    )


def own_heads(result, keep):
    kept = result * keep
    total = kept[0:TOK]
    for h in range(1, GH):
        total = total + kept[h * TOK : (h + 1) * TOK]
    return total


def cross_kernel(
    ways, per, piece, padded, used_ref, k_ref, v_ref, q_ref, keep_ref, ctx_ref, stat_ref, ctx_got, stat_got,
    ctx_out, stat_out, send, recv,
):
    c, j = pl.program_id(0), pl.program_id(1)
    mp = lax.axis_index(MP)
    span = piece * TOK

    @pl.when((c == 0) & (j == 0))
    def _():
        z_meet(ways)

    keep = keep_ref[...]
    keep_wide = keep.astype(F32)
    slot = lax.broadcasted_iota(jnp.int32, (padded, GL), 0)
    for g in range(G):
        cols = slice(g * GC, (g + 1) * GC)
        query = jnp.concatenate([q_ref[:, cols]] * GH, axis=0) * keep
        scores = product_back(k_ref[:, cols], query)
        for r in range(piece):
            rows = slice(r * padded, (r + 1) * padded)
            seen = slot < used_ref[r]
            own = jnp.where(seen, scores[rows], NEG)
            peak = jnp.max(own, axis=0, keepdims=True)
            exponent = jnp.where(seen, jnp.exp(own - peak), 0.0)
            total = jnp.sum(exponent, axis=0, keepdims=True)
            probs = (exponent * (1.0 / jnp.maximum(total, 1e-30))).astype(BF)
            ctx = own_heads(weight_grad(probs, v_ref[rows, cols]), keep_wide)
            ctx_out[c, pl.ds(j * span + r * TOK, TOK), cols] = ctx.astype(BF)
            stat_out[c, 0, j * piece + r, g : g + 1, :] = peak
            stat_out[c, 1, j * piece + r, g : g + 1, :] = total

    def copies(k):
        to = nearest(ways - 1 - k, ways)[0]
        off = lax.rem(to - mp + ways, ways)
        return [
            z_copy(a.at[k], b.at[off - 1], send.at[i, k], recv.at[i, off - 1], to)
            for i, (a, b) in enumerate([(ctx_out, ctx_got), (stat_out, stat_got)])
        ]

    for k in range(ways - 1):

        @pl.when((c == k) & (j == per - 1))
        def _(k=k):
            for copy in copies(k):
                copy.start()

    @pl.when((c == ways - 1) & (j == per - 1))
    def _():
        ctx_ref[...] = ctx_out[ways - 1]
        stat_ref[...] = stat_out[ways - 1]
        for k in range(ways - 1):
            for copy in copies(k):
                copy.wait_send()
        for off in range(1, ways):
            to = lax.rem(mp + off, ways)
            for i, (a, b) in enumerate([(ctx_out, ctx_got), (stat_out, stat_got)]):
                z_copy(a.at[0], b.at[off - 1], send.at[i, 0], recv.at[i, off - 1], to).wait_recv()


def cross_forward(used, keys, values, queries, keep, piece, padded, cid):
    ways = lax.axis_size(MP)
    per = queries.shape[0] // TOK // ways
    rows = per * ways * piece
    shard = per * piece
    at = lambda c, j: nearest(ways - 1 - c, ways)[0] * per + j
    big = pl.BlockSpec((piece * padded, D), lambda c, j: (at(c, j), 0))
    anywhere = pl.BlockSpec(memory_space=pl.ANY)
    dma = pltpu.SemaphoreType.DMA
    return pl.pallas_call(
        functools.partial(cross_kernel, ways, per, piece, padded),
        grid=(ways, per),
        in_specs=[
            pl.BlockSpec((piece, 1, GL), lambda c, j: (at(c, j), 0, 0)),
            big,
            big,
            pl.BlockSpec((TOK, D), lambda c, j: (at(c, j), 0)),
            pl.BlockSpec((GL, GC), lambda c, j: (0, 0)),
        ],
        out_specs=[
            pl.BlockSpec((shard * TOK, D), lambda c, j: (0, 0)),
            pl.BlockSpec((2, shard, G, GL), lambda c, j: (0, 0, 0, 0)),
            anywhere,
            anywhere,
        ],
        out_shape=[
            jax.ShapeDtypeStruct((shard * TOK, D), BF),
            jax.ShapeDtypeStruct((2, shard, G, GL), F32),
            jax.ShapeDtypeStruct((ways - 1, shard * TOK, D), BF),
            jax.ShapeDtypeStruct((ways - 1, 2, shard, G, GL), F32),
        ],
        scratch_shapes=[
            pltpu.VMEM((ways, shard * TOK, D), BF),
            pltpu.VMEM((ways, 2, shard, G, GL), F32),
            dma((2, ways)),
            dma((2, ways)),
        ],
        compiler_params=pltpu.CompilerParams(
            vmem_limit_bytes=VMEM_BYTES, collective_id=cid, has_side_effects=True
        ),
        cost_estimate=pl.CostEstimate(
            flops=4 * rows * padded * GL * D,
            bytes_accessed=4 * rows * padded * D,
            transcendentals=rows * padded * G * GL,
        ),
    )(used, keys, values, queries, keep)


def cross_back_kernel(
    ways, per, piece, padded, used_ref, k_ref, v_ref, q_ref, keep_ref, rows_ref, dctx_ref, stat_ref, co_ref,
    dk_ref, dv_ref, dq_ref, key_ref, value_ref, vb_ref, co_sum_ref,
    dctx_all, stat_all, dq_out, dq_got, key_sum, value_sum, low, low_got, co_own, co_got,
    left_send, left_recv, right_send, right_recv, own, send, recv, core_send, core_recv,
):
    c, j = pl.program_id(0), pl.program_id(1)
    dp, mp = lax.axis_index(DP), lax.axis_index(MP)
    parity = lax.rem(dp, 2)
    sibling = (dp + 1 - 2 * parity, mp)
    place = nearest(c, ways)[0]
    span = piece * TOK
    line = LineGather(
        [(dctx_ref, dctx_all), (stat_ref, stat_all)],
        (left_send, left_recv, right_send, right_recv, own),
        ways,
    )

    def core_copy(i):
        source, target = [
            (co_ref, co_got),
            (low.at[0], low_got.at[0]),
            (low.at[1], low_got.at[1]),
        ][i]
        return pltpu.make_async_remote_copy(
            src_ref=source.at[:, 1 - parity],
            dst_ref=target,
            send_sem=core_send.at[i],
            recv_sem=core_recv.at[i],
            device_id=sibling,
            device_id_type=MESH,
        )

    def co_local():
        return pltpu.make_async_copy(co_ref.at[:, parity], co_own, own.at[2])

    @pl.when((c == 0) & (j == 0))
    def _():
        barrier = pltpu.get_barrier_semaphore()
        pl.semaphore_signal(barrier, inc=1, device_id=sibling, device_id_type=MESH)
        for off in range(1, ways):
            pl.semaphore_signal(
                barrier, inc=1, device_id=(dp, lax.rem(mp + off, ways)), device_id_type=MESH
            )
        pl.semaphore_wait(barrier, ways)
        line.begin()
        core_copy(0).start()
        co_local().start()
        key_sum[...] = jnp.zeros_like(key_sum)
        value_sum[...] = jnp.zeros_like(value_sum)
        vb_ref[...] = jnp.zeros_like(vb_ref)

    middle_place = (mp > 0) & (mp < ways - 1)
    line.arrive(c, (j == 0) & jnp.logical_not(middle_place & (c == ways - 1)))
    line.arrive(c + 1, (j == 0) & middle_place & (c == ways - 2))
    keep = keep_ref[...]
    keep_wide = keep.astype(F32)
    slot = lax.broadcasted_iota(jnp.int32, (padded, GL), 0)
    for g in range(G):
        cols = slice(g * GC, (g + 1) * GC)
        query = jnp.concatenate([q_ref[:, cols]] * GH, axis=0) * keep
        scores = product_back(k_ref[:, cols], query)
        parts = []
        for r in range(piece):
            rows = slice(r * padded, (r + 1) * padded)
            dctx = dctx_all[place, pl.ds(j * span + r * TOK, TOK), cols]
            dctx = jnp.concatenate([dctx] * GH, axis=0) * keep
            dprobs = product_back(v_ref[rows, cols], dctx)
            seen = slot < used_ref[r]
            norm = stat_all[place, 0, j * piece + r, g : g + 1, :]
            middle = stat_all[place, 1, j * piece + r, g : g + 1, :]
            probs = jnp.where(seen, jnp.exp(scores[rows] - norm), 0.0)
            parts.append((probs * (dprobs - middle)).astype(BF))
            dv_ref[rows, cols] = product(probs.astype(BF), dctx).astype(BF)
        dscores = jnp.concatenate(parts, axis=0)
        dk_ref[:, cols] = product(dscores, query).astype(BF)
        dquery = own_heads(weight_grad(dscores, k_ref[:, cols]), keep_wide)
        dq_out[c, pl.ds(j * TOK, TOK), cols] = dquery.astype(BF)

    def copy(k):
        to = nearest(k, ways)[0]
        off = lax.rem(to - mp + ways, ways)
        return z_copy(dq_out.at[k], dq_got.at[off - 1], send.at[k], recv.at[off - 1], to)

    for k in range(1, ways):

        @pl.when((c == k) & (j == per - 1))
        def _(k=k):
            copy(k).start()

    memory_rows = rows_ref[...]
    vb_ref[...] += jnp.sum(dv_ref[...].astype(F32), axis=0, keepdims=True)
    for start in range(0, D, 512):
        cols = slice(start, start + 512)
        key_sum[:, cols] += weight_grad(memory_rows, dk_ref[:, cols])
        value_sum[:, cols] += weight_grad(memory_rows, dv_ref[:, cols])

    @pl.when((c == ways - 1) & (j == per - 1))
    def _():
        for i, total in enumerate((key_sum, value_sum)):
            low[i] = total[...].astype(BF).reshape(low.shape[1:])
            core_copy(1 + i).start()
        line.finish()
        for k in range(1, ways):
            copy(k).wait_send()
        total = dq_out[0].astype(F32)
        for off in range(1, ways):
            z_copy(
                dq_out.at[0], dq_got.at[off - 1], send.at[0], recv.at[off - 1], lax.rem(mp + off, ways)
            ).wait_recv()
            total += dq_got[off - 1].astype(F32)
        dq_ref[...] = total
        co_local().wait()
        core_copy(0).wait()
        co_sum_ref[...] = (co_own[...].astype(F32) + co_got[...].astype(F32)).astype(BF)
        for i, out in enumerate((key_ref, value_ref)):
            core_copy(1 + i).wait()
            out[...] = (low[i, :, parity].astype(F32) + low_got[i].astype(F32)).astype(BF)


def cross_back(used, keys, values, queries, memory_rows, dctx, stats, co_blocks, keep, piece, padded, cid):
    ways = lax.axis_size(MP)
    per = queries.shape[0] // TOK // ways
    rows = per * ways * piece
    shard = per * piece
    at = lambda c, j: nearest(c, ways)[0] * per + j
    big = pl.BlockSpec((piece * padded, D), lambda c, j: (at(c, j), 0))
    anywhere = pl.BlockSpec(memory_space=pl.ANY)
    chips, _, vec, _ = co_blocks.shape
    half = (chips, vec, D)
    half_spec = pl.BlockSpec(half, lambda c, j: (0, 0, 0))
    half_shape = jax.ShapeDtypeStruct(half, BF)
    line = line_sems(2, ways)
    dma = pltpu.SemaphoreType.DMA
    return pl.pallas_call(
        functools.partial(cross_back_kernel, ways, per, piece, padded),
        grid=(ways, per),
        in_specs=[
            pl.BlockSpec((piece, 1, GL), lambda c, j: (at(c, j), 0, 0)),
            big,
            big,
            pl.BlockSpec((TOK, D), lambda c, j: (at(c, j), 0)),
            pl.BlockSpec((GL, GC), lambda c, j: (0, 0)),
            big,
            anywhere,
            anywhere,
            anywhere,
        ],
        out_specs=[
            big,
            big,
            pl.BlockSpec((per * TOK, D), lambda c, j: (0, 0)),
            half_spec,
            half_spec,
            pl.BlockSpec((1, D), lambda c, j: (0, 0)),
            half_spec,
        ],
        out_shape=[
            jax.ShapeDtypeStruct((rows * padded, D), BF),
            jax.ShapeDtypeStruct((rows * padded, D), BF),
            jax.ShapeDtypeStruct((per * TOK, D), F32),
            half_shape,
            half_shape,
            jax.ShapeDtypeStruct((1, D), F32),
            half_shape,
        ],
        scratch_shapes=[
            pltpu.VMEM((ways, shard * TOK, D), BF),
            pltpu.VMEM((ways, 2, shard, G, GL), F32),
            pltpu.VMEM((ways, per * TOK, D), BF),
            pltpu.VMEM((ways - 1, per * TOK, D), BF),
            pltpu.VMEM((D, D), F32),
            pltpu.VMEM((D, D), F32),
            pltpu.VMEM((2, chips, 2, vec, D), BF),
            pltpu.VMEM((2,) + half, BF),
            pltpu.VMEM(half, BF),
            pltpu.VMEM(half, BF),
            *line[:4],
            dma((3,)),
            dma((ways,)),
            dma((ways,)),
            dma((3,)),
            dma((3,)),
        ],
        compiler_params=pltpu.CompilerParams(
            vmem_limit_bytes=VMEM_BYTES, collective_id=cid, has_side_effects=True
        ),
        cost_estimate=pl.CostEstimate(
            flops=4 * rows * padded * D * D + 10 * rows * padded * GL * D,
            bytes_accessed=10 * rows * padded * D,
            transcendentals=rows * padded * G * GL,
        ),
    )(used, keys, values, queries, keep, memory_rows, dctx, stats, co_blocks)


def table_words(table, start, count):
    if table.shape[0] == 1:
        return table[0, pl.ds(start, count), :]
    return jnp.concatenate([table[i, pl.ds(start, count), :] for i in range(table.shape[0])], axis=-1)


def table_load(table_refs, table, sems, tile, c, t):
    tiles = table.shape[1] // tile
    places = [(ref, j * tile) for ref in table_refs for j in range(ref.shape[1] // tile)]

    def copy(k):
        ref, start = places[k]
        source = ref.at[:, pl.ds(start, tile), :]
        return pltpu.make_async_copy(source, table.at[:, pl.ds(k * tile, tile), :], sems.at[k])

    @pl.when((c == 0) & (t == 0))
    def _():
        for k in range(tiles):
            copy(k).start()

    for k in range(tiles):

        @pl.when((c == 0) & (t == k))
        def _(k=k):
            copy(k).wait()


def vocab_kernel(
    ways, tile, sub, chunk, count, h_ref, target_ref, *refs
):
    table_refs, refs = refs[:count], refs[count:]
    vocab_steps(ways, tile, sub, chunk, table_refs, h_ref, target_ref, *refs)


def vocab_steps(
    ways, tile, sub, chunk, table_refs, h_ref, target_ref, exp_ref, tops_ref, stats_ref,
    table, held, run, stats, table_sem, left_send, left_recv, right_send, right_recv, own,
    stat_send, stat_recv, stat_own,
):
    c, t = pl.program_id(0), pl.program_id(1)
    last = pl.num_programs(1) - 1
    mp = lax.axis_index(MP)
    slot = nearest(c, ways)[0]
    line = LineGather(
        [(h_ref, held)], (left_send, left_recv, right_send, right_recv, own), ways
    )

    def stats_copy(off):
        return z_copy(
            stats,
            stats_ref.at[mp],
            stat_send.at[off - 1],
            stat_recv.at[off - 1],
            lax.rem(mp + off, ways),
        )

    @pl.when((c == 0) & (t == 0))
    def _():
        z_meet(ways)
        line.begin()

    line.arrive(c, t == 0)
    table_load(table_refs, table, table_sem, tile, c, t)

    @pl.when(t == 0)
    def _():
        run[0:1, :] = jnp.full((1, chunk), NEG, F32)
        run[1:3, :] = jnp.zeros((2, chunk), F32)

    tokens = held[slot]
    target = target_ref[slot]
    parts = []
    for i in range(tile // sub):
        start = t * tile + i * sub
        logits = product_back(table_words(table, start, sub), tokens)
        top = jnp.max(logits, axis=0, keepdims=True)
        exponent = jnp.exp(logits - top)
        word = lax.broadcasted_iota(jnp.int32, (sub, chunk), 0) + start
        hit = jnp.where(word == target, logits, 0.0)
        exp_ref[0, i * sub : (i + 1) * sub, :] = exponent.astype(BF)
        tops_ref[0, pl.ds(t * (tile // sub) + i, 1), :] = top
        parts.append(
            (top, jnp.sum(exponent, axis=0, keepdims=True), jnp.sum(hit, axis=0, keepdims=True))
        )
    former = run[0:1, :]
    peak = former
    for top, total, hit in parts:
        peak = jnp.maximum(peak, top)
    sums = run[1:2, :] * jnp.exp(former - peak)
    hits = run[2:3, :]
    for top, total, hit in parts:
        sums += total * jnp.exp(top - peak)
        hits += hit
    run[0:1, :] = peak
    run[1:2, :] = sums
    run[2:3, :] = hits

    @pl.when(t == last)
    def _():
        stats[slot] = run[...]

    @pl.when((c == ways - 1) & (t == last))
    def _():
        for off in range(1, ways):
            stats_copy(off).start()
        local = pltpu.make_async_copy(stats, stats_ref.at[mp], stat_own.at[0])
        local.start()
        line.finish()
        for off in range(1, ways):
            stats_copy(off).wait()
        local.wait()


def vocab_sizes(words):
    tile = 1280 if words % 1280 == 0 else words
    sub = 256 if tile % 256 == 0 else tile
    return tile, sub


def vocab_forward(hidden, target, tables, cid):
    ways = lax.axis_size(MP)
    chunk = hidden.shape[0]
    parts, _, width = tables[0].shape
    words = sum(a.shape[1] for a in tables)
    tile, sub = vocab_sizes(words)
    tiles = words // tile
    top_rows = -(-(words // sub) // 8) * 8
    dma = pltpu.SemaphoreType.DMA
    return pl.pallas_call(
        functools.partial(vocab_kernel, ways, tile, sub, chunk, len(tables)),
        grid=(ways, tiles),
        in_specs=[
            pl.BlockSpec(memory_space=pl.ANY),
            pl.BlockSpec((ways, 1, chunk), lambda c, t: (0, 0, 0)),
            *[pl.BlockSpec(memory_space=pl.ANY)] * len(tables),
        ],
        out_specs=[
            pl.BlockSpec((1, tile, chunk), lambda c, t: (c, t, 0)),
            pl.BlockSpec((1, top_rows, chunk), lambda c, t: (c, 0, 0)),
            pl.BlockSpec(memory_space=pl.ANY),
        ],
        out_shape=[
            jax.ShapeDtypeStruct((ways, words, chunk), BF),
            jax.ShapeDtypeStruct((ways, top_rows, chunk), F32),
            jax.ShapeDtypeStruct((ways, ways, 8, chunk), F32),
        ],
        scratch_shapes=[
            pltpu.VMEM((parts, words, width), BF),
            pltpu.VMEM((ways, chunk, D), BF),
            pltpu.VMEM((8, chunk), F32),
            pltpu.VMEM((ways, 8, chunk), F32),
            dma((tiles,)),
            *line_sems(1, ways),
            dma((ways,)),
            dma((ways,)),
            dma((1,)),
        ],
        compiler_params=pltpu.CompilerParams(
            vmem_limit_bytes=VMEM_BYTES, collective_id=cid, has_side_effects=True
        ),
        cost_estimate=pl.CostEstimate(
            flops=2 * ways * chunk * words * D,
            bytes_accessed=2 * ways * words * D,
            transcendentals=ways * chunk * words,
        ),
    )(hidden, target, *tables)


def vocab_back_kernel(
    ways, tile, sub, chunk, count, exp_ref, tops_ref, target_ref, norm_ref, rate_ref, *refs
):
    table_refs, refs = refs[:count], refs[count:]
    vocab_back_steps(
        ways, tile, sub, chunk, table_refs, exp_ref, tops_ref, target_ref, norm_ref, rate_ref, *refs
    )


def vocab_back_steps(
    ways, tile, sub, chunk, table_refs, exp_ref, tops_ref, target_ref, norm_ref, rate_ref, out_ref,
    table, total, terms, leaving, landing, table_sem, send, recv,
):
    c, t = pl.program_id(0), pl.program_id(1)
    last = pl.num_programs(1) - 1
    mp = lax.axis_index(MP)
    slot = nearest(ways - 1 - c, ways)[0]

    def copy(to):
        right = to > mp
        spot = jnp.where(right | (to < mp - 1), to, ways)
        return z_copy(
            leaving.at[to],
            landing.at[spot],
            send.at[to],
            recv.at[spot],
            jnp.where(right, mp + 1, mp - 1),
        )

    def arrived(spot):
        z_copy(
            leaving.at[0], landing.at[spot], send.at[0], recv.at[spot], lax.rem(mp + 1, ways)
        ).wait_recv()

    @pl.when((c == 0) & (t == 0))
    def _():
        z_meet(ways)

    table_load(table_refs, table, table_sem, tile, c, t)
    target, norm, rate = target_ref[slot], norm_ref[slot], rate_ref[slot]
    term = None
    for i in range(tile // sub):
        start = t * tile + i * sub
        factor = jnp.exp(tops_ref[0, pl.ds(t * (tile // sub) + i, 1), :] - norm) * -rate
        word = lax.broadcasted_iota(jnp.int32, (sub, chunk), 0) + start
        hit = jnp.where(word == target, rate, 0.0)
        dlogits = hit + exp_ref[0, i * sub : (i + 1) * sub, :].astype(F32) * factor
        part = weight_grad(dlogits.astype(BF), table_words(table, start, sub))
        term = part if term is None else term + part

    @pl.when(t == 0)
    def _():
        total[...] = term

    @pl.when(t > 0)
    def _():
        total[...] += term

    for k in range(ways - 1):
        to = nearest(ways - 1 - k, ways)[0]
        beyond = jnp.where(to > mp, mp > 0, mp < ways - 1)

        @pl.when((c == k) & (t == last) & jnp.logical_not(beyond))
        def _(to=to):
            leaving[to] = total[...].astype(BF)
            copy(to).start()

        @pl.when((c == k) & (t == last) & beyond)
        def _(k=k):
            terms[k] = total[...]

    for k in range(ways - 1):
        to = nearest(ways - 1 - k, ways)[0]
        beyond = jnp.where(to > mp, mp > 0, mp < ways - 1)

        @pl.when((c == min(k + 2, ways - 1)) & (t == last) & beyond)
        def _(k=k, to=to):
            arrived(to)
            leaving[to] = (terms[k] + landing[to].astype(F32)).astype(BF)
            copy(to).start()

    @pl.when((c == ways - 1) & (t == last))
    def _():
        out_ref[...] = total[...]

        @pl.when(mp > 0)
        def _():
            arrived(mp)
            out_ref[...] += landing[mp].astype(F32)

        @pl.when(mp < ways - 1)
        def _():
            arrived(ways)
            out_ref[...] += landing[ways].astype(F32)

        for k in range(ways - 1):
            copy(nearest(ways - 1 - k, ways)[0]).wait_send()


def vocab_back(exponents, tops, target, norm, rate, tables, cid):
    ways, words, chunk = exponents.shape
    tile, sub = vocab_sizes(words)
    tiles = words // tile
    whole = pl.BlockSpec((ways, 1, chunk), lambda c, t: (0, 0, 0))
    dma = pltpu.SemaphoreType.DMA
    return pl.pallas_call(
        functools.partial(vocab_back_kernel, ways, tile, sub, chunk, len(tables)),
        grid=(ways, tiles),
        in_specs=[
            pl.BlockSpec((1, tile, chunk), lambda c, t: (ways - 1 - c, t, 0)),
            pl.BlockSpec((1, tops.shape[1], chunk), lambda c, t: (ways - 1 - c, 0, 0)),
            whole,
            whole,
            whole,
            *[pl.BlockSpec(memory_space=pl.ANY)] * len(tables),
        ],
        out_specs=pl.BlockSpec((chunk, D), lambda c, t: (0, 0)),
        out_shape=jax.ShapeDtypeStruct((chunk, D), F32),
        scratch_shapes=[
            pltpu.VMEM((tables[0].shape[0], words, tables[0].shape[2]), BF),
            pltpu.VMEM((chunk, D), F32),
            pltpu.VMEM((ways - 1, chunk, D), F32),
            pltpu.VMEM((ways, chunk, D), BF),
            pltpu.VMEM((ways + 1, chunk, D), BF),
            dma((tiles,)),
            dma((ways,)),
            dma((ways + 1,)),
        ],
        compiler_params=pltpu.CompilerParams(
            vmem_limit_bytes=VMEM_BYTES, collective_id=cid, has_side_effects=True
        ),
        cost_estimate=pl.CostEstimate(
            flops=2 * ways * chunk * words * D, bytes_accessed=2 * ways * words * D, transcendentals=0
        ),
    )(exponents, tops, target, norm, rate, *tables)


HIDDEN_TILE = 512
ROOT_HALF = 0.7071067811865476
ROOT_TAU = 0.3989422804014327


def weight_tile(ref):
    return ref[...].reshape(D, ref.shape[-1])


def feed_kernel(h_ref, expand_ref, bias_ref, shrink_ref, a_ref, out_ref):
    t = pl.program_id(0)
    hidden = product(h_ref[...], weight_tile(expand_ref)) + bias_ref[0]
    a_ref[...] = hidden
    active = (hidden * (0.5 + 0.5 * lax.erf(hidden * ROOT_HALF))).astype(BF)
    term = product_back(active, weight_tile(shrink_ref))

    @pl.when(t == 0)
    def _():
        out_ref[...] = term

    @pl.when(t > 0)
    def _():
        out_ref[...] += term


def feed_specs(weights):
    parts, ways, _, rows, units = weights.shape
    per = units // HIDDEN_TILE
    tile = lambda which: pl.BlockSpec(
        (parts, 1, 1, rows, HIDDEN_TILE), lambda t: (0, t // per, which, 0, t % per)
    )
    bias = pl.BlockSpec((1, 1, HIDDEN_TILE), lambda t: (t, 0, 0))
    return tile(0), bias, tile(1), ways * per


def feed_forward(hidden, weights, bias):
    tokens = hidden.shape[0]
    expand_spec, bias_spec, shrink_spec, tiles = feed_specs(weights)
    whole = pl.BlockSpec((tokens, D), lambda t: (0, 0))
    units = tiles * HIDDEN_TILE
    return pl.pallas_call(
        feed_kernel,
        grid=(tiles,),
        in_specs=[whole, expand_spec, bias_spec, shrink_spec],
        out_specs=[pl.BlockSpec((tokens, HIDDEN_TILE), lambda t: (0, t)), whole],
        out_shape=[
            jax.ShapeDtypeStruct((tokens, units), F32),
            jax.ShapeDtypeStruct((tokens, D), F32),
        ],
        compiler_params=pltpu.CompilerParams(vmem_limit_bytes=VMEM_BYTES),
        cost_estimate=pl.CostEstimate(
            flops=4 * tokens * units * D, bytes_accessed=4 * units * D, transcendentals=tokens * units
        ),
    )(hidden, weights, bias.reshape(tiles, 1, HIDDEN_TILE), weights)


def feed_back_kernel(
    dout_ref, h_ref, a_ref, expand_ref, shrink_ref, dweights_ref, dbias_ref, dh_ref
):
    t = pl.program_id(0)
    dout = dout_ref[...]
    hidden = a_ref[...]
    below = 0.5 + 0.5 * lax.erf(hidden * ROOT_HALF)
    slope = below + hidden * (ROOT_TAU * jnp.exp(-0.5 * hidden * hidden))
    active = (hidden * below).astype(BF)
    dhidden = (slope * product(dout, weight_tile(shrink_ref))).astype(BF)
    dbias_ref[0] = jnp.sum(dhidden.astype(F32), axis=0, keepdims=True)
    parts, _, rows, width = dweights_ref.shape
    dweights_ref[:, 0] = weight_grad(h_ref[...], dhidden).astype(BF).reshape(parts, rows, width)
    dweights_ref[:, 1] = weight_grad(dout, active).astype(BF).reshape(parts, rows, width)
    term = product_back(dhidden, weight_tile(expand_ref))

    @pl.when(t == 0)
    def _():
        dh_ref[...] = term

    @pl.when(t > 0)
    def _():
        dh_ref[...] += term


def feed_back(dout, hidden, before, weights):
    tokens = hidden.shape[0]
    expand_spec, bias_spec, shrink_spec, tiles = feed_specs(weights)
    parts, rows = weights.shape[0], weights.shape[3]
    whole = pl.BlockSpec((tokens, D), lambda t: (0, 0))
    units = tiles * HIDDEN_TILE
    return pl.pallas_call(
        feed_back_kernel,
        grid=(tiles,),
        in_specs=[
            whole,
            whole,
            pl.BlockSpec((tokens, HIDDEN_TILE), lambda t: (0, t)),
            expand_spec,
            shrink_spec,
        ],
        out_specs=[
            pl.BlockSpec((parts, 2, rows, HIDDEN_TILE), lambda t: (0, 0, 0, t)),
            bias_spec,
            whole,
        ],
        out_shape=[
            jax.ShapeDtypeStruct((parts, 2, rows, units), BF),
            jax.ShapeDtypeStruct((tiles, 1, HIDDEN_TILE), F32),
            jax.ShapeDtypeStruct((tokens, D), F32),
        ],
        compiler_params=pltpu.CompilerParams(vmem_limit_bytes=VMEM_BYTES),
        cost_estimate=pl.CostEstimate(
            flops=8 * tokens * units * D, bytes_accessed=8 * units * D, transcendentals=2 * tokens * units
        ),
    )(dout, hidden, before, weights, weights)


def query_kernel(
    ways, part_ref, x_ref, bias_ref, gain_ref, shift_ref, cq_ref, cqb_ref,
    hidden_ref, normed_ref, inverse_ref, low_ref, full_ref, all_ref, got, queries, send, recv, own,
):
    mp = lax.axis_index(MP)
    count = hidden_ref.shape[0]

    def part_copy(off):
        to = lax.rem(mp + off, ways)
        return z_copy(part_ref.at[to], got.at[off - 1], send.at[0, off], recv.at[0, off], to)

    def query_copy(off):
        to = lax.rem(mp + off, ways)
        return z_copy(queries, all_ref.at[mp], send.at[1, off], recv.at[1, off], to)

    z_meet(ways)
    for off in range(1, ways):
        part_copy(off).start()
    width = full_ref.shape[1] // ways
    for m in range(ways):
        full_ref[:, m * width : (m + 1) * width] = cq_ref[:, m].reshape(D, width)
    rows = pl.ds(pl.multiple_of(mp * count, count), count)
    total = x_ref[rows, :].astype(F32) + part_ref[mp].astype(F32) + bias_ref[...]
    for off in range(1, ways):
        part_copy(off).wait()
        total += got[off - 1].astype(F32)
    hidden, normed, inverse = layer_norm(total, gain_ref[...], shift_ref[...])
    hidden_ref[...] = hidden
    normed_ref[...] = normed
    inverse_ref[...] = inverse
    low_ref[...] = hidden.astype(BF)
    queries[...] = ((product(hidden.astype(BF), full_ref[...]) + cqb_ref[...]) * SCALE).astype(BF)
    for off in range(1, ways):
        query_copy(off).start()
    local = pltpu.make_async_copy(queries, all_ref.at[mp], own.at[0])
    local.start()
    for off in range(1, ways):
        query_copy(off).wait()
    local.wait()


def cross_inputs(partial, x, bias, gain, shift, cquery, cqbias, cid):
    ways, count, _ = partial.shape
    row = lambda a: a.astype(F32).reshape(1, D)
    vmem = pl.BlockSpec(memory_space=pltpu.VMEM)
    dma = pltpu.SemaphoreType.DMA
    return pl.pallas_call(
        functools.partial(query_kernel, ways),
        in_specs=[vmem] * 7,
        out_specs=[vmem] * 5 + [pl.BlockSpec(memory_space=pl.ANY)],
        out_shape=[
            jax.ShapeDtypeStruct((count, D), F32),
            jax.ShapeDtypeStruct((count, D), F32),
            jax.ShapeDtypeStruct((count, 1), F32),
            jax.ShapeDtypeStruct((count, D), BF),
            jax.ShapeDtypeStruct((D, D), BF),
            jax.ShapeDtypeStruct((ways, count, D), BF),
        ],
        scratch_shapes=[
            pltpu.VMEM((ways - 1, count, D), BF),
            pltpu.VMEM((count, D), BF),
            dma((2, ways)),
            dma((2, ways)),
            dma((1,)),
        ],
        compiler_params=pltpu.CompilerParams(
            vmem_limit_bytes=VMEM_BYTES, collective_id=cid, has_side_effects=True
        ),
    )(partial, x, row(bias), row(gain), row(shift), cquery, row(cqbias))


def self_back_kernel(
    plan, x_ref, ctx_ref, q_ref, k_ref, v_ref, wo_ref, wqkv_ref, keep_ref, dfirst_ref, *refs
):
    n = plan.count
    sends, rest = refs[:n], refs[n:]
    bias_ref, dself_ref, dwo_ref, din_ref = rest[:4]
    lands, rest = rest[4 : 4 + n], rest[4 + n :]
    dctx, dqkv, part, part_got, din, dself, dself_got, dwo, dwo_got, dout, dout_all = rest[:11]
    send, recv, own = rest[11:14]
    plan.bind(sends, lands, rest[14:])
    ways = plan.mp_ways
    mp, parity = plan.mp, plan.parity

    def part_copy(off):
        to = plan.peer(Z, off)
        return z_copy(part.at[to], part_got.at[off - 1], send.at[0, off], recv.at[0, off], to)

    def din_copy(off):
        return z_copy(din, din_ref.at[mp], send.at[1, off], recv.at[1, off], plan.peer(Z, off))

    def core_copies():
        return [
            plan.remote(a.at[:, 1 - parity], b, send.at[2, i], recv.at[2, i], plan.device(PAIR, 1 - parity))
            for i, (a, b) in enumerate([(dself, dself_got), (dwo, dwo_got)])
        ]

    def dout_copy(off):
        return z_copy(dout, dout_all.at[mp], send.at[3, off], recv.at[3, off], plan.peer(Z, off))

    plan.meet((Z, PAIR))
    dout[...] = dfirst_ref[...].astype(BF)
    for off in range(1, ways):
        dout_copy(off).start()
    plan.start()
    dout_all[mp] = dout[...]
    keep = keep_ref[...]
    keep_wide = keep.astype(F32)
    for off in range(1, ways):
        dout_copy(off).wait()
    upstreams = dout_all[...].reshape(x_ref.shape)
    dctx[...] = product_back(upstreams, wo_ref[...]).astype(BF)
    key_place = lax.broadcasted_iota(jnp.int32, (TOK, GL), 0)
    query_place = lax.rem(lax.broadcasted_iota(jnp.int32, (TOK, GL), 1), TOK)
    seen = key_place <= query_place

    @pl.loop(0, x_ref.shape[0] // TOK)
    def _(question):
        rows = pl.ds(pl.multiple_of(question * TOK, TOK), TOK)
        keys, values = k_ref[rows, :], v_ref[rows, :]
        query = jnp.concatenate([q_ref[rows, :]] * GH, axis=0) * keep
        upstream = jnp.concatenate([dctx[rows, :]] * GH, axis=0) * keep
        scores = jnp.where(seen, product_back(keys, query), NEG)
        exponent = jnp.exp(scores - jnp.max(scores, axis=0, keepdims=True))
        probs = exponent / jnp.sum(exponent, axis=0, keepdims=True)
        dprobs = product_back(values, upstream)
        middle = jnp.sum(probs * dprobs, axis=0, keepdims=True)
        dscores = (probs * (dprobs - middle)).astype(BF)
        dquery = own_heads(weight_grad(dscores, keys), keep_wide)
        dqkv[rows, 0:GC] = (dquery * SCALE).astype(BF)
        dqkv[rows, GC : 2 * GC] = product(dscores, query).astype(BF)
        dqkv[rows, 2 * GC : 3 * GC] = product(probs.astype(BF), upstream).astype(BF)

    grads = dqkv[...]
    part[...] = product_back(grads, wqkv_ref[...]).astype(BF).reshape(part.shape)
    for off in range(1, ways):
        part_copy(off).start()
    dself[...] = weight_grad(x_ref[...], grads).astype(BF).reshape(dself.shape)
    dwo[...] = weight_grad(upstreams, ctx_ref[...]).astype(BF).reshape(dwo.shape)
    for copy in core_copies():
        copy.start()
    bias_ref[...] = jnp.sum(grads.astype(F32), axis=0, keepdims=True)
    total = dfirst_ref[...] + part[mp].astype(F32)
    for off in range(1, ways):
        part_copy(off).wait_recv()
        total += part_got[off - 1].astype(F32)
    din[...] = total.astype(BF)
    for off in range(1, ways):
        din_copy(off).start()
    local = pltpu.make_async_copy(din, din_ref.at[mp], own.at[0])
    local.start()
    for copy in core_copies():
        copy.wait()
    dself_ref[...] = (dself[:, parity].astype(F32) + dself_got[...].astype(F32)).astype(BF)
    dwo_ref[...] = (dwo[:, parity].astype(F32) + dwo_got[...].astype(F32)).astype(BF)
    plan.finish()
    for off in range(1, ways):
        part_copy(off).wait_send()
        din_copy(off).wait()
    local.wait()


def self_back(x, ctx, queries, keys, values, wo, wqkv, keep, dfirst, plan, cid):
    uniq, shard = x.shape[0], dfirst.shape[0]
    ways, chips = plan.mp_ways, plan.chips
    vec = D // plan.dp_ways
    inputs = [x, ctx, queries, keys, values, wo, wqkv, keep, dfirst]
    vmem = pl.BlockSpec(memory_space=pltpu.VMEM)
    dma = pltpu.SemaphoreType.DMA
    cols = wqkv.shape[1]
    return pl.pallas_call(
        functools.partial(self_back_kernel, plan),
        in_specs=[vmem] * len(inputs) + plan.specs,
        out_specs=[vmem, vmem, vmem, pl.BlockSpec(memory_space=pl.ANY)] + plan.specs,
        out_shape=[
            jax.ShapeDtypeStruct((1, cols), F32),
            jax.ShapeDtypeStruct((chips, vec, cols), BF),
            jax.ShapeDtypeStruct((chips, vec, GC), BF),
            jax.ShapeDtypeStruct((ways, shard, D), BF),
        ]
        + plan.shapes,
        scratch_shapes=[
            pltpu.VMEM((uniq, GC), BF),
            pltpu.VMEM((uniq, cols), BF),
            pltpu.VMEM((ways, shard, D), BF),
            pltpu.VMEM((ways - 1, shard, D), BF),
            pltpu.VMEM((shard, D), BF),
            pltpu.VMEM((chips, 2, vec, cols), BF),
            pltpu.VMEM((chips, vec, cols), BF),
            pltpu.VMEM((chips, 2, vec, GC), BF),
            pltpu.VMEM((chips, vec, GC), BF),
            pltpu.VMEM((shard, D), BF),
            pltpu.VMEM((ways, shard, D), BF),
            dma((4, ways)),
            dma((4, ways)),
            dma((1,)),
            *plan.scratch,
        ],
        compiler_params=pltpu.CompilerParams(
            vmem_limit_bytes=VMEM_BYTES, collective_id=cid, has_side_effects=True
        ),
        cost_estimate=pl.CostEstimate(
            flops=4 * uniq * D * cols, bytes_accessed=8 * uniq * D, transcendentals=uniq * GL
        ),
    )(*inputs, *plan.arrays)


def self_probs(queries, key_heads):
    causal = (
        lax.broadcasted_iota(jnp.int32, (TOK, TOK), 1)
        <= lax.broadcasted_iota(jnp.int32, (TOK, TOK), 0)
    )[None, None]
    scores = jnp.einsum("rqhe,rkhe->rhqk", queries, key_heads, preferred_element_type=F32)
    return jax.nn.softmax(jnp.where(causal, scores, NEG), axis=-1)


def column_parts(gathered):
    return jnp.concatenate([gathered[i] for i in range(gathered.shape[0])], axis=-1)


def block_rows(array, ways):
    rows, columns = array.shape
    width = columns // ways
    return jnp.stack([array[:, i * width : (i + 1) * width] for i in range(ways)])


def local(
    answers,
    targets,
    doc_scores,
    memory,
    lengths,
    self_query,
    self_key,
    self_value,
    query_bias,
    value_bias,
    self_output,
    output_bias,
    first_gain,
    first_shift,
    cross_query,
    crossq_bias,
    cross_key,
    cross_value,
    crossv_bias,
    cross_output,
    crosso_bias,
    second_gain,
    second_shift,
    expand_weight,
    expand_bias,
    shrink_weight,
    shrink_bias,
    third_gain,
    third_shift,
    word_table,
):
    dp_ways, mp_ways = lax.axis_size(DP), lax.axis_size(MP)
    chips = dp_ways // 2
    dp, mp = lax.axis_index(DP), lax.axis_index(MP)
    groups = answers.shape[0]
    rows, slots, _ = memory.shape
    piece = rows // dp_ways
    own_q = dp_ways
    uniq = own_q * TOK
    tokens = rows * TOK
    padded = -(-slots // 16) * 16
    shard_rows = rows // mp_ways
    shard_tokens = shard_rows * TOK
    shard_q = own_q // mp_ways
    shard_uniq = shard_q * TOK
    local_heads = H // mp_ways
    head_cols = local_heads * HD
    hidden_cols = expand_weight.shape[1]
    vec = D // dp_ways

    vectors = (
        output_bias,
        first_gain,
        first_shift,
        crosso_bias,
        second_gain,
        second_shift,
        shrink_bias,
        third_gain,
        third_shift,
        crossv_bias,
    )
    matrices = (query_bias, value_bias, crossq_bias, expand_bias)
    starts, top = [], 16
    for matrix in matrices:
        starts.append(top)
        top += -(-matrix.shape[0] // 8) * 8
    small_rows = -(-top // 16) * 16
    row_of = lax.broadcasted_iota(jnp.int32, (small_rows, 128), 0)
    small = jnp.zeros((small_rows, 128), BF)
    for i, vector in enumerate(vectors):
        vector = jnp.pad(vector, (0, 128 - vector.shape[0]))
        small = jnp.where(row_of == i, vector[None, :], small)
    for start, matrix in zip(starts, matrices):
        count, width = matrix.shape
        small += jnp.pad(matrix, ((start, small_rows - start - count), (0, 128 - width)))
    wide_rows = cross_key.shape[0]
    self_shard = jnp.concatenate([self_query, self_key, self_value], axis=1)
    target_rows = jnp.pad(targets, ((0, 8 - groups), (0, 128 - TOK)))
    doc_rows = jnp.pad(doc_scores, ((0, 8 - groups), (0, 128 - K)))
    if chips == groups:
        wanted = answers
    else:
        wanted = jnp.stack([answers[(2 * c * piece) // K] for c in range(chips)])
    feed_shard = jnp.stack([expand_weight, shrink_weight.T])
    key_all, value_all, small_all, cquery_z, cout_z = exchange(
        [
            (cross_key, WIDE, Z),
            (cross_value, WIDE, Z),
            (small, WIDE, Z),
            (cross_query, LATE, Z),
            (cross_output, LATE, Z),
        ],
        0,
    )
    (full_obias, gain_one, shift_one, full_cobias, gain_two, shift_two, full_sbias, gain_three, shift_three) = [
        small_all[:, 0, i, :vec].reshape(D) for i in range(9)
    ]
    cvbias = small_all[:, :, 9, :wide_rows].reshape(1, D)

    def head_bias(i):
        count, width = matrices[i].shape
        part = small_all[:, :, starts[i] : starts[i] + count, :width]
        return jnp.transpose(part, (1, 2, 0, 3)).reshape(mp_ways, -1)

    mine = lambda a: lax.dynamic_index_in_dim(a, mp, 0, keepdims=False)
    qbias = mine(head_bias(0))
    vbias = mine(head_bias(1))
    cqbias = head_bias(2).reshape(-1)
    ebias = head_bias(3).reshape(-1)
    key_weight = key_all.reshape(D, D)
    value_weight = value_all.reshape(D, D)

    plan = Exchange(
        [
            (feed_shard, GATHER, Z),
            (self_shard, NEAR, Z),
            (self_output, NEAR, Z),
            (target_rows, NEAR, Z),
            (doc_rows, NEAR, Z),
            (wanted, NEARSWAP, Z),
            (cquery_z, NEAR, Z),
            (cout_z, NEAR, Z),
        ]
    )
    (keys, values, memory_rows, feed_z, self_all, output_all, target_all, doc_all, x_all, cquery_all, cout_all) = (
        memory_products(memory, key_weight, value_weight, cvbias, padded, plan, 1)
    )
    words = word_table.shape[0]
    early = words // 1280 * 4 // 5 * 1280 if words % 1280 == 0 else 0
    tables = []
    if early:
        part = lax.all_gather(word_table[:early], DP, axis=0, tiled=False)
        feed_z, part = lax.optimization_barrier((feed_z, part))
        tables.append(part)
    feed_all = lax.all_gather(feed_z, DP, axis=0, tiled=False)
    tables.append(lax.all_gather(word_table[early:], DP, axis=0, tiled=False))
    if word_table.shape[1] < 128:
        tables = [column_parts(a)[None] for a in tables]
    rows_first = lambda a: jnp.transpose(a, (0, 2, 1, 3)).reshape(dp_ways * a.shape[2], -1)
    columns_first = lambda a: column_parts(a.reshape(dp_ways, -1, a.shape[-1]))
    self_weight = self_all.reshape(D, 3 * head_cols)
    full_output = column_parts(output_all)
    my_group = (dp * piece) // K
    row_targets = lax.dynamic_index_in_dim(
        target_all[:, :groups, :TOK], my_group, 1, keepdims=False
    )
    x_rows = x_all.reshape(uniq, D)

    qkv = product(x_rows, self_weight)
    queries = ((qkv[:, :head_cols] + qbias) * SCALE).astype(BF)
    self_keys = qkv[:, head_cols : 2 * head_cols].astype(BF)
    self_values = (qkv[:, 2 * head_cols :] + vbias).astype(BF)
    heads = lambda a: a.reshape(own_q, TOK, local_heads, HD)
    probs = self_probs(heads(queries), heads(self_keys))
    context = jnp.einsum(
        "rhqk,rkhe->rqhe", probs.astype(BF), heads(self_values), preferred_element_type=F32
    )
    context = context.astype(BF).reshape(uniq, head_cols)
    partial = product(context, full_output).astype(BF).reshape(mp_ways, shard_uniq, D)
    hidden_one, normed_one, inverse_one, hidden_low1, full_cquery, cross_queries = cross_inputs(
        partial, x_rows, full_obias, gain_one, shift_one, cquery_all, cqbias, 2
    )
    full_cout = columns_first(cout_all)
    cross_queries = cross_queries.reshape(uniq, D)

    used = jnp.clip(lengths - mp * slots, 0, slots).astype(jnp.int32)
    used = jnp.broadcast_to(used[:, None, None], (rows, 1, GL))
    keep = (
        lax.broadcasted_iota(jnp.int32, (GL, GC), 0) // TOK
        == lax.broadcasted_iota(jnp.int32, (GL, GC), 1) // HD
    ).astype(BF)
    ctx_own, stat_own, ctx_got, stat_got = cross_forward(
        used, keys, values, cross_queries, keep, piece, padded, 4
    )
    stat_got = jnp.concatenate([stat_own[None], stat_got], axis=0)
    peak_got, total_got = stat_got[:, 0], stat_got[:, 1]
    peak = jnp.max(peak_got, axis=0)
    weight = total_got * jnp.exp(peak_got - peak)
    total = jnp.sum(weight, axis=0)
    cross_norm = peak + jnp.log(total)
    weight = weight / total

    def to_token_heads(a):
        lead = a.shape[:-3]
        a = a.reshape(lead + (shard_rows, H, TOK))
        return jnp.swapaxes(a, -1, -2).reshape(lead + (shard_tokens, H))

    weight = jnp.repeat(to_token_heads(weight), HD, axis=-1)
    context_two = (
        ctx_own.astype(F32) * weight[0] + jnp.sum(ctx_got.astype(F32) * weight[1:], axis=0)
    ).astype(BF)

    def to_rows(a):
        a = jnp.broadcast_to(a.reshape(shard_q, 1, TOK, D), (shard_q, piece, TOK, D))
        return a.reshape(shard_tokens, D)

    second_in = to_rows(hidden_one) + product(context_two, full_cout) + full_cobias
    hidden_two, normed_two, inverse_two = layer_norm(second_in, gain_two, shift_two)
    hidden_low2 = hidden_two.astype(BF)

    expanded, third_in = feed_forward(hidden_low2, feed_all, ebias)
    third_in = hidden_two + third_in + full_sbias
    hidden_three, normed_three, inverse_three = layer_norm(third_in, gain_three, shift_three)

    vocab_local = words
    token_targets = jnp.broadcast_to(row_targets.reshape(own_q, 1, TOK), (own_q, piece, TOK))
    local_target = token_targets.reshape(mp_ways, 1, shard_tokens) - mp * vocab_local
    exponents, tops, stats = vocab_forward(hidden_three.astype(BF), local_target, tables, 5)
    stats = jnp.transpose(stats[:, :, :3], (0, 2, 1, 3)).reshape(mp_ways, 3, tokens)
    top = jnp.max(stats[:, 0], axis=0)
    norm_log = top + jnp.log(jnp.sum(stats[:, 1] * jnp.exp(stats[:, 0] - top), axis=0))
    loglik = jnp.sum(stats[:, 2], axis=0) - norm_log
    (loglik_all,) = exchange([(loglik.reshape(tokens // 128, 128), GATHER, DP)], 7)
    loglik_all = loglik_all.reshape(dp_ways, own_q, piece, TOK)
    loglik_all = jnp.transpose(loglik_all, (1, 0, 2, 3)).reshape(own_q, groups, K, TOK)
    doc_logp = jax.nn.log_softmax(doc_all[:, :groups, :K], axis=2)
    joined = doc_logp[..., None] + loglik_all
    marginal = jax.nn.logsumexp(joined, axis=2, keepdims=True)
    question_loss = -jnp.mean(
        lax.dynamic_index_in_dim(marginal[:, :, 0], dp, 0, keepdims=False), axis=1
    )
    posterior = jnp.exp(joined - marginal).reshape(own_q, groups * K, TOK)
    rate = -lax.dynamic_slice_in_dim(posterior, dp * piece, piece, 1)
    by_slot = lambda a: a.reshape(mp_ways, 1, shard_tokens)
    dhidden_three = vocab_back(
        exponents, tops, local_target, by_slot(norm_log), by_slot(rate), tables, 8
    )

    dthird, dgain_three, dshift_three = norm_back(
        dhidden_three, normed_three, inverse_three, gain_three
    )
    dshrink_bias = jnp.sum(dthird, axis=0)
    dshrink_in = dthird.astype(BF)
    dfeed, dexpand_bias, dhidden_two = feed_back(dshrink_in, hidden_low2, expanded, feed_all)
    dexpand_bias = dexpand_bias.reshape(-1)
    feed_dp = lax.psum_scatter(dfeed, DP, scatter_dimension=0, tiled=False)
    dhidden_two = dthird + dhidden_two

    dsecond, dgain_two, dshift_two = norm_back(dhidden_two, normed_two, inverse_two, gain_two)
    dcout_bias = jnp.sum(dsecond, axis=0)
    dcout_in = dsecond.astype(BF)
    dcontext_two = product_back(dcout_in, full_cout).astype(BF)
    middle = jnp.sum(
        (dcontext_two.astype(F32) * context_two.astype(F32)).reshape(shard_tokens, H, HD), axis=-1
    )
    middle = jnp.swapaxes(middle.reshape(shard_rows, TOK, H), 1, 2).reshape(shard_rows, G, GL)
    owners = lambda a: a.reshape(chips, 2, -1, a.shape[-1])
    cast = lambda a: a.astype(BF)
    co_blocks = owners(cast(weight_grad(dcout_in, context_two)))
    stat_all = jnp.stack([cross_norm, middle])
    dkeys, dvalues, dcross_q, key_blocks, value_blocks, dvalue_bias, co_blocks = cross_back(
        used, keys, values, cross_queries, memory_rows, dcontext_two, stat_all, co_blocks, keep, piece,
        padded, 9,
    )
    dcross_low = (dcross_q * SCALE).astype(BF)
    dcquery = weight_grad(hidden_low1, dcross_low)
    dcq_bias = jnp.sum(dcross_low, axis=0, dtype=F32)
    dhidden_one = jnp.sum(dsecond.reshape(shard_q, piece, TOK, D), axis=1).reshape(
        shard_uniq, D
    ) + product_back(dcross_low, full_cquery)

    dfirst, dgain_one, dshift_one = norm_back(dhidden_one, normed_one, inverse_one, gain_one)
    dout_bias = jnp.sum(dfirst, axis=0)
    cq_blocks = owners(cast(dcquery))
    plan = Exchange(
        [(cq_blocks, MOVE1, PAIR), (co_blocks, MOVE, CHIPS)]
    )
    dqkv_bias, self_blocks, out_blocks, dinputs, cq_got, co_got = self_back(
        x_rows, context, queries, self_keys, self_values, full_output, self_weight, keep, dfirst, plan, 12
    )
    dqkv_bias = dqkv_bias[0]
    (cq_blocks,) = sums([(cq_blocks, cq_got, MOVE1, PAIR, PLAIN, BF)])

    vectors = jnp.stack(
        [
            dout_bias,
            dgain_one,
            dshift_one,
            dcout_bias,
            dgain_two,
            dshift_two,
            dshrink_bias,
            dgain_three,
            dshift_three,
            dvalue_bias[0],
            dcq_bias,
            jnp.pad(dqkv_bias, (0, D - 3 * head_cols)),
        ]
    )
    vectors = jnp.concatenate([vectors, dexpand_bias.reshape(-1, D)], axis=0)
    answer_blocks = dinputs.reshape(chips, 2, TOK, D)
    plan = Exchange(
        [(feed_dp, COLS, Z)]
        + [
            (a, MOVE, CHIPS)
            for a in (key_blocks, value_blocks, cq_blocks, answer_blocks)
        ]
        + [(vectors, GATHER, DP)]
    )
    memory_grad, received = memory_back(
        dkeys, dvalues, key_weight, value_weight, rows, slots, padded, plan, 15
    )
    feed_got, key_got, value_got, cq_got, answer_got, vector_all = received
    key_sum, value_sum, cq_sum, co_sum, vector_sum = sums(
        [
            (key_blocks, key_got, MOVE, CHIPS, PLAIN, BF),
            (value_blocks, value_got, MOVE, CHIPS, PLAIN, BF),
            (cq_blocks, cq_got, MOVE, CHIPS, COLUMNS, BF),
            (co_blocks, co_got, MOVE, CHIPS, COLUMNS, BF),
            (vector_all, vector_all, GATHER, DP, PLAIN, F32),
        ]
    )

    own_answers = lax.dynamic_index_in_dim(answer_blocks, dp // 2, 0, keepdims=True)
    returned = jnp.concatenate([own_answers, answer_got], axis=0).astype(F32)
    source = lax.rem(dp // 2 + chips - jnp.arange(chips), chips)
    place = (2 * source * piece) // K
    pick = (place[None, :] == jnp.arange(groups)[:, None]).astype(F32)
    answer_part = cast(jnp.sum(pick[:, :, None, None, None] * returned[None], axis=1))

    zblocks = [
        key_sum.reshape(mp_ways, wide_rows, D),
        value_sum.reshape(mp_ways, wide_rows, D),
        cq_sum,
        co_sum,
    ]
    feature_part = lax.dynamic_slice_in_dim(vector_sum[:10], dp * vec, vec, 1)
    plan = Exchange(
        [(a, MOVE, Z) for a in zblocks]
        + [(feature_part, GATHER, Z), (vector_sum[10:], GATHER, Z)]
        + [(answer_part, MOVE1, PAIR), (self_blocks, MOVE, CHIPS), (out_blocks, MOVE, CHIPS)]
    )
    feed_grad, *got_z, feature_all, head_all, answer_got, self_got, out_got = feed_sum(
        feed_dp, feed_got, plan, 16
    )
    expand_grad, shrink_grad = feed_grad[0], feed_grad[1].T
    forms = [PLAIN, PLAIN, PLAIN, TURNED]
    key_grad, value_grad, cquery_grad, cout_grad, answer_grad, self_grad, out_grad = sums(
        [(a, b, MOVE, Z, form, F32) for a, b, form in zip(zblocks, got_z, forms)]
        + [
            (answer_part, answer_got, MOVE1, PAIR, PLAIN, F32),
            (self_blocks, self_got, MOVE, CHIPS, PLAIN, F32),
            (out_blocks, out_got, MOVE, CHIPS, TURNED, F32),
        ]
    )
    feature_own = jnp.sum(feature_all, axis=0)
    head_sums = jnp.sum(head_all, axis=0)
    head_own = lax.dynamic_index_in_dim(head_all, mp, 0, keepdims=False)[1]

    def vec_of(i):
        return feature_own[i]

    def of_dp(a, shape):
        a = a.reshape(-1, dp_ways, shape[1])
        return lax.dynamic_index_in_dim(a, dp, 1, keepdims=False)

    def of_mp(a, shape):
        return lax.dynamic_slice_in_dim(of_dp(a.reshape(-1), shape), mp * shape[0], shape[0], 0)

    return (
        question_loss,
        answer_grad,
        memory_grad,
        self_grad[:, :head_cols],
        self_grad[:, head_cols : 2 * head_cols],
        self_grad[:, 2 * head_cols :],
        of_dp(head_own[:head_cols], query_bias.shape),
        of_dp(head_own[2 * head_cols : 3 * head_cols], value_bias.shape),
        out_grad,
        vec_of(0),
        vec_of(1),
        vec_of(2),
        cquery_grad,
        of_mp(head_sums[0], crossq_bias.shape),
        key_grad,
        value_grad,
        lax.dynamic_slice_in_dim(vec_of(9), mp * wide_rows, wide_rows, 0),
        cout_grad,
        vec_of(3),
        vec_of(4),
        vec_of(5),
        expand_grad,
        of_mp(head_sums[2:], expand_bias.shape),
        shrink_grad,
        vec_of(6),
        vec_of(7),
        vec_of(8),
    )


def solution(mesh):
    placed = (
        P(DP, None, None),
        P(DP, None),
        P(DP, None),
        P(DP, MP, None),
        P(DP),
        P(DP, MP),
        P(DP, MP),
        P(DP, MP),
        P(MP, DP),
        P(MP, DP),
        P(MP, DP),
        P(DP),
        P(DP),
        P(DP),
        P(DP, MP),
        P(MP, DP),
        P((DP, MP), None),
        P((DP, MP), None),
        P((DP, MP)),
        P(MP, DP),
        P(DP),
        P(DP),
        P(DP),
        P(DP, MP),
        P(MP, DP),
        P(MP, DP),
        P(DP),
        P(DP),
        P(DP),
        P(MP, DP),
    )
    return jax.shard_map(
        local,
        mesh=mesh,
        in_specs=placed,
        out_specs=(
            P(DP),
            P(DP, None, None),
            P(DP, MP, None),
            P(DP, MP),
            P(DP, MP),
            P(DP, MP),
            P(MP, DP),
            P(MP, DP),
            P(MP, DP),
            P(DP),
            P(DP),
            P(DP),
            P(DP, MP),
            P(MP, DP),
            P((DP, MP), None),
            P((DP, MP), None),
            P((DP, MP)),
            P(MP, DP),
            P(DP),
            P(DP),
            P(DP),
            P(DP, MP),
            P(MP, DP),
            P(MP, DP),
            P(DP),
            P(DP),
            P(DP),
        ),
        check_vma=False,
    )
```
